32 devices in a mesh: dp: 8 (over y, x, core), mp: 4 (over z).
Axes of the slice: x: 2, y: 2, z: 4, core: 2. Of those that a mesh axis runs over, the one named last changes fastest.
Arguments:
- word_inputs: bfloat16 [8, 1024, 512], P('dp'), may hold values from -6 to 6
- character_embeddings: bfloat16 [160, 128, 16, 256], P('dp', 'mp'), may hold values from -6 to 6
- cotangent: bfloat16 [8, 1024, 512], P('dp'), may hold values from -6 to 6
- char_count: int32 [160, 128], P('dp', 'mp'), may hold values from 1 to 16, as said below
- word_place: int32 [160, 128], P('dp'), may hold values from -1 to 1023, as said below
- block_home: int32 [160], P('dp'), may hold values from -1 to 7, as said below
- documents: int32 [8, 1024], P('dp'), may hold values from 0 to 5, never falling along the last dimension, each value on 1 to 512 neighbouring positions
- char_gain: float32 [256], replicated, may hold values from 0.5 to 1.5
- word_gains: float32 [2, 512], replicated, may hold values from 0.5 to 1.5
- char_mixer: float32 [4, 256, 256], P(None, 'dp'), may hold values from -0.375 to 0.375
- char_mixer_left: float32 [4, 256, 256], P(None, 'dp'), as said below
- char_mixer_right: float32 [4, 256, 256], P(None, 'dp'), as said below
- char_mixer_left_root: float32 [4, 256, 256], P(None, 'dp'), as said below
- char_mixer_right_root: float32 [4, 256, 256], P(None, 'dp'), as said below
- char_lift: float32 [1, 256, 512], P(None, 'dp'), may hold values from -0.375 to 0.375
- char_lift_left: float32 [1, 256, 256], P(None, 'dp'), as said below
- char_lift_right: float32 [1, 512, 512], P(None, 'dp'), as said below
- char_lift_left_root: float32 [1, 256, 256], P(None, 'dp'), as said below
- char_lift_right_root: float32 [1, 512, 512], P(None, 'dp'), as said below
- word_project: float32 [3, 4, 512, 128], P(None, 'mp', 'dp'), may hold values from -0.25 to 0.25
- word_project_left: float32 [3, 4, 512, 512], P(None, 'mp', 'dp'), as said below
- word_project_right: float32 [3, 4, 128, 128], P(None, 'mp', 'dp'), as said below
- word_project_left_root: float32 [3, 4, 512, 512], P(None, 'mp', 'dp'), as said below
- word_project_right_root: float32 [3, 4, 128, 128], P(None, 'mp', 'dp'), as said below
- word_output: float32 [4, 128, 512], P('mp', 'dp'), may hold values from -1 to 1
- word_output_left: float32 [4, 128, 128], P('mp', 'dp'), as said below
- word_output_right: float32 [4, 512, 512], P('mp', 'dp'), as said below
- word_output_left_root: float32 [4, 128, 128], P('mp', 'dp'), as said below
- word_output_right_root: float32 [4, 512, 512], P('mp', 'dp'), as said below
- feed_upper: float32 [4, 512, 512], P('mp', 'dp'), may hold values from -0.25 to 0.25
- feed_upper_left: float32 [4, 512, 512], P('mp', 'dp'), as said below
- feed_upper_right: float32 [4, 512, 512], P('mp', 'dp'), as said below
- feed_upper_left_root: float32 [4, 512, 512], P('mp', 'dp'), as said below
- feed_upper_right_root: float32 [4, 512, 512], P('mp', 'dp'), as said below
- feed_lower: float32 [4, 512, 512], P('mp', 'dp'), may hold values from -0.125 to 0.125
- feed_lower_left: float32 [4, 512, 512], P('mp', 'dp'), as said below
- feed_lower_right: float32 [4, 512, 512], P('mp', 'dp'), as said below
- feed_lower_left_root: float32 [4, 512, 512], P('mp', 'dp'), as said below
- feed_lower_right_root: float32 [4, 512, 512], P('mp', 'dp'), as said below
Outputs:
- block_out: bfloat16 [8, 1024, 512], P('dp')
- word_inputs_gradient: bfloat16 [8, 1024, 512], P('dp')
- char_embeds_gradient: bfloat16 [160, 128, 16, 256], P('dp', 'mp')
- char_gain_gradient: float32 [256], replicated
- word_gains_gradient: float32 [2, 512], replicated
- char_gain_new: float32 [256], replicated
- word_gains_new: float32 [2, 512], replicated
- global_norm: float32 [], replicated
- char_mixer_gradient: float32 [4, 256, 256], P(None, 'dp')
- char_mixer_left_new: float32 [4, 256, 256], P(None, 'dp')
- char_mixer_right_new: float32 [4, 256, 256], P(None, 'dp')
- char_mixer_new: float32 [4, 256, 256], P(None, 'dp')
- char_mixer_copy: bfloat16 [4, 256, 256], P(None, 'dp')
- char_lift_gradient: float32 [1, 256, 512], P(None, 'dp')
- char_lift_left_new: float32 [1, 256, 256], P(None, 'dp')
- char_lift_right_new: float32 [1, 512, 512], P(None, 'dp')
- char_lift_new: float32 [1, 256, 512], P(None, 'dp')
- char_lift_copy: bfloat16 [1, 256, 512], P(None, 'dp')
- word_project_gradient: float32 [3, 4, 512, 128], P(None, 'mp', 'dp')
- word_project_left_new: float32 [3, 4, 512, 512], P(None, 'mp', 'dp')
- word_project_right_new: float32 [3, 4, 128, 128], P(None, 'mp', 'dp')
- word_project_new: float32 [3, 4, 512, 128], P(None, 'mp', 'dp')
- word_project_copy: bfloat16 [3, 4, 512, 128], P(None, 'mp', 'dp')
- word_output_gradient: float32 [4, 128, 512], P('mp', 'dp')
- word_output_left_new: float32 [4, 128, 128], P('mp', 'dp')
- word_output_right_new: float32 [4, 512, 512], P('mp', 'dp')
- word_output_new: float32 [4, 128, 512], P('mp', 'dp')
- word_output_copy: bfloat16 [4, 128, 512], P('mp', 'dp')
- feed_upper_gradient: float32 [4, 512, 512], P('mp', 'dp')
- feed_upper_left_new: float32 [4, 512, 512], P('mp', 'dp')
- feed_upper_right_new: float32 [4, 512, 512], P('mp', 'dp')
- feed_upper_new: float32 [4, 512, 512], P('mp', 'dp')
- feed_upper_copy: bfloat16 [4, 512, 512], P('mp', 'dp')
- feed_lower_gradient: float32 [4, 512, 512], P('mp', 'dp')
- feed_lower_left_new: float32 [4, 512, 512], P('mp', 'dp')
- feed_lower_right_new: float32 [4, 512, 512], P('mp', 'dp')
- feed_lower_new: float32 [4, 512, 512], P('mp', 'dp')
- feed_lower_copy: bfloat16 [4, 512, 512], P('mp', 'dp')
The draws below stay inside these ranges and needn't reach their ends.
Inputs may be any that keep to these rules, and one draw needn't show every extreme that they name: Slots s of index i of dp are i * 20 to (i + 1) * 20 - 1; block_home names the owner of the block in a slot, -1 an empty slot; the live slots of an index come first. Each owner has exactly 10 blocks in all; no index holds more than 3 blocks of one owner, and some index does; some index has all 20 slots live. word_place is -1 on empty places and empty slots; over the slots of one owner each of its 1024 places appears exactly once. `char_count`: within one block all counts lie in one range (k - 1) * 4 + 1 to k * 4 for some k of 1 to 4. `char_mixer_left`: statistics of the previous step. `char_mixer_right`: statistics of the previous step. `char_mixer_left_root`: inverse roots of earlier statistics. `char_mixer_right_root`: inverse roots of earlier statistics. `char_lift_left`: statistics of the previous step. `char_lift_right`: statistics of the previous step. `char_lift_left_root`: inverse roots of earlier statistics. `char_lift_right_root`: inverse roots of earlier statistics. `word_project_left`: statistics of the previous step. `word_project_right`: statistics of the previous step. `word_project_left_root`: inverse roots of earlier statistics. `word_project_right_root`: inverse roots of earlier statistics. `word_output_left`: statistics of the previous step. `word_output_right`: statistics of the previous step. `word_output_left_root`: inverse roots of earlier statistics. `word_output_right_root`: inverse roots of earlier statistics. `feed_upper_left`: statistics of the previous step. `feed_upper_right`: statistics of the previous step. `feed_upper_left_root`: inverse roots of earlier statistics. `feed_upper_right_root`: inverse roots of earlier statistics. `feed_lower_left`: statistics of the previous step. `feed_lower_right`: statistics of the previous step. `feed_lower_left_root`: inverse roots of earlier statistics. `feed_lower_right_root`: inverse roots of earlier statistics.
All inputs are finite; a program needn't handle non-finite values.
Results may differ from the reference program's by a relative error of at most 0.024.
Values may be sent and summed in bfloat16 or wider, within the bound.
A program may use at most 256 MiB of HBM per device.

```python
import math
import jax
import jax.numpy as jnp
import numpy as np
from jax import lax

D = 512
HD = 64
FF = 2048
CHAR_BLOCK_WIDTH = 256
CHEADS = 4
CHD = 64
WORD_CHAR_SPOTS = 16
BLOCK_WORD_SPOTS = 128
LEN = 1024
SEGS = 6
ROWS = 8
WORDS_DEV = 1024
OWN_BLK = 10
CAP = 20
SLOT_TOTAL_COUNT = 160
HB = 128
HPB = 2
FB = 512
N_DP = 8
N_MP = 4


def slot_layout(key):
    half_count = N_DP // 2
    steps_from = jnp.arange(half_count, dtype=jnp.int32)
    excess = OWN_BLK * (half_count - steps_from) // half_count
    ordered_loads = jnp.concatenate([OWN_BLK + excess, OWN_BLK - excess])
    shuffle = jax.random.permutation(jax.random.fold_in(key, 11), N_DP)
    loads = jnp.zeros((N_DP,), jnp.int32).at[shuffle].set(ordered_loads.astype(jnp.int32))
    starts = jnp.cumsum(loads) - loads
    slot_number = jnp.arange(CAP, dtype=jnp.int32)
    living = slot_number[None, :] < loads[:, None]
    serial = starts[:, None] + slot_number[None, :]
    offset = jax.random.randint(jax.random.fold_in(key, 12), (), 0, N_DP)
    home = jnp.where(living, (serial + offset) % N_DP, -1).astype(jnp.int32)
    owner_block = jnp.minimum(serial // N_DP, OWN_BLK - 1)
    owner_keys = jax.random.split(jax.random.fold_in(key, 13), N_DP)
    orders = jax.vmap(lambda one_key: jax.random.permutation(one_key, OWN_BLK * BLOCK_WORD_SPOTS))(owner_keys).astype(jnp.int32)
    lanes = jnp.arange(BLOCK_WORD_SPOTS, dtype=jnp.int32)
    flat_index = owner_block[..., None] * BLOCK_WORD_SPOTS + lanes
    chosen = orders[jnp.maximum(home, 0)[..., None], flat_index]
    position = jnp.where(living[..., None] & (chosen < WORDS_DEV), chosen, -1).astype(jnp.int32)
    return (home.reshape(N_DP * CAP), position.reshape(N_DP * CAP, BLOCK_WORD_SPOTS))


def draw_block_home(key, part):
    return slot_layout(jax.random.fold_in(key, 5))[0]


def draw_word_place(key, part):
    return slot_layout(jax.random.fold_in(key, 5))[1]


def draw_char_count(key, part):
    quarter_part = WORD_CHAR_SPOTS // 4
    bucket_group = jax.random.randint(jax.random.fold_in(key, 1), (SLOT_TOTAL_COUNT, 1), 0, 4)
    bucket_group = bucket_group.at[0, 0].set(3)
    within_block = jax.random.randint(jax.random.fold_in(key, 2), (SLOT_TOTAL_COUNT, BLOCK_WORD_SPOTS), 1, quarter_part + 1)
    counts = bucket_group * quarter_part + within_block
    return counts.at[0, 0].set(WORD_CHAR_SPOTS).astype(jnp.int32)


def square_stat(key, lead, size, level):
    spread = jax.random.uniform(jax.random.fold_in(key, 1), lead + (size,), jnp.float32, 0.0, 1.0)
    diagonal = level * jnp.exp(spread * math.log(4.0))
    noise = jax.random.normal(jax.random.fold_in(key, 2), lead + (size, size), jnp.float32) * (0.3 * level / math.sqrt(size))
    return (noise + jnp.eye(size, dtype=jnp.float32) * diagonal[..., None]).astype(jnp.float32)


def root_stat(key, lead, size, level):
    spread = jax.random.uniform(jax.random.fold_in(key, 3), lead + (size,), jnp.float32, -1.0, 1.0)
    diagonal = level * jnp.exp(spread * math.log(2.0))
    noise = jax.random.normal(jax.random.fold_in(key, 4), lead + (size, size), jnp.float32) * (0.25 * level / math.sqrt(size))
    return (noise + jnp.eye(size, dtype=jnp.float32) * diagonal[..., None]).astype(jnp.float32)


def draw_char_mixer_left(key, part):
    return square_stat(jax.random.fold_in(key, 21), (4,), CHAR_BLOCK_WIDTH, CHAR_BLOCK_WIDTH / 4.0)


def draw_char_mixer_right(key, part):
    return square_stat(jax.random.fold_in(key, 22), (4,), CHAR_BLOCK_WIDTH, CHAR_BLOCK_WIDTH / 4.0)


def draw_char_mixer_left_root(key, part):
    return root_stat(jax.random.fold_in(key, 23), (4,), CHAR_BLOCK_WIDTH, (CHAR_BLOCK_WIDTH / 4.0) ** (-0.25))


def draw_char_mixer_right_root(key, part):
    return root_stat(jax.random.fold_in(key, 24), (4,), CHAR_BLOCK_WIDTH, (CHAR_BLOCK_WIDTH / 4.0) ** (-0.25))


def draw_char_lift_left(key, part):
    return square_stat(jax.random.fold_in(key, 25), (1,), CHAR_BLOCK_WIDTH, D / 4.0)


def draw_char_lift_right(key, part):
    return square_stat(jax.random.fold_in(key, 26), (1,), D, CHAR_BLOCK_WIDTH / 4.0)


def draw_char_lift_left_root(key, part):
    return root_stat(jax.random.fold_in(key, 27), (1,), CHAR_BLOCK_WIDTH, (D / 4.0) ** (-0.25))


def draw_char_lift_right_root(key, part):
    return root_stat(jax.random.fold_in(key, 28), (1,), D, (CHAR_BLOCK_WIDTH / 4.0) ** (-0.25))


def draw_word_project_left(key, part):
    return square_stat(jax.random.fold_in(key, 29), (3, N_MP), D, HB / 4.0)


def draw_word_project_right(key, part):
    return square_stat(jax.random.fold_in(key, 30), (3, N_MP), HB, D / 4.0)


def draw_word_project_left_root(key, part):
    return root_stat(jax.random.fold_in(key, 31), (3, N_MP), D, (HB / 4.0) ** (-0.25))


def draw_word_project_right_root(key, part):
    return root_stat(jax.random.fold_in(key, 32), (3, N_MP), HB, (D / 4.0) ** (-0.25))


def draw_word_output_left(key, part):
    return square_stat(jax.random.fold_in(key, 33), (N_MP,), HB, D / 4.0)


def draw_word_output_right(key, part):
    return square_stat(jax.random.fold_in(key, 34), (N_MP,), D, HB / 4.0)


def draw_word_output_left_root(key, part):
    return root_stat(jax.random.fold_in(key, 35), (N_MP,), HB, (D / 4.0) ** (-0.25))


def draw_word_output_right_root(key, part):
    return root_stat(jax.random.fold_in(key, 36), (N_MP,), D, (HB / 4.0) ** (-0.25))


def draw_feed_upper_left(key, part):
    return square_stat(jax.random.fold_in(key, 37), (N_MP,), D, FB / 4.0)


def draw_feed_upper_right(key, part):
    return square_stat(jax.random.fold_in(key, 38), (N_MP,), FB, D / 4.0)


def draw_feed_upper_left_root(key, part):
    return root_stat(jax.random.fold_in(key, 39), (N_MP,), D, (FB / 4.0) ** (-0.25))


def draw_feed_upper_right_root(key, part):
    return root_stat(jax.random.fold_in(key, 40), (N_MP,), FB, (D / 4.0) ** (-0.25))


def draw_feed_lower_left(key, part):
    return square_stat(jax.random.fold_in(key, 41), (N_MP,), FB, D / 4.0)


def draw_feed_lower_right(key, part):
    return square_stat(jax.random.fold_in(key, 42), (N_MP,), D, FB / 4.0)


def draw_feed_lower_left_root(key, part):
    return root_stat(jax.random.fold_in(key, 43), (N_MP,), FB, (D / 4.0) ** (-0.25))


def draw_feed_lower_right_root(key, part):
    return root_stat(jax.random.fold_in(key, 44), (N_MP,), D, (FB / 4.0) ** (-0.25))


def block_levels(stream_key, extent, shards, low, largest):
    gain = 1.0
    for dim, blocks in shards:
        heights = jax.random.uniform(jax.random.fold_in(jax.random.fold_in(stream_key, 6), dim), (blocks,), jnp.float32, low / len(shards), largest / len(shards))
        gain = gain * jnp.repeat(jnp.exp(heights), extent[dim] // blocks).reshape((-1,) + (1,) * (len(extent) - 1 - dim))
    return gain


def split_up(amount, total, limit, lean):
    weights = [(1 << 20) // math.isqrt(rank ** lean) + 1 for rank in range(2, amount + 1)]
    spare, given = total - limit - (amount - 1), [1] * (amount - 1)
    while spare > 0:
        candidates = [i for i in range(amount - 1) if given[i] < limit]
        pool, budget = sum([weights[i] for i in candidates]), spare
        for i in candidates:
            addition = min(limit - given[i], max(1, budget * weights[i] // pool), spare)
            given[i] = given[i] + addition
            spare = spare - addition
    return np.array([limit] + given)


def ragged_sizes(stream_key, number_of, total, limit, lean):
    if number_of == 2:
        one = jax.random.randint(stream_key, (), max(1, total - limit), min(limit, total - 1) + 1)
        return jnp.stack([one, total - one])
    tallies = jnp.asarray(split_up(number_of, total, limit, lean), jnp.int32)
    pairs = (number_of - 1) // 2
    donor, taker = tallies[1:1 + 2 * pairs:2], tallies[2:2 + 2 * pairs:2]
    slack = jnp.minimum(donor - 1, limit - taker)
    passed = jax.random.randint(jax.random.fold_in(stream_key, 1), (pairs,), 0, 1 << 20) % (slack + 1)
    tallies = tallies.at[1:1 + 2 * pairs:2].set(donor - passed).at[2:2 + 2 * pairs:2].set(taker + passed)
    return tallies[jax.random.permutation(jax.random.fold_in(stream_key, 2), number_of)]


def centred(rng, shape, deviation, reach, cuts=(), kind=jnp.bfloat16):
    values = deviation * jax.random.normal(rng, shape, jnp.float32)
    if cuts:
        values = values * block_levels(rng, shape, cuts, -0.22, 0.18)
    return jnp.clip(values, -reach, reach).astype(kind)


def setup_inputs(seed: int = 0) -> dict:
    key_of = jax.random.split(jax.random.key(seed), 40)
    return {
        "word_inputs": centred(key_of[0], (ROWS, LEN, D), 1.0, 6.0, ((0, 8),)),
        "character_embeddings": centred(key_of[1], (SLOT_TOTAL_COUNT, BLOCK_WORD_SPOTS, WORD_CHAR_SPOTS, CHAR_BLOCK_WIDTH), 1.0, 6.0, ((0, 8), (1, 4))),
        "cotangent": centred(key_of[2], (ROWS, LEN, D), 1.0, 6.0, ((0, 8),)),
        "char_count": draw_char_count(jax.random.fold_in(key_of[39], 71), 0),
        "word_place": draw_word_place(jax.random.fold_in(key_of[39], 71), 0),
        "block_home": draw_block_home(jax.random.fold_in(key_of[39], 71), 0),
        "documents": jax.vmap(lambda own: jnp.searchsorted(jnp.cumsum(ragged_sizes(own, SEGS, LEN, LEN // 2, 1)), jnp.arange(LEN), side="right"))(jax.random.split(key_of[6], ROWS)).reshape((ROWS, LEN)).astype(jnp.int32),
        "char_gain": jnp.clip(1.0 + 0.1 * jax.random.normal(key_of[7], (CHAR_BLOCK_WIDTH,), jnp.float32), 0.5, 1.5),
        "word_gains": jnp.clip(1.0 + 0.1 * jax.random.normal(key_of[8], (2, D), jnp.float32), 0.5, 1.5),
        "char_mixer": centred(key_of[9], (4, CHAR_BLOCK_WIDTH, CHAR_BLOCK_WIDTH), CHAR_BLOCK_WIDTH ** -0.5, 0.375, ((1, 8),), jnp.float32),
        "char_mixer_left": draw_char_mixer_left(jax.random.fold_in(key_of[39], 71), 0),
        "char_mixer_right": draw_char_mixer_right(jax.random.fold_in(key_of[39], 71), 0),
        "char_mixer_left_root": draw_char_mixer_left_root(jax.random.fold_in(key_of[39], 71), 0),
        "char_mixer_right_root": draw_char_mixer_right_root(jax.random.fold_in(key_of[39], 71), 0),
        "char_lift": centred(key_of[14], (1, CHAR_BLOCK_WIDTH, D), CHAR_BLOCK_WIDTH ** -0.5, 0.375, ((1, 8),), jnp.float32),
        "char_lift_left": draw_char_lift_left(jax.random.fold_in(key_of[39], 71), 0),
        "char_lift_right": draw_char_lift_right(jax.random.fold_in(key_of[39], 71), 0),
        "char_lift_left_root": draw_char_lift_left_root(jax.random.fold_in(key_of[39], 71), 0),
        "char_lift_right_root": draw_char_lift_right_root(jax.random.fold_in(key_of[39], 71), 0),
        "word_project": centred(key_of[19], (3, N_MP, D, HB), D ** -0.5, 0.25, ((1, 4), (2, 8)), jnp.float32),
        "word_project_left": draw_word_project_left(jax.random.fold_in(key_of[39], 71), 0),
        "word_project_right": draw_word_project_right(jax.random.fold_in(key_of[39], 71), 0),
        "word_project_left_root": draw_word_project_left_root(jax.random.fold_in(key_of[39], 71), 0),
        "word_project_right_root": draw_word_project_right_root(jax.random.fold_in(key_of[39], 71), 0),
        "word_output": centred(key_of[24], (N_MP, HB, D), (D // 16) ** -0.5, 1.0, ((0, 4), (1, 8)), jnp.float32),
        "word_output_left": draw_word_output_left(jax.random.fold_in(key_of[39], 71), 0),
        "word_output_right": draw_word_output_right(jax.random.fold_in(key_of[39], 71), 0),
        "word_output_left_root": draw_word_output_left_root(jax.random.fold_in(key_of[39], 71), 0),
        "word_output_right_root": draw_word_output_right_root(jax.random.fold_in(key_of[39], 71), 0),
        "feed_upper": centred(key_of[29], (N_MP, D, FB), D ** -0.5, 0.25, ((0, 4), (1, 8)), jnp.float32),
        "feed_upper_left": draw_feed_upper_left(jax.random.fold_in(key_of[39], 71), 0),
        "feed_upper_right": draw_feed_upper_right(jax.random.fold_in(key_of[39], 71), 0),
        "feed_upper_left_root": draw_feed_upper_left_root(jax.random.fold_in(key_of[39], 71), 0),
        "feed_upper_right_root": draw_feed_upper_right_root(jax.random.fold_in(key_of[39], 71), 0),
        "feed_lower": centred(key_of[34], (N_MP, FB, D), FF ** -0.5, 0.125, ((0, 4), (1, 8)), jnp.float32),
        "feed_lower_left": draw_feed_lower_left(jax.random.fold_in(key_of[39], 71), 0),
        "feed_lower_right": draw_feed_lower_right(jax.random.fold_in(key_of[39], 71), 0),
        "feed_lower_left_root": draw_feed_lower_left_root(jax.random.fold_in(key_of[39], 71), 0),
        "feed_lower_right_root": draw_feed_lower_right_root(jax.random.fold_in(key_of[39], 71), 0),
    }


epsilon = 1e-05
decay_rate = 0.5
learn_rate = 1.0
gain_rate = 0.4
highest = lax.Precision.HIGHEST
negative_big = -1e+30

@jax.custom_vjp
def low(v):
    return lax.optimization_barrier(v.astype(jnp.bfloat16)).astype(jnp.float32)

@jax.custom_vjp
def low_back(v):
    return v

def low_keep(v):
    return (low(v), None)

def low_pass(kept, grad):
    return (grad,)

def back_keep(v):
    return (v, None)

def back_low(kept, grad):
    return (low(grad),)
low.defvjp(low_keep, low_pass)
low_back.defvjp(back_keep, back_low)

def product(left_mat, right_mat):
    return jnp.matmul(left_mat, right_mat, precision=highest)

def rms_normed(values, gain_row):
    return values * lax.rsqrt(lax.optimization_barrier(jnp.mean(values * values, axis=-1, keepdims=True)) + epsilon) * gain_row

def rounded_both(values):
    return low_back(low(values))

def rounded_copy(master):
    return lax.optimization_barrier(master.astype(jnp.bfloat16)).astype(jnp.float32)

def char_block(char_rows, counts, gain_char, mixer_mats, lift_mats):
    normed = low(rms_normed(char_rows, gain_char))
    split_shape = (BLOCK_WORD_SPOTS, WORD_CHAR_SPOTS, CHEADS, CHD)
    queries = rounded_both(product(normed, mixer_mats[0])).reshape(split_shape)
    keys_all = rounded_both(product(normed, mixer_mats[1])).reshape(split_shape)
    values_all = rounded_both(product(normed, mixer_mats[2])).reshape(split_shape)
    scores = low_back(jnp.einsum('wqhe,wkhe->whqk', queries, keys_all, precision=highest) / math.sqrt(CHD))
    visible = lax.broadcasted_iota(jnp.int32, (BLOCK_WORD_SPOTS, WORD_CHAR_SPOTS), 1) < counts[:, None]
    attention = low(jax.nn.softmax(jnp.where(visible[:, None, None, :], scores, negative_big), axis=-1))
    mixed_rows = rounded_both(jnp.einsum('whqk,wkhe->wqhe', attention, values_all, precision=highest).reshape(BLOCK_WORD_SPOTS, WORD_CHAR_SPOTS, CHAR_BLOCK_WIDTH))
    summed = char_rows + low_back(product(mixed_rows, mixer_mats[3]))
    pooled_sum = lax.optimization_barrier(jnp.sum(jnp.where(visible[:, :, None], summed, 0.0), axis=1))
    pooled = low(pooled_sum / counts[:, None].astype(pooled_sum.dtype))
    return rounded_both(product(pooled, lift_mats[0]))

def word_row(stream, segment_row, gains_word, project_mats, output_mats, upper_mats, lower_mats):
    normed_one = low(rms_normed(stream, gains_word[0]))
    query_at = lax.broadcasted_iota(jnp.int32, (LEN, LEN), 0)
    key_at = lax.broadcasted_iota(jnp.int32, (LEN, LEN), 1)
    allowed = (key_at <= query_at) & (segment_row[None, :] == segment_row[:, None])
    split_shape = (LEN, HPB, HD)
    attend_total = jnp.zeros_like(stream)
    for block_number in range(N_MP):
        own_rows = low_back(normed_one)
        queries = rounded_both(product(own_rows, project_mats[0, block_number])).reshape(split_shape)
        keys_all = rounded_both(product(own_rows, project_mats[1, block_number])).reshape(split_shape)
        values_all = rounded_both(product(own_rows, project_mats[2, block_number])).reshape(split_shape)
        scores = low_back(jnp.einsum('qhe,khe->hqk', queries, keys_all, precision=highest) / math.sqrt(HD))
        attention = low(jax.nn.softmax(jnp.where(allowed[None], scores, negative_big), axis=-1))
        mixed_rows = rounded_both(jnp.einsum('hqk,khe->qhe', attention, values_all, precision=highest).reshape(LEN, HB))
        attend_total = attend_total + low(product(mixed_rows, output_mats[block_number]))
    hidden = stream + low_back(attend_total)
    normed_two = low(rms_normed(hidden, gains_word[1]))
    feed_total = jnp.zeros_like(stream)
    for block_number in range(N_MP):
        own_rows = low_back(normed_two)
        upper_rows = low_back(product(own_rows, upper_mats[block_number]))
        active = low(jax.nn.gelu(upper_rows, approximate=True))
        feed_total = feed_total + low(product(active, lower_mats[block_number]))
    return hidden + low_back(feed_total)

def shampoo(master, gradient, left_stat, right_stat, left_root, right_root, factor):
    clipped = gradient * factor
    left_new = decay_rate * left_stat + (1.0 - decay_rate) * jnp.einsum('...mn,...kn->...mk', clipped, clipped, precision=highest)
    right_new = decay_rate * right_stat + (1.0 - decay_rate) * jnp.einsum('...mn,...mk->...nk', clipped, clipped, precision=highest)
    fresh_master = master - learn_rate * product(product(left_root, clipped), right_root)
    return (clipped, left_new, right_new, fresh_master, fresh_master.astype(jnp.bfloat16))

def reference(word_inputs, character_embeddings, cotangent, char_count, word_place, block_home, documents, char_gain, word_gains, char_mixer, char_mixer_left, char_mixer_right, char_mixer_left_root, char_mixer_right_root, char_lift, char_lift_left, char_lift_right, char_lift_left_root, char_lift_right_root, word_project, word_project_left, word_project_right, word_project_left_root, word_project_right_root, word_output, word_output_left, word_output_right, word_output_left_root, word_output_right_root, feed_upper, feed_upper_left, feed_upper_right, feed_upper_left_root, feed_upper_right_root, feed_lower, feed_lower_left, feed_lower_right, feed_lower_left_root, feed_lower_right_root):

    def forward(word_stream, char_rows, gain_char, gains_word, mixer_mats, lift_mats, project_mats, output_mats, upper_mats, lower_mats):

        def char_step(pieces):
            return jax.checkpoint(char_block)(pieces[0], pieces[1], gain_char, mixer_mats, lift_mats)
        word_vectors = lax.map(char_step, (char_rows, char_count))
        target = jnp.where(word_place >= 0, block_home[:, None] * WORDS_DEV + word_place, ROWS * LEN).astype(jnp.int32)
        placed = jnp.zeros((ROWS * LEN, D), word_stream.dtype).at[target.reshape(-1)].add(word_vectors.reshape(-1, D), mode='drop')
        stream = word_stream + placed.reshape(ROWS, LEN, D)

        def row_step(pieces):
            return jax.checkpoint(word_row)(pieces[0], pieces[1], gains_word, project_mats, output_mats, upper_mats, lower_mats)
        return lax.map(row_step, (stream, documents))
    masters = (char_mixer, char_lift, word_project, word_output, feed_upper, feed_lower)
    primals = (word_inputs.astype(jnp.float32), character_embeddings.astype(jnp.float32), char_gain, word_gains) + tuple((rounded_copy(w) for w in masters))
    result, pullback = jax.vjp(forward, *primals)
    gradients = pullback(cotangent.astype(jnp.float32))
    learned = gradients[2:]
    squares = sum((jnp.sum(g * g) for g in learned))
    threshold = 0.5 * math.sqrt(sum((g.size for g in learned)))
    global_norm = jnp.sqrt(squares)
    factor = jnp.minimum(1.0, threshold / global_norm)
    mixer_out = shampoo(char_mixer, gradients[4], char_mixer_left, char_mixer_right, char_mixer_left_root, char_mixer_right_root, factor)
    lift_out = shampoo(char_lift, gradients[5], char_lift_left, char_lift_right, char_lift_left_root, char_lift_right_root, factor)
    project_out = shampoo(word_project, gradients[6], word_project_left, word_project_right, word_project_left_root, word_project_right_root, factor)
    output_out = shampoo(word_output, gradients[7], word_output_left, word_output_right, word_output_left_root, word_output_right_root, factor)
    upper_out = shampoo(feed_upper, gradients[8], feed_upper_left, feed_upper_right, feed_upper_left_root, feed_upper_right_root, factor)
    lower_out = shampoo(feed_lower, gradients[9], feed_lower_left, feed_lower_right, feed_lower_left_root, feed_lower_right_root, factor)
    char_gain_clipped = factor * gradients[2]
    word_gains_clipped = factor * gradients[3]
    return (result.astype(jnp.bfloat16), gradients[0].astype(jnp.bfloat16), gradients[1].astype(jnp.bfloat16), char_gain_clipped, word_gains_clipped, char_gain - gain_rate * char_gain_clipped, word_gains - gain_rate * word_gains_clipped, global_norm, mixer_out[0], mixer_out[1], mixer_out[2], mixer_out[3], mixer_out[4], lift_out[0], lift_out[1], lift_out[2], lift_out[3], lift_out[4], project_out[0], project_out[1], project_out[2], project_out[3], project_out[4], output_out[0], output_out[1], output_out[2], output_out[3], output_out[4], upper_out[0], upper_out[1], upper_out[2], upper_out[3], upper_out[4], lower_out[0], lower_out[1], lower_out[2], lower_out[3], lower_out[4])
```

```python
import functools
import math

import jax
import jax.numpy as jnp
from jax import lax
from jax.experimental import pallas as pl
from jax.experimental.pallas import tpu as pltpu
from jax.sharding import PartitionSpec as P

D = 512
HD = 64
FF = 2048
CHAR_BLOCK_WIDTH = 256
OWNER_BLOCKS = 10
decay_rate = 0.5
learn_rate = 1.0
gain_rate = 0.4
negative_big = -1e30

CW = 256
CHEADS = 4
CHD = 64
SPOTS = 16
KEPT = 3 * CW + CHEADS * 128 + CW
epsilon = 1e-05
BF = jnp.bfloat16
F32 = jnp.float32


def nn(a, b):
    return lax.dot_general(a, b, (((1,), (0,)), ((), ())), preferred_element_type=F32)


def nt(a, b):
    return lax.dot_general(a, b, (((1,), (1,)), ((), ())), preferred_element_type=F32)


def tn(a, b):
    return lax.dot_general(a, b, (((0,), (0,)), ((), ())), preferred_element_type=F32)


def char_classes(share):
    listed = [(1, 4, 32), (2, 8, 16), (4, 16, 8)]
    return [c for c in listed if c[2] <= share]


def order_matrix(places, words):
    row = lax.broadcasted_iota(jnp.int32, (128, SPOTS * words), 0)
    col = lax.broadcasted_iota(jnp.int32, (128, SPOTS * words), 1)
    return ((row % words) * SPOTS + row // words == col).astype(BF)


def head_stack(rows, scale):
    lane = lax.broadcasted_iota(jnp.int32, (1, CW), 1) // CHD
    return jnp.concatenate(
        [rows * jnp.where(lane == h, scale, 0.0).astype(BF) for h in range(CHEADS)], axis=0
    )


def char_forward_kernel(
    classes, kind, x_ref, count_ref, gain_ref, mats_ref, *refs
):
    orders = refs[: len(classes)]
    vec_ref, kept_ref, pooled_ref, msum_ref, sumx, counts = refs[len(classes) :]
    step = pl.program_id(0)
    share = count_ref.shape[1]
    own = pl.ds(pl.multiple_of(step * share, share), share)
    counts[own, :] = count_ref[0]

    @pl.when(kind[step] == 0)
    def _():
        sumx[own, :] = jnp.zeros((share, CW), F32)
        msum_ref[own, :] = jnp.zeros((share, CW), F32)

    def block(places, words, order_ref):
        groups = share // words
        kept_x = []
        normed = []
        for g in range(groups):
            x = nn(order_ref[...], x_ref[0, pl.ds(g * words * SPOTS, words * SPOTS), :])
            scale = lax.rsqrt(jnp.mean(x * x, axis=-1, keepdims=True) + epsilon)
            normed.append((x * scale * gain_ref[...]).astype(BF))
            cnt = count_ref[0, pl.ds(g * words, words), :]
            cnt2 = jnp.concatenate([cnt, cnt], axis=1)
            place = lax.broadcasted_iota(jnp.int32, (places, words, CW), 0).astype(F32)
            x3 = x.reshape(places, words, CW)
            sumx[pl.ds(pl.multiple_of(step * share + g * words, words), words), :] = jnp.sum(
                jnp.where(place < cnt2[None], x3, 0.0), axis=0
            )
        rows = groups * 128
        normed = jnp.concatenate(normed, axis=0) if groups > 1 else normed[0]
        for t in range(3):
            kept_ref[0, :rows, t * CW : (t + 1) * CW] = nn(
                normed, mats_ref[:, t * CW : (t + 1) * CW]
            ).astype(BF)
        lane = lax.broadcasted_iota(jnp.int32, (words, CHEADS * 128), 1) % 128
        word = lax.broadcasted_iota(jnp.int32, (words, CHEADS * 128), 0)
        mine = lane % words == word
        spot = (lane // words).astype(F32)
        head_row = lax.broadcasted_iota(jnp.int32, (CHEADS * 128, CW), 0) // 128
        head_col = lax.broadcasted_iota(jnp.int32, (CHEADS * 128, CW), 1) // CHD
        same_head = (head_row == head_col).astype(BF)
        for g in range(groups):
            at = g * 128
            q = kept_ref[0, at : at + 128, :CW]
            k = kept_ref[0, at : at + 128, CW : 2 * CW]
            v = kept_ref[0, at : at + 128, 2 * CW : 3 * CW]
            s = nt(k, head_stack(q, 1.0 / math.sqrt(CHD))).reshape(places, words, CHEADS * 128)
            cnt = count_ref[0, pl.ds(g * words, words), :]
            cnt4 = jnp.concatenate([cnt] * CHEADS, axis=1)
            place = lax.broadcasted_iota(jnp.int32, (places, words, CHEADS * 128), 0).astype(F32)
            s = jnp.where(place < cnt4[None], s, -1e30)
            e = jnp.exp(s - jnp.max(s, axis=0)[None])
            r = jnp.where(mine & (spot < cnt4), 1.0 / jnp.sum(e, axis=0), 0.0)
            p = (e * r[None]).astype(BF).reshape(128, CHEADS * 128)
            kept_ref[0, at : at + 128, 3 * CW : 3 * CW + CHEADS * 128] = p
            c = nn(p, same_head)
            kept_ref[0, at : at + 128, 3 * CW + CHEADS * 128 :] = c.astype(BF)
            msum_ref[pl.ds(pl.multiple_of(step * share + g * words, words), words), :] = jnp.sum(
                (c * v.astype(F32)).reshape(places, words, CW), axis=0
            )

    for (number, places, words), order_ref in zip(classes, orders):
        pl.when(kind[step] == number)(functools.partial(block, places, words, order_ref))

    @pl.when(step == pl.num_programs(0) - 1)
    def _():
        cnt2 = jnp.concatenate([counts[...]] * 2, axis=1)
        summed = sumx[...] + nn(msum_ref[...].astype(BF), mats_ref[:, 3 * CW : 4 * CW])
        pooled = (summed / cnt2).astype(BF)
        pooled_ref[...] = pooled
        vec_ref[...] = nn(pooled, mats_ref[:, 4 * CW :]).astype(BF)


def char_kind(block_home, char_count, share):
    places = jnp.max(char_count, axis=1)
    kind = jnp.where(places <= 8, 2, 4)
    if share >= 32:
        kind = jnp.where(places <= 4, 1, kind)
    return jnp.where(block_home >= 0, kind, 0).astype(jnp.int32)


def whole(shape):
    return pl.BlockSpec(shape, lambda i, *_: (0,) * len(shape))


def char_forward(x, kind, counts, gain, mats):
    slots, share = x.shape[:2]
    classes = char_classes(share)
    rows = share * SPOTS
    orders = [order_matrix(p, w) for _, p, w in classes]
    words_all = slots * share
    per_slot = lambda shape: pl.BlockSpec((1,) + shape, lambda i, *_: (i,) + (0,) * len(shape))
    return pl.pallas_call(
        functools.partial(char_forward_kernel, classes),
        grid_spec=pltpu.PrefetchScalarGridSpec(
            num_scalar_prefetch=1,
            grid=(slots,),
            in_specs=[
                per_slot((rows, CW)),
                per_slot((share, 128)),
                whole((1, CW)),
                whole(mats.shape),
            ]
            + [whole(o.shape) for o in orders],
            out_specs=[
                whole((words_all, D)),
                per_slot((rows, KEPT)),
                whole((words_all, CW)),
                whole((words_all, CW)),
            ],
            scratch_shapes=[
                pltpu.VMEM((words_all, CW), F32),
                pltpu.VMEM((words_all, 128), F32),
            ],
        ),
        out_shape=[
            jax.ShapeDtypeStruct((words_all, D), BF),
            jax.ShapeDtypeStruct((slots, rows, KEPT), BF),
            jax.ShapeDtypeStruct((words_all, CW), BF),
            jax.ShapeDtypeStruct((words_all, CW), F32),
        ],
        compiler_params=pltpu.CompilerParams(vmem_limit_bytes=40 << 20),
        cost_estimate=pl.CostEstimate(
            flops=slots * rows * CW * CW * 16, bytes_accessed=slots * rows * KEPT * 3, transcendentals=0
        ),
        name="char_forward",
    )(kind, x.reshape(slots, rows, CW), counts, gain.reshape(1, CW), mats, *orders)


def char_backward_kernel(
    classes, kind, x_ref, count_ref, kept_ref, all_counts_ref, gv_ref, pooled_ref, msum_ref,
    gain_ref, mats_ref, *refs
):
    orders = refs[: len(classes)]
    dx_ref, dqkv_ref, dout_ref, dlift_ref, dgain_ref, gp_all, gm_all, dh, normed_all = refs[len(classes) :]
    step = pl.program_id(0)
    share = count_ref.shape[1]
    base = step * share

    @pl.when(step == 0)
    def _():
        gv = gv_ref[...]
        cnt2 = jnp.concatenate([all_counts_ref[...]] * 2, axis=1)
        gp = nt(gv, mats_ref[:, 4 * CW :]) / cnt2
        gp_all[...] = gp
        gpb = gp.astype(BF)
        gm_all[...] = nt(gpb, mats_ref[:, 3 * CW : 4 * CW]).astype(BF).astype(F32)
        dlift_ref[...] = tn(pooled_ref[...], gv)
        dout_ref[...] = tn(msum_ref[...].astype(BF), gpb)
        dqkv_ref[...] = jnp.zeros_like(dqkv_ref)
        dgain_ref[...] = jnp.zeros_like(dgain_ref)

    @pl.when(kind[step] == 0)
    def _():
        dx_ref[...] = jnp.zeros_like(dx_ref)

    def block(places, words, order_ref):
        groups = share // words
        rows = groups * 128
        gain = gain_ref[...]
        xs = []
        scales = []
        gps = []
        for g in range(groups):
            at = g * 128
            x = nn(order_ref[...], x_ref[0, pl.ds(g * words * SPOTS, words * SPOTS), :])
            scale = lax.rsqrt(jnp.mean(x * x, axis=-1, keepdims=True) + epsilon)
            normed_all[at : at + 128, :] = (x * scale * gain).astype(BF)
            xs.append(x)
            scales.append(scale)
            mine = pl.ds(pl.multiple_of(base + g * words, words), words)
            cnt = count_ref[0, pl.ds(g * words, words), :]
            cnt2 = jnp.concatenate([cnt, cnt], axis=1)
            place = lax.broadcasted_iota(jnp.int32, (places, words, CW), 0).astype(F32)
            shown = place < cnt2[None]
            gps.append(jnp.where(shown, gp_all[mine, :][None], 0.0).reshape(128, CW))
            gm_word = gm_all[mine, :]
            gm = jnp.where(shown, gm_word[None], 0.0).reshape(128, CW).astype(BF)
            q = kept_ref[0, at : at + 128, :CW]
            k = kept_ref[0, at : at + 128, CW : 2 * CW]
            v = kept_ref[0, at : at + 128, 2 * CW : 3 * CW]
            p = kept_ref[0, at : at + 128, 3 * CW : 3 * CW + CHEADS * 128].astype(F32)
            c = kept_ref[0, at : at + 128, 3 * CW + CHEADS * 128 :].astype(F32)
            dp = nt(v, head_stack(gm, 1.0))
            p3 = p.reshape(places, words, CHEADS * 128)
            t = p3 * dp.reshape(places, words, CHEADS * 128)
            ds = (t - p3 * jnp.sum(t, axis=0)[None]).astype(BF).reshape(128, CHEADS * 128)
            eighth = 1.0 / math.sqrt(CHD)
            dk = nn(ds, head_stack(q, eighth))
            ds_rows = jnp.concatenate([ds[:, h * 128 : (h + 1) * 128] for h in range(CHEADS)], axis=0)
            dq = tn(ds_rows, head_stack(k, eighth))
            dv = (c.reshape(places, words, CW) * gm_word[None]).reshape(128, CW)
            dh[at : at + 128, :CW] = dq.astype(BF)
            dh[at : at + 128, CW : 2 * CW] = dk.astype(BF)
            dh[at : at + 128, 2 * CW :] = dv.astype(BF)
        grads = dh[:rows, :]
        dqkv_ref[...] += tn(normed_all[:rows, :], grads)
        dn_all = nt(grads, mats_ref[:, : 3 * CW])
        dgain = jnp.zeros((1, CW), F32)
        for g in range(groups):
            x, scale = xs[g], scales[g]
            dn = dn_all[g * 128 : (g + 1) * 128]
            xr = x * scale
            dgain = dgain + jnp.sum(xr * dn, axis=0, keepdims=True)
            w = dn * gain
            inner = jnp.mean(xr * w, axis=-1, keepdims=True)
            dx = gps[g] + scale * (w - xr * inner)
            dx_ref[0, pl.ds(g * words * SPOTS, words * SPOTS), :] = tn(
                order_ref[...], dx.astype(BF)
            ).astype(BF)
        dgain_ref[...] += dgain

    for (number, places, words), order_ref in zip(classes, orders):
        pl.when(kind[step] == number)(functools.partial(block, places, words, order_ref))


def char_backward(x, kind, counts, gain, mats, kept, pooled, msum, grad_vectors):
    slots, share = x.shape[:2]
    classes = char_classes(share)
    rows = share * SPOTS
    orders = [order_matrix(p, w) for _, p, w in classes]
    words_all = slots * share
    per_slot = lambda shape: pl.BlockSpec((1,) + shape, lambda i, *_: (i,) + (0,) * len(shape))
    dx, dqkv, dout, dlift, dgain = pl.pallas_call(
        functools.partial(char_backward_kernel, classes),
        grid_spec=pltpu.PrefetchScalarGridSpec(
            num_scalar_prefetch=1,
            grid=(slots,),
            in_specs=[
                per_slot((rows, CW)),
                per_slot((share, 128)),
                per_slot((rows, KEPT)),
                whole((words_all, 128)),
                whole((words_all, D)),
                whole((words_all, CW)),
                whole((words_all, CW)),
                whole((1, CW)),
                whole(mats.shape),
            ]
            + [whole(o.shape) for o in orders],
            out_specs=[
                per_slot((rows, CW)),
                whole((CW, 3 * CW)),
                whole((CW, CW)),
                whole((CW, D)),
                whole((1, CW)),
            ],
            scratch_shapes=[
                pltpu.VMEM((words_all, CW), F32),
                pltpu.VMEM((words_all, CW), F32),
                pltpu.VMEM((rows, 3 * CW), BF),
                pltpu.VMEM((rows, CW), BF),
            ],
        ),
        out_shape=[
            jax.ShapeDtypeStruct((slots, rows, CW), BF),
            jax.ShapeDtypeStruct((CW, 3 * CW), F32),
            jax.ShapeDtypeStruct((CW, CW), F32),
            jax.ShapeDtypeStruct((CW, D), F32),
            jax.ShapeDtypeStruct((1, CW), F32),
        ],
        compiler_params=pltpu.CompilerParams(vmem_limit_bytes=40 << 20),
        cost_estimate=pl.CostEstimate(
            flops=slots * rows * CW * CW * 28, bytes_accessed=slots * rows * KEPT * 3, transcendentals=0
        ),
        name="char_backward",
    )(
        kind, x.reshape(slots, rows, CW), counts, kept, counts.reshape(words_all, 128), grad_vectors,
        pooled, msum, gain.reshape(1, CW), mats, *orders,
    )
    return dx.reshape(x.shape), dqkv, dout, dlift, dgain


def norm_forward(values, gain_row):
    row_scale = lax.rsqrt(jnp.mean(values * values, axis=-1, keepdims=True) + epsilon)
    return (values * row_scale * gain_row, row_scale)


def norm_backward(values, row_scale, gain_row, grad_output):
    weighted = grad_output * gain_row
    row_inner = jnp.mean(values * weighted, axis=-1, keepdims=True)
    grad_values = row_scale * weighted - values * (row_scale * row_scale * row_scale) * row_inner
    return (grad_values, jnp.sum(values * row_scale * grad_output, axis=0))


def gelu_tanh(values):
    return jax.nn.gelu(values, approximate=True)


def word_softmax(row_queries, row_keys, query_docs, key_docs, first_row):
    scores = jnp.einsum(
        "qhe,khe->hqk", row_queries, row_keys, preferred_element_type=jnp.float32
    ) / math.sqrt(HD)
    table_shape = (row_queries.shape[0], row_keys.shape[0])
    query_at = first_row + lax.broadcasted_iota(jnp.int32, table_shape, 0)
    key_at = lax.broadcasted_iota(jnp.int32, table_shape, 1)
    allowed = (key_at <= query_at) & (key_docs[None, :] == query_docs[:, None])
    return jax.nn.softmax(jnp.where(allowed[None], scores, negative_big), axis=-1)


def word_attention(queries, keys_all, values_all, documents):
    length = queries.shape[1]
    block_rows = min(512, length)

    def one_row(pieces):
        row_queries, row_keys, row_values, row_docs = pieces
        outputs = []
        for first_row in range(0, length, block_rows):
            last_row = first_row + block_rows
            attention = word_softmax(
                row_queries[first_row:last_row],
                row_keys,
                row_docs[first_row:last_row],
                row_docs,
                first_row,
            )
            outputs.append(
                jnp.einsum(
                    "hqk,khe->qhe",
                    attention.astype(jnp.bfloat16),
                    row_values,
                    preferred_element_type=jnp.float32,
                ).astype(jnp.bfloat16)
            )
        return jnp.concatenate(outputs, axis=0)

    return lax.map(one_row, (queries, keys_all, values_all, documents))


def word_attention_back(queries, keys_all, values_all, grad_mixed, documents):
    length = queries.shape[1]
    block_rows = min(512, length)
    root_size = math.sqrt(HD)

    def one_row(pieces):
        row_queries, row_keys, row_values, row_grads, row_docs = pieces
        query_parts = []
        grad_keys = jnp.zeros(row_keys.shape, jnp.float32)
        grad_values = jnp.zeros(row_values.shape, jnp.float32)
        for first_row in range(0, length, block_rows):
            last_row = first_row + block_rows
            attention = word_softmax(
                row_queries[first_row:last_row],
                row_keys,
                row_docs[first_row:last_row],
                row_docs,
                first_row,
            )
            grad_attention = jnp.einsum(
                "qhe,khe->hqk",
                row_grads[first_row:last_row],
                row_values,
                preferred_element_type=jnp.float32,
            )
            row_inner = jnp.sum(attention * grad_attention, axis=-1, keepdims=True)
            grad_scores = (attention * (grad_attention - row_inner)).astype(jnp.bfloat16)
            query_parts.append(
                jnp.einsum(
                    "hqk,khe->qhe", grad_scores, row_keys, preferred_element_type=jnp.float32
                )
                / root_size
            )
            grad_keys = (
                grad_keys
                + jnp.einsum(
                    "hqk,qhe->khe",
                    grad_scores,
                    row_queries[first_row:last_row],
                    preferred_element_type=jnp.float32,
                )
                / root_size
            )
            grad_values = grad_values + jnp.einsum(
                "hqk,qhe->khe",
                attention.astype(jnp.bfloat16),
                row_grads[first_row:last_row],
                preferred_element_type=jnp.float32,
            )
        grad_queries = jnp.concatenate(query_parts, axis=0)
        return (
            grad_queries.astype(jnp.bfloat16),
            grad_keys.astype(jnp.bfloat16),
            grad_values.astype(jnp.bfloat16),
        )

    return lax.map(one_row, (queries, keys_all, values_all, grad_mixed, documents))


def pack(array):
    rows, cols = array.shape[-2:]
    if cols % 128:
        return array.reshape(-1, 128)
    split = array.reshape(-1, rows, cols // 128, 128)
    return split.transpose(0, 2, 1, 3).reshape(-1, 128)


def unpack(gathered, shapes):
    devices = gathered.shape[0]
    whole_ones = []
    first = 0
    for shape in shapes:
        lead, (rows, cols) = shape[:-2], shape[-2:]
        count = math.prod(shape) // 128
        piece = gathered[:, first : first + count]
        first += count
        if cols % 128:
            piece = piece.reshape(devices, -1, rows, cols).transpose(1, 0, 2, 3)
        else:
            piece = piece.reshape(devices, -1, cols // 128, rows, 128).transpose(1, 0, 3, 2, 4)
        whole_ones.append(piece.reshape(lead + (devices * rows, cols)))
    return whole_ones


def refresh(master, gradient, left_stat, right_stat, left_root, right_root, factor, owner_index):
    clipped = gradient * factor
    near = clipped.astype(BF)
    rows_own = master.shape[-2]
    cols_own = right_stat.shape[-2]
    own_rows = lax.dynamic_slice_in_dim(clipped, owner_index * rows_own, rows_own, clipped.ndim - 2)
    own_cols = lax.dynamic_slice_in_dim(near, owner_index * cols_own, cols_own, clipped.ndim - 1)
    left_new = decay_rate * left_stat + (1.0 - decay_rate) * jnp.einsum(
        "...mn,...kn->...mk", own_rows.astype(BF), near, preferred_element_type=F32
    )
    right_new = decay_rate * right_stat + (1.0 - decay_rate) * jnp.einsum(
        "...mn,...mk->...nk", own_cols, near, preferred_element_type=F32
    )
    half_step = jnp.matmul(left_root.astype(BF), near, preferred_element_type=F32)
    shampoo_step = jnp.matmul(half_step.astype(BF), right_root, preferred_element_type=F32)
    fresh_master = master - learn_rate * shampoo_step
    return (own_rows, left_new, right_new, fresh_master, fresh_master.astype(BF))


def local(
    word_inputs,
    character_embeddings,
    cotangent,
    char_count,
    word_place,
    block_home,
    documents,
    char_gain,
    word_gains,
    char_mixer,
    char_mixer_left,
    char_mixer_right,
    char_mixer_left_root,
    char_mixer_right_root,
    char_lift,
    char_lift_left,
    char_lift_right,
    char_lift_left_root,
    char_lift_right_root,
    word_project,
    word_project_left,
    word_project_right,
    word_project_left_root,
    word_project_right_root,
    word_output,
    word_output_left,
    word_output_right,
    word_output_left_root,
    word_output_right_root,
    feed_upper,
    feed_upper_left,
    feed_upper_right,
    feed_upper_left_root,
    feed_upper_right_root,
    feed_lower,
    feed_lower_left,
    feed_lower_right,
    feed_lower_left_root,
    feed_lower_right_root,
):
    slot_count, share_rows = (character_embeddings.shape[0], character_embeddings.shape[1])
    peer_count = lax.axis_size("dp")
    part_count = lax.axis_size("mp")
    owner_index = lax.axis_index("dp")
    pair_cap = -(-slot_count // peer_count)
    slot_total = peer_count * pair_cap
    rows_dev, length = (word_inputs.shape[0], word_inputs.shape[1])
    words_dev = rows_dev * length
    block_words = share_rows * part_count

    char_pack = jnp.concatenate(
        [char_mixer[0], char_mixer[1], char_mixer[2], char_mixer[3], char_lift[0]], axis=1
    ).astype(BF)
    char_whole = lax.all_gather(char_pack, "dp", axis=0, tiled=True)
    word_whole = lax.all_gather(
        jnp.concatenate([pack(w) for w in (word_project, word_output, feed_upper, feed_lower)]).astype(BF),
        "dp",
        axis=0,
    )
    project_mats, output_mats, upper_mats, lower_mats = unpack(
        word_whole, [w.shape for w in (word_project, word_output, feed_upper, feed_lower)]
    )
    roots = (
        char_mixer_right_root,
        char_lift_right_root,
        word_project_right_root,
        word_output_right_root,
        feed_upper_right_root,
        feed_lower_right_root,
    )
    root_whole = lax.all_gather(
        jnp.concatenate([pack(w) for w in roots]).astype(BF), "dp", axis=0
    )

    peers = lax.broadcasted_iota(jnp.int32, (slot_count, peer_count), 1)
    owner_match = (block_home[:, None] == peers).astype(jnp.int32)
    earlier = (
        lax.broadcasted_iota(jnp.int32, (slot_count, slot_count), 1)
        < lax.broadcasted_iota(jnp.int32, (slot_count, slot_count), 0)
    )
    same_owner = block_home[:, None] == block_home[None, :]
    slot_rank = jnp.sum((earlier & same_owner).astype(jnp.int32), axis=1)
    slot_target = jnp.where(block_home >= 0, block_home * pair_cap + slot_rank, slot_total)
    to_slot = lax.broadcasted_iota(jnp.int32, (slot_total, slot_count), 0) == slot_target[None, :]

    kind = char_kind(block_home, char_count, share_rows)
    counts = jnp.broadcast_to(
        char_count.astype(F32)[..., None], (slot_count, share_rows, 128)
    )
    word_vectors, kept, pooled, msum = char_forward(
        character_embeddings, kind, counts, char_gain, char_whole
    )

    sent_place = jnp.max(
        jnp.where(to_slot[:, :, None], word_place[None] + 1, 0), axis=1
    ) - 1
    came_place = lax.all_to_all(sent_place, "dp", split_axis=0, concat_axis=0, tiled=True)
    live = jnp.max(came_place, axis=1) >= 0
    slots_before = (
        lax.broadcasted_iota(jnp.int32, (slot_total, slot_total), 1)
        < lax.broadcasted_iota(jnp.int32, (slot_total, slot_total), 0)
    )
    live_rank = jnp.sum((slots_before & live[None, :]).astype(jnp.int32), axis=1)
    live_rank = jnp.where(live, live_rank, OWNER_BLOCKS)
    to_live = lax.broadcasted_iota(jnp.int32, (OWNER_BLOCKS, slot_total), 0) == live_rank[None, :]
    live_place = jnp.max(jnp.where(to_live[:, :, None], came_place[None] + 1, 0), axis=1) - 1

    wide = share_rows * D
    sent = jnp.dot(
        to_slot.astype(BF), word_vectors.reshape(slot_count, wide), preferred_element_type=F32
    ).astype(BF)
    came = lax.all_to_all(
        sent.reshape(slot_total, share_rows, D), "dp", split_axis=0, concat_axis=0, tiled=True
    )
    compact = jnp.dot(
        to_live.astype(BF), came.reshape(slot_total, wide), preferred_element_type=F32
    ).astype(BF)
    live_vectors = lax.all_gather(compact.reshape(OWNER_BLOCKS * share_rows, D), "mp", axis=0)
    place_parts = live_place.reshape(OWNER_BLOCKS, part_count, share_rows)
    place_flat = place_parts.transpose(1, 0, 2).reshape(-1)
    numbers = lax.broadcasted_iota(jnp.int32, (words_dev, place_flat.shape[0]), 0)
    placed = jnp.dot(
        (numbers == place_flat[None, :]).astype(BF),
        live_vectors.reshape(-1, D),
        preferred_element_type=F32,
    )
    stream = word_inputs.reshape(words_dev, D).astype(F32) + placed
    normed_float, scale_one = norm_forward(stream, word_gains[0])
    normed_one = normed_float.astype(BF)
    block_width = output_mats.shape[1]
    local_heads = block_width // HD
    projected = jnp.einsum(
        "rd,tde->tre", normed_one, project_mats[:, 0], preferred_element_type=F32
    ).astype(BF)
    heads_view = projected.reshape(3, rows_dev, length, local_heads, HD)
    mixed_rows = word_attention(heads_view[0], heads_view[1], heads_view[2], documents).reshape(
        words_dev, block_width
    )
    attend_total = lax.psum(
        jnp.dot(mixed_rows, output_mats[0], preferred_element_type=F32).astype(BF), "mp"
    ).astype(F32)
    hidden = stream + attend_total
    normed_float_two, scale_two = norm_forward(hidden, word_gains[1])
    normed_two = normed_float_two.astype(BF)
    upper_rows = jnp.dot(normed_two, upper_mats[0], preferred_element_type=F32)
    active = gelu_tanh(upper_rows).astype(BF)
    feed_total = lax.psum(
        jnp.dot(active, lower_mats[0], preferred_element_type=F32).astype(BF), "mp"
    ).astype(F32)
    block_out = (hidden + feed_total).astype(BF).reshape(word_inputs.shape)
    grad_output = cotangent.reshape(words_dev, D).astype(F32)
    grad_feed = grad_output.astype(BF)
    grad_lower = jnp.einsum("rf,rd->fd", active, grad_feed, preferred_element_type=F32)
    grad_active = jnp.einsum("rd,fd->rf", grad_feed, lower_mats[0], preferred_element_type=F32)
    unused_value, gelu_pull = jax.vjp(gelu_tanh, upper_rows)
    grad_upper_rows = gelu_pull(grad_active)[0].astype(BF)
    grad_upper = jnp.einsum("rd,rf->df", normed_two, grad_upper_rows, preferred_element_type=F32)
    part_two = jnp.einsum("rf,df->rd", grad_upper_rows, upper_mats[0], preferred_element_type=F32)
    grad_normed_two = lax.psum(part_two.astype(BF), "mp").astype(F32)
    grad_hidden_norm, gain_two = norm_backward(hidden, scale_two, word_gains[1], grad_normed_two)
    grad_hidden = grad_output + grad_hidden_norm
    grad_attend = grad_hidden.astype(BF)
    grad_output_mat = jnp.einsum("re,rd->ed", mixed_rows, grad_attend, preferred_element_type=F32)
    grad_mixed = jnp.einsum(
        "rd,ed->re", grad_attend, output_mats[0], preferred_element_type=F32
    ).astype(BF)
    grad_queries, grad_keys, grad_values = word_attention_back(
        heads_view[0],
        heads_view[1],
        heads_view[2],
        grad_mixed.reshape(rows_dev, length, local_heads, HD),
        documents,
    )
    grad_heads = jnp.stack([grad_queries, grad_keys, grad_values]).reshape(3, words_dev, block_width)
    grad_project = jnp.einsum("rd,tre->tde", normed_one, grad_heads, preferred_element_type=F32)
    part_one = jnp.einsum(
        "tre,tde->rd", grad_heads, project_mats[:, 0], preferred_element_type=F32
    )
    grad_normed_one = lax.psum(part_one.astype(BF), "mp").astype(F32)
    grad_stream_norm, gain_one = norm_backward(stream, scale_one, word_gains[0], grad_normed_one)
    grad_stream = grad_hidden + grad_stream_norm
    grad_words = grad_stream.astype(BF)
    word_inputs_gradient = grad_words.reshape(word_inputs.shape)

    own_place = lax.dynamic_slice_in_dim(
        came_place.reshape(slot_total, part_count, share_rows), lax.axis_index("mp"), 1, 1
    ).reshape(-1)
    picked = jnp.dot(
        (
            own_place[:, None]
            == lax.broadcasted_iota(jnp.int32, (own_place.shape[0], words_dev), 1)
        ).astype(BF),
        grad_words,
        preferred_element_type=F32,
    ).astype(BF)
    returned = lax.all_to_all(
        picked.reshape(slot_total, share_rows, D), "dp", split_axis=0, concat_axis=0, tiled=True
    )
    grad_vectors = (
        jnp.dot(to_slot.astype(BF).T, returned.reshape(slot_total, wide), preferred_element_type=F32)
        .astype(BF)
        .reshape(slot_count * share_rows, D)
    )
    char_embeds_gradient, grad_wide, grad_out, grad_lift, grad_char_gain = char_backward(
        character_embeddings, kind, counts, char_gain, char_whole, kept, pooled, msum, grad_vectors
    )
    sum_project, sum_output, sum_upper, sum_lower, sum_word_gains = (
        s.astype(F32)
        for s in lax.psum(
            (
                grad_project[:, None].astype(BF),
                grad_output_mat[None].astype(BF),
                grad_upper[None].astype(BF),
                grad_lower[None].astype(BF),
                jnp.stack([gain_one, gain_two]).astype(BF),
            ),
            "dp",
        )
    )
    word_squares = (
        jnp.sum(sum_project * sum_project)
        + jnp.sum(sum_output * sum_output)
        + jnp.sum(sum_upper * sum_upper)
        + jnp.sum(sum_lower * sum_lower)
    )
    sum_wide, sum_out, sum_lift, sum_char_gain, spread_squares = lax.psum(
        (grad_wide, grad_out, grad_lift, grad_char_gain[0], word_squares), ("dp", "mp")
    )
    width = CHAR_BLOCK_WIDTH
    sum_mixer = jnp.stack(
        [sum_wide[:, t * width : (t + 1) * width] for t in range(3)] + [sum_out]
    )
    sum_lift = sum_lift[None]
    other_squares = (
        jnp.sum(sum_mixer * sum_mixer)
        + jnp.sum(sum_lift * sum_lift)
        + jnp.sum(sum_char_gain * sum_char_gain)
        + jnp.sum(sum_word_gains * sum_word_gains)
    )
    global_norm = jnp.sqrt(spread_squares / float(peer_count) + other_squares)
    parameter_count = (
        sum(
            part_count * w.size * peer_count
            for w in (word_project, word_output, feed_upper, feed_lower)
        )
        + peer_count * (char_mixer.size + char_lift.size)
        + char_gain.size
        + word_gains.size
    )
    factor = jnp.minimum(1.0, 0.5 * math.sqrt(parameter_count) / global_norm)
    mixer_root, lift_root, project_root, output_root, upper_root, lower_root = unpack(
        root_whole, [w.shape for w in roots]
    )
    mixer_out = refresh(char_mixer, sum_mixer, char_mixer_left, char_mixer_right, char_mixer_left_root, mixer_root, factor, owner_index)
    lift_out = refresh(char_lift, sum_lift, char_lift_left, char_lift_right, char_lift_left_root, lift_root, factor, owner_index)
    project_out = refresh(word_project, sum_project, word_project_left, word_project_right, word_project_left_root, project_root, factor, owner_index)
    output_out = refresh(word_output, sum_output, word_output_left, word_output_right, word_output_left_root, output_root, factor, owner_index)
    upper_out = refresh(feed_upper, sum_upper, feed_upper_left, feed_upper_right, feed_upper_left_root, upper_root, factor, owner_index)
    lower_out = refresh(feed_lower, sum_lower, feed_lower_left, feed_lower_right, feed_lower_left_root, lower_root, factor, owner_index)
    char_gain_clipped = factor * sum_char_gain
    word_gains_clipped = factor * sum_word_gains
    return (
        block_out,
        word_inputs_gradient,
        char_embeds_gradient,
        char_gain_clipped,
        word_gains_clipped,
        char_gain - gain_rate * char_gain_clipped,
        word_gains - gain_rate * word_gains_clipped,
        global_norm,
        mixer_out[0],
        mixer_out[1],
        mixer_out[2],
        mixer_out[3],
        mixer_out[4],
        lift_out[0],
        lift_out[1],
        lift_out[2],
        lift_out[3],
        lift_out[4],
        project_out[0],
        project_out[1],
        project_out[2],
        project_out[3],
        project_out[4],
        output_out[0],
        output_out[1],
        output_out[2],
        output_out[3],
        output_out[4],
        upper_out[0],
        upper_out[1],
        upper_out[2],
        upper_out[3],
        upper_out[4],
        lower_out[0],
        lower_out[1],
        lower_out[2],
        lower_out[3],
        lower_out[4],
    )


def solution(mesh):
    placed = (
        P("dp", None, None),
        P("dp", "mp", None, None),
        P("dp", None, None),
        P("dp", "mp"),
        P("dp", None),
        P("dp"),
        P("dp", None),
        P(),
        P(),
        P(None, "dp", None),
        P(None, "dp", None),
        P(None, "dp", None),
        P(None, "dp", None),
        P(None, "dp", None),
        P(None, "dp", None),
        P(None, "dp", None),
        P(None, "dp", None),
        P(None, "dp", None),
        P(None, "dp", None),
        P(None, "mp", "dp", None),
        P(None, "mp", "dp", None),
        P(None, "mp", "dp", None),
        P(None, "mp", "dp", None),
        P(None, "mp", "dp", None),
        P("mp", "dp", None),
        P("mp", "dp", None),
        P("mp", "dp", None),
        P("mp", "dp", None),
        P("mp", "dp", None),
        P("mp", "dp", None),
        P("mp", "dp", None),
        P("mp", "dp", None),
        P("mp", "dp", None),
        P("mp", "dp", None),
        P("mp", "dp", None),
        P("mp", "dp", None),
        P("mp", "dp", None),
        P("mp", "dp", None),
        P("mp", "dp", None),
    )
    return jax.shard_map(
        local,
        mesh=mesh,
        in_specs=placed,
        out_specs=(
            P("dp", None, None),
            P("dp", None, None),
            P("dp", "mp", None, None),
            P(),
            P(),
            P(),
            P(),
            P(),
            P(None, "dp", None),
            P(None, "dp", None),
            P(None, "dp", None),
            P(None, "dp", None),
            P(None, "dp", None),
            P(None, "dp", None),
            P(None, "dp", None),
            P(None, "dp", None),
            P(None, "dp", None),
            P(None, "dp", None),
            P(None, "mp", "dp", None),
            P(None, "mp", "dp", None),
            P(None, "mp", "dp", None),
            P(None, "mp", "dp", None),
            P(None, "mp", "dp", None),
            P("mp", "dp", None),
            P("mp", "dp", None),
            P("mp", "dp", None),
            P("mp", "dp", None),
            P("mp", "dp", None),
            P("mp", "dp", None),
            P("mp", "dp", None),
            P("mp", "dp", None),
            P("mp", "dp", None),
            P("mp", "dp", None),
            P("mp", "dp", None),
            P("mp", "dp", None),
            P("mp", "dp", None),
            P("mp", "dp", None),
            P("mp", "dp", None),
        ),
        check_vma=False,
    )
```

```python
import functools
import math

import jax
import jax.numpy as jnp
from jax import lax
from jax.experimental import pallas as pl
from jax.experimental.pallas import tpu as pltpu
from jax.sharding import PartitionSpec as P

D = 512
HD = 64
FF = 2048
CHAR_BLOCK_WIDTH = 256
OWNER_BLOCKS = 10
decay_rate = 0.5
learn_rate = 1.0
gain_rate = 0.4
negative_big = -1e30

CW = 256
CHEADS = 4
CHD = 64
SPOTS = 16
KEPT = 3 * CW + CHEADS * 128 + CW
epsilon = 1e-05
BF = jnp.bfloat16
F32 = jnp.float32


def nn(a, b):
    return lax.dot_general(a, b, (((1,), (0,)), ((), ())), preferred_element_type=F32)


def nt(a, b):
    return lax.dot_general(a, b, (((1,), (1,)), ((), ())), preferred_element_type=F32)


def tn(a, b):
    return lax.dot_general(a, b, (((0,), (0,)), ((), ())), preferred_element_type=F32)


def char_classes(share):
    listed = [(1, 4, 32), (2, 8, 16), (4, 16, 8)]
    return [c for c in listed if c[2] <= share]


def order_matrix(places, words):
    row = lax.broadcasted_iota(jnp.int32, (128, SPOTS * words), 0)
    col = lax.broadcasted_iota(jnp.int32, (128, SPOTS * words), 1)
    return ((row % words) * SPOTS + row // words == col).astype(BF)


def head_stack(rows, scale):
    lane = lax.broadcasted_iota(jnp.int32, (1, CW), 1) // CHD
    return jnp.concatenate(
        [rows * jnp.where(lane == h, scale, 0.0).astype(BF) for h in range(CHEADS)], axis=0
    )


def char_forward_kernel(
    classes, kind, x_ref, count_ref, gain_ref, mats_ref, *refs
):
    orders = refs[: len(classes)]
    vec_ref, kept_ref, pooled_ref, msum_ref, sumx, counts = refs[len(classes) :]
    step = pl.program_id(0)
    share = count_ref.shape[1]
    own = pl.ds(pl.multiple_of(step * share, share), share)
    counts[own, :] = count_ref[0]

    @pl.when(kind[step] == 0)
    def _():
        sumx[own, :] = jnp.zeros((share, CW), F32)
        msum_ref[own, :] = jnp.zeros((share, CW), F32)

    def block(places, words, order_ref):
        groups = share // words
        kept_x = []
        normed = []
        for g in range(groups):
            x = nn(order_ref[...], x_ref[0, pl.ds(g * words * SPOTS, words * SPOTS), :])
            scale = lax.rsqrt(jnp.mean(x * x, axis=-1, keepdims=True) + epsilon)
            normed.append((x * scale * gain_ref[...]).astype(BF))
            cnt = count_ref[0, pl.ds(g * words, words), :]
            cnt2 = jnp.concatenate([cnt, cnt], axis=1)
            place = lax.broadcasted_iota(jnp.int32, (places, words, CW), 0).astype(F32)
            x3 = x.reshape(places, words, CW)
            sumx[pl.ds(pl.multiple_of(step * share + g * words, words), words), :] = jnp.sum(
                jnp.where(place < cnt2[None], x3, 0.0), axis=0
            )
        rows = groups * 128
        normed = jnp.concatenate(normed, axis=0) if groups > 1 else normed[0]
        for t in range(3):
            kept_ref[0, :rows, t * CW : (t + 1) * CW] = nn(
                normed, mats_ref[:, t * CW : (t + 1) * CW]
            ).astype(BF)
        lane = lax.broadcasted_iota(jnp.int32, (words, CHEADS * 128), 1) % 128
        word = lax.broadcasted_iota(jnp.int32, (words, CHEADS * 128), 0)
        mine = lane % words == word
        spot = (lane // words).astype(F32)
        head_row = lax.broadcasted_iota(jnp.int32, (CHEADS * 128, CW), 0) // 128
        head_col = lax.broadcasted_iota(jnp.int32, (CHEADS * 128, CW), 1) // CHD
        same_head = (head_row == head_col).astype(BF)
        for g in range(groups):
            at = g * 128
            q = kept_ref[0, at : at + 128, :CW]
            k = kept_ref[0, at : at + 128, CW : 2 * CW]
            v = kept_ref[0, at : at + 128, 2 * CW : 3 * CW]
            s = nt(k, head_stack(q, 1.0 / math.sqrt(CHD))).reshape(places, words, CHEADS * 128)
            cnt = count_ref[0, pl.ds(g * words, words), :]
            cnt4 = jnp.concatenate([cnt] * CHEADS, axis=1)
            place = lax.broadcasted_iota(jnp.int32, (places, words, CHEADS * 128), 0).astype(F32)
            s = jnp.where(place < cnt4[None], s, -1e30)
            e = jnp.exp(s - jnp.max(s, axis=0)[None])
            r = jnp.where(mine & (spot < cnt4), 1.0 / jnp.sum(e, axis=0), 0.0)
            p = (e * r[None]).astype(BF).reshape(128, CHEADS * 128)
            kept_ref[0, at : at + 128, 3 * CW : 3 * CW + CHEADS * 128] = p
            c = nn(p, same_head)
            kept_ref[0, at : at + 128, 3 * CW + CHEADS * 128 :] = c.astype(BF)
            msum_ref[pl.ds(pl.multiple_of(step * share + g * words, words), words), :] = jnp.sum(
                (c * v.astype(F32)).reshape(places, words, CW), axis=0
            )

    for (number, places, words), order_ref in zip(classes, orders):
        pl.when(kind[step] == number)(functools.partial(block, places, words, order_ref))

    @pl.when(step == pl.num_programs(0) - 1)
    def _():
        cnt2 = jnp.concatenate([counts[...]] * 2, axis=1)
        summed = sumx[...] + nn(msum_ref[...].astype(BF), mats_ref[:, 3 * CW : 4 * CW])
        pooled = (summed / cnt2).astype(BF)
        pooled_ref[...] = pooled
        vec_ref[...] = nn(pooled, mats_ref[:, 4 * CW :]).astype(BF)


def char_kind(block_home, char_count, share):
    places = jnp.max(char_count, axis=1)
    kind = jnp.where(places <= 8, 2, 4)
    if share >= 32:
        kind = jnp.where(places <= 4, 1, kind)
    return jnp.where(block_home >= 0, kind, 0).astype(jnp.int32)


def whole(shape):
    return pl.BlockSpec(shape, lambda i, *_: (0,) * len(shape))


def char_forward(x, kind, counts, gain, mats):
    slots, share = x.shape[:2]
    classes = char_classes(share)
    rows = share * SPOTS
    orders = [order_matrix(p, w) for _, p, w in classes]
    words_all = slots * share
    per_slot = lambda shape: pl.BlockSpec((1,) + shape, lambda i, *_: (i,) + (0,) * len(shape))
    return pl.pallas_call(
        functools.partial(char_forward_kernel, classes),
        grid_spec=pltpu.PrefetchScalarGridSpec(
            num_scalar_prefetch=1,
            grid=(slots,),
            in_specs=[
                per_slot((rows, CW)),
                per_slot((share, 128)),
                whole((1, CW)),
                whole(mats.shape),
            ]
            + [whole(o.shape) for o in orders],
            out_specs=[
                whole((words_all, D)),
                per_slot((rows, KEPT)),
                whole((words_all, CW)),
                whole((words_all, CW)),
            ],
            scratch_shapes=[
                pltpu.VMEM((words_all, CW), F32),
                pltpu.VMEM((words_all, 128), F32),
            ],
        ),
        out_shape=[
            jax.ShapeDtypeStruct((words_all, D), BF),
            jax.ShapeDtypeStruct((slots, rows, KEPT), BF),
            jax.ShapeDtypeStruct((words_all, CW), BF),
            jax.ShapeDtypeStruct((words_all, CW), F32),
        ],
        compiler_params=pltpu.CompilerParams(vmem_limit_bytes=40 << 20),
        cost_estimate=pl.CostEstimate(
            flops=slots * rows * CW * CW * 16, bytes_accessed=slots * rows * KEPT * 3, transcendentals=0
        ),
        name="char_forward",
    )(kind, x.reshape(slots, rows, CW), counts, gain.reshape(1, CW), mats, *orders)


def char_backward_kernel(
    classes, kind, x_ref, count_ref, kept_ref, all_counts_ref, gv_ref, pooled_ref, msum_ref,
    gain_ref, mats_ref, *refs
):
    orders = refs[: len(classes)]
    dx_ref, dqkv_ref, dout_ref, dlift_ref, dgain_ref, gp_all, gm_all, dh, normed_all = refs[len(classes) :]
    step = pl.program_id(0)
    share = count_ref.shape[1]
    base = step * share

    @pl.when(step == 0)
    def _():
        gv = gv_ref[...]
        cnt2 = jnp.concatenate([all_counts_ref[...]] * 2, axis=1)
        gp = nt(gv, mats_ref[:, 4 * CW :]) / cnt2
        gp_all[...] = gp
        gpb = gp.astype(BF)
        gm_all[...] = nt(gpb, mats_ref[:, 3 * CW : 4 * CW]).astype(BF).astype(F32)
        dlift_ref[...] = tn(pooled_ref[...], gv)
        dout_ref[...] = tn(msum_ref[...].astype(BF), gpb)
        dqkv_ref[...] = jnp.zeros_like(dqkv_ref)
        dgain_ref[...] = jnp.zeros_like(dgain_ref)

    @pl.when(kind[step] == 0)
    def _():
        dx_ref[...] = jnp.zeros_like(dx_ref)

    def block(places, words, order_ref):
        groups = share // words
        rows = groups * 128
        gain = gain_ref[...]
        xs = []
        scales = []
        gps = []
        for g in range(groups):
            at = g * 128
            x = nn(order_ref[...], x_ref[0, pl.ds(g * words * SPOTS, words * SPOTS), :])
            scale = lax.rsqrt(jnp.mean(x * x, axis=-1, keepdims=True) + epsilon)
            normed_all[at : at + 128, :] = (x * scale * gain).astype(BF)
            xs.append(x)
            scales.append(scale)
            mine = pl.ds(pl.multiple_of(base + g * words, words), words)
            cnt = count_ref[0, pl.ds(g * words, words), :]
            cnt2 = jnp.concatenate([cnt, cnt], axis=1)
            place = lax.broadcasted_iota(jnp.int32, (places, words, CW), 0).astype(F32)
            shown = place < cnt2[None]
            gps.append(jnp.where(shown, gp_all[mine, :][None], 0.0).reshape(128, CW))
            gm_word = gm_all[mine, :]
            gm = jnp.where(shown, gm_word[None], 0.0).reshape(128, CW).astype(BF)
            q = kept_ref[0, at : at + 128, :CW]
            k = kept_ref[0, at : at + 128, CW : 2 * CW]
            v = kept_ref[0, at : at + 128, 2 * CW : 3 * CW]
            p = kept_ref[0, at : at + 128, 3 * CW : 3 * CW + CHEADS * 128].astype(F32)
            c = kept_ref[0, at : at + 128, 3 * CW + CHEADS * 128 :].astype(F32)
            dp = nt(v, head_stack(gm, 1.0))
            p3 = p.reshape(places, words, CHEADS * 128)
            t = p3 * dp.reshape(places, words, CHEADS * 128)
            ds = (t - p3 * jnp.sum(t, axis=0)[None]).astype(BF).reshape(128, CHEADS * 128)
            eighth = 1.0 / math.sqrt(CHD)
            dk = nn(ds, head_stack(q, eighth))
            ds_rows = jnp.concatenate([ds[:, h * 128 : (h + 1) * 128] for h in range(CHEADS)], axis=0)
            dq = tn(ds_rows, head_stack(k, eighth))
            dv = (c.reshape(places, words, CW) * gm_word[None]).reshape(128, CW)
            dh[at : at + 128, :CW] = dq.astype(BF)
            dh[at : at + 128, CW : 2 * CW] = dk.astype(BF)
            dh[at : at + 128, 2 * CW :] = dv.astype(BF)
        grads = dh[:rows, :]
        dqkv_ref[...] += tn(normed_all[:rows, :], grads)
        dn_all = nt(grads, mats_ref[:, : 3 * CW])
        dgain = jnp.zeros((1, CW), F32)
        for g in range(groups):
            x, scale = xs[g], scales[g]
            dn = dn_all[g * 128 : (g + 1) * 128]
            xr = x * scale
            dgain = dgain + jnp.sum(xr * dn, axis=0, keepdims=True)
            w = dn * gain
            inner = jnp.mean(xr * w, axis=-1, keepdims=True)
            dx = gps[g] + scale * (w - xr * inner)
            dx_ref[0, pl.ds(g * words * SPOTS, words * SPOTS), :] = tn(
                order_ref[...], dx.astype(BF)
            ).astype(BF)
        dgain_ref[...] += dgain

    for (number, places, words), order_ref in zip(classes, orders):
        pl.when(kind[step] == number)(functools.partial(block, places, words, order_ref))


def char_backward(x, kind, counts, gain, mats, kept, pooled, msum, grad_vectors):
    slots, share = x.shape[:2]
    classes = char_classes(share)
    rows = share * SPOTS
    orders = [order_matrix(p, w) for _, p, w in classes]
    words_all = slots * share
    per_slot = lambda shape: pl.BlockSpec((1,) + shape, lambda i, *_: (i,) + (0,) * len(shape))
    dx, dqkv, dout, dlift, dgain = pl.pallas_call(
        functools.partial(char_backward_kernel, classes),
        grid_spec=pltpu.PrefetchScalarGridSpec(
            num_scalar_prefetch=1,
            grid=(slots,),
            in_specs=[
                per_slot((rows, CW)),
                per_slot((share, 128)),
                per_slot((rows, KEPT)),
                whole((words_all, 128)),
                whole((words_all, D)),
                whole((words_all, CW)),
                whole((words_all, CW)),
                whole((1, CW)),
                whole(mats.shape),
            ]
            + [whole(o.shape) for o in orders],
            out_specs=[
                per_slot((rows, CW)),
                whole((CW, 3 * CW)),
                whole((CW, CW)),
                whole((CW, D)),
                whole((1, CW)),
            ],
            scratch_shapes=[
                pltpu.VMEM((words_all, CW), F32),
                pltpu.VMEM((words_all, CW), F32),
                pltpu.VMEM((rows, 3 * CW), BF),
                pltpu.VMEM((rows, CW), BF),
            ],
        ),
        out_shape=[
            jax.ShapeDtypeStruct((slots, rows, CW), BF),
            jax.ShapeDtypeStruct((CW, 3 * CW), F32),
            jax.ShapeDtypeStruct((CW, CW), F32),
            jax.ShapeDtypeStruct((CW, D), F32),
            jax.ShapeDtypeStruct((1, CW), F32),
        ],
        compiler_params=pltpu.CompilerParams(vmem_limit_bytes=40 << 20),
        cost_estimate=pl.CostEstimate(
            flops=slots * rows * CW * CW * 28, bytes_accessed=slots * rows * KEPT * 3, transcendentals=0
        ),
        name="char_backward",
    )(
        kind, x.reshape(slots, rows, CW), counts, kept, counts.reshape(words_all, 128), grad_vectors,
        pooled, msum, gain.reshape(1, CW), mats, *orders,
    )
    return dx.reshape(x.shape), dqkv, dout, dlift, dgain


def norm_forward(values, gain_row):
    row_scale = lax.rsqrt(jnp.mean(values * values, axis=-1, keepdims=True) + epsilon)
    return (values * row_scale * gain_row, row_scale)


def norm_backward(values, row_scale, gain_row, grad_output):
    weighted = grad_output * gain_row
    row_inner = jnp.mean(values * weighted, axis=-1, keepdims=True)
    grad_values = row_scale * weighted - values * (row_scale * row_scale * row_scale) * row_inner
    return (grad_values, jnp.sum(values * row_scale * grad_output, axis=0))


def gelu_tanh(values):
    return jax.nn.gelu(values, approximate=True)


def word_softmax(row_queries, row_keys, query_docs, key_docs, first_row):
    scores = jnp.einsum(
        "qhe,khe->hqk", row_queries, row_keys, preferred_element_type=jnp.float32
    ) / math.sqrt(HD)
    table_shape = (row_queries.shape[0], row_keys.shape[0])
    query_at = first_row + lax.broadcasted_iota(jnp.int32, table_shape, 0)
    key_at = lax.broadcasted_iota(jnp.int32, table_shape, 1)
    allowed = (key_at <= query_at) & (key_docs[None, :] == query_docs[:, None])
    return jax.nn.softmax(jnp.where(allowed[None], scores, negative_big), axis=-1)


def word_attention(queries, keys_all, values_all, documents):
    length = queries.shape[1]
    block_rows = min(512, length)

    def one_row(pieces):
        row_queries, row_keys, row_values, row_docs = pieces
        outputs = []
        for first_row in range(0, length, block_rows):
            last_row = first_row + block_rows
            attention = word_softmax(
                row_queries[first_row:last_row],
                row_keys,
                row_docs[first_row:last_row],
                row_docs,
                first_row,
            )
            outputs.append(
                jnp.einsum(
                    "hqk,khe->qhe",
                    attention.astype(jnp.bfloat16),
                    row_values,
                    preferred_element_type=jnp.float32,
                ).astype(jnp.bfloat16)
            )
        return jnp.concatenate(outputs, axis=0)

    return lax.map(one_row, (queries, keys_all, values_all, documents))


def word_attention_back(queries, keys_all, values_all, grad_mixed, documents):
    length = queries.shape[1]
    block_rows = min(512, length)
    root_size = math.sqrt(HD)

    def one_row(pieces):
        row_queries, row_keys, row_values, row_grads, row_docs = pieces
        query_parts = []
        grad_keys = jnp.zeros(row_keys.shape, jnp.float32)
        grad_values = jnp.zeros(row_values.shape, jnp.float32)
        for first_row in range(0, length, block_rows):
            last_row = first_row + block_rows
            attention = word_softmax(
                row_queries[first_row:last_row],
                row_keys,
                row_docs[first_row:last_row],
                row_docs,
                first_row,
            )
            grad_attention = jnp.einsum(
                "qhe,khe->hqk",
                row_grads[first_row:last_row],
                row_values,
                preferred_element_type=jnp.float32,
            )
            row_inner = jnp.sum(attention * grad_attention, axis=-1, keepdims=True)
            grad_scores = (attention * (grad_attention - row_inner)).astype(jnp.bfloat16)
            query_parts.append(
                jnp.einsum(
                    "hqk,khe->qhe", grad_scores, row_keys, preferred_element_type=jnp.float32
                )
                / root_size
            )
            grad_keys = (
                grad_keys
                + jnp.einsum(
                    "hqk,qhe->khe",
                    grad_scores,
                    row_queries[first_row:last_row],
                    preferred_element_type=jnp.float32,
                )
                / root_size
            )
            grad_values = grad_values + jnp.einsum(
                "hqk,qhe->khe",
                attention.astype(jnp.bfloat16),
                row_grads[first_row:last_row],
                preferred_element_type=jnp.float32,
            )
        grad_queries = jnp.concatenate(query_parts, axis=0)
        return (
            grad_queries.astype(jnp.bfloat16),
            grad_keys.astype(jnp.bfloat16),
            grad_values.astype(jnp.bfloat16),
        )

    return lax.map(one_row, (queries, keys_all, values_all, grad_mixed, documents))


MESH_ID = pl.DeviceIdType.MESH


def exchange(name, number, tasks):
    sizes = {axis: lax.axis_size(axis) for _, axis, _ in tasks}
    outs, scratch = [], []
    for kind, axis, array in tasks:
        n = sizes[axis]
        block = array.shape if kind == "gather" else array.shape[1:]
        outs.append(
            jax.ShapeDtypeStruct(
                block if kind == "part" else (n,) + block, F32 if kind == "part" else array.dtype
            )
        )
        scratch += [pltpu.SemaphoreType.DMA((2, n)), pltpu.SemaphoreType.DMA((2, n))]
        if kind in ("part", "sum"):
            scratch.append(pltpu.VMEM((n,) + block, array.dtype))

    def kernel(*refs):
        ins, results = refs[: len(tasks)], refs[len(tasks) : 2 * len(tasks)]
        rest = list(refs[2 * len(tasks) :])
        me = {axis: lax.axis_index(axis) for axis in sizes}
        barrier = pltpu.get_barrier_semaphore()
        for axis, n in sizes.items():
            for d in range(1, n):
                pl.semaphore_signal(
                    barrier, inc=1, device_id={axis: lax.rem(me[axis] + d, n)}, device_id_type=MESH_ID
                )
        pl.semaphore_wait(barrier, sum(n - 1 for n in sizes.values()))

        def send(axis, source, target, sems, phase):
            n = sizes[axis]
            copies = []
            for d in range(1, n):
                peer = lax.rem(me[axis] + d, n)
                copies.append(
                    pltpu.make_async_remote_copy(
                        src_ref=source(peer),
                        dst_ref=target.at[me[axis]],
                        send_sem=sems[0].at[phase, d],
                        recv_sem=sems[1].at[phase, d],
                        device_id={axis: peer},
                        device_id_type=MESH_ID,
                    )
                )
            for copy in copies:
                copy.start()
            return copies

        plans = []
        for (kind, axis, _), x, out in zip(tasks, ins, results):
            sems = (rest.pop(0), rest.pop(0))
            held = rest.pop(0) if kind in ("part", "sum") else out
            source = (lambda p, x=x: x) if kind == "gather" else (lambda p, x=x: x.at[p])
            plans.append((kind, axis, x, out, sems, held, send(axis, source, held, sems, 0)))
        for kind, axis, x, out, sems, held, copies in plans:
            held[me[axis]] = x[...] if kind == "gather" else x[me[axis]]
        waiting = []
        for kind, axis, x, out, sems, held, copies in plans:
            if kind in ("gather", "swap"):
                waiting += copies
                continue
            for copy in copies:
                copy.wait()
            total = held[0].astype(F32)
            for p in range(1, sizes[axis]):
                total = total + held[p].astype(F32)
            if kind == "part":
                out[...] = total
            else:
                out[me[axis]] = total.astype(out.dtype)
                waiting += send(axis, lambda p, out=out, axis=axis: out.at[me[axis]], out, sems, 1)
        for copy in waiting:
            copy.wait()

    vmem = pl.BlockSpec(memory_space=pltpu.VMEM)
    return pl.pallas_call(
        kernel,
        out_shape=outs,
        in_specs=[vmem] * len(tasks),
        out_specs=[vmem] * len(tasks),
        scratch_shapes=scratch,
        compiler_params=pltpu.CompilerParams(
            collective_id=number, has_side_effects=True, vmem_limit_bytes=48 << 20
        ),
        name=name,
    )(*[array for _, _, array in tasks])


def sum_char_grads(grads, small):
    n, m = lax.axis_size("dp"), lax.axis_size("mp")
    block = grads.shape[1:]

    def kernel(x, s, out, small_out, held, held_z, small_dp, small_mp, ss, rs):
        i, j = lax.axis_index("dp"), lax.axis_index("mp")
        barrier = pltpu.get_barrier_semaphore()
        for d in range(1, n):
            pl.semaphore_signal(barrier, inc=1, device_id={"dp": lax.rem(i + d, n)}, device_id_type=MESH_ID)
        for d in range(1, m):
            pl.semaphore_signal(barrier, inc=1, device_id={"mp": lax.rem(j + d, m)}, device_id_type=MESH_ID)
        pl.semaphore_wait(barrier, n + m - 2)

        def send(axis, me, count, source, target, phase):
            copies = []
            for d in range(1, count):
                peer = lax.rem(me + d, count)
                copies.append(
                    pltpu.make_async_remote_copy(
                        src_ref=source(peer), dst_ref=target.at[me], send_sem=ss.at[phase, d],
                        recv_sem=rs.at[phase, d], device_id={axis: peer}, device_id_type=MESH_ID,
                    )
                )
            for copy in copies:
                copy.start()
            return copies

        small_one = send("dp", i, n, lambda p: s, small_dp, 0)
        one = send("dp", i, n, lambda p: x.at[p], held, 1)
        held[i] = x[i]
        small_dp[i] = s[...]
        for copy in small_one:
            copy.wait()
        total = small_dp[0]
        for p in range(1, n):
            total = total + small_dp[p]
        small_mp[j] = total
        small_two = send("mp", j, m, lambda p: small_mp.at[j], small_mp, 2)
        for copy in one:
            copy.wait()
        total = held[0].astype(F32)
        for p in range(1, n):
            total = total + held[p].astype(F32)
        held_z[j] = total.astype(BF)
        two = send("mp", j, m, lambda p: held_z.at[j], held_z, 3)
        for copy in small_two:
            copy.wait()
        total = small_mp[0]
        for p in range(1, m):
            total = total + small_mp[p]
        small_out[...] = total
        for copy in two:
            copy.wait()
        total = held_z[0].astype(F32)
        for p in range(1, m):
            total = total + held_z[p].astype(F32)
        out[i] = total.astype(BF)
        three = send("dp", i, n, lambda p: out.at[i], out, 4)
        for copy in three:
            copy.wait()

    vmem = pl.BlockSpec(memory_space=pltpu.VMEM)
    return pl.pallas_call(
        kernel,
        out_shape=[
            jax.ShapeDtypeStruct(grads.shape, BF),
            jax.ShapeDtypeStruct(small.shape, F32),
        ],
        in_specs=[vmem] * 2,
        out_specs=[vmem] * 2,
        scratch_shapes=[
            pltpu.VMEM((n,) + block, BF),
            pltpu.VMEM((m,) + block, BF),
            pltpu.VMEM((n,) + small.shape, F32),
            pltpu.VMEM((m,) + small.shape, F32),
            pltpu.SemaphoreType.DMA((5, max(n, m))),
            pltpu.SemaphoreType.DMA((5, max(n, m))),
        ],
        compiler_params=pltpu.CompilerParams(
            collective_id=20, has_side_effects=True, vmem_limit_bytes=48 << 20
        ),
        name="sum_char_grads",
    )(grads, small)


def pack(array):
    rows, cols = array.shape[-2:]
    if cols % 128:
        return array.reshape(-1, 128)
    split = array.reshape(-1, rows, cols // 128, 128)
    return split.transpose(0, 2, 1, 3).reshape(-1, 128)


def unpack(gathered, shapes):
    devices = gathered.shape[0]
    whole_ones = []
    first = 0
    for shape in shapes:
        lead, (rows, cols) = shape[:-2], shape[-2:]
        count = math.prod(shape) // 128
        piece = gathered[:, first : first + count]
        first += count
        if cols % 128:
            piece = piece.reshape(devices, -1, rows, cols).transpose(1, 0, 2, 3)
        else:
            piece = piece.reshape(devices, -1, cols // 128, rows, 128).transpose(1, 0, 3, 2, 4)
        whole_ones.append(piece.reshape(lead + (devices * rows, cols)))
    return whole_ones


def refresh(master, gradient, left_stat, right_stat, left_root, right_root, factor, owner_index):
    clipped = gradient * factor
    near = clipped.astype(BF)
    rows_own = master.shape[-2]
    cols_own = right_stat.shape[-2]
    own_rows = lax.dynamic_slice_in_dim(clipped, owner_index * rows_own, rows_own, clipped.ndim - 2)
    own_cols = lax.dynamic_slice_in_dim(near, owner_index * cols_own, cols_own, clipped.ndim - 1)
    left_new = decay_rate * left_stat + (1.0 - decay_rate) * jnp.einsum(
        "...mn,...kn->...mk", own_rows.astype(BF), near, preferred_element_type=F32
    )
    right_new = decay_rate * right_stat + (1.0 - decay_rate) * jnp.einsum(
        "...mn,...mk->...nk", own_cols, near, preferred_element_type=F32
    )
    half_step = jnp.matmul(left_root.astype(BF), near, preferred_element_type=F32)
    shampoo_step = jnp.matmul(half_step.astype(BF), right_root, preferred_element_type=F32)
    fresh_master = master - learn_rate * shampoo_step
    return (own_rows, left_new, right_new, fresh_master, fresh_master.astype(BF))


def local(
    word_inputs,
    character_embeddings,
    cotangent,
    char_count,
    word_place,
    block_home,
    documents,
    char_gain,
    word_gains,
    char_mixer,
    char_mixer_left,
    char_mixer_right,
    char_mixer_left_root,
    char_mixer_right_root,
    char_lift,
    char_lift_left,
    char_lift_right,
    char_lift_left_root,
    char_lift_right_root,
    word_project,
    word_project_left,
    word_project_right,
    word_project_left_root,
    word_project_right_root,
    word_output,
    word_output_left,
    word_output_right,
    word_output_left_root,
    word_output_right_root,
    feed_upper,
    feed_upper_left,
    feed_upper_right,
    feed_upper_left_root,
    feed_upper_right_root,
    feed_lower,
    feed_lower_left,
    feed_lower_right,
    feed_lower_left_root,
    feed_lower_right_root,
):
    slot_count, share_rows = (character_embeddings.shape[0], character_embeddings.shape[1])
    peer_count = lax.axis_size("dp")
    part_count = lax.axis_size("mp")
    owner_index = lax.axis_index("dp")
    pair_cap = -(-slot_count // peer_count)
    slot_total = peer_count * pair_cap
    rows_dev, length = (word_inputs.shape[0], word_inputs.shape[1])
    words_dev = rows_dev * length
    block_words = share_rows * part_count

    char_pack = jnp.concatenate(
        [char_mixer[0], char_mixer[1], char_mixer[2], char_mixer[3], char_lift[0]], axis=1
    ).astype(BF)
    word_masters = (word_project, word_output, feed_upper, feed_lower)
    roots = (
        char_mixer_right_root,
        char_lift_right_root,
        word_project_right_root,
        word_output_right_root,
        feed_upper_right_root,
        feed_lower_right_root,
    )
    peers = lax.broadcasted_iota(jnp.int32, (slot_count, peer_count), 1)
    owner_match = (block_home[:, None] == peers).astype(jnp.int32)
    earlier = (
        lax.broadcasted_iota(jnp.int32, (slot_count, slot_count), 1)
        < lax.broadcasted_iota(jnp.int32, (slot_count, slot_count), 0)
    )
    same_owner = block_home[:, None] == block_home[None, :]
    slot_rank = jnp.sum((earlier & same_owner).astype(jnp.int32), axis=1)
    slot_target = jnp.where(block_home >= 0, block_home * pair_cap + slot_rank, slot_total)
    to_slot = lax.broadcasted_iota(jnp.int32, (slot_total, slot_count), 0) == slot_target[None, :]

    sent_place = jnp.max(
        jnp.where(to_slot[:, :, None], word_place[None] + 1, 0), axis=1
    ) - 1
    gathered, came_place = exchange(
        "gather_char",
        0,
        [
            ("gather", "dp", char_pack),
            ("swap", "dp", sent_place.reshape(peer_count, pair_cap, block_words)),
        ],
    )
    char_whole = gathered.reshape(-1, char_pack.shape[1])
    came_place = came_place.reshape(slot_total, block_words)
    kind = char_kind(block_home, char_count, share_rows)
    counts = jnp.broadcast_to(
        char_count.astype(F32)[..., None], (slot_count, share_rows, 128)
    )
    word_vectors, kept, pooled, msum = char_forward(
        character_embeddings, kind, counts, char_gain, char_whole
    )

    live = jnp.max(came_place, axis=1) >= 0
    slots_before = (
        lax.broadcasted_iota(jnp.int32, (slot_total, slot_total), 1)
        < lax.broadcasted_iota(jnp.int32, (slot_total, slot_total), 0)
    )
    live_rank = jnp.sum((slots_before & live[None, :]).astype(jnp.int32), axis=1)
    live_rank = jnp.where(live, live_rank, OWNER_BLOCKS)
    to_live = lax.broadcasted_iota(jnp.int32, (OWNER_BLOCKS, slot_total), 0) == live_rank[None, :]
    live_place = jnp.max(jnp.where(to_live[:, :, None], came_place[None] + 1, 0), axis=1) - 1

    wide = share_rows * D
    sent = jnp.dot(
        to_slot.astype(BF), word_vectors.reshape(slot_count, wide), preferred_element_type=F32
    ).astype(BF)
    (came,) = exchange(
        "send_vectors", 1, [("swap", "dp", sent.reshape(peer_count, pair_cap * share_rows, D))]
    )
    compact = jnp.dot(
        to_live.astype(BF), came.reshape(slot_total, wide), preferred_element_type=F32
    ).astype(BF)
    live_vectors, word_whole = exchange(
        "gather_words",
        2,
        [
            ("gather", "mp", compact.reshape(OWNER_BLOCKS * share_rows, D)),
            ("gather", "dp", jnp.concatenate([pack(w) for w in word_masters]).astype(BF)),
        ],
    )
    project_mats, output_mats, upper_mats, lower_mats = unpack(
        word_whole, [w.shape for w in word_masters]
    )
    place_parts = live_place.reshape(OWNER_BLOCKS, part_count, share_rows)
    place_flat = place_parts.transpose(1, 0, 2).reshape(-1)
    numbers = lax.broadcasted_iota(jnp.int32, (words_dev, place_flat.shape[0]), 0)
    placed = jnp.dot(
        (numbers == place_flat[None, :]).astype(BF),
        live_vectors.reshape(-1, D),
        preferred_element_type=F32,
    )
    stream = word_inputs.reshape(words_dev, D).astype(F32) + placed
    normed_float, scale_one = norm_forward(stream, word_gains[0])
    normed_one = normed_float.astype(BF)
    block_width = output_mats.shape[1]
    local_heads = block_width // HD
    projected = jnp.einsum(
        "rd,tde->tre", normed_one, project_mats[:, 0], preferred_element_type=F32
    ).astype(BF)
    heads_view = projected.reshape(3, rows_dev, length, local_heads, HD)
    mixed_rows = word_attention(heads_view[0], heads_view[1], heads_view[2], documents).reshape(
        words_dev, block_width
    )
    shares = (part_count, words_dev // part_count, D)
    attend_part = jnp.dot(mixed_rows, output_mats[0], preferred_element_type=F32).astype(BF)
    attend_total, root_whole = exchange(
        "sum_attend",
        3,
        [
            ("sum", "mp", attend_part.reshape(shares)),
            ("gather", "dp", jnp.concatenate([pack(w) for w in roots]).astype(BF)),
        ],
    )
    hidden = stream + attend_total.reshape(words_dev, D).astype(F32)
    normed_float_two, scale_two = norm_forward(hidden, word_gains[1])
    normed_two = normed_float_two.astype(BF)
    upper_rows = jnp.dot(normed_two, upper_mats[0], preferred_element_type=F32)
    active = gelu_tanh(upper_rows).astype(BF)
    feed_part = jnp.dot(active, lower_mats[0], preferred_element_type=F32).astype(BF)
    grad_output = cotangent.reshape(words_dev, D).astype(F32)
    grad_feed = grad_output.astype(BF)
    grad_lower = jnp.einsum("rf,rd->fd", active, grad_feed, preferred_element_type=F32)
    grad_active = jnp.einsum("rd,fd->rf", grad_feed, lower_mats[0], preferred_element_type=F32)
    unused_value, gelu_pull = jax.vjp(gelu_tanh, upper_rows)
    grad_upper_rows = gelu_pull(grad_active)[0].astype(BF)
    grad_upper = jnp.einsum("rd,rf->df", normed_two, grad_upper_rows, preferred_element_type=F32)
    part_two = jnp.einsum("rf,df->rd", grad_upper_rows, upper_mats[0], preferred_element_type=F32)
    (grad_normed_two,) = exchange(
        "sum_part_two", 4, [("sum", "mp", part_two.astype(BF).reshape(shares))]
    )
    grad_normed_two = grad_normed_two.reshape(words_dev, D).astype(F32)
    grad_hidden_norm, gain_two = norm_backward(hidden, scale_two, word_gains[1], grad_normed_two)
    grad_hidden = grad_output + grad_hidden_norm
    grad_attend = grad_hidden.astype(BF)
    grad_output_mat = jnp.einsum("re,rd->ed", mixed_rows, grad_attend, preferred_element_type=F32)
    grad_mixed = jnp.einsum(
        "rd,ed->re", grad_attend, output_mats[0], preferred_element_type=F32
    ).astype(BF)
    grad_queries, grad_keys, grad_values = word_attention_back(
        heads_view[0],
        heads_view[1],
        heads_view[2],
        grad_mixed.reshape(rows_dev, length, local_heads, HD),
        documents,
    )
    grad_heads = jnp.stack([grad_queries, grad_keys, grad_values]).reshape(3, words_dev, block_width)
    grad_project = jnp.einsum("rd,tre->tde", normed_one, grad_heads, preferred_element_type=F32)
    part_one = jnp.einsum(
        "tre,tde->rd", grad_heads, project_mats[:, 0], preferred_element_type=F32
    )
    word_grads = [
        jnp.moveaxis(
            g.astype(BF).reshape(g.shape[:-2] + (peer_count, -1, g.shape[-1])), -3, 0
        )
        for g in (grad_project, grad_output_mat, grad_upper, grad_lower)
    ]
    grad_normed_one, *word_sums = exchange(
        "sum_part_one",
        5,
        [("sum", "mp", part_one.astype(BF).reshape(shares))]
        + [("sum", "dp", g) for g in word_grads],
    )
    grad_normed_one = grad_normed_one.reshape(words_dev, D).astype(F32)
    sum_project, sum_output, sum_upper, sum_lower = (
        jnp.moveaxis(g, 0, -3).reshape(w.shape[:-2] + (-1, w.shape[-1])).astype(F32)
        for g, w in zip(word_sums, word_masters)
    )
    grad_stream_norm, gain_one = norm_backward(stream, scale_one, word_gains[0], grad_normed_one)
    grad_stream = grad_hidden + grad_stream_norm
    grad_words = grad_stream.astype(BF)
    word_inputs_gradient = grad_words.reshape(word_inputs.shape)

    own_place = lax.dynamic_slice_in_dim(
        came_place.reshape(slot_total, part_count, share_rows), lax.axis_index("mp"), 1, 1
    ).reshape(-1)
    picked = jnp.dot(
        (
            own_place[:, None]
            == lax.broadcasted_iota(jnp.int32, (own_place.shape[0], words_dev), 1)
        ).astype(BF),
        grad_words,
        preferred_element_type=F32,
    ).astype(BF)
    (returned,) = exchange(
        "return_vectors", 6, [("swap", "dp", picked.reshape(peer_count, pair_cap * share_rows, D))]
    )
    grad_vectors = (
        jnp.dot(to_slot.astype(BF).T, returned.reshape(slot_total, wide), preferred_element_type=F32)
        .astype(BF)
        .reshape(slot_count * share_rows, D)
    )
    grad_vectors, feed_part = lax.optimization_barrier((grad_vectors, feed_part))
    feed_total = lax.psum(feed_part, "mp").astype(F32)
    block_out = (hidden + feed_total).astype(BF).reshape(word_inputs.shape)
    char_embeds_gradient, grad_wide, grad_out, grad_lift, grad_char_gain = char_backward(
        character_embeddings, kind, counts, char_gain, char_whole, kept, pooled, msum, grad_vectors
    )
    word_squares = (
        jnp.sum(sum_project * sum_project)
        + jnp.sum(sum_output * sum_output)
        + jnp.sum(sum_upper * sum_upper)
        + jnp.sum(sum_lower * sum_lower)
    )
    width = CHAR_BLOCK_WIDTH
    small = jnp.zeros((8, D), F32)
    small = small.at[0, :width].set(grad_char_gain[0])
    small = small.at[1:3].set(jnp.stack([gain_one, gain_two]) / part_count)
    small = small.at[3, 0].set(word_squares / peer_count)
    char_grads = jnp.concatenate([grad_wide, grad_out, grad_lift], axis=1).astype(BF)
    char_sums, small_sums = sum_char_grads(
        char_grads.reshape(peer_count, -1, char_grads.shape[1]), small
    )
    char_sums = char_sums.reshape(char_grads.shape).astype(F32)
    sum_mixer = jnp.stack([char_sums[:, t * width : (t + 1) * width] for t in range(4)])
    sum_lift = char_sums[None, :, 4 * width :]
    sum_char_gain, sum_word_gains = small_sums[0, :width], small_sums[1:3]
    other_squares = (
        jnp.sum(sum_mixer * sum_mixer)
        + jnp.sum(sum_lift * sum_lift)
        + jnp.sum(sum_char_gain * sum_char_gain)
        + jnp.sum(sum_word_gains * sum_word_gains)
    )
    global_norm = jnp.sqrt(small_sums[3, 0] + other_squares)
    parameter_count = (
        sum(
            part_count * w.size * peer_count
            for w in (word_project, word_output, feed_upper, feed_lower)
        )
        + peer_count * (char_mixer.size + char_lift.size)
        + char_gain.size
        + word_gains.size
    )
    factor = jnp.minimum(1.0, 0.5 * math.sqrt(parameter_count) / global_norm)
    mixer_root, lift_root, project_root, output_root, upper_root, lower_root = unpack(
        root_whole, [w.shape for w in roots]
    )
    mixer_out = refresh(char_mixer, sum_mixer, char_mixer_left, char_mixer_right, char_mixer_left_root, mixer_root, factor, owner_index)
    lift_out = refresh(char_lift, sum_lift, char_lift_left, char_lift_right, char_lift_left_root, lift_root, factor, owner_index)
    project_out = refresh(word_project, sum_project, word_project_left, word_project_right, word_project_left_root, project_root, factor, owner_index)
    output_out = refresh(word_output, sum_output, word_output_left, word_output_right, word_output_left_root, output_root, factor, owner_index)
    upper_out = refresh(feed_upper, sum_upper, feed_upper_left, feed_upper_right, feed_upper_left_root, upper_root, factor, owner_index)
    lower_out = refresh(feed_lower, sum_lower, feed_lower_left, feed_lower_right, feed_lower_left_root, lower_root, factor, owner_index)
    char_gain_clipped = factor * sum_char_gain
    word_gains_clipped = factor * sum_word_gains
    return (
        block_out,
        word_inputs_gradient,
        char_embeds_gradient,
        char_gain_clipped,
        word_gains_clipped,
        char_gain - gain_rate * char_gain_clipped,
        word_gains - gain_rate * word_gains_clipped,
        global_norm,
        mixer_out[0],
        mixer_out[1],
        mixer_out[2],
        mixer_out[3],
        mixer_out[4],
        lift_out[0],
        lift_out[1],
        lift_out[2],
        lift_out[3],
        lift_out[4],
        project_out[0],
        project_out[1],
        project_out[2],
        project_out[3],
        project_out[4],
        output_out[0],
        output_out[1],
        output_out[2],
        output_out[3],
        output_out[4],
        upper_out[0],
        upper_out[1],
        upper_out[2],
        upper_out[3],
        upper_out[4],
        lower_out[0],
        lower_out[1],
        lower_out[2],
        lower_out[3],
        lower_out[4],
    )


def solution(mesh):
    placed = (
        P("dp", None, None),
        P("dp", "mp", None, None),
        P("dp", None, None),
        P("dp", "mp"),
        P("dp", None),
        P("dp"),
        P("dp", None),
        P(),
        P(),
        P(None, "dp", None),
        P(None, "dp", None),
        P(None, "dp", None),
        P(None, "dp", None),
        P(None, "dp", None),
        P(None, "dp", None),
        P(None, "dp", None),
        P(None, "dp", None),
        P(None, "dp", None),
        P(None, "dp", None),
        P(None, "mp", "dp", None),
        P(None, "mp", "dp", None),
        P(None, "mp", "dp", None),
        P(None, "mp", "dp", None),
        P(None, "mp", "dp", None),
        P("mp", "dp", None),
        P("mp", "dp", None),
        P("mp", "dp", None),
        P("mp", "dp", None),
        P("mp", "dp", None),
        P("mp", "dp", None),
        P("mp", "dp", None),
        P("mp", "dp", None),
        P("mp", "dp", None),
        P("mp", "dp", None),
        P("mp", "dp", None),
        P("mp", "dp", None),
        P("mp", "dp", None),
        P("mp", "dp", None),
        P("mp", "dp", None),
    )
    return jax.shard_map(
        local,
        mesh=mesh,
        in_specs=placed,
        out_specs=(
            P("dp", None, None),
            P("dp", None, None),
            P("dp", "mp", None, None),
            P(),
            P(),
            P(),
            P(),
            P(),
            P(None, "dp", None),
            P(None, "dp", None),
            P(None, "dp", None),
            P(None, "dp", None),
            P(None, "dp", None),
            P(None, "dp", None),
            P(None, "dp", None),
            P(None, "dp", None),
            P(None, "dp", None),
            P(None, "dp", None),
            P(None, "mp", "dp", None),
            P(None, "mp", "dp", None),
            P(None, "mp", "dp", None),
            P(None, "mp", "dp", None),
            P(None, "mp", "dp", None),
            P("mp", "dp", None),
            P("mp", "dp", None),
            P("mp", "dp", None),
            P("mp", "dp", None),
            P("mp", "dp", None),
            P("mp", "dp", None),
            P("mp", "dp", None),
            P("mp", "dp", None),
            P("mp", "dp", None),
            P("mp", "dp", None),
            P("mp", "dp", None),
            P("mp", "dp", None),
            P("mp", "dp", None),
            P("mp", "dp", None),
            P("mp", "dp", None),
        ),
        check_vma=False,
    )
```

```python
import functools
import math

import jax
import jax.numpy as jnp
from jax import lax
from jax.experimental import pallas as pl
from jax.experimental.pallas import tpu as pltpu
from jax.sharding import PartitionSpec as P

D = 512
HD = 64
FF = 2048
CHAR_BLOCK_WIDTH = 256
OWNER_BLOCKS = 10
decay_rate = 0.5
learn_rate = 1.0
gain_rate = 0.4
negative_big = -1e30

CW = 256
CHEADS = 4
CHD = 64
SPOTS = 16
KEPT = 3 * CW + CHEADS * 128 + CW
epsilon = 1e-05
BF = jnp.bfloat16
F32 = jnp.float32


def nn(a, b):
    return lax.dot_general(a, b, (((1,), (0,)), ((), ())), preferred_element_type=F32)


def nt(a, b):
    return lax.dot_general(a, b, (((1,), (1,)), ((), ())), preferred_element_type=F32)


def tn(a, b):
    return lax.dot_general(a, b, (((0,), (0,)), ((), ())), preferred_element_type=F32)


def char_classes(share):
    listed = [(1, 4, 32), (2, 8, 16), (4, 16, 8)]
    return [c for c in listed if c[2] <= share]


def order_matrix(places, words):
    row = lax.broadcasted_iota(jnp.int32, (128, SPOTS * words), 0)
    col = lax.broadcasted_iota(jnp.int32, (128, SPOTS * words), 1)
    return ((row % words) * SPOTS + row // words == col).astype(BF)


def head_stack(rows, scale):
    lane = lax.broadcasted_iota(jnp.int32, (1, CW), 1) // CHD
    return jnp.concatenate(
        [rows * jnp.where(lane == h, scale, 0.0).astype(BF) for h in range(CHEADS)], axis=0
    )


def char_forward_kernel(
    classes, kind, x_ref, count_ref, gain_ref, mats_ref, *refs
):
    orders = refs[: len(classes)]
    vec_ref, kept_ref, pooled_ref, msum_ref, sumx, counts = refs[len(classes) :]
    step = pl.program_id(0)
    share = count_ref.shape[1]
    own = pl.ds(pl.multiple_of(step * share, share), share)
    counts[own, :] = count_ref[0]

    @pl.when(kind[step] == 0)
    def _():
        sumx[own, :] = jnp.zeros((share, CW), F32)
        msum_ref[own, :] = jnp.zeros((share, CW), F32)

    def block(places, words, order_ref):
        groups = share // words
        kept_x = []
        normed = []
        for g in range(groups):
            x = nn(order_ref[...], x_ref[0, pl.ds(g * words * SPOTS, words * SPOTS), :])
            scale = lax.rsqrt(jnp.mean(x * x, axis=-1, keepdims=True) + epsilon)
            normed.append((x * scale * gain_ref[...]).astype(BF))
            cnt = count_ref[0, pl.ds(g * words, words), :]
            cnt2 = jnp.concatenate([cnt, cnt], axis=1)
            place = lax.broadcasted_iota(jnp.int32, (places, words, CW), 0).astype(F32)
            x3 = x.reshape(places, words, CW)
            sumx[pl.ds(pl.multiple_of(step * share + g * words, words), words), :] = jnp.sum(
                jnp.where(place < cnt2[None], x3, 0.0), axis=0
            )
        rows = groups * 128
        normed = jnp.concatenate(normed, axis=0) if groups > 1 else normed[0]
        for t in range(3):
            kept_ref[0, :rows, t * CW : (t + 1) * CW] = nn(
                normed, mats_ref[:, t * CW : (t + 1) * CW]
            ).astype(BF)
        lane = lax.broadcasted_iota(jnp.int32, (words, CHEADS * 128), 1) % 128
        word = lax.broadcasted_iota(jnp.int32, (words, CHEADS * 128), 0)
        mine = lane % words == word
        spot = (lane // words).astype(F32)
        head_row = lax.broadcasted_iota(jnp.int32, (CHEADS * 128, CW), 0) // 128
        head_col = lax.broadcasted_iota(jnp.int32, (CHEADS * 128, CW), 1) // CHD
        same_head = (head_row == head_col).astype(BF)
        for g in range(groups):
            at = g * 128
            q = kept_ref[0, at : at + 128, :CW]
            k = kept_ref[0, at : at + 128, CW : 2 * CW]
            v = kept_ref[0, at : at + 128, 2 * CW : 3 * CW]
            s = nt(k, head_stack(q, 1.0 / math.sqrt(CHD))).reshape(places, words, CHEADS * 128)
            cnt = count_ref[0, pl.ds(g * words, words), :]
            cnt4 = jnp.concatenate([cnt] * CHEADS, axis=1)
            place = lax.broadcasted_iota(jnp.int32, (places, words, CHEADS * 128), 0).astype(F32)
            s = jnp.where(place < cnt4[None], s, -1e30)
            e = jnp.exp(s - jnp.max(s, axis=0)[None])
            r = jnp.where(mine & (spot < cnt4), 1.0 / jnp.sum(e, axis=0), 0.0)
            p = (e * r[None]).astype(BF).reshape(128, CHEADS * 128)
            kept_ref[0, at : at + 128, 3 * CW : 3 * CW + CHEADS * 128] = p
            c = nn(p, same_head)
            kept_ref[0, at : at + 128, 3 * CW + CHEADS * 128 :] = c.astype(BF)
            msum_ref[pl.ds(pl.multiple_of(step * share + g * words, words), words), :] = jnp.sum(
                (c * v.astype(F32)).reshape(places, words, CW), axis=0
            )

    for (number, places, words), order_ref in zip(classes, orders):
        pl.when(kind[step] == number)(functools.partial(block, places, words, order_ref))

    @pl.when(step == pl.num_programs(0) - 1)
    def _():
        cnt2 = jnp.concatenate([counts[...]] * 2, axis=1)
        summed = sumx[...] + nn(msum_ref[...].astype(BF), mats_ref[:, 3 * CW : 4 * CW])
        pooled = (summed / cnt2).astype(BF)
        pooled_ref[...] = pooled
        vec_ref[...] = nn(pooled, mats_ref[:, 4 * CW :]).astype(BF)


def char_kind(block_home, char_count, share):
    places = jnp.max(char_count, axis=1)
    kind = jnp.where(places <= 8, 2, 4)
    if share >= 32:
        kind = jnp.where(places <= 4, 1, kind)
    return jnp.where(block_home >= 0, kind, 0).astype(jnp.int32)


def whole(shape):
    return pl.BlockSpec(shape, lambda i, *_: (0,) * len(shape))


def char_forward(x, kind, counts, gain, mats):
    slots, share = x.shape[:2]
    classes = char_classes(share)
    rows = share * SPOTS
    orders = [order_matrix(p, w) for _, p, w in classes]
    words_all = slots * share
    per_slot = lambda shape: pl.BlockSpec((1,) + shape, lambda i, *_: (i,) + (0,) * len(shape))
    return pl.pallas_call(
        functools.partial(char_forward_kernel, classes),
        grid_spec=pltpu.PrefetchScalarGridSpec(
            num_scalar_prefetch=1,
            grid=(slots,),
            in_specs=[
                per_slot((rows, CW)),
                per_slot((share, 128)),
                whole((1, CW)),
                whole(mats.shape),
            ]
            + [whole(o.shape) for o in orders],
            out_specs=[
                whole((words_all, D)),
                per_slot((rows, KEPT)),
                whole((words_all, CW)),
                whole((words_all, CW)),
            ],
            scratch_shapes=[
                pltpu.VMEM((words_all, CW), F32),
                pltpu.VMEM((words_all, 128), F32),
            ],
        ),
        out_shape=[
            jax.ShapeDtypeStruct((words_all, D), BF),
            jax.ShapeDtypeStruct((slots, rows, KEPT), BF),
            jax.ShapeDtypeStruct((words_all, CW), BF),
            jax.ShapeDtypeStruct((words_all, CW), F32),
        ],
        compiler_params=pltpu.CompilerParams(vmem_limit_bytes=40 << 20),
        cost_estimate=pl.CostEstimate(
            flops=slots * rows * CW * CW * 16, bytes_accessed=slots * rows * KEPT * 3, transcendentals=0
        ),
        name="char_forward",
    )(kind, x.reshape(slots, rows, CW), counts, gain.reshape(1, CW), mats, *orders)


def char_backward_kernel(
    classes, kind, x_ref, count_ref, kept_ref, all_counts_ref, gv_ref, pooled_ref, msum_ref,
    gain_ref, mats_ref, *refs
):
    orders = refs[: len(classes)]
    dx_ref, grads_ref, dgain_ref, gp_all, gm_all, dh, normed_all, dqkv_sum = refs[len(classes) :]
    step = pl.program_id(0)
    share = count_ref.shape[1]
    base = step * share

    @pl.when(step == 0)
    def _():
        gv = gv_ref[...]
        cnt2 = jnp.concatenate([all_counts_ref[...]] * 2, axis=1)
        gp = nt(gv, mats_ref[:, 4 * CW :]) / cnt2
        gp_all[...] = gp
        gpb = gp.astype(BF)
        gm_all[...] = nt(gpb, mats_ref[:, 3 * CW : 4 * CW]).astype(BF).astype(F32)
        grads_ref[:, 4 * CW :] = tn(pooled_ref[...], gv).astype(BF)
        grads_ref[:, 3 * CW : 4 * CW] = tn(msum_ref[...].astype(BF), gpb).astype(BF)
        dqkv_sum[...] = jnp.zeros_like(dqkv_sum)
        dgain_ref[...] = jnp.zeros_like(dgain_ref)

    @pl.when(kind[step] == 0)
    def _():
        dx_ref[...] = jnp.zeros_like(dx_ref)

    def block(places, words, order_ref):
        groups = share // words
        rows = groups * 128
        gain = gain_ref[...]
        xs = []
        scales = []
        gps = []
        for g in range(groups):
            at = g * 128
            x = nn(order_ref[...], x_ref[0, pl.ds(g * words * SPOTS, words * SPOTS), :])
            scale = lax.rsqrt(jnp.mean(x * x, axis=-1, keepdims=True) + epsilon)
            normed_all[at : at + 128, :] = (x * scale * gain).astype(BF)
            xs.append(x)
            scales.append(scale)
            mine = pl.ds(pl.multiple_of(base + g * words, words), words)
            cnt = count_ref[0, pl.ds(g * words, words), :]
            cnt2 = jnp.concatenate([cnt, cnt], axis=1)
            place = lax.broadcasted_iota(jnp.int32, (places, words, CW), 0).astype(F32)
            shown = place < cnt2[None]
            gps.append(jnp.where(shown, gp_all[mine, :][None], 0.0).reshape(128, CW))
            gm_word = gm_all[mine, :]
            gm = jnp.where(shown, gm_word[None], 0.0).reshape(128, CW).astype(BF)
            q = kept_ref[0, at : at + 128, :CW]
            k = kept_ref[0, at : at + 128, CW : 2 * CW]
            v = kept_ref[0, at : at + 128, 2 * CW : 3 * CW]
            p = kept_ref[0, at : at + 128, 3 * CW : 3 * CW + CHEADS * 128].astype(F32)
            c = kept_ref[0, at : at + 128, 3 * CW + CHEADS * 128 :].astype(F32)
            dp = nt(v, head_stack(gm, 1.0))
            p3 = p.reshape(places, words, CHEADS * 128)
            t = p3 * dp.reshape(places, words, CHEADS * 128)
            ds = (t - p3 * jnp.sum(t, axis=0)[None]).astype(BF).reshape(128, CHEADS * 128)
            eighth = 1.0 / math.sqrt(CHD)
            dk = nn(ds, head_stack(q, eighth))
            ds_rows = jnp.concatenate([ds[:, h * 128 : (h + 1) * 128] for h in range(CHEADS)], axis=0)
            dq = tn(ds_rows, head_stack(k, eighth))
            dv = (c.reshape(places, words, CW) * gm_word[None]).reshape(128, CW)
            dh[at : at + 128, :CW] = dq.astype(BF)
            dh[at : at + 128, CW : 2 * CW] = dk.astype(BF)
            dh[at : at + 128, 2 * CW :] = dv.astype(BF)
        grads = dh[:rows, :]
        dqkv_sum[...] += tn(normed_all[:rows, :], grads)
        dn_all = nt(grads, mats_ref[:, : 3 * CW])
        dgain = jnp.zeros((1, CW), F32)
        for g in range(groups):
            x, scale = xs[g], scales[g]
            dn = dn_all[g * 128 : (g + 1) * 128]
            xr = x * scale
            dgain = dgain + jnp.sum(xr * dn, axis=0, keepdims=True)
            w = dn * gain
            inner = jnp.mean(xr * w, axis=-1, keepdims=True)
            dx = gps[g] + scale * (w - xr * inner)
            dx_ref[0, pl.ds(g * words * SPOTS, words * SPOTS), :] = tn(
                order_ref[...], dx.astype(BF)
            ).astype(BF)
        dgain_ref[...] += dgain

    for (number, places, words), order_ref in zip(classes, orders):
        pl.when(kind[step] == number)(functools.partial(block, places, words, order_ref))

    @pl.when(step == pl.num_programs(0) - 1)
    def _():
        grads_ref[:, : 3 * CW] = dqkv_sum[...].astype(BF)


def char_backward(x, kind, counts, gain, mats, kept, pooled, msum, grad_vectors):
    slots, share = x.shape[:2]
    classes = char_classes(share)
    rows = share * SPOTS
    orders = [order_matrix(p, w) for _, p, w in classes]
    words_all = slots * share
    per_slot = lambda shape: pl.BlockSpec((1,) + shape, lambda i, *_: (i,) + (0,) * len(shape))
    dx, grads, dgain = pl.pallas_call(
        functools.partial(char_backward_kernel, classes),
        grid_spec=pltpu.PrefetchScalarGridSpec(
            num_scalar_prefetch=1,
            grid=(slots,),
            in_specs=[
                per_slot((rows, CW)),
                per_slot((share, 128)),
                per_slot((rows, KEPT)),
                whole((words_all, 128)),
                whole((words_all, D)),
                whole((words_all, CW)),
                whole((words_all, CW)),
                whole((1, CW)),
                whole(mats.shape),
            ]
            + [whole(o.shape) for o in orders],
            out_specs=[
                per_slot((rows, CW)),
                whole(mats.shape),
                whole((1, CW)),
            ],
            scratch_shapes=[
                pltpu.VMEM((words_all, CW), F32),
                pltpu.VMEM((words_all, CW), F32),
                pltpu.VMEM((rows, 3 * CW), BF),
                pltpu.VMEM((rows, CW), BF),
                pltpu.VMEM((CW, 3 * CW), F32),
            ],
        ),
        out_shape=[
            jax.ShapeDtypeStruct((slots, rows, CW), BF),
            jax.ShapeDtypeStruct(mats.shape, BF),
            jax.ShapeDtypeStruct((1, CW), F32),
        ],
        compiler_params=pltpu.CompilerParams(vmem_limit_bytes=40 << 20),
        cost_estimate=pl.CostEstimate(
            flops=slots * rows * CW * CW * 28, bytes_accessed=slots * rows * KEPT * 3, transcendentals=0
        ),
        name="char_backward",
    )(
        kind, x.reshape(slots, rows, CW), counts, kept, counts.reshape(words_all, 128), grad_vectors,
        pooled, msum, gain.reshape(1, CW), mats, *orders,
    )
    return dx.reshape(x.shape), grads, dgain


MESH_ID = pl.DeviceIdType.MESH


def exchange(name, number, tasks):
    sizes = {axis: lax.axis_size(axis) for _, axis, _ in tasks}
    outs, scratch, counts, shapers = [], [], [], []
    for kind, axis, arrays in tasks:
        n = sizes[axis]
        array = arrays[0]
        shaper = lambda a: a
        if kind == "gather":
            rows = array.shape[1]
            cols = sum(a.shape[0] * a.shape[2] for a in arrays)
            made = jax.ShapeDtypeStruct((n * rows, cols) if rows % 16 == 0 else (n, rows, cols), BF)
            shaper = lambda a, rows=rows, cols=cols, n=n: a.reshape(n * rows, cols)
        elif kind == "gather_mid":
            lead, rows, cols = array.shape
            made = jax.ShapeDtypeStruct(
                (lead, n * rows, cols) if rows % 16 == 0 else (n, lead, rows, cols), array.dtype
            )
            if rows % 16:
                shaper = lambda a, lead=lead, rows=rows, cols=cols, n=n: a.transpose(1, 0, 2, 3).reshape(
                    lead, n * rows, cols
                )
        else:
            block = array.shape if kind in ("line_gather", "total") else array.shape[1:]
            summed = kind in ("part", "line_part", "total")
            made = jax.ShapeDtypeStruct(block if summed else (n,) + block, F32 if summed else array.dtype)
        outs.append(made)
        shapers.append(shaper)
        counts.append(len(arrays))
        scratch += [pltpu.SemaphoreType.DMA((2, n)), pltpu.SemaphoreType.DMA((2, n))]
        if kind in ("part", "total"):
            scratch.append(pltpu.VMEM((n,) + block, array.dtype))
        if kind == "line_part":
            scratch.append(pltpu.VMEM((2, n) + block, array.dtype))
    total_ins = sum(counts)

    def kernel(*refs):
        ins, at = [], 0
        for count in counts:
            ins.append(refs[at : at + count])
            at += count
        results = refs[at : at + len(tasks)]
        rest = list(refs[at + len(tasks) :])
        me = {axis: lax.axis_index(axis) for axis in sizes}
        barrier = pltpu.get_barrier_semaphore()
        for axis, n in sizes.items():
            for d in range(1, n):
                pl.semaphore_signal(
                    barrier, inc=1, device_id={axis: lax.rem(me[axis] + d, n)}, device_id_type=MESH_ID
                )
        pl.semaphore_wait(barrier, sum(n - 1 for n in sizes.values()))

        def remote(source, target, sems, row, at, axis, peer):
            return pltpu.make_async_remote_copy(
                src_ref=source,
                dst_ref=target,
                send_sem=sems[0].at[row, at],
                recv_sem=sems[1].at[row, at],
                device_id={axis: peer},
                device_id_type=MESH_ID,
            )

        plans = []
        for (kind, axis, _), x, out in zip(tasks, ins, results):
            sems = (rest.pop(0), rest.pop(0))
            held = rest.pop(0) if kind in ("part", "line_part", "total") else out
            plans.append([kind, axis, x if kind == "gather" else x[0], out, sems, held, []])

        steps = []
        for plan in plans:
            kind, axis, x, out, sems, held, copies = plan
            n, mine = sizes[axis], me[axis]
            if kind == "line_gather":
                out[mine] = x[...]
                steps.append([line_gather_step(remote, out, sems, axis, n, mine, k) for k in range(n)])
            if kind == "line_part":
                steps.append([line_part_step(remote, x, held, sems, axis, n, mine, k) for k in range(n - 1)])
        for step in steps:
            step[0]()
        for plan in plans:
            kind, axis, x, out, sems, held, copies = plan
            n, mine = sizes[axis], me[axis]
            if "line" in kind:
                continue
            if kind == "gather":
                rows = x[0].shape[1]
                if rows % 16 == 0:
                    own = out.at[pl.ds(pl.multiple_of(mine * rows, 16), rows), :]
                else:
                    own = out.at[mine]
                col = 0
                for piece in x:
                    for t in range(piece.shape[0]):
                        own[:, col : col + piece.shape[2]] = piece[t].astype(BF)
                        col += piece.shape[2]
            elif kind == "gather_mid":
                rows = x.shape[1]
                if rows % 16 == 0:
                    own = out.at[:, pl.ds(pl.multiple_of(mine * rows, 16), rows), :]
                else:
                    own = out.at[mine]
                own[...] = x[...]
            else:
                own = held.at[mine]
                held[mine] = x[...] if kind == "total" else x[mine]
            for d in range(1, n):
                peer = lax.rem(mine + d, n)
                source = x.at[peer] if kind in ("swap", "part") else own
                copies.append(remote(source, own, sems, 0, d, axis, peer))
            for copy in copies:
                copy.start()
        for step in steps:
            for run in step[1:]:
                run()
        for kind, axis, x, out, sems, held, copies in plans:
            n, mine = sizes[axis], me[axis]
            for copy in copies:
                copy.wait()
            if kind in ("part", "total"):
                total = held[0].astype(F32)
                for p in range(1, n):
                    total = total + held[p].astype(F32)
                out[...] = total
            if kind == "line_part":
                out[...] = x[mine].astype(F32)
                for way, there in ((0, mine > 0), (1, mine < n - 1)):

                    @pl.when(there)
                    def _(way=way):
                        remote(held.at[way, mine], held.at[way, mine], sems, way, mine, axis, mine).wait_recv()
                        out[...] += held[way, mine].astype(F32)

            if "line" in kind:
                for way in range(2):
                    for k in range(n):
                        if kind == "line_gather":
                            block = mine - k if way == 0 else mine + k
                            sent = (mine < n - 1) & (block >= 0) if way == 0 else (mine > 0) & (block < n)
                            sent = sent & (k < n - 1)
                            at = k
                            block = jnp.clip(block, 0, n - 1)
                            piece = out.at[block]
                        else:
                            sent = k > mine if way == 0 else k < mine
                            at = k
                            piece = held.at[way, k]

                        @pl.when(sent)
                        def _(way=way, at=at, piece=piece):
                            remote(piece, piece, sems, way, at, axis, mine).wait_send()

    vmem = pl.BlockSpec(memory_space=pltpu.VMEM)
    results = pl.pallas_call(
        kernel,
        out_shape=outs,
        in_specs=[vmem] * total_ins,
        out_specs=[vmem] * len(tasks),
        scratch_shapes=scratch,
        compiler_params=pltpu.CompilerParams(
            collective_id=number, has_side_effects=True, vmem_limit_bytes=48 << 20
        ),
        name=name,
    )(*[array for _, _, arrays in tasks for array in arrays])
    return [shaper(a) for shaper, a in zip(shapers, results)]


def line_gather_step(remote, out, sems, axis, n, mine, k):
    def run():
        for way in range(2):
            block = mine - k if way == 0 else mine + k
            held_here = (block >= 0) & (block < n)
            block = jnp.clip(block, 0, n - 1)
            onward = mine + 1 if way == 0 else mine - 1
            room = (onward >= 0) & (onward < n)
            peer = jnp.clip(onward, 0, n - 1)
            if k > 0:

                @pl.when(held_here)
                def _(way=way, block=block):
                    remote(out.at[block], out.at[block], sems, way, k - 1, axis, mine).wait_recv()

            if k < n - 1:

                @pl.when(held_here & room)
                def _(way=way, block=block, peer=peer):
                    remote(out.at[block], out.at[block], sems, way, k, axis, peer).start()

    return run


def line_part_step(remote, x, held, sems, axis, n, mine, k):
    def run():
        for way in range(2):
            block = n - 1 - k if way == 0 else k
            further = block > mine if way == 0 else block < mine
            first = mine == 0 if way == 0 else mine == n - 1
            peer = jnp.clip(mine + 1 if way == 0 else mine - 1, 0, n - 1)

            @pl.when(further & first)
            def _(way=way, block=block, peer=peer):
                remote(x.at[block], held.at[way, block], sems, way, block, axis, peer).start()

            @pl.when(further & jnp.logical_not(first))
            def _(way=way, block=block, peer=peer):
                here = held.at[way, block]
                remote(here, here, sems, way, block, axis, mine).wait_recv()
                held[way, block] = (held[way, block].astype(F32) + x[block].astype(F32)).astype(x.dtype)
                remote(here, here, sems, way, block, axis, peer).start()

    return run


def sum_char_grads(grads, small, word_sums):
    n, m = lax.axis_size("dp"), lax.axis_size("mp")
    block = grads.shape[1:]

    def kernel(x, s, *refs):
        words = refs[: len(word_sums)]
        out, small_out, held, held_z, small_dp, small_mp, ss, rs = refs[len(word_sums) :]
        i, j = lax.axis_index("dp"), lax.axis_index("mp")
        barrier = pltpu.get_barrier_semaphore()
        for d in range(1, n):
            pl.semaphore_signal(barrier, inc=1, device_id={"dp": lax.rem(i + d, n)}, device_id_type=MESH_ID)
        for d in range(1, m):
            pl.semaphore_signal(barrier, inc=1, device_id={"mp": lax.rem(j + d, m)}, device_id_type=MESH_ID)
        pl.semaphore_wait(barrier, n + m - 2)

        def send(axis, me, count, source, target, phase):
            copies = []
            for d in range(1, count):
                peer = lax.rem(me + d, count)
                copies.append(
                    pltpu.make_async_remote_copy(
                        src_ref=source(peer), dst_ref=target.at[me], send_sem=ss.at[phase, d],
                        recv_sem=rs.at[phase, d], device_id={axis: peer}, device_id_type=MESH_ID,
                    )
                )
            for copy in copies:
                copy.start()
            return copies

        one = send("dp", i, n, lambda p: x.at[p], held, 1)
        held[i] = x[i]
        squares = jnp.zeros((1, 1), F32)
        for word in words:
            wide = word[...].astype(F32)
            squares = squares + jnp.sum(
                jnp.sum(wide * wide, axis=0, keepdims=True), axis=1, keepdims=True
            )
        row = lax.broadcasted_iota(jnp.int32, s.shape, 0)
        small_dp[i] = s[...] + jnp.where(row == 3, squares * (1.0 / n), 0.0)
        small_one = send("dp", i, n, lambda p: small_dp.at[i], small_dp, 0)
        for copy in small_one:
            copy.wait()
        total = small_dp[0]
        for p in range(1, n):
            total = total + small_dp[p]
        small_mp[j] = total
        small_two = send("mp", j, m, lambda p: small_mp.at[j], small_mp, 2)
        for copy in one:
            copy.wait()
        total = held[0].astype(F32)
        for p in range(1, n):
            total = total + held[p].astype(F32)
        held_z[j] = total.astype(BF)
        two = send("mp", j, m, lambda p: held_z.at[j], held_z, 3)
        for copy in small_two:
            copy.wait()
        total = small_mp[0]
        for p in range(1, m):
            total = total + small_mp[p]
        small_out[...] = total
        for copy in two:
            copy.wait()
        total = held_z[0].astype(F32)
        for p in range(1, m):
            total = total + held_z[p].astype(F32)
        out[i] = total.astype(BF)
        three = send("dp", i, n, lambda p: out.at[i], out, 4)
        for copy in three:
            copy.wait()

    vmem = pl.BlockSpec(memory_space=pltpu.VMEM)
    return pl.pallas_call(
        kernel,
        out_shape=[
            jax.ShapeDtypeStruct(grads.shape, BF),
            jax.ShapeDtypeStruct(small.shape, F32),
        ],
        in_specs=[vmem] * (2 + len(word_sums)),
        out_specs=[vmem] * 2,
        scratch_shapes=[
            pltpu.VMEM((n,) + block, BF),
            pltpu.VMEM((m,) + block, BF),
            pltpu.VMEM((n,) + small.shape, F32),
            pltpu.VMEM((m,) + small.shape, F32),
            pltpu.SemaphoreType.DMA((5, max(n, m))),
            pltpu.SemaphoreType.DMA((5, max(n, m))),
        ],
        compiler_params=pltpu.CompilerParams(
            collective_id=20, has_side_effects=True, vmem_limit_bytes=48 << 20
        ),
        name="sum_char_grads",
    )(grads, small, *word_sums)


ROWS = 256


def rms_scale(values):
    return lax.rsqrt(jnp.mean(values * values, axis=-1, keepdims=True) + epsilon)


def norm_back(values, scale, gain_row, grad):
    weighted = grad * gain_row
    inner = jnp.mean(values * weighted, axis=-1, keepdims=True)
    return scale * weighted - values * (scale * scale * scale) * inner


def word_forward_kernel(
    width, vec_ref, place_ref, words_ref, doc_ref, doc_row_ref, gain_ref, project_ref,
    stream_ref, normed_ref, qkv_ref, probs_ref, mixed_ref, keys, values
):
    step = pl.program_id(0)
    numbers = lax.broadcasted_iota(jnp.int32, (ROWS, place_ref.shape[1]), 0) + step * ROWS
    placed = nn((numbers == place_ref[...]).astype(BF), vec_ref[...])
    stream = words_ref[...].astype(F32) + placed
    stream_ref[...] = stream
    normed = (stream * rms_scale(stream) * gain_ref[...]).astype(BF)
    normed_ref[...] = normed
    qkv = nn(normed, project_ref[...]).astype(BF)
    qkv_ref[...] = qkv
    first = pl.ds(pl.multiple_of(step * ROWS, ROWS), ROWS)
    keys[first, :] = qkv[:, width : 2 * width]
    values[first, :] = qkv[:, 2 * width :]
    queries = (qkv[:, :width].astype(F32) * (1.0 / math.sqrt(HD))).astype(BF)

    def attend(number):
        count = (number + 1) * ROWS
        same = doc_ref[:count, :] == doc_row_ref[...]
        key_at = lax.broadcasted_iota(jnp.int32, (count, ROWS), 0)
        query_at = lax.broadcasted_iota(jnp.int32, (count, ROWS), 1) + number * ROWS
        allowed = same & (key_at <= query_at)
        parts = []
        for head in range(width // HD):
            at = slice(head * HD, (head + 1) * HD)
            scores = jnp.where(allowed, nt(keys[:count, at], queries[:, at]), negative_big)
            raised = jnp.exp(scores - jnp.max(scores, axis=0, keepdims=True))
            probs = (raised * (1.0 / jnp.sum(raised, axis=0, keepdims=True))).astype(BF)
            probs_ref[head, :count, :] = probs
            parts.append(tn(values[:count, at], probs).T)
        mixed_ref[...] = jnp.concatenate(parts, axis=1).astype(BF)

    for number in range(doc_ref.shape[0] // ROWS):
        pl.when(step == number)(functools.partial(attend, number))


def word_forward(vectors, places, words, documents, gain, project):
    length = words.shape[0]
    width = project.shape[1] // 3
    heads = width // HD
    rows = lambda cols: pl.BlockSpec((ROWS, cols), lambda i: (i, 0))
    full = lambda shape: pl.BlockSpec(shape, lambda i: (0,) * len(shape))
    return pl.pallas_call(
        functools.partial(word_forward_kernel, width),
        grid=(length // ROWS,),
        in_specs=[
            full(vectors.shape),
            full((1, places.shape[0])),
            rows(D),
            full((length, 1)),
            pl.BlockSpec((1, ROWS), lambda i: (0, i)),
            full((1, D)),
            full(project.shape),
        ],
        out_specs=[
            rows(D),
            rows(D),
            rows(3 * width),
            pl.BlockSpec((heads, length, ROWS), lambda i: (0, 0, i)),
            rows(width),
        ],
        out_shape=[
            jax.ShapeDtypeStruct((length, D), F32),
            jax.ShapeDtypeStruct((length, D), BF),
            jax.ShapeDtypeStruct((length, 3 * width), BF),
            jax.ShapeDtypeStruct((heads, length, length), BF),
            jax.ShapeDtypeStruct((length, width), BF),
        ],
        scratch_shapes=[pltpu.VMEM((length, width), BF), pltpu.VMEM((length, width), BF)],
        compiler_params=pltpu.CompilerParams(vmem_limit_bytes=48 << 20),
        name="word_forward",
    )(
        vectors,
        places.reshape(1, -1),
        words,
        documents.reshape(length, 1),
        documents.reshape(1, length),
        gain.reshape(1, D),
        project,
    )


def feed_kernel(
    mixed_ref, output_ref, stream_ref, cot_ref, gain_ref, upper_ref, lower_ref,
    hidden_ref, feed_ref, part_ref, grad_upper_ref, grad_lower_ref, upper_sum, lower_sum
):
    step = pl.program_id(0)

    @pl.when(step == 0)
    def _():
        upper_sum[...] = jnp.zeros_like(upper_sum)
        lower_sum[...] = jnp.zeros_like(lower_sum)

    parts, _, width = mixed_ref.shape
    hidden = stream_ref[...]
    for j in range(parts):
        hidden = hidden + nn(mixed_ref[j], output_ref[j * width : (j + 1) * width, :])
    hidden_ref[...] = hidden
    normed = (hidden * rms_scale(hidden) * gain_ref[...]).astype(BF)
    raised = nn(normed, upper_ref[...])
    constant = math.sqrt(2.0 / math.pi)
    square = raised * raised
    curve = jnp.tanh(constant * raised * (1.0 + 0.044715 * square))
    half = 0.5 * (1.0 + curve)
    active = (raised * half).astype(BF)
    slope = half + 0.5 * raised * (1.0 - curve * curve) * constant * (1.0 + 3.0 * 0.044715 * square)
    feed_ref[...] = nn(active, lower_ref[...]).astype(BF)
    grad_feed = cot_ref[...]
    grad_raised = (nt(grad_feed, lower_ref[...]) * slope).astype(BF)
    part_ref[...] = nt(grad_raised, upper_ref[...]).astype(BF)
    lower_sum[...] += tn(active, grad_feed)
    upper_sum[...] += tn(normed, grad_raised)

    @pl.when(step == pl.num_programs(0) - 1)
    def _():
        grad_upper_ref[...] = upper_sum[...].astype(BF)
        grad_lower_ref[...] = lower_sum[...].astype(BF)


def feed(mixed, output, stream, cotangent, gain, upper, lower):
    length = stream.shape[0]
    rows = pl.BlockSpec((ROWS, D), lambda i: (i, 0))
    full = lambda shape: pl.BlockSpec(shape, lambda i: (0,) * len(shape))
    return pl.pallas_call(
        feed_kernel,
        grid=(length // ROWS,),
        in_specs=[
            pl.BlockSpec((mixed.shape[0], ROWS, mixed.shape[2]), lambda i: (0, i, 0)),
            full(output.shape),
            rows,
            rows,
            full((1, D)),
            full(upper.shape),
            full(lower.shape),
        ],
        out_specs=[rows, rows, rows, full(upper.shape), full(lower.shape)],
        out_shape=[
            jax.ShapeDtypeStruct((length, D), F32),
            jax.ShapeDtypeStruct((length, D), BF),
            jax.ShapeDtypeStruct((length, D), BF),
            jax.ShapeDtypeStruct(upper.shape, BF),
            jax.ShapeDtypeStruct(lower.shape, BF),
        ],
        scratch_shapes=[pltpu.VMEM(upper.shape, F32), pltpu.VMEM(lower.shape, F32)],
        compiler_params=pltpu.CompilerParams(vmem_limit_bytes=48 << 20),
        name="feed",
    )(mixed, output, stream, cotangent, gain.reshape(1, D), upper, lower)


def hidden_back_kernel(
    own, grad_ref, hidden_ref, cot_ref, mixed_ref, output_ref, gain_ref,
    grad_hidden_ref, grad_mixed_ref, grad_output_ref, gain_grad_ref
):
    hidden = hidden_ref[...]
    scale = rms_scale(hidden)
    grad = grad_ref[...]
    grad_hidden = cot_ref[...].astype(F32) + norm_back(hidden, scale, gain_ref[...], grad)
    grad_hidden_ref[...] = grad_hidden
    gain_grad_ref[...] = jnp.sum(hidden * scale * grad, axis=0, keepdims=True)
    attend = grad_hidden.astype(BF)
    parts, _, width = mixed_ref.shape
    for j in range(parts):
        at = slice(j * width, (j + 1) * width)
        grad_mixed_ref[j] = nt(attend, output_ref[at, :]).astype(BF)
        grad_output_ref[at, :] = tn(mixed_ref[j], attend).astype(BF)


def hidden_back(own, grad, hidden, cotangent, mixed, output, gain):
    share = grad.shape[0]
    parts, _, width = mixed.shape
    mine = pl.BlockSpec((share, D), lambda i, own: (own[0], 0))
    full = lambda shape: pl.BlockSpec(shape, lambda i, own: (0,) * len(shape))
    return pl.pallas_call(
        hidden_back_kernel,
        grid_spec=pltpu.PrefetchScalarGridSpec(
            num_scalar_prefetch=1,
            grid=(1,),
            in_specs=[
                full((share, D)),
                mine,
                mine,
                pl.BlockSpec((parts, share, width), lambda i, own: (0, own[0], 0)),
                full(output.shape),
                full((1, D)),
            ],
            out_specs=[
                full((share, D)),
                full((parts, share, width)),
                full(output.shape),
                full((1, D)),
            ],
        ),
        out_shape=[
            jax.ShapeDtypeStruct((share, D), F32),
            jax.ShapeDtypeStruct((parts, share, width), BF),
            jax.ShapeDtypeStruct(output.shape, BF),
            jax.ShapeDtypeStruct((1, D), F32),
        ],
        compiler_params=pltpu.CompilerParams(vmem_limit_bytes=48 << 20),
        name="hidden_back",
    )(own, grad, hidden, cotangent, mixed, output, gain.reshape(1, D))


def word_backward_kernel(
    width, probs_ref, qkv_ref, all_ref, grad_ref, normed_ref, project_ref,
    part_ref, grad_project_ref, grads, key_sum, value_sum
):
    step = pl.program_id(0)
    steps = all_ref.shape[0] // ROWS
    first = pl.ds(pl.multiple_of(step * ROWS, ROWS), ROWS)
    eighth = 1.0 / math.sqrt(HD)
    queries = (qkv_ref[:, :width].astype(F32) * eighth).astype(BF)

    @pl.when(step == 0)
    def _():
        key_sum[...] = jnp.zeros_like(key_sum)
        value_sum[...] = jnp.zeros_like(value_sum)

    def attend(number):
        count = (number + 1) * ROWS
        parts = []
        for head in range(width // HD):
            at = slice(head * HD, (head + 1) * HD)
            keys = all_ref[:count, width + head * HD : width + (head + 1) * HD]
            values = all_ref[:count, 2 * width + head * HD : 2 * width + (head + 1) * HD]
            grad = grad_ref[:, at]
            probs = probs_ref[head, :count, :]
            wide = probs.astype(F32)
            product = wide * nt(values, grad)
            scores = (product - wide * jnp.sum(product, axis=0, keepdims=True)).astype(BF)
            key_sum[head, :count, :] += nn(scores, queries[:, at])
            value_sum[head, :count, :] += nn(probs, grad)
            parts.append(tn(keys, scores).T * eighth)
        grads[first, :width] = jnp.concatenate(parts, axis=1).astype(BF)

    for number in range(steps):
        pl.when(step == number)(functools.partial(attend, number))

    @pl.when(step == steps - 1)
    def _():
        for head in range(width // HD):
            grads[:, width + head * HD : width + (head + 1) * HD] = key_sum[head].astype(BF)
            grads[:, 2 * width + head * HD : 2 * width + (head + 1) * HD] = value_sum[head].astype(BF)
        grad_project_ref[...] = tn(normed_ref[...], grads[...]).astype(BF)
        part_ref[...] = nt(grads[...], project_ref[...]).astype(BF)


def word_backward(probs, qkv, grad_mixed, normed, project):
    length = qkv.shape[0]
    width = project.shape[1] // 3
    heads = width // HD
    rows = lambda cols: pl.BlockSpec((ROWS, cols), lambda i: (i, 0))
    full = lambda shape: pl.BlockSpec(shape, lambda i: (0,) * len(shape))
    return pl.pallas_call(
        functools.partial(word_backward_kernel, width),
        grid=(length // ROWS,),
        in_specs=[
            pl.BlockSpec((heads, length, ROWS), lambda i: (0, 0, i)),
            rows(3 * width),
            full(qkv.shape),
            rows(width),
            full(normed.shape),
            full(project.shape),
        ],
        out_specs=[full((length, D)), full(project.shape)],
        out_shape=[
            jax.ShapeDtypeStruct((length, D), BF),
            jax.ShapeDtypeStruct(project.shape, BF),
        ],
        scratch_shapes=[
            pltpu.VMEM(qkv.shape, BF),
            pltpu.VMEM((heads, length, HD), F32),
            pltpu.VMEM((heads, length, HD), F32),
        ],
        compiler_params=pltpu.CompilerParams(vmem_limit_bytes=48 << 20),
        name="word_backward",
    )(probs, qkv, qkv, grad_mixed, normed, project)


def stream_back_kernel(own, grad_ref, stream_ref, hidden_grad_ref, gain_ref, out_ref, gain_grad_ref):
    stream = stream_ref[...]
    scale = rms_scale(stream)
    grad = grad_ref[...]
    total = hidden_grad_ref[...] + norm_back(stream, scale, gain_ref[...], grad)
    out_ref[...] = total.astype(BF)
    gain_grad_ref[...] = jnp.sum(stream * scale * grad, axis=0, keepdims=True)


def stream_back(own, grad, stream, hidden_grad, gain):
    share = grad.shape[0]
    full = lambda shape: pl.BlockSpec(shape, lambda i, own: (0,) * len(shape))
    return pl.pallas_call(
        stream_back_kernel,
        grid_spec=pltpu.PrefetchScalarGridSpec(
            num_scalar_prefetch=1,
            grid=(1,),
            in_specs=[
                full((share, D)),
                pl.BlockSpec((share, D), lambda i, own: (own[0], 0)),
                full((share, D)),
                full((1, D)),
            ],
            out_specs=[full((share, D)), full((1, D))],
        ),
        out_shape=[
            jax.ShapeDtypeStruct((share, D), BF),
            jax.ShapeDtypeStruct((1, D), F32),
        ],
        name="stream_back",
    )(own, grad, stream, hidden_grad, gain.reshape(1, D))


def shampoo_kernel(threshold, position, char_ref, small_ref, gain_ref, gains_ref, *refs):
    sums, refs = refs[:4], refs[4:]
    given, refs = [refs[5 * t : 5 * t + 5] for t in range(6)], refs[30:]
    norm_ref, gain_grad_ref, gains_grad_ref, gain_new_ref, gains_new_ref = refs[:5]
    made = [refs[5 + 5 * t : 10 + 5 * t] for t in range(6)]
    me = position[0]
    char = char_ref[...].astype(F32)
    small = small_ref[...]
    lanes = lax.broadcasted_iota(jnp.int32, small.shape, 0)
    squares = (
        jnp.sum(jnp.sum(char * char, axis=0, keepdims=True), axis=1, keepdims=True)
        + jnp.sum(
            jnp.sum(jnp.where(lanes < 3, small * small, 0.0), axis=0, keepdims=True),
            axis=1,
            keepdims=True,
        )
        + small[3:4, :1]
    )
    norm = jnp.sqrt(squares)
    factor = jnp.minimum(1.0, threshold / norm)
    norm_ref[...] = norm
    gain_grad = small[0:1, :CW] * factor
    gain_grad_ref[...] = gain_grad
    gain_new_ref[...] = gain_ref[...] - gain_rate * gain_grad
    gains_grad = small[1:3, :] * factor
    gains_grad_ref[...] = gains_grad
    gains_new_ref[...] = gains_ref[...] - gain_rate * gains_grad
    width = sums[0].shape[1] // 3

    def whole_of(number, t):
        if number == 0:
            return char_ref[:, t * CW : (t + 1) * CW]
        if number == 1:
            return char_ref[:, 4 * CW :]
        if number == 2:
            return sums[0][:, t * width : (t + 1) * width]
        return sums[number - 2][...]

    def chosen(rows, cols):
        row = lax.broadcasted_iota(jnp.int32, (rows, cols), 0) + me * rows
        return (row == lax.broadcasted_iota(jnp.int32, (rows, cols), 1)).astype(BF)

    half = (1.0 - decay_rate) * factor * factor
    for number in range(6):
        master, left, right, left_root, right_root = given[number]
        grad_out, left_out, right_out, new_out, copy_out = made[number]
        for t in range(master.shape[0]):
            grad = whole_of(number, t)
            own = nn(chosen(master.shape[1], grad.shape[0]), grad)
            grad_out[t] = own * factor
            left_out[t] = decay_rate * left[t] + half * nt(own.astype(BF), grad)
            cols = nt(grad, chosen(right.shape[1], grad.shape[1])).astype(BF)
            right_out[t] = decay_rate * right[t] + half * tn(cols, grad)
            turned = (nn(left_root[t].astype(BF), grad) * factor).astype(BF)
            new = master[t] - learn_rate * nn(turned, right_root[:, t * grad.shape[1] : (t + 1) * grad.shape[1]])
            new_out[t] = new
            copy_out[t] = new.astype(BF)


def shampoo(threshold, position, char_sums, small, gain, gains, word_sums, given):
    flat = []
    shapes = [
        jax.ShapeDtypeStruct((1, 1), F32),
        jax.ShapeDtypeStruct((1, CW), F32),
        jax.ShapeDtypeStruct((2, D), F32),
        jax.ShapeDtypeStruct((1, CW), F32),
        jax.ShapeDtypeStruct((2, D), F32),
    ]
    for master, left, right, left_root, right_root in given:
        flat += [master, left, right, left_root, right_root]
        shapes += [
            jax.ShapeDtypeStruct(a.shape, F32) for a in (master, left, right, master)
        ] + [jax.ShapeDtypeStruct(master.shape, BF)]
    vmem = pl.BlockSpec(memory_space=pltpu.VMEM)
    smem = pl.BlockSpec(memory_space=pltpu.SMEM)
    return pl.pallas_call(
        functools.partial(shampoo_kernel, threshold),
        in_specs=[smem] + [vmem] * (4 + len(word_sums) + len(flat)),
        out_specs=[vmem] * len(shapes),
        out_shape=shapes,
        compiler_params=pltpu.CompilerParams(vmem_limit_bytes=56 << 20),
        name="shampoo",
    )(position, char_sums, small, gain.reshape(1, CW), gains, *word_sums, *flat)


def local(
    word_inputs,
    character_embeddings,
    cotangent,
    char_count,
    word_place,
    block_home,
    documents,
    char_gain,
    word_gains,
    char_mixer,
    char_mixer_left,
    char_mixer_right,
    char_mixer_left_root,
    char_mixer_right_root,
    char_lift,
    char_lift_left,
    char_lift_right,
    char_lift_left_root,
    char_lift_right_root,
    word_project,
    word_project_left,
    word_project_right,
    word_project_left_root,
    word_project_right_root,
    word_output,
    word_output_left,
    word_output_right,
    word_output_left_root,
    word_output_right_root,
    feed_upper,
    feed_upper_left,
    feed_upper_right,
    feed_upper_left_root,
    feed_upper_right_root,
    feed_lower,
    feed_lower_left,
    feed_lower_right,
    feed_lower_left_root,
    feed_lower_right_root,
):
    slot_count, share_rows = (character_embeddings.shape[0], character_embeddings.shape[1])
    peer_count = lax.axis_size("dp")
    part_count = lax.axis_size("mp")
    owner_index = lax.axis_index("dp")
    pair_cap = -(-slot_count // peer_count)
    slot_total = peer_count * pair_cap
    rows_dev, length = (word_inputs.shape[0], word_inputs.shape[1])
    words_dev = rows_dev * length
    block_words = share_rows * part_count

    length = word_inputs.shape[1]
    own = lax.axis_index("mp").astype(jnp.int32).reshape(1)
    position = owner_index.astype(jnp.int32).reshape(1)
    peers = lax.broadcasted_iota(jnp.int32, (slot_count, peer_count), 1)
    owner_match = (block_home[:, None] == peers).astype(jnp.int32)
    earlier = (
        lax.broadcasted_iota(jnp.int32, (slot_count, slot_count), 1)
        < lax.broadcasted_iota(jnp.int32, (slot_count, slot_count), 0)
    )
    same_owner = block_home[:, None] == block_home[None, :]
    slot_rank = jnp.sum((earlier & same_owner).astype(jnp.int32), axis=1)
    slot_target = jnp.where(block_home >= 0, block_home * pair_cap + slot_rank, slot_total)
    to_slot = lax.broadcasted_iota(jnp.int32, (slot_total, slot_count), 0) == slot_target[None, :]

    sent_place = jnp.max(
        jnp.where(to_slot[:, :, None], word_place[None] + 1, 0), axis=1
    ) - 1
    char_whole, came_place, output_line = exchange(
        "gather_char",
        0,
        [
            ("gather", "dp", [char_mixer, char_lift]),
            ("swap", "dp", [sent_place.reshape(peer_count, pair_cap, block_words)]),
            ("gather", "mp", [word_output]),
        ],
    )
    came_place = came_place.reshape(slot_total, block_words)
    kind = char_kind(block_home, char_count, share_rows)
    counts = jnp.broadcast_to(
        char_count.astype(F32)[..., None], (slot_count, share_rows, 128)
    )
    word_vectors, kept, pooled, msum = char_forward(
        character_embeddings, kind, counts, char_gain, char_whole
    )

    live = jnp.max(came_place, axis=1) >= 0
    slots_before = (
        lax.broadcasted_iota(jnp.int32, (slot_total, slot_total), 1)
        < lax.broadcasted_iota(jnp.int32, (slot_total, slot_total), 0)
    )
    live_rank = jnp.sum((slots_before & live[None, :]).astype(jnp.int32), axis=1)
    live_rank = jnp.where(live, live_rank, OWNER_BLOCKS)
    to_live = lax.broadcasted_iota(jnp.int32, (OWNER_BLOCKS, slot_total), 0) == live_rank[None, :]
    live_place = jnp.max(jnp.where(to_live[:, :, None], came_place[None] + 1, 0), axis=1) - 1

    wide = share_rows * D
    sent = jnp.dot(
        to_slot.astype(BF), word_vectors.reshape(slot_count, wide), preferred_element_type=F32
    ).astype(BF)
    (came,) = exchange(
        "send_vectors", 1, [("swap", "dp", [sent.reshape(peer_count, pair_cap * share_rows, D)])]
    )
    compact = jnp.dot(
        to_live.astype(BF), came.reshape(slot_total, wide), preferred_element_type=F32
    ).astype(BF)
    live_vectors, project_mat, upper_mat, lower_mat, output_mat = exchange(
        "gather_words",
        2,
        [
            ("line_gather", "mp", [compact.reshape(OWNER_BLOCKS * share_rows, D)]),
            ("gather", "dp", [word_project.reshape((3,) + word_project.shape[2:])]),
            ("gather", "dp", [feed_upper]),
            ("gather", "dp", [feed_lower]),
            ("gather_mid", "dp", [output_line.reshape((part_count,) + word_output.shape[1:])]),
        ],
    )
    output_mat = output_mat.reshape(-1, D)
    place_parts = live_place.reshape(OWNER_BLOCKS, part_count, share_rows)
    place_flat = place_parts.transpose(1, 0, 2).reshape(-1)
    stream, normed_one, qkv, probs, mixed = word_forward(
        live_vectors.reshape(-1, D),
        place_flat,
        word_inputs.reshape(words_dev, D),
        documents,
        word_gains[0],
        project_mat,
    )
    mixed_all, mixer_root, lift_root = exchange(
        "gather_mixed",
        3,
        [
            ("line_gather", "mp", [mixed]),
            ("gather", "dp", [char_mixer_right_root]),
            ("gather", "dp", [char_lift_right_root]),
        ],
    )
    flat_cotangent = cotangent.reshape(words_dev, D)
    hidden, feed_part, part_two, grad_upper, grad_lower = feed(
        mixed_all, output_mat, stream, flat_cotangent, word_gains[1], upper_mat, lower_mat
    )
    shares = (part_count, words_dev // part_count, D)
    grad_two, project_root, output_root, upper_root, lower_root = exchange(
        "sum_part_two",
        4,
        [
            ("line_part", "mp", [part_two.reshape(shares)]),
            ("gather", "dp", [word_project_right_root.reshape((3,) + word_project_right_root.shape[2:])]),
            ("gather", "dp", [word_output_right_root]),
            ("gather", "dp", [feed_upper_right_root]),
            ("gather", "dp", [feed_lower_right_root]),
        ],
    )
    grad_hidden, grad_mixed, grad_output_mat, gain_two = hidden_back(
        own, grad_two, hidden, flat_cotangent, mixed_all, output_mat, word_gains[1]
    )
    by_peer = lambda g: g.reshape(peer_count, -1, g.shape[1])
    grad_mixed, part_upper = exchange(
        "swap_mixed",
        5,
        [("swap", "mp", [grad_mixed]), ("part", "dp", [by_peer(grad_upper)])],
    )
    part_one, grad_project = word_backward(
        probs, qkv, grad_mixed.reshape(words_dev, -1), normed_one, project_mat
    )
    grad_one, part_lower, part_project, part_output = exchange(
        "sum_part_one",
        6,
        [
            ("line_part", "mp", [part_one.reshape(shares)]),
            ("part", "dp", [by_peer(grad_lower)]),
            ("part", "dp", [by_peer(grad_project)]),
            ("part", "dp", [by_peer(grad_output_mat)]),
        ],
    )
    grad_own, gain_one = stream_back(own, grad_one, stream, grad_hidden, word_gains[0])
    grad_words, sum_upper, sum_lower, sum_project, total_output = exchange(
        "gather_stream",
        7,
        [
            ("line_gather", "mp", [grad_own]),
            ("gather", "dp", [part_upper[None]]),
            ("gather", "dp", [part_lower[None]]),
            ("gather", "dp", [part_project[None]]),
            ("total", "mp", [part_output.astype(BF)]),
        ],
    )
    grad_words = grad_words.reshape(words_dev, D)
    word_inputs_gradient = grad_words.reshape(word_inputs.shape)

    own_place = lax.dynamic_slice_in_dim(
        came_place.reshape(slot_total, part_count, share_rows), lax.axis_index("mp"), 1, 1
    ).reshape(-1)
    picked = jnp.dot(
        (
            own_place[:, None]
            == lax.broadcasted_iota(jnp.int32, (own_place.shape[0], words_dev), 1)
        ).astype(BF),
        grad_words,
        preferred_element_type=F32,
    ).astype(BF)
    returned, sum_output = exchange(
        "return_vectors",
        8,
        [
            ("swap", "dp", [picked.reshape(peer_count, pair_cap * share_rows, D)]),
            ("gather", "dp", [total_output[None]]),
        ],
    )
    own_rows = word_output.shape[1] * peer_count
    sum_output = lax.dynamic_slice_in_dim(sum_output, own[0] * own_rows, own_rows, 0)
    grad_vectors = (
        jnp.dot(to_slot.astype(BF).T, returned.reshape(slot_total, wide), preferred_element_type=F32)
        .astype(BF)
        .reshape(slot_count * share_rows, D)
    )
    grad_vectors, feed_part = lax.optimization_barrier((grad_vectors, feed_part))
    feed_total = lax.psum(feed_part, "mp").astype(F32)
    block_out = (hidden + feed_total).astype(BF).reshape(word_inputs.shape)
    char_embeds_gradient, char_grads, grad_char_gain = char_backward(
        character_embeddings, kind, counts, char_gain, char_whole, kept, pooled, msum, grad_vectors
    )
    small = jnp.concatenate(
        [
            jnp.pad(grad_char_gain, ((0, 0), (0, D - CHAR_BLOCK_WIDTH))),
            gain_one,
            gain_two,
            jnp.zeros((5, D), F32),
        ]
    )
    word_sums = (sum_project, sum_output, sum_upper, sum_lower)
    char_sums, small_sums = sum_char_grads(by_peer(char_grads), small, word_sums)
    parameter_count = (
        sum(
            part_count * w.size * peer_count
            for w in (word_project, word_output, feed_upper, feed_lower)
        )
        + peer_count * (char_mixer.size + char_lift.size)
        + char_gain.size
        + word_gains.size
    )
    flat = lambda a: a.reshape((-1,) + a.shape[-2:])
    results = shampoo(
        0.5 * math.sqrt(parameter_count),
        position,
        char_sums.reshape(char_grads.shape),
        small_sums,
        char_gain,
        word_gains,
        word_sums,
        [
            tuple(flat(a) for a in group[:4]) + (group[4],)
            for group in (
                (char_mixer, char_mixer_left, char_mixer_right, char_mixer_left_root, mixer_root),
                (char_lift, char_lift_left, char_lift_right, char_lift_left_root, lift_root),
                (word_project, word_project_left, word_project_right, word_project_left_root, project_root),
                (word_output, word_output_left, word_output_right, word_output_left_root, output_root),
                (feed_upper, feed_upper_left, feed_upper_right, feed_upper_left_root, upper_root),
                (feed_lower, feed_lower_left, feed_lower_right, feed_lower_left_root, lower_root),
            )
        ],
    )
    norm, gain_grad, gains_grad, gain_new, gains_new = results[:5]
    stepped = []
    for t, group in enumerate(
        (
            (char_mixer, char_mixer_left, char_mixer_right),
            (char_lift, char_lift_left, char_lift_right),
            (word_project, word_project_left, word_project_right),
            (word_output, word_output_left, word_output_right),
            (feed_upper, feed_upper_left, feed_upper_right),
            (feed_lower, feed_lower_left, feed_lower_right),
        )
    ):
        master, left, right = group
        stepped += [
            a.reshape(b.shape)
            for a, b in zip(results[5 + 5 * t : 10 + 5 * t], (master, left, right, master, master))
        ]
    return (
        block_out,
        word_inputs_gradient,
        char_embeds_gradient,
        gain_grad[0],
        gains_grad,
        gain_new[0],
        gains_new,
        norm[0, 0],
        *stepped,
    )


def solution(mesh):
    placed = (
        P("dp", None, None),
        P("dp", "mp", None, None),
        P("dp", None, None),
        P("dp", "mp"),
        P("dp", None),
        P("dp"),
        P("dp", None),
        P(),
        P(),
        P(None, "dp", None),
        P(None, "dp", None),
        P(None, "dp", None),
        P(None, "dp", None),
        P(None, "dp", None),
        P(None, "dp", None),
        P(None, "dp", None),
        P(None, "dp", None),
        P(None, "dp", None),
        P(None, "dp", None),
        P(None, "mp", "dp", None),
        P(None, "mp", "dp", None),
        P(None, "mp", "dp", None),
        P(None, "mp", "dp", None),
        P(None, "mp", "dp", None),
        P("mp", "dp", None),
        P("mp", "dp", None),
        P("mp", "dp", None),
        P("mp", "dp", None),
        P("mp", "dp", None),
        P("mp", "dp", None),
        P("mp", "dp", None),
        P("mp", "dp", None),
        P("mp", "dp", None),
        P("mp", "dp", None),
        P("mp", "dp", None),
        P("mp", "dp", None),
        P("mp", "dp", None),
        P("mp", "dp", None),
        P("mp", "dp", None),
    )
    return jax.shard_map(
        local,
        mesh=mesh,
        in_specs=placed,
        out_specs=(
            P("dp", None, None),
            P("dp", None, None),
            P("dp", "mp", None, None),
            P(),
            P(),
            P(),
            P(),
            P(),
            P(None, "dp", None),
            P(None, "dp", None),
            P(None, "dp", None),
            P(None, "dp", None),
            P(None, "dp", None),
            P(None, "dp", None),
            P(None, "dp", None),
            P(None, "dp", None),
            P(None, "dp", None),
            P(None, "dp", None),
            P(None, "mp", "dp", None),
            P(None, "mp", "dp", None),
            P(None, "mp", "dp", None),
            P(None, "mp", "dp", None),
            P(None, "mp", "dp", None),
            P("mp", "dp", None),
            P("mp", "dp", None),
            P("mp", "dp", None),
            P("mp", "dp", None),
            P("mp", "dp", None),
            P("mp", "dp", None),
            P("mp", "dp", None),
            P("mp", "dp", None),
            P("mp", "dp", None),
            P("mp", "dp", None),
            P("mp", "dp", None),
            P("mp", "dp", None),
            P("mp", "dp", None),
            P("mp", "dp", None),
            P("mp", "dp", None),
        ),
        check_vma=False,
    )
```

```python
import functools
import math

import jax
import jax.numpy as jnp
from jax import lax
from jax.experimental import pallas as pl
from jax.experimental.pallas import tpu as pltpu
from jax.sharding import PartitionSpec as P

D = 512
HD = 64
FF = 2048
CHAR_BLOCK_WIDTH = 256
OWNER_BLOCKS = 10
decay_rate = 0.5
learn_rate = 1.0
gain_rate = 0.4
negative_big = -1e30

CW = 256
CHEADS = 4
CHD = 64
SPOTS = 16
KEPT = 3 * CW + CHEADS * 128 + CW
epsilon = 1e-05
BF = jnp.bfloat16
F32 = jnp.float32


def nn(a, b):
    return lax.dot_general(a, b, (((1,), (0,)), ((), ())), preferred_element_type=F32)


def nt(a, b):
    return lax.dot_general(a, b, (((1,), (1,)), ((), ())), preferred_element_type=F32)


def tn(a, b):
    return lax.dot_general(a, b, (((0,), (0,)), ((), ())), preferred_element_type=F32)


def char_classes(share):
    listed = [(1, 4, 32), (2, 8, 16), (4, 16, 8)]
    return [c for c in listed if c[2] <= share]


def order_matrix(places, words):
    row = lax.broadcasted_iota(jnp.int32, (128, SPOTS * words), 0)
    col = lax.broadcasted_iota(jnp.int32, (128, SPOTS * words), 1)
    return ((row % words) * SPOTS + row // words == col).astype(BF)


def head_stack(rows, scale):
    lane = lax.broadcasted_iota(jnp.int32, (1, CW), 1) // CHD
    return jnp.concatenate(
        [rows * jnp.where(lane == h, scale, 0.0).astype(BF) for h in range(CHEADS)], axis=0
    )


def char_forward_kernel(
    classes, kind, x_ref, count_ref, gain_ref, mats_ref, *refs
):
    orders = refs[: len(classes)]
    vec_ref, kept_ref, pooled_ref, msum_ref, sumx, counts = refs[len(classes) :]
    step = pl.program_id(0)
    share = count_ref.shape[1]
    own = pl.ds(pl.multiple_of(step * share, share), share)
    counts[own, :] = count_ref[0]

    @pl.when(kind[step] == 0)
    def _():
        sumx[own, :] = jnp.zeros((share, CW), F32)
        msum_ref[own, :] = jnp.zeros((share, CW), F32)

    def block(places, words, order_ref):
        groups = share // words
        kept_x = []
        normed = []
        for g in range(groups):
            x = nn(order_ref[...], x_ref[0, pl.ds(g * words * SPOTS, words * SPOTS), :])
            scale = lax.rsqrt(jnp.mean(x * x, axis=-1, keepdims=True) + epsilon)
            normed.append((x * scale * gain_ref[...]).astype(BF))
            cnt = count_ref[0, pl.ds(g * words, words), :]
            cnt2 = jnp.concatenate([cnt, cnt], axis=1)
            place = lax.broadcasted_iota(jnp.int32, (places, words, CW), 0).astype(F32)
            x3 = x.reshape(places, words, CW)
            sumx[pl.ds(pl.multiple_of(step * share + g * words, words), words), :] = jnp.sum(
                jnp.where(place < cnt2[None], x3, 0.0), axis=0
            )
        rows = groups * 128
        normed = jnp.concatenate(normed, axis=0) if groups > 1 else normed[0]
        for t in range(3):
            kept_ref[0, :rows, t * CW : (t + 1) * CW] = nn(
                normed, mats_ref[:, t * CW : (t + 1) * CW]
            ).astype(BF)
        lane = lax.broadcasted_iota(jnp.int32, (words, CHEADS * 128), 1) % 128
        word = lax.broadcasted_iota(jnp.int32, (words, CHEADS * 128), 0)
        mine = lane % words == word
        spot = (lane // words).astype(F32)
        head_row = lax.broadcasted_iota(jnp.int32, (CHEADS * 128, CW), 0) // 128
        head_col = lax.broadcasted_iota(jnp.int32, (CHEADS * 128, CW), 1) // CHD
        same_head = (head_row == head_col).astype(BF)
        for g in range(groups):
            at = g * 128
            q = kept_ref[0, at : at + 128, :CW]
            k = kept_ref[0, at : at + 128, CW : 2 * CW]
            v = kept_ref[0, at : at + 128, 2 * CW : 3 * CW]
            s = nt(k, head_stack(q, 1.0 / math.sqrt(CHD))).reshape(places, words, CHEADS * 128)
            cnt = count_ref[0, pl.ds(g * words, words), :]
            cnt4 = jnp.concatenate([cnt] * CHEADS, axis=1)
            place = lax.broadcasted_iota(jnp.int32, (places, words, CHEADS * 128), 0).astype(F32)
            s = jnp.where(place < cnt4[None], s, -1e30)
            e = jnp.exp(s - jnp.max(s, axis=0)[None])
            r = jnp.where(mine & (spot < cnt4), 1.0 / jnp.sum(e, axis=0), 0.0)
            p = (e * r[None]).astype(BF).reshape(128, CHEADS * 128)
            kept_ref[0, at : at + 128, 3 * CW : 3 * CW + CHEADS * 128] = p
            c = nn(p, same_head)
            kept_ref[0, at : at + 128, 3 * CW + CHEADS * 128 :] = c.astype(BF)
            msum_ref[pl.ds(pl.multiple_of(step * share + g * words, words), words), :] = jnp.sum(
                (c * v.astype(F32)).reshape(places, words, CW), axis=0
            )

    for (number, places, words), order_ref in zip(classes, orders):
        pl.when(kind[step] == number)(functools.partial(block, places, words, order_ref))

    @pl.when(step == pl.num_programs(0) - 1)
    def _():
        cnt2 = jnp.concatenate([counts[...]] * 2, axis=1)
        summed = sumx[...] + nn(msum_ref[...].astype(BF), mats_ref[:, 3 * CW : 4 * CW])
        pooled = (summed / cnt2).astype(BF)
        pooled_ref[...] = pooled
        vec_ref[...] = nn(pooled, mats_ref[:, 4 * CW :]).astype(BF)


def char_kind(block_home, char_count, share):
    places = jnp.max(char_count, axis=1)
    kind = jnp.where(places <= 8, 2, 4)
    if share >= 32:
        kind = jnp.where(places <= 4, 1, kind)
    return jnp.where(block_home >= 0, kind, 0).astype(jnp.int32)


def whole(shape):
    return pl.BlockSpec(shape, lambda i, *_: (0,) * len(shape))


def char_forward(x, kind, counts, gain, mats):
    slots, share = x.shape[:2]
    classes = char_classes(share)
    rows = share * SPOTS
    orders = [order_matrix(p, w) for _, p, w in classes]
    words_all = slots * share
    per_slot = lambda shape: pl.BlockSpec((1,) + shape, lambda i, *_: (i,) + (0,) * len(shape))
    return pl.pallas_call(
        functools.partial(char_forward_kernel, classes),
        grid_spec=pltpu.PrefetchScalarGridSpec(
            num_scalar_prefetch=1,
            grid=(slots,),
            in_specs=[
                per_slot((rows, CW)),
                per_slot((share, 128)),
                whole((1, CW)),
                whole(mats.shape),
            ]
            + [whole(o.shape) for o in orders],
            out_specs=[
                whole((words_all, D)),
                per_slot((rows, KEPT)),
                whole((words_all, CW)),
                whole((words_all, CW)),
            ],
            scratch_shapes=[
                pltpu.VMEM((words_all, CW), F32),
                pltpu.VMEM((words_all, 128), F32),
            ],
        ),
        out_shape=[
            jax.ShapeDtypeStruct((words_all, D), BF),
            jax.ShapeDtypeStruct((slots, rows, KEPT), BF),
            jax.ShapeDtypeStruct((words_all, CW), BF),
            jax.ShapeDtypeStruct((words_all, CW), F32),
        ],
        compiler_params=pltpu.CompilerParams(vmem_limit_bytes=60 << 20),
        cost_estimate=pl.CostEstimate(
            flops=slots * rows * CW * CW * 16, bytes_accessed=slots * rows * KEPT * 3, transcendentals=0
        ),
        name="char_forward",
    )(kind, x.reshape(slots, rows, CW), counts, gain.reshape(1, CW), mats, *orders)


def char_backward_kernel(
    classes, kind, x_ref, count_ref, kept_ref, all_counts_ref, gv_ref, pooled_ref, msum_ref,
    gain_ref, mats_ref, *refs
):
    orders = refs[: len(classes)]
    dx_ref, grads_ref, dgain_ref, gp_all, gm_all, dh, normed_all, dqkv_sum = refs[len(classes) :]
    step = pl.program_id(0)
    share = count_ref.shape[1]
    base = step * share

    @pl.when(step == 0)
    def _():
        gv = gv_ref[...]
        cnt2 = jnp.concatenate([all_counts_ref[...]] * 2, axis=1)
        gp = nt(gv, mats_ref[:, 4 * CW :]) / cnt2
        gp_all[...] = gp
        gpb = gp.astype(BF)
        gm_all[...] = nt(gpb, mats_ref[:, 3 * CW : 4 * CW]).astype(BF).astype(F32)
        grads_ref[:, 4 * CW :] = tn(pooled_ref[...], gv).astype(BF)
        grads_ref[:, 3 * CW : 4 * CW] = tn(msum_ref[...].astype(BF), gpb).astype(BF)
        dqkv_sum[...] = jnp.zeros_like(dqkv_sum)
        dgain_ref[...] = jnp.zeros_like(dgain_ref)

    @pl.when(kind[step] == 0)
    def _():
        dx_ref[...] = jnp.zeros_like(dx_ref)

    def block(places, words, order_ref):
        groups = share // words
        rows = groups * 128
        gain = gain_ref[...]
        xs = []
        scales = []
        gps = []
        for g in range(groups):
            at = g * 128
            x = nn(order_ref[...], x_ref[0, pl.ds(g * words * SPOTS, words * SPOTS), :])
            scale = lax.rsqrt(jnp.mean(x * x, axis=-1, keepdims=True) + epsilon)
            normed_all[at : at + 128, :] = (x * scale * gain).astype(BF)
            xs.append(x)
            scales.append(scale)
            mine = pl.ds(pl.multiple_of(base + g * words, words), words)
            cnt = count_ref[0, pl.ds(g * words, words), :]
            cnt2 = jnp.concatenate([cnt, cnt], axis=1)
            place = lax.broadcasted_iota(jnp.int32, (places, words, CW), 0).astype(F32)
            shown = place < cnt2[None]
            gps.append(jnp.where(shown, gp_all[mine, :][None], 0.0).reshape(128, CW))
            gm_word = gm_all[mine, :]
            gm = jnp.where(shown, gm_word[None], 0.0).reshape(128, CW).astype(BF)
            q = kept_ref[0, at : at + 128, :CW]
            k = kept_ref[0, at : at + 128, CW : 2 * CW]
            v = kept_ref[0, at : at + 128, 2 * CW : 3 * CW]
            p = kept_ref[0, at : at + 128, 3 * CW : 3 * CW + CHEADS * 128].astype(F32)
            c = kept_ref[0, at : at + 128, 3 * CW + CHEADS * 128 :].astype(F32)
            dp = nt(v, head_stack(gm, 1.0))
            p3 = p.reshape(places, words, CHEADS * 128)
            t = p3 * dp.reshape(places, words, CHEADS * 128)
            ds = (t - p3 * jnp.sum(t, axis=0)[None]).astype(BF).reshape(128, CHEADS * 128)
            eighth = 1.0 / math.sqrt(CHD)
            dk = nn(ds, head_stack(q, eighth))
            ds_rows = jnp.concatenate([ds[:, h * 128 : (h + 1) * 128] for h in range(CHEADS)], axis=0)
            dq = tn(ds_rows, head_stack(k, eighth))
            dv = (c.reshape(places, words, CW) * gm_word[None]).reshape(128, CW)
            dh[at : at + 128, :CW] = dq.astype(BF)
            dh[at : at + 128, CW : 2 * CW] = dk.astype(BF)
            dh[at : at + 128, 2 * CW :] = dv.astype(BF)
        grads = dh[:rows, :]
        dqkv_sum[...] += tn(normed_all[:rows, :], grads)
        dn_all = nt(grads, mats_ref[:, : 3 * CW])
        dgain = jnp.zeros((1, CW), F32)
        for g in range(groups):
            x, scale = xs[g], scales[g]
            dn = dn_all[g * 128 : (g + 1) * 128]
            xr = x * scale
            dgain = dgain + jnp.sum(xr * dn, axis=0, keepdims=True)
            w = dn * gain
            inner = jnp.mean(xr * w, axis=-1, keepdims=True)
            dx = gps[g] + scale * (w - xr * inner)
            dx_ref[0, pl.ds(g * words * SPOTS, words * SPOTS), :] = tn(
                order_ref[...], dx.astype(BF)
            ).astype(BF)
        dgain_ref[...] += dgain

    for (number, places, words), order_ref in zip(classes, orders):
        pl.when(kind[step] == number)(functools.partial(block, places, words, order_ref))

    @pl.when(step == pl.num_programs(0) - 1)
    def _():
        grads_ref[:, : 3 * CW] = dqkv_sum[...].astype(BF)


def char_backward(x, kind, counts, gain, mats, kept, pooled, msum, grad_vectors):
    slots, share = x.shape[:2]
    classes = char_classes(share)
    rows = share * SPOTS
    orders = [order_matrix(p, w) for _, p, w in classes]
    words_all = slots * share
    per_slot = lambda shape: pl.BlockSpec((1,) + shape, lambda i, *_: (i,) + (0,) * len(shape))
    dx, grads, dgain = pl.pallas_call(
        functools.partial(char_backward_kernel, classes),
        grid_spec=pltpu.PrefetchScalarGridSpec(
            num_scalar_prefetch=1,
            grid=(slots,),
            in_specs=[
                per_slot((rows, CW)),
                per_slot((share, 128)),
                per_slot((rows, KEPT)),
                whole((words_all, 128)),
                whole((words_all, D)),
                whole((words_all, CW)),
                whole((words_all, CW)),
                whole((1, CW)),
                whole(mats.shape),
            ]
            + [whole(o.shape) for o in orders],
            out_specs=[
                per_slot((rows, CW)),
                whole(mats.shape),
                whole((1, CW)),
            ],
            scratch_shapes=[
                pltpu.VMEM((words_all, CW), F32),
                pltpu.VMEM((words_all, CW), F32),
                pltpu.VMEM((rows, 3 * CW), BF),
                pltpu.VMEM((rows, CW), BF),
                pltpu.VMEM((CW, 3 * CW), F32),
            ],
        ),
        out_shape=[
            jax.ShapeDtypeStruct((slots, rows, CW), BF),
            jax.ShapeDtypeStruct(mats.shape, BF),
            jax.ShapeDtypeStruct((1, CW), F32),
        ],
        compiler_params=pltpu.CompilerParams(vmem_limit_bytes=60 << 20),
        cost_estimate=pl.CostEstimate(
            flops=slots * rows * CW * CW * 28, bytes_accessed=slots * rows * KEPT * 3, transcendentals=0
        ),
        name="char_backward",
    )(
        kind, x.reshape(slots, rows, CW), counts, kept, counts.reshape(words_all, 128), grad_vectors,
        pooled, msum, gain.reshape(1, CW), mats, *orders,
    )
    return dx.reshape(x.shape), grads, dgain


MESH_ID = pl.DeviceIdType.MESH


def greet(sizes, me):
    barrier = pltpu.get_barrier_semaphore()
    for axis, n in sizes.items():
        for d in range(1, n):
            pl.semaphore_signal(
                barrier, inc=1, device_id={axis: lax.rem(me[axis] + d, n)}, device_id_type=MESH_ID
            )
    pl.semaphore_wait(barrier, sum(n - 1 for n in sizes.values()))


def remote(source, target, sems, at, axis, peer):
    return pltpu.make_async_remote_copy(
        src_ref=source,
        dst_ref=target,
        send_sem=sems[0].at[at],
        recv_sem=sems[1].at[at],
        device_id={axis: peer},
        device_id_type=MESH_ID,
    )


def pair_gather_stages(own_of, sems, axis, n, mine, begin, late):
    chips = n // 2
    core = lax.rem(mine, 2)
    chip = mine // 2
    sibling = chip * 2 + 1 - core

    def start():
        for d in range(1, chips):
            there = lax.rem(chip + d, chips) * 2 + core
            remote(own_of(mine), own_of(mine), sems, d, axis, there).start()
        remote(own_of(mine), own_of(mine), sems, chips, axis, sibling).start()

    def hand_on():
        for d in range(1, chips):
            came = lax.rem(chip + chips - d, chips) * 2 + core
            remote(own_of(mine), own_of(came), sems, d, axis, sibling).wait_recv()
            remote(own_of(came), own_of(came), sems, chips + d, axis, sibling).start()

    def finish():
        for d in range(1, 2 * chips):
            remote(own_of(mine), own_of(mine), sems, d, axis, sibling).wait_send()
            if d >= chips:
                remote(own_of(mine), own_of(mine), sems, d, axis, sibling).wait_recv()

    return [(begin, start), (late, hand_on), (90.0, finish)]


def pair_part_stages(x, held, came, out, sems, axis, n, mine, begin, late):
    chips = n // 2
    core = lax.rem(mine, 2)
    chip = mine // 2
    sibling = chip * 2 + 1 - core

    def start():
        remote(x.at[:, 1 - core], came, sems, 0, axis, sibling).start()

    def onward():
        remote(x.at[:, 1 - core], came, sems, 0, axis, sibling).wait()
        for d in range(chips):
            there = lax.rem(chip + 1 + d, chips)
            came[there] = (came[there].astype(F32) + x[there, core].astype(F32)).astype(came.dtype)
            if d < chips - 1:
                remote(
                    came.at[there], held.at[chip], sems, 1 + d, axis, there * 2 + core
                ).start()

    def finish():
        held[chip] = came[chip]
        for d in range(chips - 1):
            remote(came.at[chip], held.at[chip], sems, 1 + d, axis, sibling).wait()
        total = held[0].astype(F32)
        for p in range(1, chips):
            total = total + held[p].astype(F32)
        out[...] = total.astype(out.dtype)

    return [(begin, start), (late, onward), (80.0, finish)]


def line_gather_stages(out, sems, axis, n, mine, begin, each):
    def step(k):
        for way in range(2):
            block = mine - k if way == 0 else mine + k
            here = (block >= 0) & (block < n)
            block = jnp.clip(block, 0, n - 1)
            onward = mine + 1 if way == 0 else mine - 1
            room = (onward >= 0) & (onward < n)
            peer = jnp.clip(onward, 0, n - 1)
            if k > 0:

                @pl.when(here)
                def _(way=way, block=block):
                    remote(out.at[block], out.at[block], sems, way * n + k - 1, axis, mine).wait_recv()

            if k < n - 1:

                @pl.when(here & room)
                def _(way=way, block=block, peer=peer):
                    remote(out.at[block], out.at[block], sems, way * n + k, axis, peer).start()

    def finish():
        for way in range(2):
            for k in range(n - 1):
                block = mine - k if way == 0 else mine + k
                sent = (mine < n - 1) & (block >= 0) if way == 0 else (mine > 0) & (block < n)

                @pl.when(sent)
                def _(way=way, k=k):
                    remote(out.at[mine], out.at[mine], sems, way * n + k, axis, mine).wait_send()

    stages = [(begin + each * k, functools.partial(step, k)) for k in range(n)]
    return stages + [(95.0, finish)]


def line_part_stages(x, held, out, sems, axis, n, mine, begin, each):
    def step(t):
        for way in range(2):
            distance = mine if way == 0 else n - 1 - mine
            turn = t - distance
            here = (turn >= 0) & (turn < n - 1 - distance)
            turn = jnp.clip(turn, 0, n - 1)
            block = n - 1 - turn if way == 0 else turn
            peer = jnp.clip(mine + 1 if way == 0 else mine - 1, 0, n - 1)
            at = way * n + block

            @pl.when(here & (distance == 0))
            def _(way=way, block=block, peer=peer, at=at):
                remote(x.at[block], held.at[way, block], sems, at, axis, peer).start()

            @pl.when(here & (distance > 0))
            def _(way=way, block=block, peer=peer, at=at):
                place = held.at[way, block]
                remote(place, place, sems, at, axis, mine).wait_recv()
                held[way, block] = (held[way, block].astype(F32) + x[block].astype(F32)).astype(x.dtype)
                remote(place, place, sems, at, axis, peer).start()

    def finish():
        out[...] = x[mine].astype(F32)
        for way, there in ((0, mine > 0), (1, mine < n - 1)):

            @pl.when(there)
            def _(way=way):
                here = held.at[way, mine]
                remote(here, here, sems, way * n + mine, axis, mine).wait_recv()
                out[...] += held[way, mine].astype(F32)

        for way in range(2):
            for block in range(n):
                further = block > mine if way == 0 else block < mine

                @pl.when(further)
                def _(way=way, block=block):
                    here = held.at[way, block]
                    remote(here, here, sems, way * n + block, axis, mine).wait_send()

    stages = [(begin + each * k, functools.partial(step, k)) for k in range(n - 1)]
    return stages + [(70.0, finish)]


def direct_stages(source_of, target, sems, axis, n, mine, begin, done, end):
    def start():
        for d in range(1, n):
            peer = lax.rem(mine + d, n)
            remote(source_of(peer), target.at[mine], sems, d, axis, peer).start()

    def finish():
        for d in range(1, n):
            remote(source_of(mine), target.at[mine], sems, d, axis, mine).wait()
        done()

    return [(begin, start), (end, finish)]


def exchange(name, number, tasks):
    sizes = {axis: lax.axis_size(axis) for _, axis, _ in tasks}
    outs, scratch, counts, shapers = [], [], [], []
    for kind, axis, arrays in tasks:
        n = sizes[axis]
        array = arrays[0]
        shaper = lambda a: a
        if kind == "gather":
            rows = array.shape[1]
            cols = sum(a.shape[0] * a.shape[2] for a in arrays)
            made = jax.ShapeDtypeStruct((n * rows, cols) if rows % 16 == 0 else (n, rows, cols), BF)
            shaper = lambda a, rows=rows, cols=cols, n=n: a.reshape(n * rows, cols)
        elif kind == "gather_mid":
            lead, rows, cols = array.shape
            made = jax.ShapeDtypeStruct(
                (lead, n * rows, cols) if rows % 16 == 0 else (n, lead, rows, cols), array.dtype
            )
            if rows % 16:
                shaper = lambda a, lead=lead, rows=rows, cols=cols, n=n: a.transpose(1, 0, 2, 3).reshape(
                    lead, n * rows, cols
                )
        else:
            block = array.shape if kind in ("line_gather", "total") else array.shape[1:]
            if kind == "part":
                block = array.shape[2:]
            summed = kind in ("part", "line_part", "total")
            made = jax.ShapeDtypeStruct(block if summed else (n,) + block, F32 if summed else array.dtype)
        outs.append(made)
        shapers.append(shaper)
        counts.append(len(arrays))
        scratch += [pltpu.SemaphoreType.DMA((2 * n,)), pltpu.SemaphoreType.DMA((2 * n,))]
        if kind == "part":
            scratch += [pltpu.VMEM((n // 2,) + block, array.dtype)] * 2
        if kind == "total":
            scratch.append(pltpu.VMEM((n,) + block, array.dtype))
        if kind == "line_part":
            scratch.append(pltpu.VMEM((2, n) + block, array.dtype))
    total_ins = sum(counts)

    def kernel(*refs):
        ins, at = [], 0
        for count in counts:
            ins.append(refs[at : at + count])
            at += count
        results = refs[at : at + len(tasks)]
        rest = list(refs[at + len(tasks) :])
        me = {axis: lax.axis_index(axis) for axis in sizes}
        greet(sizes, me)
        stages = []
        for (kind, axis, _), xs, out in zip(tasks, ins, results):
            sems = (rest.pop(0), rest.pop(0))
            n, mine, x = sizes[axis], me[axis], xs[0]
            if kind == "line_gather":
                out[mine] = x[...]
                stages += line_gather_stages(out, sems, axis, n, mine, 0.0, 6.0)
            elif kind == "line_part":
                stages += line_part_stages(x, rest.pop(0), out, sems, axis, n, mine, 0.0, 6.0)
            elif kind == "part":
                held, came = rest.pop(0), rest.pop(0)
                stages += pair_part_stages(x, held, came, out, sems, axis, n, mine, 0.1, 1.0)
            elif kind in ("gather", "gather_mid"):
                if kind == "gather":
                    rows = x.shape[1]
                    if rows % 16 == 0:
                        own_of = lambda i, out=out, rows=rows: out.at[
                            pl.ds(pl.multiple_of(i * rows, 16), rows), :
                        ]
                    else:
                        own_of = lambda i, out=out: out.at[i]
                    own, col = own_of(mine), 0
                    for piece in xs:
                        for t in range(piece.shape[0]):
                            own[:, col : col + piece.shape[2]] = piece[t].astype(BF)
                            col += piece.shape[2]
                else:
                    rows = x.shape[1]
                    if rows % 16 == 0:
                        own_of = lambda i, out=out, rows=rows: out.at[
                            :, pl.ds(pl.multiple_of(i * rows, 16), rows), :
                        ]
                    else:
                        own_of = lambda i, out=out: out.at[i]
                    own_of(mine)[...] = x[...]
                if axis == "dp":
                    stages += pair_gather_stages(own_of, sems, axis, n, mine, 0.2, 7.0)
                else:

                    def start(own_of=own_of, sems=sems, axis=axis, n=n, mine=mine):
                        for d in range(1, n):
                            peer = lax.rem(mine + d, n)
                            remote(own_of(mine), own_of(mine), sems, d, axis, peer).start()

                    def finish(own_of=own_of, sems=sems, axis=axis, n=n, mine=mine):
                        for d in range(1, n):
                            remote(own_of(mine), own_of(mine), sems, d, axis, mine).wait()

                    stages += [(0.15, start), (90.0, finish)]
            elif kind == "total":
                held = rest.pop(0)
                held[mine] = x[...]

                def done(held=held, out=out, n=n):
                    total = held[0].astype(F32)
                    for p in range(1, n):
                        total = total + held[p].astype(F32)
                    out[...] = total

                stages += direct_stages(
                    lambda p, held=held, mine=mine: held.at[mine], held, sems, axis, n, mine, 0.3, done, 60.0
                )
            else:
                out[mine] = x[mine]
                stages += direct_stages(
                    lambda p, x=x: x.at[p], out, sems, axis, n, mine, 0.0, lambda: None, 60.0
                )
        for _, run in sorted(stages, key=lambda stage: stage[0]):
            run()

    vmem = pl.BlockSpec(memory_space=pltpu.VMEM)
    results = pl.pallas_call(
        kernel,
        out_shape=outs,
        in_specs=[vmem] * total_ins,
        out_specs=[vmem] * len(tasks),
        scratch_shapes=scratch,
        compiler_params=pltpu.CompilerParams(
            collective_id=number, has_side_effects=True, vmem_limit_bytes=48 << 20
        ),
        name=name,
    )(*[array for _, _, arrays in tasks for array in arrays])
    return [shaper(a) for shaper, a in zip(shapers, results)]


def by_chip(array):
    return array.reshape(lax.axis_size("dp") // 2, 2, -1, array.shape[-1])


def sum_char_grads(grads, small, word_sums):
    n, m = lax.axis_size("dp"), lax.axis_size("mp")
    grads = by_chip(grads)
    rows, cols = grads.shape[2:]
    slim = cols // m

    def kernel(x, s, *refs):
        words = refs[: len(word_sums)]
        (out, small_out, held, came, total_dp, cut, cut_held, merged, small_dp, small_mp, *sems) = refs[len(word_sums) :]
        pairs = [tuple(sems[2 * t : 2 * t + 2]) for t in range(6)]
        i, j = lax.axis_index("dp"), lax.axis_index("mp")
        greet({"dp": n, "mp": m}, {"dp": i, "mp": j})
        part = [
            run for _, run in pair_part_stages(x, held, came, total_dp, pairs[0], "dp", n, i, 0.0, 0.0)
        ]
        part[0]()
        squares = jnp.zeros((1, 1), F32)
        for word in words:
            wide = word[...].astype(F32)
            squares = squares + jnp.sum(jnp.sum(wide * wide, axis=0, keepdims=True), axis=1, keepdims=True)
        row = lax.broadcasted_iota(jnp.int32, s.shape, 0)
        small_dp[i] = s[...] + jnp.where(row == 3, squares * (1.0 / n), 0.0)
        part[1]()

        def small_done():
            total = small_dp[0]
            for p in range(1, n):
                total = total + small_dp[p]
            small_mp[j] = total

        def small_end():
            total = small_mp[0]
            for p in range(1, m):
                total = total + small_mp[p]
            small_out[...] = total

        def cut_done():
            total = cut_held[0].astype(F32)
            for p in range(1, m):
                total = total + cut_held[p].astype(F32)
            merged[j] = total.astype(BF)

        one = direct_stages(lambda p: small_dp.at[i], small_dp, pairs[1], "dp", n, i, 0, small_done, 0)
        two = direct_stages(lambda p: small_mp.at[j], small_mp, pairs[2], "mp", m, j, 0, small_end, 0)
        three = direct_stages(lambda p: cut.at[p], cut_held, pairs[3], "mp", m, j, 0, cut_done, 0)
        four = direct_stages(lambda p: merged.at[j], merged, pairs[4], "mp", m, j, 0, lambda: None, 0)
        one[0][1]()
        part[2]()
        for p in range(m):
            cut[p] = total_dp[:, p * slim : (p + 1) * slim]
        cut_held[j] = cut[j]
        three[0][1]()
        one[1][1]()
        two[0][1]()
        three[1][1]()
        four[0][1]()
        two[1][1]()
        four[1][1]()
        if rows % 16 == 0:
            own_of = lambda d: out.at[pl.ds(pl.multiple_of(d * rows, 16), rows), :]
        else:
            own_of = lambda d: out.at[d]
        own = own_of(i)
        for p in range(m):
            own[:, p * slim : (p + 1) * slim] = merged[p]
        for _, run in pair_gather_stages(own_of, pairs[5], "dp", n, i, 0, 0):
            run()

    vmem = pl.BlockSpec(memory_space=pltpu.VMEM)
    sums, smalls = pl.pallas_call(
        kernel,
        out_shape=[
            jax.ShapeDtypeStruct((n * rows, cols) if rows % 16 == 0 else (n, rows, cols), BF),
            jax.ShapeDtypeStruct(small.shape, F32),
        ],
        in_specs=[vmem] * (2 + len(word_sums)),
        out_specs=[vmem] * 2,
        scratch_shapes=[
            pltpu.VMEM((n // 2, rows, cols), BF),
            pltpu.VMEM((n // 2, rows, cols), BF),
            pltpu.VMEM((rows, cols), BF),
            pltpu.VMEM((m, rows, slim), BF),
            pltpu.VMEM((m, rows, slim), BF),
            pltpu.VMEM((m, rows, slim), BF),
            pltpu.VMEM((n,) + small.shape, F32),
            pltpu.VMEM((m,) + small.shape, F32),
        ]
        + [pltpu.SemaphoreType.DMA((2 * max(n, m),))] * 12,
        compiler_params=pltpu.CompilerParams(
            collective_id=20, has_side_effects=True, vmem_limit_bytes=48 << 20
        ),
        name="sum_char_grads",
    )(grads, small, *word_sums)
    return sums.reshape(n * rows, cols), smalls


ROWS = 256


def rms_scale(values):
    return lax.rsqrt(jnp.mean(values * values, axis=-1, keepdims=True) + epsilon)


def norm_back(values, scale, gain_row, grad):
    weighted = grad * gain_row
    inner = jnp.mean(values * weighted, axis=-1, keepdims=True)
    return scale * weighted - values * (scale * scale * scale) * inner


def word_forward_kernel(
    width, vec_ref, place_ref, words_ref, doc_ref, doc_row_ref, gain_ref, project_ref,
    stream_ref, normed_ref, qkv_ref, probs_ref, mixed_ref, keys, values
):
    step = pl.program_id(0)
    numbers = lax.broadcasted_iota(jnp.int32, (ROWS, place_ref.shape[1]), 0) + step * ROWS
    placed = nn((numbers == place_ref[...]).astype(BF), vec_ref[...])
    stream = words_ref[...].astype(F32) + placed
    stream_ref[...] = stream
    normed = (stream * rms_scale(stream) * gain_ref[...]).astype(BF)
    normed_ref[...] = normed
    qkv = nn(normed, project_ref[...]).astype(BF)
    qkv_ref[...] = qkv
    first = pl.ds(pl.multiple_of(step * ROWS, ROWS), ROWS)
    keys[first, :] = qkv[:, width : 2 * width]
    values[first, :] = qkv[:, 2 * width :]
    queries = (qkv[:, :width].astype(F32) * (1.0 / math.sqrt(HD))).astype(BF)

    def attend(number):
        count = (number + 1) * ROWS
        same = doc_ref[:count, :] == doc_row_ref[...]
        key_at = lax.broadcasted_iota(jnp.int32, (count, ROWS), 0)
        query_at = lax.broadcasted_iota(jnp.int32, (count, ROWS), 1) + number * ROWS
        allowed = same & (key_at <= query_at)
        parts = []
        for head in range(width // HD):
            at = slice(head * HD, (head + 1) * HD)
            scores = jnp.where(allowed, nt(keys[:count, at], queries[:, at]), negative_big)
            raised = jnp.exp(scores - jnp.max(scores, axis=0, keepdims=True))
            probs = (raised * (1.0 / jnp.sum(raised, axis=0, keepdims=True))).astype(BF)
            probs_ref[head, :count, :] = probs
            parts.append(tn(values[:count, at], probs).T)
        mixed_ref[...] = jnp.concatenate(parts, axis=1).astype(BF)

    for number in range(doc_ref.shape[0] // ROWS):
        pl.when(step == number)(functools.partial(attend, number))


def word_forward(vectors, places, words, documents, gain, project):
    length = words.shape[0]
    width = project.shape[1] // 3
    heads = width // HD
    rows = lambda cols: pl.BlockSpec((ROWS, cols), lambda i: (i, 0))
    full = lambda shape: pl.BlockSpec(shape, lambda i: (0,) * len(shape))
    return pl.pallas_call(
        functools.partial(word_forward_kernel, width),
        grid=(length // ROWS,),
        in_specs=[
            full(vectors.shape),
            full((1, places.shape[0])),
            rows(D),
            full((length, 1)),
            pl.BlockSpec((1, ROWS), lambda i: (0, i)),
            full((1, D)),
            full(project.shape),
        ],
        out_specs=[
            rows(D),
            rows(D),
            rows(3 * width),
            pl.BlockSpec((heads, length, ROWS), lambda i: (0, 0, i)),
            rows(width),
        ],
        out_shape=[
            jax.ShapeDtypeStruct((length, D), F32),
            jax.ShapeDtypeStruct((length, D), BF),
            jax.ShapeDtypeStruct((length, 3 * width), BF),
            jax.ShapeDtypeStruct((heads, length, length), BF),
            jax.ShapeDtypeStruct((length, width), BF),
        ],
        scratch_shapes=[pltpu.VMEM((length, width), BF), pltpu.VMEM((length, width), BF)],
        compiler_params=pltpu.CompilerParams(vmem_limit_bytes=48 << 20),
        name="word_forward",
    )(
        vectors,
        places.reshape(1, -1),
        words,
        documents.reshape(length, 1),
        documents.reshape(1, length),
        gain.reshape(1, D),
        project,
    )


def feed_kernel(
    mixed_ref, output_ref, stream_ref, cot_ref, gain_ref, upper_ref, lower_ref,
    hidden_ref, feed_ref, part_ref, grad_upper_ref, grad_lower_ref, upper_sum, lower_sum
):
    step = pl.program_id(0)

    @pl.when(step == 0)
    def _():
        upper_sum[...] = jnp.zeros_like(upper_sum)
        lower_sum[...] = jnp.zeros_like(lower_sum)

    parts, _, width = mixed_ref.shape
    hidden = stream_ref[...]
    for j in range(parts):
        hidden = hidden + nn(mixed_ref[j], output_ref[j * width : (j + 1) * width, :])
    hidden_ref[...] = hidden
    normed = (hidden * rms_scale(hidden) * gain_ref[...]).astype(BF)
    raised = nn(normed, upper_ref[...])
    constant = math.sqrt(2.0 / math.pi)
    square = raised * raised
    curve = jnp.tanh(constant * raised * (1.0 + 0.044715 * square))
    half = 0.5 * (1.0 + curve)
    active = (raised * half).astype(BF)
    slope = half + 0.5 * raised * (1.0 - curve * curve) * constant * (1.0 + 3.0 * 0.044715 * square)
    feed_ref[...] = nn(active, lower_ref[...]).astype(BF)
    grad_feed = cot_ref[...]
    grad_raised = (nt(grad_feed, lower_ref[...]) * slope).astype(BF)
    part_ref[...] = nt(grad_raised, upper_ref[...]).astype(BF)
    lower_sum[...] += tn(active, grad_feed)
    upper_sum[...] += tn(normed, grad_raised)

    @pl.when(step == pl.num_programs(0) - 1)
    def _():
        grad_upper_ref[...] = upper_sum[...].astype(BF)
        grad_lower_ref[...] = lower_sum[...].astype(BF)


def feed(mixed, output, stream, cotangent, gain, upper, lower):
    length = stream.shape[0]
    rows = pl.BlockSpec((ROWS, D), lambda i: (i, 0))
    full = lambda shape: pl.BlockSpec(shape, lambda i: (0,) * len(shape))
    return pl.pallas_call(
        feed_kernel,
        grid=(length // ROWS,),
        in_specs=[
            pl.BlockSpec((mixed.shape[0], ROWS, mixed.shape[2]), lambda i: (0, i, 0)),
            full(output.shape),
            rows,
            rows,
            full((1, D)),
            full(upper.shape),
            full(lower.shape),
        ],
        out_specs=[rows, rows, rows, full(upper.shape), full(lower.shape)],
        out_shape=[
            jax.ShapeDtypeStruct((length, D), F32),
            jax.ShapeDtypeStruct((length, D), BF),
            jax.ShapeDtypeStruct((length, D), BF),
            jax.ShapeDtypeStruct(upper.shape, BF),
            jax.ShapeDtypeStruct(lower.shape, BF),
        ],
        scratch_shapes=[pltpu.VMEM(upper.shape, F32), pltpu.VMEM(lower.shape, F32)],
        compiler_params=pltpu.CompilerParams(vmem_limit_bytes=48 << 20),
        name="feed",
    )(mixed, output, stream, cotangent, gain.reshape(1, D), upper, lower)


def hidden_back_kernel(
    own, grad_ref, hidden_ref, cot_ref, mixed_ref, output_ref, gain_ref,
    grad_hidden_ref, grad_mixed_ref, grad_output_ref, gain_grad_ref
):
    hidden = hidden_ref[...]
    scale = rms_scale(hidden)
    grad = grad_ref[...]
    grad_hidden = cot_ref[...].astype(F32) + norm_back(hidden, scale, gain_ref[...], grad)
    grad_hidden_ref[...] = grad_hidden
    gain_grad_ref[...] = jnp.sum(hidden * scale * grad, axis=0, keepdims=True)
    attend = grad_hidden.astype(BF)
    parts, _, width = mixed_ref.shape
    for j in range(parts):
        at = slice(j * width, (j + 1) * width)
        grad_mixed_ref[j] = nt(attend, output_ref[at, :]).astype(BF)
        grad_output_ref[at, :] = tn(mixed_ref[j], attend).astype(BF)


def hidden_back(own, grad, hidden, cotangent, mixed, output, gain):
    share = grad.shape[0]
    parts, _, width = mixed.shape
    mine = pl.BlockSpec((share, D), lambda i, own: (own[0], 0))
    full = lambda shape: pl.BlockSpec(shape, lambda i, own: (0,) * len(shape))
    return pl.pallas_call(
        hidden_back_kernel,
        grid_spec=pltpu.PrefetchScalarGridSpec(
            num_scalar_prefetch=1,
            grid=(1,),
            in_specs=[
                full((share, D)),
                mine,
                mine,
                pl.BlockSpec((parts, share, width), lambda i, own: (0, own[0], 0)),
                full(output.shape),
                full((1, D)),
            ],
            out_specs=[
                full((share, D)),
                full((parts, share, width)),
                full(output.shape),
                full((1, D)),
            ],
        ),
        out_shape=[
            jax.ShapeDtypeStruct((share, D), F32),
            jax.ShapeDtypeStruct((parts, share, width), BF),
            jax.ShapeDtypeStruct(output.shape, BF),
            jax.ShapeDtypeStruct((1, D), F32),
        ],
        compiler_params=pltpu.CompilerParams(vmem_limit_bytes=48 << 20),
        name="hidden_back",
    )(own, grad, hidden, cotangent, mixed, output, gain.reshape(1, D))


def word_backward_kernel(
    width, probs_ref, qkv_ref, all_ref, grad_ref, normed_ref, project_ref,
    part_ref, grad_project_ref, grads, key_sum, value_sum
):
    step = pl.program_id(0)
    steps = all_ref.shape[0] // ROWS
    first = pl.ds(pl.multiple_of(step * ROWS, ROWS), ROWS)
    eighth = 1.0 / math.sqrt(HD)
    queries = (qkv_ref[:, :width].astype(F32) * eighth).astype(BF)

    @pl.when(step == 0)
    def _():
        key_sum[...] = jnp.zeros_like(key_sum)
        value_sum[...] = jnp.zeros_like(value_sum)

    def attend(number):
        count = (number + 1) * ROWS
        parts = []
        for head in range(width // HD):
            at = slice(head * HD, (head + 1) * HD)
            keys = all_ref[:count, width + head * HD : width + (head + 1) * HD]
            values = all_ref[:count, 2 * width + head * HD : 2 * width + (head + 1) * HD]
            grad = grad_ref[:, at]
            probs = probs_ref[head, :count, :]
            wide = probs.astype(F32)
            product = wide * nt(values, grad)
            scores = (product - wide * jnp.sum(product, axis=0, keepdims=True)).astype(BF)
            key_sum[head, :count, :] += nn(scores, queries[:, at])
            value_sum[head, :count, :] += nn(probs, grad)
            parts.append(tn(keys, scores).T * eighth)
        grads[first, :width] = jnp.concatenate(parts, axis=1).astype(BF)

    for number in range(steps):
        pl.when(step == number)(functools.partial(attend, number))

    @pl.when(step == steps - 1)
    def _():
        for head in range(width // HD):
            grads[:, width + head * HD : width + (head + 1) * HD] = key_sum[head].astype(BF)
            grads[:, 2 * width + head * HD : 2 * width + (head + 1) * HD] = value_sum[head].astype(BF)
        grad_project_ref[...] = tn(normed_ref[...], grads[...]).astype(BF)
        part_ref[...] = nt(grads[...], project_ref[...]).astype(BF)


def word_backward(probs, qkv, grad_mixed, normed, project):
    length = qkv.shape[0]
    width = project.shape[1] // 3
    heads = width // HD
    rows = lambda cols: pl.BlockSpec((ROWS, cols), lambda i: (i, 0))
    full = lambda shape: pl.BlockSpec(shape, lambda i: (0,) * len(shape))
    return pl.pallas_call(
        functools.partial(word_backward_kernel, width),
        grid=(length // ROWS,),
        in_specs=[
            pl.BlockSpec((heads, length, ROWS), lambda i: (0, 0, i)),
            rows(3 * width),
            full(qkv.shape),
            rows(width),
            full(normed.shape),
            full(project.shape),
        ],
        out_specs=[full((length, D)), full(project.shape)],
        out_shape=[
            jax.ShapeDtypeStruct((length, D), BF),
            jax.ShapeDtypeStruct(project.shape, BF),
        ],
        scratch_shapes=[
            pltpu.VMEM(qkv.shape, BF),
            pltpu.VMEM((heads, length, HD), F32),
            pltpu.VMEM((heads, length, HD), F32),
        ],
        compiler_params=pltpu.CompilerParams(vmem_limit_bytes=48 << 20),
        name="word_backward",
    )(probs, qkv, qkv, grad_mixed, normed, project)


def stream_back_kernel(own, grad_ref, stream_ref, hidden_grad_ref, gain_ref, out_ref, gain_grad_ref):
    stream = stream_ref[...]
    scale = rms_scale(stream)
    grad = grad_ref[...]
    total = hidden_grad_ref[...] + norm_back(stream, scale, gain_ref[...], grad)
    out_ref[...] = total.astype(BF)
    gain_grad_ref[...] = jnp.sum(stream * scale * grad, axis=0, keepdims=True)


def stream_back(own, grad, stream, hidden_grad, gain):
    share = grad.shape[0]
    full = lambda shape: pl.BlockSpec(shape, lambda i, own: (0,) * len(shape))
    return pl.pallas_call(
        stream_back_kernel,
        grid_spec=pltpu.PrefetchScalarGridSpec(
            num_scalar_prefetch=1,
            grid=(1,),
            in_specs=[
                full((share, D)),
                pl.BlockSpec((share, D), lambda i, own: (own[0], 0)),
                full((share, D)),
                full((1, D)),
            ],
            out_specs=[full((share, D)), full((1, D))],
        ),
        out_shape=[
            jax.ShapeDtypeStruct((share, D), BF),
            jax.ShapeDtypeStruct((1, D), F32),
        ],
        name="stream_back",
    )(own, grad, stream, hidden_grad, gain.reshape(1, D))


def shampoo_kernel(threshold, position, char_ref, small_ref, gain_ref, gains_ref, *refs):
    sums, refs = refs[:4], refs[4:]
    given, refs = [refs[5 * t : 5 * t + 5] for t in range(6)], refs[30:]
    norm_ref, gain_grad_ref, gains_grad_ref, gain_new_ref, gains_new_ref = refs[:5]
    made = [refs[5 + 5 * t : 10 + 5 * t] for t in range(6)]
    me = position[0]
    char = char_ref[...].astype(F32)
    small = small_ref[...]
    lanes = lax.broadcasted_iota(jnp.int32, small.shape, 0)
    squares = (
        jnp.sum(jnp.sum(char * char, axis=0, keepdims=True), axis=1, keepdims=True)
        + jnp.sum(
            jnp.sum(jnp.where(lanes < 3, small * small, 0.0), axis=0, keepdims=True),
            axis=1,
            keepdims=True,
        )
        + small[3:4, :1]
    )
    norm = jnp.sqrt(squares)
    factor = jnp.minimum(1.0, threshold / norm)
    norm_ref[...] = norm
    gain_grad = small[0:1, :CW] * factor
    gain_grad_ref[...] = gain_grad
    gain_new_ref[...] = gain_ref[...] - gain_rate * gain_grad
    gains_grad = small[1:3, :] * factor
    gains_grad_ref[...] = gains_grad
    gains_new_ref[...] = gains_ref[...] - gain_rate * gains_grad
    width = sums[0].shape[1] // 3

    def whole_of(number, t):
        if number == 0:
            return char_ref[:, t * CW : (t + 1) * CW]
        if number == 1:
            return char_ref[:, 4 * CW :]
        if number == 2:
            return sums[0][:, t * width : (t + 1) * width]
        return sums[number - 2][...]

    def chosen(rows, cols):
        row = lax.broadcasted_iota(jnp.int32, (rows, cols), 0) + me * rows
        return (row == lax.broadcasted_iota(jnp.int32, (rows, cols), 1)).astype(BF)

    half = (1.0 - decay_rate) * factor * factor
    for number in range(6):
        master, left, right, left_root, right_root = given[number]
        grad_out, left_out, right_out, new_out, copy_out = made[number]
        for t in range(master.shape[0]):
            grad = whole_of(number, t)
            own = nn(chosen(master.shape[1], grad.shape[0]), grad)
            grad_out[t] = own * factor
            left_out[t] = decay_rate * left[t] + half * nt(own.astype(BF), grad)
            cols = nt(grad, chosen(right.shape[1], grad.shape[1])).astype(BF)
            right_out[t] = decay_rate * right[t] + half * tn(cols, grad)
            turned = (nn(left_root[t].astype(BF), grad) * factor).astype(BF)
            new = master[t] - learn_rate * nn(turned, right_root[:, t * grad.shape[1] : (t + 1) * grad.shape[1]])
            new_out[t] = new
            copy_out[t] = new.astype(BF)


def shampoo(threshold, position, char_sums, small, gain, gains, word_sums, given):
    flat = []
    shapes = [
        jax.ShapeDtypeStruct((1, 1), F32),
        jax.ShapeDtypeStruct((1, CW), F32),
        jax.ShapeDtypeStruct((2, D), F32),
        jax.ShapeDtypeStruct((1, CW), F32),
        jax.ShapeDtypeStruct((2, D), F32),
    ]
    for master, left, right, left_root, right_root in given:
        flat += [master, left, right, left_root, right_root]
        shapes += [
            jax.ShapeDtypeStruct(a.shape, F32) for a in (master, left, right, master)
        ] + [jax.ShapeDtypeStruct(master.shape, BF)]
    vmem = pl.BlockSpec(memory_space=pltpu.VMEM)
    smem = pl.BlockSpec(memory_space=pltpu.SMEM)
    return pl.pallas_call(
        functools.partial(shampoo_kernel, threshold),
        in_specs=[smem] + [vmem] * (4 + len(word_sums) + len(flat)),
        out_specs=[vmem] * len(shapes),
        out_shape=shapes,
        compiler_params=pltpu.CompilerParams(vmem_limit_bytes=56 << 20),
        name="shampoo",
    )(position, char_sums, small, gain.reshape(1, CW), gains, *word_sums, *flat)


def run_stages(stages):
    for _, run in sorted(stages, key=lambda stage: stage[0]):
        run()


def spread_blocks(chosen, rows, cols, share):
    up = lax.broadcasted_iota(jnp.int32, (rows, chosen.shape[0]), 0) // share
    up = (up == lax.broadcasted_iota(jnp.int32, (rows, chosen.shape[0]), 1)).astype(BF)
    down = lax.broadcasted_iota(jnp.int32, (chosen.shape[1], cols), 1) // share
    down = (down == lax.broadcasted_iota(jnp.int32, (chosen.shape[1], cols), 0)).astype(BF)
    wide = nn(nn(up, chosen).astype(BF), down)
    row = lax.broadcasted_iota(jnp.int32, (rows, cols), 0) % share
    col = lax.broadcasted_iota(jnp.int32, (rows, cols), 1) % share
    return jnp.where(row == col, wide, 0.0).astype(BF)


def gather_setup(xs, out):
    rows = xs[0].shape[1]

    def own_of(i):
        if rows % 16 == 0:
            return out.at[pl.ds(pl.multiple_of(i * rows, 16), rows), :]
        return out.at[i]

    def put(mine):
        own, col = own_of(mine), 0
        for piece in xs:
            for t in range(piece.shape[0]):
                own[:, col : col + piece.shape[2]] = piece[t].astype(BF)
                col += piece.shape[2]

    return own_of, put


def gather_shape(arrays, n):
    rows = arrays[0].shape[1]
    cols = sum(a.shape[0] * a.shape[2] for a in arrays)
    shape = (n * rows, cols) if rows % 16 == 0 else (n, rows, cols)
    return jax.ShapeDtypeStruct(shape, BF), lambda a: a.reshape(n * rows, cols)


def dma_sems(count):
    return [pltpu.SemaphoreType.DMA((count,))] * 2


def call_remote(kernel, name, number, outs, scratch, inputs):
    vmem = pl.BlockSpec(memory_space=pltpu.VMEM)
    return pl.pallas_call(
        kernel,
        out_shape=outs,
        in_specs=[vmem] * len(inputs),
        out_specs=[vmem] * len(outs),
        scratch_shapes=scratch,
        compiler_params=pltpu.CompilerParams(
            collective_id=number, has_side_effects=True, vmem_limit_bytes=56 << 20
        ),
        name=name,
    )(*inputs)


def send_vectors(vectors, to_slot, to_live, share, project, upper, lower, output_line):
    n, m = lax.axis_size("dp"), lax.axis_size("mp")
    total = to_slot.shape[0] * share
    block = total // n
    kept = OWNER_BLOCKS * share
    made = [gather_shape([a], n) for a in (project, upper, lower)]
    made[0] = gather_shape([project], n)
    lead, line_rows, line_cols = output_line.shape
    aligned = line_rows % 16 == 0
    output_shape = (lead, n * line_rows, line_cols) if aligned else (n, lead, line_rows, line_cols)

    def kernel(vec, slots, live, *refs):
        weights, line = refs[:3], refs[3]
        out, wides, output = refs[4], refs[5:8], refs[8]
        sent, came, *sems = refs[9:]
        pairs = [tuple(sems[2 * t : 2 * t + 2]) for t in range(6)]
        i, j = lax.axis_index("dp"), lax.axis_index("mp")
        sent[...] = (
            nn(spread_blocks(slots[...], total, vec.shape[0], share), vec[...])
            .astype(BF)
            .reshape(sent.shape)
        )
        greet({"dp": n, "mp": m}, {"dp": i, "mp": j})
        came[i] = sent[i]
        stages = []

        def compact():
            out[j] = nn(
                spread_blocks(live[...], kept, total, share), came[...].reshape(total, D)
            ).astype(BF)

        stages += direct_stages(lambda p: sent.at[p], came, pairs[0], "dp", n, i, 0.0, compact, 1.0)
        stages += line_gather_stages(out, pairs[1], "mp", m, j, 2.0, 6.0)
        for t, (x, wide) in enumerate(zip(weights, wides)):
            own_of, put = gather_setup([x], wide)
            put(i)
            stages += pair_gather_stages(own_of, pairs[2 + t], "dp", n, i, 2.1, 9.0)
        if aligned:
            output_of = lambda d: output.at[:, pl.ds(pl.multiple_of(d * line_rows, 16), line_rows), :]
        else:
            output_of = lambda d: output.at[d]
        output_of(i)[...] = line[...]
        stages += pair_gather_stages(output_of, pairs[5], "dp", n, i, 2.1, 9.0)
        run_stages(stages)

    results = call_remote(
        kernel,
        "send_vectors",
        1,
        [jax.ShapeDtypeStruct((m, kept, D), BF)]
        + [shape for shape, _ in made]
        + [jax.ShapeDtypeStruct(output_shape, BF)],
        [pltpu.VMEM((n, block, D), BF)] * 2 + dma_sems(2 * max(n, m)) * 6,
        [vectors, to_slot, to_live, project, upper, lower, output_line],
    )
    output = results[4]
    if not aligned:
        output = output.transpose(1, 0, 2, 3)
    return (
        [results[0]]
        + [shaper(a) for (_, shaper), a in zip(made, results[1:4])]
        + [output.reshape(-1, line_cols)]
    )


def hidden_grads(part_two, hidden, cotangent, mixed, output, gain, grad_upper, grad_lower, roots):
    n, m = lax.axis_size("dp"), lax.axis_size("mp")
    share = part_two.shape[1]
    width = mixed.shape[2]
    made = [gather_shape([a], n) for a in roots]
    parts = [by_chip(grad_upper), by_chip(grad_lower)]

    def kernel(part, hidden_ref, cot, mix, out_mat, gain_ref, up, low, *refs):
        roots_in, refs = refs[: len(roots)], refs[len(roots) :]
        grad_hidden, grad_mixed, grad_output, gain_grad, up_sum, low_sum = refs[:6]
        roots_out, refs = refs[6 : 6 + len(roots)], refs[6 + len(roots) :]
        held, total, swapped, up_held, up_came, low_held, low_came, *sems = refs
        pairs = [tuple(sems[2 * t : 2 * t + 2]) for t in range(4 + len(roots))]
        i, j = lax.axis_index("dp"), lax.axis_index("mp")
        greet({"dp": n, "mp": m}, {"dp": i, "mp": j})
        stages = line_part_stages(part, held, total, pairs[0], "mp", m, j, 0.0, 6.0)
        stages += pair_part_stages(up, up_held, up_came, up_sum, pairs[1], "dp", n, i, 0.1, 1.0)
        stages += pair_part_stages(low, low_held, low_came, low_sum, pairs[2], "dp", n, i, 0.1, 1.0)
        for t, (x, out) in enumerate(zip(roots_in, roots_out)):
            own_of, put = gather_setup([x], out)
            put(i)
            stages += pair_gather_stages(own_of, pairs[4 + t], "dp", n, i, 2.0, 11.0)

        def back():
            mine = pl.ds(pl.multiple_of(j * share, share), share)
            hidden_own = hidden_ref[mine, :]
            scale = rms_scale(hidden_own)
            grad = total[...]
            whole_grad = cot[mine, :].astype(F32) + norm_back(hidden_own, scale, gain_ref[...], grad)
            grad_hidden[...] = whole_grad
            gain_grad[...] = jnp.sum(hidden_own * scale * grad, axis=0, keepdims=True)
            attend = whole_grad.astype(BF)
            for p in range(m):
                swapped[p] = nt(attend, out_mat[p * width : (p + 1) * width, :]).astype(BF)
            grad_mixed[j] = swapped[j]

        def output_grad():
            mine = pl.ds(pl.multiple_of(j * share, share), share)
            attend = grad_hidden[...].astype(BF)
            for p in range(m):
                grad_output[p * width : (p + 1) * width, :] = tn(mix[p, mine, :], attend).astype(BF)

        stages += [(71.0, back), (73.0, output_grad)]
        stages += direct_stages(
            lambda p: swapped.at[p], grad_mixed, pairs[3], "mp", m, j, 72.0, lambda: None, 75.0
        )
        run_stages(stages)

    block = lambda a: pltpu.VMEM(a.shape[:1] + a.shape[2:], BF)
    results = call_remote(
        kernel,
        "hidden_grads",
        4,
        [
            jax.ShapeDtypeStruct((share, D), F32),
            jax.ShapeDtypeStruct((m, share, width), BF),
            jax.ShapeDtypeStruct(output.shape, BF),
            jax.ShapeDtypeStruct((1, D), F32),
            jax.ShapeDtypeStruct(parts[0].shape[2:], F32),
            jax.ShapeDtypeStruct(parts[1].shape[2:], F32),
        ]
        + [shape for shape, _ in made],
        [
            pltpu.VMEM((2, m, share, D), BF),
            pltpu.VMEM((share, D), F32),
            pltpu.VMEM((m, share, width), BF),
            block(parts[0]),
            block(parts[0]),
            block(parts[1]),
            block(parts[1]),
        ]
        + dma_sems(2 * max(n, m)) * (4 + len(roots)),
        [part_two, hidden, cotangent, mixed, output, gain.reshape(1, D)] + parts + roots,
    )
    return list(results[:6]) + [shaper(a) for (_, shaper), a in zip(made, results[6:])]


def stream_grads(part_one, stream, grad_hidden, gain, own_row, to_slot, sums, grad_project, grad_output, slots):
    n, m = lax.axis_size("dp"), lax.axis_size("mp")
    share = part_one.shape[1]
    total_words = own_row.shape[1]
    block = total_words // n
    words = share * m
    width = total_words // to_slot.shape[0]
    parts = [by_chip(grad_project), by_chip(grad_output)]
    chunk = lambda a: jax.ShapeDtypeStruct((1,) + a.shape[-2:], F32)
    made = [gather_shape([chunk(a)], n) for a in (sums[0], sums[1], parts[0], parts[1])]

    def kernel(part, stream_ref, hidden_ref, gain_ref, row_ref, slot_ref, up, low, project, output, *refs):
        out, gain_grad, vectors, up_out, low_out, project_out, output_out = refs[:7]
        (held, total, project_sum, output_sum, line_held, picked, came,
         p_held, p_came, o_held, o_came, *sems) = refs[7:]
        pairs = [tuple(sems[2 * t : 2 * t + 2]) for t in range(10)]
        i, j = lax.axis_index("dp"), lax.axis_index("mp")
        greet({"dp": n, "mp": m}, {"dp": i, "mp": j})
        stages = line_part_stages(part, held, total, pairs[0], "mp", m, j, 0.0, 6.0)
        stages += pair_part_stages(project, p_held, p_came, project_sum.at[0], pairs[1], "dp", n, i, 0.1, 1.0)
        stages += pair_part_stages(output, o_held, o_came, output_sum.at[0], pairs[2], "dp", n, i, 0.1, 1.0)
        up_of, put_up = gather_setup([up], up_out)
        low_of, put_low = gather_setup([low], low_out)
        put_up(i)
        put_low(i)
        stages += pair_gather_stages(up_of, pairs[3], "dp", n, i, 2.0, 11.0)
        stages += pair_gather_stages(low_of, pairs[4], "dp", n, i, 2.0, 11.0)

        def back():
            mine = pl.ds(pl.multiple_of(j * share, share), share)
            stream_own = stream_ref[mine, :]
            scale = rms_scale(stream_own)
            grad = total[...]
            out[j] = (hidden_ref[...] + norm_back(stream_own, scale, gain_ref[...], grad)).astype(BF)
            gain_grad[...] = jnp.sum(stream_own * scale * grad, axis=0, keepdims=True)

        stages.append((71.0, back))
        stages += [
            (when if when < 90 else 199.0, run)
            for when, run in line_gather_stages(out, pairs[5], "mp", m, j, 72.0, 0.1)
        ]
        project_of, put_project = gather_setup([project_sum], project_out)
        output_of, put_output = gather_setup([output_sum], output_out)
        late = []

        def put_sums():
            put_project(i)
            line_held[j] = output_sum[0].astype(BF)

        def line_done():
            summed = line_held[0].astype(F32)
            for p in range(1, m):
                summed = summed + line_held[p].astype(F32)
            output_sum[0] = summed
            put_output(i)

        stages = [(60.0 if when == 80.0 else when, run) for when, run in stages]
        stages.append((72.01, put_sums))
        stages += [
            (when, run)
            for when, run in zip(
                (72.02, 72.25, 198.0),
                [run for _, run in pair_gather_stages(project_of, pairs[6], "dp", n, i, 0, 0)],
            )
        ]
        stages += direct_stages(
            lambda p: line_held.at[j], line_held, pairs[7], "mp", m, j, 72.03, line_done, 76.0
        )
        stages += [
            (when, run)
            for when, run in zip(
                (77.0, 81.5, 198.5),
                [run for _, run in pair_gather_stages(output_of, pairs[8], "dp", n, i, 0, 0)],
            )
        ]

        def pick(d):
            peer = lax.rem(i + d, n)
            rows = out[...].reshape(words, D)
            number = lax.broadcasted_iota(jnp.int32, (words, block), 0)
            picked[peer] = tn((number == row_ref[peer]).astype(BF), rows).astype(BF)
            if d:
                remote(picked.at[peer], came.at[i], pairs[9], d, "dp", peer).start()
            else:
                came[i] = picked[i]

        for d in range(n):
            stages.append((78.0 + (d - 1) % n * 0.1, functools.partial(pick, d)))

        def place():
            for d in range(1, n):
                remote(picked.at[i], came.at[i], pairs[9], d, "dp", i).wait()
            spread = spread_blocks(slot_ref[...], total_words, vectors.shape[0], width)
            vectors[...] = tn(spread, came[...].reshape(total_words, D)).astype(BF)

        stages.append((82.0, place))
        run_stages(stages)

    held_of = lambda a: pltpu.VMEM(a.shape[:1] + a.shape[2:], BF)
    results = call_remote(
        kernel,
        "stream_grads",
        6,
        [
            jax.ShapeDtypeStruct((m, share, D), BF),
            jax.ShapeDtypeStruct((1, D), F32),
            jax.ShapeDtypeStruct((slots * width, D), BF),
        ]
        + [shape for shape, _ in made],
        [
            pltpu.VMEM((2, m, share, D), BF),
            pltpu.VMEM((share, D), F32),
            pltpu.VMEM((1,) + parts[0].shape[2:], F32),
            pltpu.VMEM((1,) + parts[1].shape[2:], F32),
            pltpu.VMEM((m,) + parts[1].shape[2:], BF),
            pltpu.VMEM((n, block, D), BF),
            pltpu.VMEM((n, block, D), BF),
            held_of(parts[0]),
            held_of(parts[0]),
            held_of(parts[1]),
            held_of(parts[1]),
        ]
        + dma_sems(2 * max(n, m)) * 10,
        [
            part_one,
            stream,
            grad_hidden,
            gain.reshape(1, D),
            own_row.reshape(n, 1, block),
            to_slot,
            sums[0][None],
            sums[1][None],
        ]
        + parts,
    )
    return list(results[:3]) + [shaper(a) for (_, shaper), a in zip(made, results[3:])]


def local(
    word_inputs,
    character_embeddings,
    cotangent,
    char_count,
    word_place,
    block_home,
    documents,
    char_gain,
    word_gains,
    char_mixer,
    char_mixer_left,
    char_mixer_right,
    char_mixer_left_root,
    char_mixer_right_root,
    char_lift,
    char_lift_left,
    char_lift_right,
    char_lift_left_root,
    char_lift_right_root,
    word_project,
    word_project_left,
    word_project_right,
    word_project_left_root,
    word_project_right_root,
    word_output,
    word_output_left,
    word_output_right,
    word_output_left_root,
    word_output_right_root,
    feed_upper,
    feed_upper_left,
    feed_upper_right,
    feed_upper_left_root,
    feed_upper_right_root,
    feed_lower,
    feed_lower_left,
    feed_lower_right,
    feed_lower_left_root,
    feed_lower_right_root,
):
    slot_count, share_rows = (character_embeddings.shape[0], character_embeddings.shape[1])
    peer_count = lax.axis_size("dp")
    part_count = lax.axis_size("mp")
    owner_index = lax.axis_index("dp")
    pair_cap = -(-slot_count // peer_count)
    slot_total = peer_count * pair_cap
    rows_dev, length = (word_inputs.shape[0], word_inputs.shape[1])
    words_dev = rows_dev * length
    block_words = share_rows * part_count

    length = word_inputs.shape[1]
    own = lax.axis_index("mp").astype(jnp.int32).reshape(1)
    position = owner_index.astype(jnp.int32).reshape(1)
    peers = lax.broadcasted_iota(jnp.int32, (slot_count, peer_count), 1)
    owner_match = (block_home[:, None] == peers).astype(jnp.int32)
    earlier = (
        lax.broadcasted_iota(jnp.int32, (slot_count, slot_count), 1)
        < lax.broadcasted_iota(jnp.int32, (slot_count, slot_count), 0)
    )
    same_owner = block_home[:, None] == block_home[None, :]
    slot_rank = jnp.sum((earlier & same_owner).astype(jnp.int32), axis=1)
    slot_target = jnp.where(block_home >= 0, block_home * pair_cap + slot_rank, slot_total)
    to_slot = lax.broadcasted_iota(jnp.int32, (slot_total, slot_count), 0) == slot_target[None, :]

    sent_place = jnp.max(
        jnp.where(to_slot[:, :, None], word_place[None] + 1, 0), axis=1
    ) - 1
    char_whole, came_place, output_line = exchange(
        "gather_char",
        0,
        [
            ("gather", "dp", [char_mixer, char_lift]),
            ("swap", "dp", [sent_place.reshape(peer_count, pair_cap, block_words)]),
            ("gather", "mp", [word_output]),
        ],
    )
    came_place = came_place.reshape(slot_total, block_words)
    kind = char_kind(block_home, char_count, share_rows)
    counts = jnp.broadcast_to(
        char_count.astype(F32)[..., None], (slot_count, share_rows, 128)
    )
    word_vectors, kept, pooled, msum = char_forward(
        character_embeddings, kind, counts, char_gain, char_whole
    )

    live = jnp.max(came_place, axis=1) >= 0
    slots_before = (
        lax.broadcasted_iota(jnp.int32, (slot_total, slot_total), 1)
        < lax.broadcasted_iota(jnp.int32, (slot_total, slot_total), 0)
    )
    live_rank = jnp.sum((slots_before & live[None, :]).astype(jnp.int32), axis=1)
    live_rank = jnp.where(live, live_rank, OWNER_BLOCKS)
    to_live = lax.broadcasted_iota(jnp.int32, (OWNER_BLOCKS, slot_total), 0) == live_rank[None, :]
    live_place = jnp.max(jnp.where(to_live[:, :, None], came_place[None] + 1, 0), axis=1) - 1
    own_row = lax.dynamic_slice_in_dim(
        came_place.reshape(slot_total, part_count, share_rows), own[0], 1, 1
    ).reshape(1, -1)

    live_vectors, project_mat, upper_mat, lower_mat, output_mat = send_vectors(
        word_vectors,
        to_slot.astype(BF),
        to_live.astype(BF),
        share_rows,
        word_project.reshape((3,) + word_project.shape[2:]),
        feed_upper,
        feed_lower,
        output_line.reshape((part_count,) + word_output.shape[1:]),
    )
    place_parts = live_place.reshape(OWNER_BLOCKS, part_count, share_rows)
    place_flat = place_parts.transpose(1, 0, 2).reshape(-1)
    stream, normed_one, qkv, probs, mixed = word_forward(
        live_vectors.reshape(-1, D),
        place_flat,
        word_inputs.reshape(words_dev, D),
        documents,
        word_gains[0],
        project_mat,
    )
    mixed_all, mixer_root, lift_root = exchange(
        "gather_mixed",
        3,
        [
            ("line_gather", "mp", [mixed]),
            ("gather", "dp", [char_mixer_right_root]),
            ("gather", "dp", [char_lift_right_root]),
        ],
    )
    flat_cotangent = cotangent.reshape(words_dev, D)
    hidden, feed_part, part_two, grad_upper, grad_lower = feed(
        mixed_all, output_mat, stream, flat_cotangent, word_gains[1], upper_mat, lower_mat
    )
    shares = (part_count, words_dev // part_count, D)
    grad_hidden, grad_mixed, grad_output_mat, gain_two, part_upper, part_lower, *word_roots = hidden_grads(
        part_two.reshape(shares),
        hidden,
        flat_cotangent,
        mixed_all,
        output_mat,
        word_gains[1],
        grad_upper,
        grad_lower,
        [
            word_project_right_root.reshape((3,) + word_project_right_root.shape[2:]),
            word_output_right_root,
            feed_upper_right_root,
            feed_lower_right_root,
        ],
    )
    project_root, output_root, upper_root, lower_root = word_roots
    part_one, grad_project = word_backward(
        probs, qkv, grad_mixed.reshape(words_dev, -1), normed_one, project_mat
    )
    grad_words, gain_one, grad_vectors, sum_upper, sum_lower, sum_project, sum_output = stream_grads(
        part_one.reshape(shares),
        stream,
        grad_hidden,
        word_gains[0],
        own_row,
        to_slot.astype(BF),
        (part_upper, part_lower),
        grad_project,
        grad_output_mat,
        slot_count,
    )
    word_inputs_gradient = grad_words.reshape(word_inputs.shape)
    own_rows = word_output.shape[1] * peer_count
    sum_output = lax.dynamic_slice_in_dim(sum_output, own[0] * own_rows, own_rows, 0)
    grad_vectors, feed_part = lax.optimization_barrier((grad_vectors, feed_part))
    feed_total = lax.psum(feed_part, "mp").astype(F32)
    block_out = (hidden + feed_total).astype(BF).reshape(word_inputs.shape)
    char_embeds_gradient, char_grads, grad_char_gain = char_backward(
        character_embeddings, kind, counts, char_gain, char_whole, kept, pooled, msum, grad_vectors
    )
    small = jnp.concatenate(
        [
            jnp.pad(grad_char_gain, ((0, 0), (0, D - CHAR_BLOCK_WIDTH))),
            gain_one,
            gain_two,
            jnp.zeros((5, D), F32),
        ]
    )
    word_sums = (sum_project, sum_output, sum_upper, sum_lower)
    char_sums, small_sums = sum_char_grads(char_grads, small, word_sums)
    parameter_count = (
        sum(
            part_count * w.size * peer_count
            for w in (word_project, word_output, feed_upper, feed_lower)
        )
        + peer_count * (char_mixer.size + char_lift.size)
        + char_gain.size
        + word_gains.size
    )
    flat = lambda a: a.reshape((-1,) + a.shape[-2:])
    results = shampoo(
        0.5 * math.sqrt(parameter_count),
        position,
        char_sums,
        small_sums,
        char_gain,
        word_gains,
        word_sums,
        [
            tuple(flat(a) for a in group[:4]) + (group[4],)
            for group in (
                (char_mixer, char_mixer_left, char_mixer_right, char_mixer_left_root, mixer_root),
                (char_lift, char_lift_left, char_lift_right, char_lift_left_root, lift_root),
                (word_project, word_project_left, word_project_right, word_project_left_root, project_root),
                (word_output, word_output_left, word_output_right, word_output_left_root, output_root),
                (feed_upper, feed_upper_left, feed_upper_right, feed_upper_left_root, upper_root),
                (feed_lower, feed_lower_left, feed_lower_right, feed_lower_left_root, lower_root),
            )
        ],
    )
    norm, gain_grad, gains_grad, gain_new, gains_new = results[:5]
    stepped = []
    for t, group in enumerate(
        (
            (char_mixer, char_mixer_left, char_mixer_right),
            (char_lift, char_lift_left, char_lift_right),
            (word_project, word_project_left, word_project_right),
            (word_output, word_output_left, word_output_right),
            (feed_upper, feed_upper_left, feed_upper_right),
            (feed_lower, feed_lower_left, feed_lower_right),
        )
    ):
        master, left, right = group
        stepped += [
            a.reshape(b.shape)
            for a, b in zip(results[5 + 5 * t : 10 + 5 * t], (master, left, right, master, master))
        ]
    return (
        block_out,
        word_inputs_gradient,
        char_embeds_gradient,
        gain_grad[0],
        gains_grad,
        gain_new[0],
        gains_new,
        norm[0, 0],
        *stepped,
    )


def solution(mesh):
    placed = (
        P("dp", None, None),
        P("dp", "mp", None, None),
        P("dp", None, None),
        P("dp", "mp"),
        P("dp", None),
        P("dp"),
        P("dp", None),
        P(),
        P(),
        P(None, "dp", None),
        P(None, "dp", None),
        P(None, "dp", None),
        P(None, "dp", None),
        P(None, "dp", None),
        P(None, "dp", None),
        P(None, "dp", None),
        P(None, "dp", None),
        P(None, "dp", None),
        P(None, "dp", None),
        P(None, "mp", "dp", None),
        P(None, "mp", "dp", None),
        P(None, "mp", "dp", None),
        P(None, "mp", "dp", None),
        P(None, "mp", "dp", None),
        P("mp", "dp", None),
        P("mp", "dp", None),
        P("mp", "dp", None),
        P("mp", "dp", None),
        P("mp", "dp", None),
        P("mp", "dp", None),
        P("mp", "dp", None),
        P("mp", "dp", None),
        P("mp", "dp", None),
        P("mp", "dp", None),
        P("mp", "dp", None),
        P("mp", "dp", None),
        P("mp", "dp", None),
        P("mp", "dp", None),
        P("mp", "dp", None),
    )
    return jax.shard_map(
        local,
        mesh=mesh,
        in_specs=placed,
        out_specs=(
            P("dp", None, None),
            P("dp", None, None),
            P("dp", "mp", None, None),
            P(),
            P(),
            P(),
            P(),
            P(),
            P(None, "dp", None),
            P(None, "dp", None),
            P(None, "dp", None),
            P(None, "dp", None),
            P(None, "dp", None),
            P(None, "dp", None),
            P(None, "dp", None),
            P(None, "dp", None),
            P(None, "dp", None),
            P(None, "dp", None),
            P(None, "mp", "dp", None),
            P(None, "mp", "dp", None),
            P(None, "mp", "dp", None),
            P(None, "mp", "dp", None),
            P(None, "mp", "dp", None),
            P("mp", "dp", None),
            P("mp", "dp", None),
            P("mp", "dp", None),
            P("mp", "dp", None),
            P("mp", "dp", None),
            P("mp", "dp", None),
            P("mp", "dp", None),
            P("mp", "dp", None),
            P("mp", "dp", None),
            P("mp", "dp", None),
            P("mp", "dp", None),
            P("mp", "dp", None),
            P("mp", "dp", None),
            P("mp", "dp", None),
            P("mp", "dp", None),
        ),
        check_vma=False,
    )
```

```python
import functools
import math

import jax
import jax.numpy as jnp
from jax import lax
from jax.experimental import pallas as pl
from jax.experimental.pallas import tpu as pltpu
from jax.sharding import PartitionSpec as P

D = 512
HD = 64
FF = 2048
CHAR_BLOCK_WIDTH = 256
OWNER_BLOCKS = 10
decay_rate = 0.5
learn_rate = 1.0
gain_rate = 0.4
negative_big = -1e30

CW = 256
CHEADS = 4
CHD = 64
SPOTS = 16
KEPT = 3 * CW + CHEADS * 128 + CW
epsilon = 1e-05
BF = jnp.bfloat16
F32 = jnp.float32


def nn(a, b):
    return lax.dot_general(a, b, (((1,), (0,)), ((), ())), preferred_element_type=F32)


def nt(a, b):
    return lax.dot_general(a, b, (((1,), (1,)), ((), ())), preferred_element_type=F32)


def tn(a, b):
    return lax.dot_general(a, b, (((0,), (0,)), ((), ())), preferred_element_type=F32)


GROUPS = 4


def char_classes(share):
    listed = [(1, 4, 32), (2, 8, 16), (4, 16, 8)]
    return [(c, p, w, GROUPS // (share // w)) for c, p, w in listed if w <= share]


def order_matrix(places, words):
    row = lax.broadcasted_iota(jnp.int32, (128, SPOTS * words), 0)
    col = lax.broadcasted_iota(jnp.int32, (128, SPOTS * words), 1)
    return ((row % words) * SPOTS + row // words == col).astype(BF)


def head_stack(rows, scale):
    lane = lax.broadcasted_iota(jnp.int32, (1, CW), 1) // CHD
    return jnp.concatenate(
        [rows * jnp.where(lane == h, scale, 0.0).astype(BF) for h in range(CHEADS)], axis=0
    )


def char_forward_kernel(
    classes, home, first, x_ref, counts_in, gain_ref, mats_ref, *refs
):
    orders, refs = refs[-len(classes) :], refs[: -len(classes)]
    vec_ref, kept_out, pooled_ref, msum_ref, kept, sumx, count_ref, kind, ids, batch_kind, sems = refs
    slots, share = count_ref.shape[:2]
    batches = plan_batches(classes, home, first, kind, ids, batch_kind)
    count_ref[...] = spread_counts(counts_in[...]).reshape(count_ref.shape)
    for (_, places, words, _), order_ref in zip(classes, orders):
        order_ref[...] = order_matrix(places, words)
    sumx[...] = jnp.zeros_like(sumx)
    msum_ref[...] = jnp.zeros_like(msum_ref)

    def save(slot, rows):
        return pltpu.make_async_copy(
            kept.at[slot, pl.ds(0, rows)], kept_out.at[slot, pl.ds(0, rows)], sems.at[slot]
        )

    def block(places, words, per, order_ref, number):
        chosen = [ids[number * GROUPS + t] for t in range(per)]
        chosen = [jnp.where(c < 0, chosen[0], c) for c in chosen]
        groups = [(c, g) for c in chosen for g in range(share // words)]
        cnts = [count_ref[c, pl.ds(g * words, words), :] for c, g in groups]
        xs = [
            nn(order_ref[...], x_ref[c, pl.ds(g * words * SPOTS, words * SPOTS), :]) for c, g in groups
        ]
        normed = jnp.concatenate(
            [
                (
                    x * lax.rsqrt(jnp.mean(x * x, axis=-1, keepdims=True) + epsilon) * gain_ref[...]
                ).astype(BF)
                for x in xs
            ],
            axis=0,
        )
        qkv = nn(normed, mats_ref[:, : 3 * CW]).astype(BF)
        place = lax.broadcasted_iota(jnp.int32, (places, words, CW), 0).astype(F32)
        lane = lax.broadcasted_iota(jnp.int32, (words, CHEADS * 128), 1) % 128
        word = lax.broadcasted_iota(jnp.int32, (words, CHEADS * 128), 0)
        mine = lane % words == word
        spot = (lane // words).astype(F32)
        head_row = lax.broadcasted_iota(jnp.int32, (CHEADS * 128, CW), 0) // 128
        head_col = lax.broadcasted_iota(jnp.int32, (CHEADS * 128, CW), 1) // CHD
        same_head = (head_row == head_col).astype(BF)
        far = lax.broadcasted_iota(jnp.int32, (places, words, CHEADS * 128), 0).astype(F32)
        scores = []
        for t in range(GROUPS):
            rows = qkv[t * 128 : (t + 1) * 128]
            scores.append(nt(rows[:, CW : 2 * CW], head_stack(rows[:, :CW], 1.0 / math.sqrt(CHD))))
        sums = []
        for t in range(GROUPS):
            shown = place < jnp.concatenate([cnts[t], cnts[t]], axis=1)[None]
            sums.append(jnp.sum(jnp.where(shown, xs[t].reshape(places, words, CW), 0.0), axis=0))
        probs = []
        for t in range(GROUPS):
            cnt4 = jnp.concatenate([cnts[t]] * CHEADS, axis=1)
            s = jnp.where(far < cnt4[None], scores[t].reshape(places, words, CHEADS * 128), -1e30)
            e = jnp.exp(s - jnp.max(s, axis=0)[None])
            r = jnp.where(mine & (spot < cnt4), 1.0 / jnp.sum(e, axis=0), 0.0)
            probs.append((e * r[None]).astype(BF).reshape(128, CHEADS * 128))
        columns = [nn(p, same_head) for p in probs]
        for t, (c, g) in enumerate(groups):
            rows = qkv[t * 128 : (t + 1) * 128]
            at = pl.ds(g * 128, 128)
            kept[c, at, : 3 * CW] = rows
            kept[c, at, 3 * CW : 3 * CW + CHEADS * 128] = probs[t]
            kept[c, at, 3 * CW + CHEADS * 128 :] = columns[t].astype(BF)
            own = pl.ds(pl.multiple_of(c * share + g * words, words), words)
            msum_ref[own, :] = jnp.sum(
                (columns[t] * rows[:, 2 * CW :].astype(F32)).reshape(places, words, CW), axis=0
            )
            sumx[own, :] = sums[t]
        for t in range(per):
            slot = ids[number * GROUPS + t]

            @pl.when(slot >= 0)
            def _(slot=slot):
                save(slot, share * places).start()

    def batch(number, carry):
        for (which, places, words, per), order_ref in zip(classes, orders):
            pl.when(batch_kind[number] == which)(
                functools.partial(block, places, words, per, order_ref, number)
            )
        return carry

    lax.fori_loop(0, batches, batch, 0)
    cnt2 = jnp.concatenate([count_ref[...].reshape(slots * share, 128)] * 2, axis=1)
    summed = sumx[...] + nn(msum_ref[...].astype(BF), mats_ref[:, 3 * CW : 4 * CW])
    pooled = (summed / cnt2).astype(BF)
    pooled_ref[...] = pooled
    vec_ref[...] = nn(pooled, mats_ref[:, 4 * CW :]).astype(BF)

    def finish(slot, carry):
        for which, places, words, per in classes:

            @pl.when(kind[slot] == which)
            def _(places=places):
                save(slot, share * places).wait()

        return carry

    lax.fori_loop(0, slots, finish, 0)


def plan_batches(classes, home, count, kind, ids, batch_kind):
    slots = home.shape[0]
    coarse = classes[0][0] == 1

    def sort(slot, carry):
        places = count[slot, 0]
        which = jnp.where(places <= 8, 2, 4)
        if coarse:
            which = jnp.where(places <= 4, 1, which)
        kind[slot] = jnp.where(home[slot] >= 0, which, 0)
        for t in range(GROUPS):
            ids[slot * GROUPS + t] = -1
        return carry

    lax.fori_loop(0, slots, sort, 0)
    batch = jnp.int32(0)
    for which, _, _, per in classes:

        def take(slot, carry):
            batch, place = carry
            hit = kind[slot] == which

            @pl.when(hit)
            def _():
                ids[batch * GROUPS + place] = slot
                batch_kind[batch] = which

            place = jnp.where(hit, place + 1, place)
            full = place == per
            return jnp.where(full, batch + 1, batch), jnp.where(full, 0, place)

        batch, place = lax.fori_loop(0, slots, take, (batch, jnp.int32(0)))
        batch = jnp.where(place > 0, batch + 1, batch)
    return batch


def spread_counts(count):
    slots, share = count.shape
    row = lax.broadcasted_iota(jnp.int32, (slots * share, slots), 0) // share
    pick = (row == lax.broadcasted_iota(jnp.int32, (slots * share, slots), 1)).astype(BF)
    wide = nn(pick, count.astype(F32).astype(BF))
    mine = lax.broadcasted_iota(jnp.int32, (slots * share, share), 0) % share
    mine = mine == lax.broadcasted_iota(jnp.int32, (slots * share, share), 1)
    return nn(jnp.where(mine, wide, 0.0).astype(BF), jnp.ones((share, 128), BF))


def char_call(kernel, name, inputs, scalars, outs, scratch, in_hbm, out_hbm, flops, limit):
    vmem = pl.BlockSpec(memory_space=pltpu.VMEM)
    smem = pl.BlockSpec(memory_space=pltpu.SMEM)
    hbm = pl.BlockSpec(memory_space=pltpu.HBM)
    return pl.pallas_call(
        kernel,
        in_specs=[smem] * len(scalars) + [hbm if t in in_hbm else vmem for t in range(len(inputs))],
        out_specs=[hbm if t in out_hbm else vmem for t in range(len(outs))],
        out_shape=outs,
        scratch_shapes=scratch,
        cost_estimate=pl.CostEstimate(flops=flops, bytes_accessed=60 << 20, transcendentals=0),
        compiler_params=pltpu.CompilerParams(vmem_limit_bytes=limit << 20),
        name=name,
    )(*scalars, *inputs)


def plan_scratch(slots, share):
    return [
        pltpu.VMEM((slots, share, 128), F32),
        pltpu.SMEM((slots,), jnp.int32),
        pltpu.SMEM((slots * GROUPS,), jnp.int32),
        pltpu.SMEM((slots,), jnp.int32),
    ]


def char_forward(x, home, counts, gain, mats):
    slots, share = x.shape[:2]
    classes = char_classes(share)
    rows = share * SPOTS
    orders = [pltpu.VMEM((128, SPOTS * c[2]), BF) for c in classes]
    words_all = slots * share
    return char_call(
        functools.partial(char_forward_kernel, classes),
        "char_forward",
        [x.reshape(slots, rows, CW), counts, gain.reshape(1, CW), mats],
        (home, counts),
        [
            jax.ShapeDtypeStruct((words_all, D), BF),
            jax.ShapeDtypeStruct((slots, rows, KEPT), BF),
            jax.ShapeDtypeStruct((words_all, CW), BF),
            jax.ShapeDtypeStruct((words_all, CW), F32),
        ],
        [
            pltpu.VMEM((slots, rows, KEPT), BF),
            pltpu.VMEM((words_all, CW), F32),
        ]
        + plan_scratch(slots, share)
        + [pltpu.SemaphoreType.DMA((slots,))]
        + orders,
        (),
        (1,),
        slots * rows * CW * CW * 16,
        46,
    )


def char_backward_kernel(
    classes, home, first, x_in, counts_in, kept_in, gv_ref, pooled_ref, msum_ref, gain_ref, mats_ref, *refs
):
    orders, refs = refs[-len(classes) :], refs[: -len(classes)]
    dx_out, grads_ref, dgain_ref, x_ref, kept, dx_ref, gp_all, gm_all, dqkv_sum, count_ref = refs[:10]
    kind, ids, batch_kind, x_sems, kept_sems, dx_sems = refs[10:]
    slots, share = count_ref.shape[:2]
    batches = plan_batches(classes, home, first, kind, ids, batch_kind)

    def load_x(slot):
        return pltpu.make_async_copy(x_in.at[slot], x_ref.at[slot], x_sems.at[slot])

    def load_kept(slot, rows):
        return pltpu.make_async_copy(
            kept_in.at[slot, pl.ds(0, rows)], kept.at[slot, pl.ds(0, rows)], kept_sems.at[slot]
        )

    def save(slot):
        return pltpu.make_async_copy(dx_ref.at[slot], dx_out.at[slot], dx_sems.at[slot])

    def begin(number, carry):
        for which, places, words, per in classes:

            @pl.when(batch_kind[number] == which)
            def _(places=places, per=per):
                for t in range(per):
                    slot = ids[number * GROUPS + t]

                    @pl.when(slot >= 0)
                    def _(slot=slot):
                        load_x(slot).start()
                        load_kept(slot, share * places).start()

        return carry

    lax.fori_loop(0, batches, begin, 0)

    count_ref[...] = spread_counts(counts_in[...]).reshape(count_ref.shape)
    for (_, places, words, _), order_ref in zip(classes, orders):
        order_ref[...] = order_matrix(places, words)
    gv = gv_ref[...]
    cnt2 = jnp.concatenate([count_ref[...].reshape(slots * share, 128)] * 2, axis=1)
    gp = nt(gv, mats_ref[:, 4 * CW :]) / cnt2
    gp_all[...] = gp
    gpb = gp.astype(BF)
    gm_all[...] = nt(gpb, mats_ref[:, 3 * CW : 4 * CW]).astype(BF).astype(F32)
    grads_ref[:, 4 * CW :] = tn(pooled_ref[...], gv).astype(BF)
    grads_ref[:, 3 * CW : 4 * CW] = tn(msum_ref[...].astype(BF), gpb).astype(BF)
    dqkv_sum[...] = jnp.zeros_like(dqkv_sum)
    dgain_ref[...] = jnp.zeros_like(dgain_ref)

    def block(places, words, per, order_ref, number):
        picked = [ids[number * GROUPS + t] for t in range(per)]
        chosen = [jnp.where(c < 0, picked[0], c) for c in picked]
        weights = [jnp.where(c < 0, 0.0, 1.0) for c in picked]
        targets = [jnp.where(c < 0, slots, c) for c in picked]
        for slot in picked:

            @pl.when(slot >= 0)
            def _(slot=slot):
                load_x(slot).wait()
                load_kept(slot, share * places).wait()

        groups = [
            (c, g, weight, target)
            for c, weight, target in zip(chosen, weights, targets)
            for g in range(share // words)
        ]
        gain = gain_ref[...]
        eighth = 1.0 / math.sqrt(CHD)
        place = lax.broadcasted_iota(jnp.int32, (places, words, CW), 0).astype(F32)
        word_grads = []
        row_grads = []
        out_grads = []
        for t, (c, g, weight, _) in enumerate(groups):
            mine = pl.ds(pl.multiple_of(c * share + g * words, words), words)
            cnt = count_ref[c, pl.ds(g * words, words), :]
            shown = place < jnp.concatenate([cnt, cnt], axis=1)[None]
            word_grads.append(gm_all[mine, :] * weight)
            out_grads.append(jnp.where(shown, (gp_all[mine, :] * weight)[None], 0.0).reshape(128, CW))
            row_grads.append(
                jnp.where(shown, word_grads[t][None], 0.0).reshape(128, CW).astype(BF)
            )
        at = [pl.ds(g * 128, 128) for _, g, _, _ in groups]
        queries = [kept[c, at[t], :CW] for t, (c, *_) in enumerate(groups)]
        keys = [kept[c, at[t], CW : 2 * CW] for t, (c, *_) in enumerate(groups)]
        products = [
            nt(kept[c, at[t], 2 * CW : 3 * CW], head_stack(row_grads[t], 1.0))
            for t, (c, *_) in enumerate(groups)
        ]
        scores = []
        for t, (c, *_) in enumerate(groups):
            p = kept[c, at[t], 3 * CW : 3 * CW + CHEADS * 128].astype(F32)
            p3 = p.reshape(places, words, CHEADS * 128)
            u = p3 * products[t].reshape(places, words, CHEADS * 128)
            scores.append((u - p3 * jnp.sum(u, axis=0)[None]).astype(BF).reshape(128, CHEADS * 128))
        xs = [
            nn(order_ref[...], x_ref[c, pl.ds(g * words * SPOTS, words * SPOTS), :])
            for c, g, _, _ in groups
        ]
        scales = [lax.rsqrt(jnp.mean(x * x, axis=-1, keepdims=True) + epsilon) for x in xs]
        normed = jnp.concatenate([(x * s * gain).astype(BF) for x, s in zip(xs, scales)], axis=0)
        grads = []
        for t, (c, *_) in enumerate(groups):
            dk = nn(scores[t], head_stack(queries[t], eighth))
            stacked = jnp.concatenate(
                [scores[t][:, h * 128 : (h + 1) * 128] for h in range(CHEADS)], axis=0
            )
            dq = tn(stacked, head_stack(keys[t], eighth))
            column = kept[c, at[t], 3 * CW + CHEADS * 128 :].astype(F32)
            dv = (column.reshape(places, words, CW) * word_grads[t][None]).reshape(128, CW)
            grads.append(jnp.concatenate([dq.astype(BF), dk.astype(BF), dv.astype(BF)], axis=1))
        grads = jnp.concatenate(grads, axis=0)
        dn_all = nt(grads, mats_ref[:, : 3 * CW])
        dqkv_sum[...] += tn(normed, grads)
        dgain = jnp.zeros((1, CW), F32)
        for t, (c, g, _, target) in enumerate(groups):
            x, scale = xs[t], scales[t]
            dn = dn_all[t * 128 : (t + 1) * 128]
            xr = x * scale
            dgain = dgain + jnp.sum(xr * dn, axis=0, keepdims=True)
            w = dn * gain
            inner = jnp.mean(xr * w, axis=-1, keepdims=True)
            dx = out_grads[t] + scale * (w - xr * inner)
            dx_ref[target, pl.ds(g * words * SPOTS, words * SPOTS), :] = tn(
                order_ref[...], dx.astype(BF)
            ).astype(BF)
        dgain_ref[...] += dgain
        for slot in picked:

            @pl.when(slot >= 0)
            def _(slot=slot):
                save(slot).start()

    def batch(number, carry):
        for (which, places, words, per), order_ref in zip(classes, orders):
            pl.when(batch_kind[number] == which)(
                functools.partial(block, places, words, per, order_ref, number)
            )
        return carry

    lax.fori_loop(0, batches, batch, 0)
    grads_ref[:, : 3 * CW] = dqkv_sum[...].astype(BF)

    def empty(slot, carry):
        @pl.when(kind[slot] == 0)
        def _():
            dx_ref[slot] = jnp.zeros(dx_ref.shape[1:], BF)
            save(slot).start()

        return carry

    lax.fori_loop(0, slots, empty, 0)

    def finish(slot, carry):
        save(slot).wait()
        return carry

    lax.fori_loop(0, slots, finish, 0)


def char_backward(x, home, counts, gain, mats, kept, pooled, msum, grad_vectors):
    slots, share = x.shape[:2]
    classes = char_classes(share)
    rows = share * SPOTS
    orders = [pltpu.VMEM((128, SPOTS * c[2]), BF) for c in classes]
    words_all = slots * share
    dx, grads, dgain = char_call(
        functools.partial(char_backward_kernel, classes),
        "char_backward",
        [
            x.reshape(slots, rows, CW), counts, kept, grad_vectors, pooled, msum, gain.reshape(1, CW), mats,
        ],
        (home, counts),
        [
            jax.ShapeDtypeStruct((slots, rows, CW), BF),
            jax.ShapeDtypeStruct(mats.shape, BF),
            jax.ShapeDtypeStruct((1, CW), F32),
        ],
        [
            pltpu.VMEM((slots, rows, CW), BF),
            pltpu.VMEM((slots, rows, KEPT), BF),
            pltpu.VMEM((slots + 1, rows, CW), BF),
            pltpu.VMEM((words_all, CW), F32),
            pltpu.VMEM((words_all, CW), F32),
            pltpu.VMEM((CW, 3 * CW), F32),
        ]
        + plan_scratch(slots, share)
        + [pltpu.SemaphoreType.DMA((slots,))] * 3
        + orders,
        (0, 2),
        (0,),
        slots * rows * CW * CW * 28,
        53,
    )
    return dx.reshape(x.shape), grads, dgain


MESH_ID = pl.DeviceIdType.MESH


def greet(sizes, me):
    barrier = pltpu.get_barrier_semaphore()
    for axis, n in sizes.items():
        for d in range(1, n):
            pl.semaphore_signal(
                barrier, inc=1, device_id={axis: lax.rem(me[axis] + d, n)}, device_id_type=MESH_ID
            )
    pl.semaphore_wait(barrier, sum(n - 1 for n in sizes.values()))


def remote(source, target, sems, at, axis, peer):
    return pltpu.make_async_remote_copy(
        src_ref=source,
        dst_ref=target,
        send_sem=sems[0].at[at],
        recv_sem=sems[1].at[at],
        device_id={axis: peer},
        device_id_type=MESH_ID,
    )


def pair_gather_stages(own_of, sems, axis, n, mine, begin, late):
    chips = n // 2
    core = lax.rem(mine, 2)
    chip = mine // 2
    sibling = chip * 2 + 1 - core

    def start():
        for d in range(1, chips):
            there = lax.rem(chip + d, chips) * 2 + core
            remote(own_of(mine), own_of(mine), sems, d, axis, there).start()
        remote(own_of(mine), own_of(mine), sems, chips, axis, sibling).start()

    def hand_on():
        for d in range(1, chips):
            came = lax.rem(chip + chips - d, chips) * 2 + core
            remote(own_of(mine), own_of(came), sems, d, axis, sibling).wait_recv()
            remote(own_of(came), own_of(came), sems, chips + d, axis, sibling).start()

    def finish():
        for d in range(1, 2 * chips):
            remote(own_of(mine), own_of(mine), sems, d, axis, sibling).wait_send()
            if d >= chips:
                remote(own_of(mine), own_of(mine), sems, d, axis, sibling).wait_recv()

    return [(begin, start), (late, hand_on), (90.0, finish)]


def pair_part_stages(x, held, came, out, sems, axis, n, mine, begin, late):
    chips = n // 2
    core = lax.rem(mine, 2)
    chip = mine // 2
    sibling = chip * 2 + 1 - core

    def start():
        remote(x.at[:, 1 - core], came, sems, 0, axis, sibling).start()

    def onward():
        remote(x.at[:, 1 - core], came, sems, 0, axis, sibling).wait()
        for d in range(chips):
            there = lax.rem(chip + 1 + d, chips)
            came[there] = (came[there].astype(F32) + x[there, core].astype(F32)).astype(came.dtype)
            if d < chips - 1:
                remote(
                    came.at[there], held.at[chip], sems, 1 + d, axis, there * 2 + core
                ).start()

    def finish():
        held[chip] = came[chip]
        for d in range(chips - 1):
            remote(came.at[chip], held.at[chip], sems, 1 + d, axis, sibling).wait()
        total = held[0].astype(F32)
        for p in range(1, chips):
            total = total + held[p].astype(F32)
        out[...] = total.astype(out.dtype)

    return [(begin, start), (late, onward), (80.0, finish)]


def line_gather_stages(out, sems, axis, n, mine, begin, each, cols=None):
    def piece(block):
        return out.at[block] if cols is None else out.at[block, :, cols]

    def step(k):
        for way in range(2):
            block = mine - k if way == 0 else mine + k
            here = (block >= 0) & (block < n)
            block = jnp.clip(block, 0, n - 1)
            onward = mine + 1 if way == 0 else mine - 1
            room = (onward >= 0) & (onward < n)
            peer = jnp.clip(onward, 0, n - 1)
            if k > 0:

                @pl.when(here)
                def _(way=way, block=block):
                    remote(piece(block), piece(block), sems, way * n + k - 1, axis, mine).wait_recv()

            if k < n - 1:

                @pl.when(here & room)
                def _(way=way, block=block, peer=peer):
                    remote(piece(block), piece(block), sems, way * n + k, axis, peer).start()

    def finish():
        for way in range(2):
            for k in range(n - 1):
                block = mine - k if way == 0 else mine + k
                sent = (mine < n - 1) & (block >= 0) if way == 0 else (mine > 0) & (block < n)

                @pl.when(sent)
                def _(way=way, k=k):
                    remote(piece(mine), piece(mine), sems, way * n + k, axis, mine).wait_send()

    stages = [(begin + each * k, functools.partial(step, k)) for k in range(n)]
    return stages + [(95.0, finish)]


def line_part_stages(x, held, out, sems, axis, n, mine, begin, each):
    def step(t):
        for way in range(2):
            distance = mine if way == 0 else n - 1 - mine
            turn = t - distance
            here = (turn >= 0) & (turn < n - 1 - distance)
            turn = jnp.clip(turn, 0, n - 1)
            block = n - 1 - turn if way == 0 else turn
            peer = jnp.clip(mine + 1 if way == 0 else mine - 1, 0, n - 1)
            at = way * n + block

            @pl.when(here & (distance == 0))
            def _(way=way, block=block, peer=peer, at=at):
                remote(x.at[block], held.at[way, block], sems, at, axis, peer).start()

            @pl.when(here & (distance > 0))
            def _(way=way, block=block, peer=peer, at=at):
                place = held.at[way, block]
                remote(place, place, sems, at, axis, mine).wait_recv()
                held[way, block] = (held[way, block].astype(F32) + x[block].astype(F32)).astype(x.dtype)
                remote(place, place, sems, at, axis, peer).start()

    def finish():
        out[...] = x[mine].astype(F32)
        for way, there in ((0, mine > 0), (1, mine < n - 1)):

            @pl.when(there)
            def _(way=way):
                here = held.at[way, mine]
                remote(here, here, sems, way * n + mine, axis, mine).wait_recv()
                out[...] += held[way, mine].astype(F32)

        for way in range(2):
            for block in range(n):
                further = block > mine if way == 0 else block < mine

                @pl.when(further)
                def _(way=way, block=block):
                    here = held.at[way, block]
                    remote(here, here, sems, way * n + block, axis, mine).wait_send()

    stages = [(begin + each * k, functools.partial(step, k)) for k in range(n - 1)]
    return stages + [(70.0, finish)]


def direct_stages(source_of, target, sems, axis, n, mine, begin, done, end, cols=None):
    def piece(block):
        return target.at[block] if cols is None else target.at[block, :, cols]

    def start():
        for d in range(1, n):
            peer = lax.rem(mine + d, n)
            remote(source_of(peer), piece(mine), sems, d, axis, peer).start()

    def finish():
        for d in range(1, n):
            remote(source_of(mine), piece(mine), sems, d, axis, mine).wait()
        done()

    return [(begin, start), (end, finish)]


def exchange(name, number, tasks):
    sizes = {axis: lax.axis_size(axis) for _, axis, _ in tasks}
    outs, scratch, counts, shapers = [], [], [], []
    for kind, axis, arrays in tasks:
        n = sizes[axis]
        array = arrays[0]
        shaper = lambda a: a
        if kind == "gather":
            rows = array.shape[1]
            cols = sum(a.shape[0] * a.shape[2] for a in arrays)
            made = jax.ShapeDtypeStruct((n * rows, cols) if rows % 16 == 0 else (n, rows, cols), BF)
            shaper = lambda a, rows=rows, cols=cols, n=n: a.reshape(n * rows, cols)
        elif kind == "gather_mid":
            lead, rows, cols = array.shape
            made = jax.ShapeDtypeStruct(
                (lead, n * rows, cols) if rows % 16 == 0 else (n, lead, rows, cols), array.dtype
            )
            if rows % 16:
                shaper = lambda a, lead=lead, rows=rows, cols=cols, n=n: a.transpose(1, 0, 2, 3).reshape(
                    lead, n * rows, cols
                )
        else:
            block = array.shape if kind in ("line_gather", "total") else array.shape[1:]
            if kind == "part":
                block = array.shape[2:]
            summed = kind in ("part", "line_part", "total")
            made = jax.ShapeDtypeStruct(block if summed else (n,) + block, F32 if summed else array.dtype)
        outs.append(made)
        shapers.append(shaper)
        counts.append(len(arrays))
        scratch += [pltpu.SemaphoreType.DMA((2 * n,)), pltpu.SemaphoreType.DMA((2 * n,))]
        if kind == "part":
            scratch += [pltpu.VMEM((n // 2,) + block, array.dtype)] * 2
        if kind == "total":
            scratch.append(pltpu.VMEM((n,) + block, array.dtype))
        if kind == "line_part":
            scratch.append(pltpu.VMEM((2, n) + block, array.dtype))
    total_ins = sum(counts)

    def kernel(*refs):
        ins, at = [], 0
        for count in counts:
            ins.append(refs[at : at + count])
            at += count
        results = refs[at : at + len(tasks)]
        rest = list(refs[at + len(tasks) :])
        me = {axis: lax.axis_index(axis) for axis in sizes}
        greet(sizes, me)
        stages = []
        for (kind, axis, _), xs, out in zip(tasks, ins, results):
            sems = (rest.pop(0), rest.pop(0))
            n, mine, x = sizes[axis], me[axis], xs[0]
            if kind == "line_gather":
                out[mine] = x[...]
                stages += line_gather_stages(out, sems, axis, n, mine, 0.0, 6.0)
            elif kind == "line_part":
                stages += line_part_stages(x, rest.pop(0), out, sems, axis, n, mine, 0.0, 6.0)
            elif kind == "part":
                held, came = rest.pop(0), rest.pop(0)
                stages += pair_part_stages(x, held, came, out, sems, axis, n, mine, 0.1, 1.0)
            elif kind in ("gather", "gather_mid"):
                if kind == "gather":
                    rows = x.shape[1]
                    if rows % 16 == 0:
                        own_of = lambda i, out=out, rows=rows: out.at[
                            pl.ds(pl.multiple_of(i * rows, 16), rows), :
                        ]
                    else:
                        own_of = lambda i, out=out: out.at[i]
                    own, col = own_of(mine), 0
                    for piece in xs:
                        for t in range(piece.shape[0]):
                            own[:, col : col + piece.shape[2]] = piece[t].astype(BF)
                            col += piece.shape[2]
                else:
                    rows = x.shape[1]
                    if rows % 16 == 0:
                        own_of = lambda i, out=out, rows=rows: out.at[
                            :, pl.ds(pl.multiple_of(i * rows, 16), rows), :
                        ]
                    else:
                        own_of = lambda i, out=out: out.at[i]
                    own_of(mine)[...] = x[...]
                if axis == "dp":
                    stages += pair_gather_stages(own_of, sems, axis, n, mine, 0.2, 6.0 * lax.axis_size("mp") - 11.5)
                else:

                    def start(own_of=own_of, sems=sems, axis=axis, n=n, mine=mine):
                        for d in range(1, n):
                            peer = lax.rem(mine + d, n)
                            remote(own_of(mine), own_of(mine), sems, d, axis, peer).start()

                    def finish(own_of=own_of, sems=sems, axis=axis, n=n, mine=mine):
                        for d in range(1, n):
                            remote(own_of(mine), own_of(mine), sems, d, axis, mine).wait()

                    stages += [(0.15, start), (90.0, finish)]
            elif kind == "total":
                held = rest.pop(0)
                held[mine] = x[...]

                def done(held=held, out=out, n=n):
                    total = held[0].astype(F32)
                    for p in range(1, n):
                        total = total + held[p].astype(F32)
                    out[...] = total

                stages += direct_stages(
                    lambda p, held=held, mine=mine: held.at[mine], held, sems, axis, n, mine, 0.3, done, 60.0
                )
            else:
                out[mine] = x[mine]
                stages += direct_stages(
                    lambda p, x=x: x.at[p], out, sems, axis, n, mine, 0.0, lambda: None, 60.0
                )
        for _, run in sorted(stages, key=lambda stage: stage[0]):
            run()

    vmem = pl.BlockSpec(memory_space=pltpu.VMEM)
    results = pl.pallas_call(
        kernel,
        out_shape=outs,
        in_specs=[vmem] * total_ins,
        out_specs=[vmem] * len(tasks),
        scratch_shapes=scratch,
        compiler_params=pltpu.CompilerParams(
            collective_id=number, has_side_effects=True, vmem_limit_bytes=24 << 20
        ),
        name=name,
    )(*[array for _, _, arrays in tasks for array in arrays])
    return [shaper(a) for shaper, a in zip(shapers, results)]


def by_chip(array):
    return array.reshape(lax.axis_size("dp") // 2, 2, -1, array.shape[-1])


def sum_char_grads(grads, gains, word_sums, block_rows):
    n, m = lax.axis_size("dp"), lax.axis_size("mp")
    grads = by_chip(grads)
    rows, cols = grads.shape[2:]
    slim = cols // m
    small = jax.ShapeDtypeStruct((8, D), F32)

    def kernel(x, gain_char, gain_one, gain_two, *refs):
        words = refs[: len(word_sums)]
        (out, small_out, held, came, total_dp, cut, cut_held, merged, small_dp, small_mp, *sems) = refs[len(word_sums) :]
        pairs = [tuple(sems[2 * t : 2 * t + 2]) for t in range(6)]
        i, j = lax.axis_index("dp"), lax.axis_index("mp")
        greet({"dp": n, "mp": m}, {"dp": i, "mp": j})
        part = [
            run for _, run in pair_part_stages(x, held, came, total_dp, pairs[0], "dp", n, i, 0.0, 0.0)
        ]
        part[0]()
        squares = jnp.zeros((1, 1), F32)
        for t, word in enumerate(words):
            if t == 1:
                wide = word[pl.ds(pl.multiple_of(j * block_rows, 16), block_rows), :].astype(F32)
            else:
                wide = word[...].astype(F32)
            squares = squares + jnp.sum(jnp.sum(wide * wide, axis=0, keepdims=True), axis=1, keepdims=True)
        row = lax.broadcasted_iota(jnp.int32, (8, D), 0)
        small_dp[i] = jnp.where(row == 3, squares * (1.0 / n), 0.0)
        small_dp[i, 0:1, : gain_char.shape[1]] = gain_char[...]
        small_dp[i, 1:2, :] = gain_one[...]
        small_dp[i, 2:3, :] = gain_two[...]
        part[1]()

        def small_done():
            total = small_dp[0]
            for p in range(1, n):
                total = total + small_dp[p]
            small_mp[j] = total

        def small_end():
            total = small_mp[0]
            for p in range(1, m):
                total = total + small_mp[p]
            small_out[...] = total

        def cut_done():
            total = cut_held[0].astype(F32)
            for p in range(1, m):
                total = total + cut_held[p].astype(F32)
            merged[j] = total.astype(BF)

        one = direct_stages(lambda p: small_dp.at[i], small_dp, pairs[1], "dp", n, i, 0, small_done, 0)
        two = direct_stages(lambda p: small_mp.at[j], small_mp, pairs[2], "mp", m, j, 0, small_end, 0)
        three = direct_stages(lambda p: cut.at[p], cut_held, pairs[3], "mp", m, j, 0, cut_done, 0)
        four = direct_stages(lambda p: merged.at[j], merged, pairs[4], "mp", m, j, 0, lambda: None, 0)
        one[0][1]()
        part[2]()
        for p in range(m):
            cut[p] = total_dp[:, p * slim : (p + 1) * slim]
        cut_held[j] = cut[j]
        three[0][1]()
        one[1][1]()
        two[0][1]()
        three[1][1]()
        four[0][1]()
        two[1][1]()
        four[1][1]()
        if rows % 16 == 0:
            own_of = lambda d: out.at[pl.ds(pl.multiple_of(d * rows, 16), rows), :]
        else:
            own_of = lambda d: out.at[d]
        own = own_of(i)
        for p in range(m):
            own[:, p * slim : (p + 1) * slim] = merged[p]
        for _, run in pair_gather_stages(own_of, pairs[5], "dp", n, i, 0, 0):
            run()

    vmem = pl.BlockSpec(memory_space=pltpu.VMEM)
    sums, smalls = pl.pallas_call(
        kernel,
        out_shape=[
            jax.ShapeDtypeStruct((n * rows, cols) if rows % 16 == 0 else (n, rows, cols), BF),
            jax.ShapeDtypeStruct(small.shape, F32),
        ],
        in_specs=[vmem] * (4 + len(word_sums)),
        out_specs=[vmem] * 2,
        scratch_shapes=[
            pltpu.VMEM((n // 2, rows, cols), BF),
            pltpu.VMEM((n // 2, rows, cols), BF),
            pltpu.VMEM((rows, cols), BF),
            pltpu.VMEM((m, rows, slim), BF),
            pltpu.VMEM((m, rows, slim), BF),
            pltpu.VMEM((m, rows, slim), BF),
            pltpu.VMEM((n,) + small.shape, F32),
            pltpu.VMEM((m,) + small.shape, F32),
        ]
        + [pltpu.SemaphoreType.DMA((2 * max(n, m),))] * 12,
        compiler_params=pltpu.CompilerParams(
            collective_id=20, has_side_effects=True, vmem_limit_bytes=24 << 20
        ),
        name="sum_char_grads",
    )(grads, *gains, *word_sums)
    return sums.reshape(n * rows, cols), smalls


ROWS = 256


def rms_scale(values):
    return lax.rsqrt(jnp.mean(values * values, axis=-1, keepdims=True) + epsilon)


def norm_back(values, scale, gain_row, grad):
    weighted = grad * gain_row
    inner = jnp.mean(values * weighted, axis=-1, keepdims=True)
    return scale * weighted - values * (scale * scale * scale) * inner


def word_forward_kernel(
    width, vec_ref, place_ref, words_ref, doc_all_ref, doc_row_ref, gain_ref, project_ref,
    stream_ref, normed_ref, qkv_ref, probs_ref, mixed_ref, keys, values, doc_ref
):
    step = pl.program_id(0)
    parts, kept_rows = vec_ref.shape[:2]
    words = kept_rows // OWNER_BLOCKS

    @pl.when(step == 0)
    def _():
        doc_ref[...] = tn(doc_all_ref[...].astype(F32).astype(BF), jnp.ones((1, 128), BF))

    numbers = lax.broadcasted_iota(jnp.int32, (ROWS, parts * words), 0) + step * ROWS
    placed = jnp.zeros((ROWS, D), F32)
    for k in range(0, OWNER_BLOCKS, 2):
        pair = range(k, min(k + 2, OWNER_BLOCKS))
        hits = [(numbers == place_ref[b : b + 1, :]).astype(BF) for b in pair]
        vectors = [vec_ref[p, b * words : (b + 1) * words, :] for b in pair for p in range(parts)]
        placed = placed + nn(jnp.concatenate(hits, axis=1), jnp.concatenate(vectors, axis=0))
    stream = words_ref[...].astype(F32) + placed
    stream_ref[...] = stream
    normed = (stream * rms_scale(stream) * gain_ref[...]).astype(BF)
    normed_ref[...] = normed
    qkv = nn(normed, project_ref[...]).astype(BF)
    qkv_ref[...] = qkv
    first = pl.ds(pl.multiple_of(step * ROWS, ROWS), ROWS)
    keys[first, :] = qkv[:, width : 2 * width]
    values[first, :] = qkv[:, 2 * width :]
    queries = (qkv[:, :width].astype(F32) * (1.0 / math.sqrt(HD))).astype(BF)

    def attend(number):
        count = (number + 1) * ROWS
        same = jnp.concatenate([doc_ref[:count, :]] * (ROWS // 128), axis=1) == doc_row_ref[...].astype(F32)
        key_at = lax.broadcasted_iota(jnp.int32, (count, ROWS), 0)
        query_at = lax.broadcasted_iota(jnp.int32, (count, ROWS), 1) + number * ROWS
        allowed = same & (key_at <= query_at)
        parts = []
        for head in range(width // HD):
            at = slice(head * HD, (head + 1) * HD)
            scores = jnp.where(allowed, nt(keys[:count, at], queries[:, at]), negative_big)
            raised = jnp.exp(scores - jnp.max(scores, axis=0, keepdims=True))
            probs = (raised * (1.0 / jnp.sum(raised, axis=0, keepdims=True))).astype(BF)
            probs_ref[head, :count, :] = probs
            parts.append(tn(values[:count, at], probs).T)
        mixed_ref[...] = jnp.concatenate(parts, axis=1).astype(BF)

    for number in range(doc_all_ref.shape[1] // ROWS):
        pl.when(step == number)(functools.partial(attend, number))


def word_forward(vectors, places, words, documents, gain, project):
    length = words.shape[0]
    width = project.shape[1] // 3
    heads = width // HD
    rows = lambda cols: pl.BlockSpec((ROWS, cols), lambda i: (i, 0))
    full = lambda shape: pl.BlockSpec(shape, lambda i: (0,) * len(shape))
    return pl.pallas_call(
        functools.partial(word_forward_kernel, width),
        grid=(length // ROWS,),
        in_specs=[
            full(vectors.shape),
            full(places.shape),
            rows(D),
            full((1, length)),
            pl.BlockSpec((1, ROWS), lambda i: (0, i)),
            full((1, D)),
            full(project.shape),
        ],
        out_specs=[
            rows(D),
            rows(D),
            rows(3 * width),
            pl.BlockSpec((heads, length, ROWS), lambda i: (0, 0, i)),
            rows(width),
        ],
        out_shape=[
            jax.ShapeDtypeStruct((length, D), F32),
            jax.ShapeDtypeStruct((length, D), BF),
            jax.ShapeDtypeStruct((length, 3 * width), BF),
            jax.ShapeDtypeStruct((heads, length, length), BF),
            jax.ShapeDtypeStruct((length, width), BF),
        ],
        scratch_shapes=[
            pltpu.VMEM((length, width), BF),
            pltpu.VMEM((length, width), BF),
            pltpu.VMEM((length, 128), F32),
        ],
        compiler_params=pltpu.CompilerParams(vmem_limit_bytes=32 << 20),
        name="word_forward",
    )(
        vectors,
        places,
        words,
        documents.reshape(1, length),
        documents.reshape(1, length),
        gain.reshape(1, D),
        project,
    )


def feed_kernel(
    mixed_ref, output_ref, stream_ref, cot_ref, gain_ref, upper_ref, lower_ref,
    hidden_ref, feed_ref, part_ref, grad_upper_ref, grad_lower_ref, upper_sum, lower_sum
):
    step = pl.program_id(0)

    @pl.when(step == 0)
    def _():
        upper_sum[...] = jnp.zeros_like(upper_sum)
        lower_sum[...] = jnp.zeros_like(lower_sum)

    parts, _, width = mixed_ref.shape
    hidden = stream_ref[...]
    for j in range(parts):
        hidden = hidden + nn(mixed_ref[j], output_ref[j * width : (j + 1) * width, :])
    hidden_ref[...] = hidden
    normed = (hidden * rms_scale(hidden) * gain_ref[...]).astype(BF)
    raised = nn(normed, upper_ref[...])
    constant = math.sqrt(2.0 / math.pi)
    square = raised * raised
    curve = jnp.tanh(constant * raised * (1.0 + 0.044715 * square))
    half = 0.5 * (1.0 + curve)
    active = (raised * half).astype(BF)
    slope = half + 0.5 * raised * (1.0 - curve * curve) * constant * (1.0 + 3.0 * 0.044715 * square)
    feed_ref[...] = nn(active, lower_ref[...]).astype(BF)
    grad_feed = cot_ref[...]
    grad_raised = (nt(grad_feed, lower_ref[...]) * slope).astype(BF)
    part_ref[...] = nt(grad_raised, upper_ref[...]).astype(BF)
    lower_sum[...] += tn(active, grad_feed)
    upper_sum[...] += tn(normed, grad_raised)

    @pl.when(step == pl.num_programs(0) - 1)
    def _():
        grad_upper_ref[...] = upper_sum[...].astype(BF)
        grad_lower_ref[...] = lower_sum[...].astype(BF)


def feed(mixed, output, stream, cotangent, gain, upper, lower):
    length = stream.shape[0]
    rows = pl.BlockSpec((ROWS, D), lambda i: (i, 0))
    full = lambda shape: pl.BlockSpec(shape, lambda i: (0,) * len(shape))
    return pl.pallas_call(
        feed_kernel,
        grid=(length // ROWS,),
        in_specs=[
            pl.BlockSpec((mixed.shape[0], ROWS, mixed.shape[2]), lambda i: (0, i, 0)),
            full(output.shape),
            rows,
            rows,
            full((1, D)),
            full(upper.shape),
            full(lower.shape),
        ],
        out_specs=[rows, rows, rows, full(upper.shape), full(lower.shape)],
        out_shape=[
            jax.ShapeDtypeStruct((length, D), F32),
            jax.ShapeDtypeStruct((length, D), BF),
            jax.ShapeDtypeStruct((length, D), BF),
            jax.ShapeDtypeStruct(upper.shape, BF),
            jax.ShapeDtypeStruct(lower.shape, BF),
        ],
        scratch_shapes=[pltpu.VMEM(upper.shape, F32), pltpu.VMEM(lower.shape, F32)],
        compiler_params=pltpu.CompilerParams(vmem_limit_bytes=32 << 20),
        name="feed",
    )(mixed, output, stream, cotangent, gain.reshape(1, D), upper, lower)


def hidden_back_kernel(
    own, grad_ref, hidden_ref, cot_ref, mixed_ref, output_ref, gain_ref,
    grad_hidden_ref, grad_mixed_ref, grad_output_ref, gain_grad_ref
):
    hidden = hidden_ref[...]
    scale = rms_scale(hidden)
    grad = grad_ref[...]
    grad_hidden = cot_ref[...].astype(F32) + norm_back(hidden, scale, gain_ref[...], grad)
    grad_hidden_ref[...] = grad_hidden
    gain_grad_ref[...] = jnp.sum(hidden * scale * grad, axis=0, keepdims=True)
    attend = grad_hidden.astype(BF)
    parts, _, width = mixed_ref.shape
    for j in range(parts):
        at = slice(j * width, (j + 1) * width)
        grad_mixed_ref[j] = nt(attend, output_ref[at, :]).astype(BF)
        grad_output_ref[at, :] = tn(mixed_ref[j], attend).astype(BF)


def hidden_back(own, grad, hidden, cotangent, mixed, output, gain):
    share = grad.shape[0]
    parts, _, width = mixed.shape
    mine = pl.BlockSpec((share, D), lambda i, own: (own[0], 0))
    full = lambda shape: pl.BlockSpec(shape, lambda i, own: (0,) * len(shape))
    return pl.pallas_call(
        hidden_back_kernel,
        grid_spec=pltpu.PrefetchScalarGridSpec(
            num_scalar_prefetch=1,
            grid=(1,),
            in_specs=[
                full((share, D)),
                mine,
                mine,
                pl.BlockSpec((parts, share, width), lambda i, own: (0, own[0], 0)),
                full(output.shape),
                full((1, D)),
            ],
            out_specs=[
                full((share, D)),
                full((parts, share, width)),
                full(output.shape),
                full((1, D)),
            ],
        ),
        out_shape=[
            jax.ShapeDtypeStruct((share, D), F32),
            jax.ShapeDtypeStruct((parts, share, width), BF),
            jax.ShapeDtypeStruct(output.shape, BF),
            jax.ShapeDtypeStruct((1, D), F32),
        ],
        compiler_params=pltpu.CompilerParams(vmem_limit_bytes=32 << 20),
        name="hidden_back",
    )(own, grad, hidden, cotangent, mixed, output, gain.reshape(1, D))


def word_backward_kernel(
    width, probs_ref, qkv_ref, all_ref, grad_ref, normed_ref, project_ref,
    part_ref, grad_project_ref, grads, key_sum, value_sum
):
    step = pl.program_id(0)
    steps = all_ref.shape[0] // ROWS
    first = pl.ds(pl.multiple_of(step * ROWS, ROWS), ROWS)
    eighth = 1.0 / math.sqrt(HD)
    queries = (qkv_ref[:, :width].astype(F32) * eighth).astype(BF)

    @pl.when(step == 0)
    def _():
        key_sum[...] = jnp.zeros_like(key_sum)
        value_sum[...] = jnp.zeros_like(value_sum)

    def attend(number):
        count = (number + 1) * ROWS
        parts = []
        for head in range(width // HD):
            at = slice(head * HD, (head + 1) * HD)
            keys = all_ref[:count, width + head * HD : width + (head + 1) * HD]
            values = all_ref[:count, 2 * width + head * HD : 2 * width + (head + 1) * HD]
            grad = grad_ref[:, at]
            probs = probs_ref[head, :count, :]
            wide = probs.astype(F32)
            product = wide * nt(values, grad)
            scores = (product - wide * jnp.sum(product, axis=0, keepdims=True)).astype(BF)
            key_sum[head, :count, :] += nn(scores, queries[:, at])
            value_sum[head, :count, :] += nn(probs, grad)
            parts.append(tn(keys, scores).T * eighth)
        grads[first, :width] = jnp.concatenate(parts, axis=1).astype(BF)

    for number in range(steps):
        pl.when(step == number)(functools.partial(attend, number))

    @pl.when(step == steps - 1)
    def _():
        for head in range(width // HD):
            grads[:, width + head * HD : width + (head + 1) * HD] = key_sum[head].astype(BF)
            grads[:, 2 * width + head * HD : 2 * width + (head + 1) * HD] = value_sum[head].astype(BF)
        grad_project_ref[...] = tn(normed_ref[...], grads[...]).astype(BF)
        part_ref[...] = nt(grads[...], project_ref[...]).astype(BF)


def word_backward(probs, qkv, grad_mixed, normed, project):
    length = qkv.shape[0]
    width = project.shape[1] // 3
    heads = width // HD
    rows = lambda cols: pl.BlockSpec((ROWS, cols), lambda i: (i, 0))
    full = lambda shape: pl.BlockSpec(shape, lambda i: (0,) * len(shape))
    return pl.pallas_call(
        functools.partial(word_backward_kernel, width),
        grid=(length // ROWS,),
        in_specs=[
            pl.BlockSpec((heads, length, ROWS), lambda i: (0, 0, i)),
            rows(3 * width),
            full(qkv.shape),
            rows(width),
            full(normed.shape),
            full(project.shape),
        ],
        out_specs=[full((length, D)), full(project.shape)],
        out_shape=[
            jax.ShapeDtypeStruct((length, D), BF),
            jax.ShapeDtypeStruct(project.shape, BF),
        ],
        scratch_shapes=[
            pltpu.VMEM(qkv.shape, BF),
            pltpu.VMEM((heads, length, HD), F32),
            pltpu.VMEM((heads, length, HD), F32),
        ],
        compiler_params=pltpu.CompilerParams(vmem_limit_bytes=32 << 20),
        name="word_backward",
    )(probs, qkv, qkv, grad_mixed, normed, project)


def stream_back_kernel(own, grad_ref, stream_ref, hidden_grad_ref, gain_ref, out_ref, gain_grad_ref):
    stream = stream_ref[...]
    scale = rms_scale(stream)
    grad = grad_ref[...]
    total = hidden_grad_ref[...] + norm_back(stream, scale, gain_ref[...], grad)
    out_ref[...] = total.astype(BF)
    gain_grad_ref[...] = jnp.sum(stream * scale * grad, axis=0, keepdims=True)


def stream_back(own, grad, stream, hidden_grad, gain):
    share = grad.shape[0]
    full = lambda shape: pl.BlockSpec(shape, lambda i, own: (0,) * len(shape))
    return pl.pallas_call(
        stream_back_kernel,
        grid_spec=pltpu.PrefetchScalarGridSpec(
            num_scalar_prefetch=1,
            grid=(1,),
            in_specs=[
                full((share, D)),
                pl.BlockSpec((share, D), lambda i, own: (own[0], 0)),
                full((share, D)),
                full((1, D)),
            ],
            out_specs=[full((share, D)), full((1, D))],
        ),
        out_shape=[
            jax.ShapeDtypeStruct((share, D), BF),
            jax.ShapeDtypeStruct((1, D), F32),
        ],
        name="stream_back",
    )(own, grad, stream, hidden_grad, gain.reshape(1, D))


def shampoo_kernel(
    threshold, position, char_ref, small_ref, gain_ref, gains_ref, project, output, upper, lower, hidden_in, feed_in, *refs
):
    given_in, refs = refs[:30], refs[30:]
    norm_ref, gain_grad_ref, gains_grad_ref, gain_new_ref, gains_new_ref, block_out = refs[:6]
    made_out, refs = refs[6:36], refs[36:]
    given, made = refs[:30], refs[30:60]
    hidden, feed_sum, total, in_sems, out_sems = refs[60:]
    loads = [pltpu.make_async_copy(a, b, in_sems.at[t]) for t, (a, b) in enumerate(zip(given_in, given))]
    loads += [
        pltpu.make_async_copy(hidden_in, hidden, in_sems.at[30]),
        pltpu.make_async_copy(feed_in, feed_sum, in_sems.at[31]),
    ]
    order = (4, 5, 2, 3, 0, 1)
    for number in order:
        for t in range(5):
            loads[5 * number + t].start()
    loads[30].start()
    loads[31].start()
    saves = [pltpu.make_async_copy(a, b, out_sems.at[t]) for t, (a, b) in enumerate(zip(made, made_out))]
    saves.append(pltpu.make_async_copy(total, block_out, out_sems.at[30]))
    me = position[0]
    char = char_ref[...].astype(F32)
    small = small_ref[...]
    lanes = lax.broadcasted_iota(jnp.int32, small.shape, 0)
    squares = (
        jnp.sum(jnp.sum(char * char, axis=0, keepdims=True), axis=1, keepdims=True)
        + jnp.sum(
            jnp.sum(jnp.where(lanes < 3, small * small, 0.0), axis=0, keepdims=True),
            axis=1,
            keepdims=True,
        )
        + small[3:4, :1]
    )
    norm = jnp.sqrt(squares)
    factor = jnp.minimum(1.0, threshold / norm)
    norm_ref[...] = norm
    gain_grad = small[0:1, :CW] * factor
    gain_grad_ref[...] = gain_grad
    gain_new_ref[...] = gain_ref[...] - gain_rate * gain_grad
    gains_grad = small[1:3, :] * factor
    gains_grad_ref[...] = gains_grad
    gains_new_ref[...] = gains_ref[...] - gain_rate * gains_grad
    width = project.shape[1] // 3
    own = pl.ds(pl.multiple_of(position[1] * width, 16), width)

    def whole_of(number, t):
        if number == 0:
            return char_ref[:, t * CW : (t + 1) * CW]
        if number == 1:
            return char_ref[:, 4 * CW :]
        if number == 2:
            return project[:, t * width : (t + 1) * width]
        return (output[own, :], upper[...], lower[...])[number - 3]

    def chosen(rows, cols):
        row = lax.broadcasted_iota(jnp.int32, (rows, cols), 0) + me * rows
        return (row == lax.broadcasted_iota(jnp.int32, (rows, cols), 1)).astype(BF)

    half = (1.0 - decay_rate) * factor * factor
    for number in order:
        for t in range(5):
            loads[5 * number + t].wait()
        master, left, right, left_root, right_root = given[5 * number : 5 * number + 5]
        grad_out, left_out, right_out, new_out, copy_out = made[5 * number : 5 * number + 5]
        for t in range(master.shape[0]):
            grad = whole_of(number, t)
            rows = nn(chosen(master.shape[1], grad.shape[0]), grad)
            grad_out[t] = rows * factor
            left_out[t] = decay_rate * left[t] + half * nt(rows.astype(BF), grad)
            cols = nt(grad, chosen(right.shape[1], grad.shape[1])).astype(BF)
            right_out[t] = decay_rate * right[t] + half * tn(cols, grad)
            turned = (nn(left_root[t].astype(BF), grad) * factor).astype(BF)
            root = right_root[:, t * grad.shape[1] : (t + 1) * grad.shape[1]]
            new = master[t] - learn_rate * nn(turned, root)
            new_out[t] = new
            copy_out[t] = new.astype(BF)
        for t in range(5):
            saves[5 * number + t].start()
    loads[30].wait()
    loads[31].wait()
    total[...] = (hidden[...] + feed_sum[...].astype(F32)).astype(BF)
    saves[30].start()
    for save in saves:
        save.wait()


def shampoo(threshold, position, char_sums, small, gain, gains, word_sums, hidden, feed_sum, given):
    flat = []
    shapes = []
    for master, left, right, left_root, right_root in given:
        flat += [master, left, right, left_root, right_root]
        shapes += [
            jax.ShapeDtypeStruct(a.shape, F32) for a in (master, left, right, master)
        ] + [jax.ShapeDtypeStruct(master.shape, BF)]
    first = [
        jax.ShapeDtypeStruct((1, 1), F32),
        jax.ShapeDtypeStruct((1, CW), F32),
        jax.ShapeDtypeStruct((2, D), F32),
        jax.ShapeDtypeStruct((1, CW), F32),
        jax.ShapeDtypeStruct((2, D), F32),
    ]
    vmem = pl.BlockSpec(memory_space=pltpu.VMEM)
    smem = pl.BlockSpec(memory_space=pltpu.SMEM)
    hbm = pl.BlockSpec(memory_space=pltpu.HBM)
    return pl.pallas_call(
        functools.partial(shampoo_kernel, threshold),
        in_specs=[smem] + [vmem] * 8 + [hbm] * 32,
        out_specs=[vmem] * 5 + [hbm] * 31,
        out_shape=first + [jax.ShapeDtypeStruct(feed_sum.shape, BF)] + shapes,
        scratch_shapes=[pltpu.VMEM(a.shape, a.dtype) for a in flat]
        + [pltpu.VMEM(a.shape, a.dtype) for a in shapes]
        + [
            pltpu.VMEM(hidden.shape, F32),
            pltpu.VMEM(feed_sum.shape, BF),
            pltpu.VMEM(feed_sum.shape, BF),
            pltpu.SemaphoreType.DMA((32,)),
            pltpu.SemaphoreType.DMA((31,)),
        ],
        compiler_params=pltpu.CompilerParams(vmem_limit_bytes=60 << 20),
        name="shampoo",
    )(position, char_sums, small, gain.reshape(1, CW), gains, *word_sums, hidden, feed_sum, *flat)


def run_stages(stages):
    for _, run in sorted(stages, key=lambda stage: stage[0]):
        run()


def spread_blocks(chosen, rows, cols, share):
    up = lax.broadcasted_iota(jnp.int32, (rows, chosen.shape[0]), 0) // share
    up = (up == lax.broadcasted_iota(jnp.int32, (rows, chosen.shape[0]), 1)).astype(BF)
    down = lax.broadcasted_iota(jnp.int32, (chosen.shape[1], cols), 1) // share
    down = (down == lax.broadcasted_iota(jnp.int32, (chosen.shape[1], cols), 0)).astype(BF)
    wide = nn(nn(up, chosen).astype(BF), down)
    row = lax.broadcasted_iota(jnp.int32, (rows, cols), 0) % share
    col = lax.broadcasted_iota(jnp.int32, (rows, cols), 1) % share
    return jnp.where(row == col, wide, 0.0).astype(BF)


def gather_setup(xs, out):
    rows = xs[0].shape[1]

    def own_of(i):
        if rows % 16 == 0:
            return out.at[pl.ds(pl.multiple_of(i * rows, 16), rows), :]
        return out.at[i]

    def put(mine):
        own, col = own_of(mine), 0
        for piece in xs:
            for t in range(piece.shape[0]):
                own[:, col : col + piece.shape[2]] = piece[t].astype(BF)
                col += piece.shape[2]

    return own_of, put


def gather_shape(arrays, n):
    rows = arrays[0].shape[1]
    cols = sum(a.shape[0] * a.shape[2] for a in arrays)
    shape = (n * rows, cols) if rows % 16 == 0 else (n, rows, cols)
    return jax.ShapeDtypeStruct(shape, BF), lambda a: a.reshape(n * rows, cols)


def dma_sems(count):
    return [pltpu.SemaphoreType.DMA((count,))] * 2


def call_remote(kernel, name, number, outs, scratch, inputs):
    vmem = pl.BlockSpec(memory_space=pltpu.VMEM)
    return pl.pallas_call(
        kernel,
        out_shape=outs,
        in_specs=[vmem] * len(inputs),
        out_specs=[vmem] * len(outs),
        scratch_shapes=scratch,
        compiler_params=pltpu.CompilerParams(
            collective_id=number, has_side_effects=True, vmem_limit_bytes=28 << 20
        ),
        name=name,
    )(*inputs)


def gather_char(mixer, lift, output, home, places):
    n, m = lax.axis_size("dp"), lax.axis_size("mp")
    slots, block_words = places.shape
    cap = -(-slots // n)
    total = n * cap
    share = block_words // m
    shape, shaper = gather_shape([mixer, lift], n)
    rows = output.shape[1]

    def kernel(
        mixer_in, lift_in, output_in, home_row, place_ref,
        mats, line, to_slot, live, live_place, own_row, mixer_ref, lift_ref, output_ref, sent, came, local, *sems
    ):
        pairs = [tuple(sems[2 * t : 2 * t + 2]) for t in range(3)]
        i, j = lax.axis_index("dp"), lax.axis_index("mp")
        loads = [
            pltpu.make_async_copy(a, b, local.at[t])
            for t, (a, b) in enumerate(
                ((mixer_in, mixer_ref), (lift_in, lift_ref), (output_in, output_ref))
            )
        ]
        for load in loads:
            load.start()
        own_of, put = gather_setup([mixer_ref, lift_ref], mats)
        greet({"dp": n, "mp": m}, {"dp": i, "mp": j})
        for load in loads:
            load.wait()
        put(i)
        line[j] = output_ref[0].astype(BF)
        stages = pair_gather_stages(own_of, pairs[0], "dp", n, i, 0.0, 2.0)

        def send_places():
            before = lax.broadcasted_iota(jnp.int32, (slots, slots), 0)
            before = before < lax.broadcasted_iota(jnp.int32, (slots, slots), 1)
            home_col = tn(home_row[...].astype(F32).astype(BF), jnp.ones((1, 128), BF))[:, :slots]
            same = (home_col == home_row[...].astype(F32)) & before
            rank = jnp.sum(same.astype(F32), axis=0, keepdims=True)
            target = jnp.where(
                home_row[...] >= 0, home_row[...].astype(F32) * cap + rank, float(total)
            )
            hit = lax.broadcasted_iota(jnp.int32, (total, slots), 0).astype(F32) == target
            chosen = hit.astype(F32)
            to_slot[...] = chosen.astype(BF)
            placed = jnp.zeros((total, block_words), F32) - 1.0
            for s in range(slots):
                placed = jnp.where(
                    chosen[:, s : s + 1] > 0.0, place_ref[s : s + 1, :].astype(F32), placed
                )
            for p in range(n):
                sent[p] = placed[p * cap : (p + 1) * cap, :].astype(jnp.int32)
            came[i] = sent[i]

        def use_places():
            placed = jnp.concatenate([came[p] for p in range(n)], axis=0).astype(F32)
            held = jnp.max(placed, axis=1, keepdims=True) >= 0.0
            filled = jnp.where(held, jnp.ones((total, 128), F32), 0.0)
            lower = lax.broadcasted_iota(jnp.int32, (total, total), 1)
            lower = (lower < lax.broadcasted_iota(jnp.int32, (total, total), 0)).astype(BF)
            rank = nn(lower, filled.astype(BF))
            lane = lax.broadcasted_iota(jnp.int32, (total, 128), 1).astype(F32)
            chosen = jnp.where((rank == lane) & (filled > 0.0), 1.0, 0.0).astype(BF)
            live[...] = chosen
            high = jnp.floor((placed + 1.0) * (1.0 / 32.0))
            low = placed + 1.0 - high * 32.0
            high, low = high.astype(BF), low.astype(BF)
            found = tn(chosen, high) * 32.0 + tn(chosen, low) - 1.0
            live_place[...] = found[: live_place.shape[0], :].astype(jnp.int32)
            block = cap * share
            for p in range(n):
                col = lax.broadcasted_iota(jnp.int32, (block_words, block), 1) % share + j * share
                pick = (col == lax.broadcasted_iota(jnp.int32, (block_words, block), 0)).astype(BF)
                row = lax.broadcasted_iota(jnp.int32, (total, block), 0) - p * cap
                mine = row == lax.broadcasted_iota(jnp.int32, (total, block), 1) // share
                value = nn(high, pick) * 32.0 + nn(low, pick) - 1.0
                own_row[p] = jnp.sum(jnp.where(mine, value, 0.0), axis=0, keepdims=True).astype(jnp.int32)

        stages.append((0.1, send_places))
        stages += direct_stages(lambda p: sent.at[p], came, pairs[1], "dp", n, i, 0.2, lambda: None, 1.0)
        stages += direct_stages(lambda p: line.at[j], line, pairs[2], "mp", m, j, 0.3, lambda: None, 50.0)
        stages.append((1.5, use_places))
        run_stages(stages)

    vmem = pl.BlockSpec(memory_space=pltpu.VMEM)
    hbm = pl.BlockSpec(memory_space=pltpu.HBM)
    lines = max(16, -(-OWNER_BLOCKS // 8) * 8)
    results = pl.pallas_call(
        kernel,
        out_shape=[
            shape,
            jax.ShapeDtypeStruct((m, rows, D), BF),
            jax.ShapeDtypeStruct((total, slots), BF),
            jax.ShapeDtypeStruct((total, 128), BF),
            jax.ShapeDtypeStruct((lines, block_words), jnp.int32),
            jax.ShapeDtypeStruct((n, 1, cap * share), jnp.int32),
        ],
        in_specs=[hbm] * 3 + [vmem] * 2,
        out_specs=[vmem] * 6,
        scratch_shapes=[
            pltpu.VMEM(mixer.shape, F32),
            pltpu.VMEM(lift.shape, F32),
            pltpu.VMEM(output.shape, F32),
            pltpu.VMEM((n, cap, block_words), jnp.int32),
            pltpu.VMEM((n, cap, block_words), jnp.int32),
            pltpu.SemaphoreType.DMA((3,)),
        ]
        + dma_sems(2 * max(n, m)) * 3,
        compiler_params=pltpu.CompilerParams(
            collective_id=0, has_side_effects=True, vmem_limit_bytes=60 << 20
        ),
        name="gather_char",
    )(mixer, lift, output, home.reshape(1, slots), places)
    return [shaper(results[0])] + list(results[1:])


def send_vectors(vectors, to_slot, to_live, share, project, upper, lower, output_line):
    n, m = lax.axis_size("dp"), lax.axis_size("mp")
    total = to_slot.shape[0] * share
    block = total // n
    kept = OWNER_BLOCKS * share
    made = [gather_shape([a], n) for a in (project, upper, lower)]
    made[0] = gather_shape([project], n)
    lead, line_rows, line_cols = output_line.shape
    aligned = line_rows % 16 == 0
    output_shape = (lead, n * line_rows, line_cols) if aligned else (n, lead, line_rows, line_cols)

    def kernel(vec, slots, live, *refs):
        weights, line = refs[:3], refs[3]
        out, wides, output = refs[4], refs[5:8], refs[8]
        sent, came, *sems = refs[9:]
        pairs = [tuple(sems[2 * t : 2 * t + 2]) for t in range(8)]
        i, j = lax.axis_index("dp"), lax.axis_index("mp")
        sent[...] = (
            nn(spread_blocks(slots[...], total, vec.shape[0], share), vec[...])
            .astype(BF)
            .reshape(sent.shape)
        )
        greet({"dp": n, "mp": m}, {"dp": i, "mp": j})
        came[i] = sent[i]
        stages = []

        def compact(cols):
            up = lax.broadcasted_iota(jnp.int32, (kept, 128), 0) // share
            up = (up == lax.broadcasted_iota(jnp.int32, (kept, 128), 1)).astype(BF)
            blocks = nt(up, live[...]).astype(BF)
            down = lax.broadcasted_iota(jnp.int32, (blocks.shape[1], total), 1) // share
            down = (down == lax.broadcasted_iota(jnp.int32, (blocks.shape[1], total), 0)).astype(BF)
            row = lax.broadcasted_iota(jnp.int32, (kept, total), 0) % share
            col = lax.broadcasted_iota(jnp.int32, (kept, total), 1) % share
            spread = jnp.where(row == col, nn(blocks, down), 0.0).astype(BF)
            out[j, :, cols] = nn(spread, came[:, :, cols].reshape(total, D // 2)).astype(BF)

        for half in range(2):
            cols = slice(half * (D // 2), (half + 1) * (D // 2))
            stages += direct_stages(
                lambda p, cols=cols: sent.at[p, :, cols], came, pairs[6 * half], "dp", n, i, 0.1 * half,
                functools.partial(compact, cols), 1.0 + half, cols,
            )
            begin = 1.5 + half * (m - 1.5)
            stages += line_gather_stages(out, pairs[1 + 6 * half], "mp", m, j, begin, 1.0, cols)
        for t, (x, wide) in enumerate(zip(weights, wides)):
            own_of, put = gather_setup([x], wide)
            put(i)
            stages += pair_gather_stages(own_of, pairs[2 + t], "dp", n, i, 0.3, 2.0 * m + 0.5)
        if aligned:
            output_of = lambda d: output.at[:, pl.ds(pl.multiple_of(d * line_rows, 16), line_rows), :]
        else:
            output_of = lambda d: output.at[d]
        output_of(i)[...] = line[...]
        stages += pair_gather_stages(output_of, pairs[5], "dp", n, i, 0.3, 2.0 * m + 0.5)
        run_stages(stages)

    results = call_remote(
        kernel,
        "send_vectors",
        1,
        [jax.ShapeDtypeStruct((m, kept, D), BF)]
        + [shape for shape, _ in made]
        + [jax.ShapeDtypeStruct(output_shape, BF)],
        [pltpu.VMEM((n, block, D), BF)] * 2 + dma_sems(2 * max(n, m)) * 8,
        [vectors, to_slot, to_live, project, upper, lower, output_line],
    )
    output = results[4]
    if not aligned:
        output = output.transpose(1, 0, 2, 3)
    return (
        [results[0]]
        + [shaper(a) for (_, shaper), a in zip(made, results[1:4])]
        + [output.reshape(-1, line_cols)]
    )


def hidden_grads(part_two, hidden, cotangent, mixed, output, gain, grad_upper, grad_lower, roots):
    n, m = lax.axis_size("dp"), lax.axis_size("mp")
    share = part_two.shape[1]
    width = mixed.shape[2]
    made = [gather_shape([a], n) for a in roots]
    parts = [by_chip(grad_upper), by_chip(grad_lower)]

    def kernel(part, hidden_ref, cot, mix, out_mat, gain_ref, up, low, *refs):
        roots_in, refs = refs[: len(roots)], refs[len(roots) :]
        grad_hidden, grad_mixed, grad_output, gain_grad, up_sum, low_sum = refs[:6]
        roots_out, refs = refs[6 : 6 + len(roots)], refs[6 + len(roots) :]
        held, total, swapped, up_held, up_came, low_held, low_came, *sems = refs
        pairs = [tuple(sems[2 * t : 2 * t + 2]) for t in range(4 + len(roots))]
        i, j = lax.axis_index("dp"), lax.axis_index("mp")
        greet({"dp": n, "mp": m}, {"dp": i, "mp": j})
        stages = line_part_stages(part, held, total, pairs[0], "mp", m, j, 0.0, 6.0)
        stages += pair_part_stages(up, up_held, up_came, up_sum, pairs[1], "dp", n, i, 0.1, 1.0)
        stages += pair_part_stages(low, low_held, low_came, low_sum, pairs[2], "dp", n, i, 0.1, 1.0)
        for t, (x, out) in enumerate(zip(roots_in, roots_out)):
            own_of, put = gather_setup([x], out)
            put(i)
            stages += pair_gather_stages(own_of, pairs[4 + t], "dp", n, i, 2.0, 72.5)

        def back():
            mine = pl.ds(pl.multiple_of(j * share, share), share)
            hidden_own = hidden_ref[mine, :]
            scale = rms_scale(hidden_own)
            grad = total[...]
            whole_grad = cot[mine, :].astype(F32) + norm_back(hidden_own, scale, gain_ref[...], grad)
            grad_hidden[...] = whole_grad
            gain_grad[...] = jnp.sum(hidden_own * scale * grad, axis=0, keepdims=True)
            attend = whole_grad.astype(BF)
            for p in range(m):
                swapped[p] = nt(attend, out_mat[p * width : (p + 1) * width, :]).astype(BF)
            grad_mixed[j] = swapped[j]

        def output_grad():
            mine = pl.ds(pl.multiple_of(j * share, share), share)
            attend = grad_hidden[...].astype(BF)
            for p in range(m):
                grad_output[p * width : (p + 1) * width, :] = tn(mix[p, mine, :], attend).astype(BF)

        stages += [(71.0, back), (73.0, output_grad)]
        stages += direct_stages(
            lambda p: swapped.at[p], grad_mixed, pairs[3], "mp", m, j, 72.0, lambda: None, 75.0
        )
        run_stages(stages)

    block = lambda a: pltpu.VMEM(a.shape[:1] + a.shape[2:], BF)
    results = call_remote(
        kernel,
        "hidden_grads",
        4,
        [
            jax.ShapeDtypeStruct((share, D), F32),
            jax.ShapeDtypeStruct((m, share, width), BF),
            jax.ShapeDtypeStruct(output.shape, BF),
            jax.ShapeDtypeStruct((1, D), F32),
            jax.ShapeDtypeStruct(parts[0].shape[2:], F32),
            jax.ShapeDtypeStruct(parts[1].shape[2:], F32),
        ]
        + [shape for shape, _ in made],
        [
            pltpu.VMEM((2, m, share, D), BF),
            pltpu.VMEM((share, D), F32),
            pltpu.VMEM((m, share, width), BF),
            block(parts[0]),
            block(parts[0]),
            block(parts[1]),
            block(parts[1]),
        ]
        + dma_sems(2 * max(n, m)) * (4 + len(roots)),
        [part_two, hidden, cotangent, mixed, output, gain.reshape(1, D)] + parts + roots,
    )
    return list(results[:6]) + [shaper(a) for (_, shaper), a in zip(made, results[6:])]


def stream_grads(part_one, stream, grad_hidden, gain, own_row, to_slot, sums, grad_project, grad_output, slots):
    n, m = lax.axis_size("dp"), lax.axis_size("mp")
    share = part_one.shape[1]
    block = own_row.shape[2]
    total_words = n * block
    words = share * m
    width = total_words // to_slot.shape[0]
    parts = [by_chip(grad_project), by_chip(grad_output)]
    chunk = lambda a: jax.ShapeDtypeStruct((1,) + a.shape[-2:], F32)
    made = [gather_shape([chunk(a)], n) for a in (sums[0], sums[1], parts[0], parts[1])]

    def kernel(part, stream_ref, hidden_ref, gain_ref, row_ref, slot_ref, up, low, project, output, *refs):
        out, gain_grad, vectors, up_out, low_out, project_out, output_out = refs[:7]
        (held, total, project_sum, output_sum, line_held, picked, came,
         p_held, p_came, o_held, o_came, *sems) = refs[7:]
        pairs = [tuple(sems[2 * t : 2 * t + 2]) for t in range(12)]
        i, j = lax.axis_index("dp"), lax.axis_index("mp")
        greet({"dp": n, "mp": m}, {"dp": i, "mp": j})
        stages = line_part_stages(part, held, total, pairs[0], "mp", m, j, 0.0, 6.0)
        stages += pair_part_stages(project, p_held, p_came, project_sum.at[0], pairs[1], "dp", n, i, 0.1, 1.0)
        stages += pair_part_stages(output, o_held, o_came, output_sum.at[0], pairs[2], "dp", n, i, 0.1, 1.0)
        up_of, put_up = gather_setup([up], up_out)
        low_of, put_low = gather_setup([low], low_out)
        put_up(i)
        put_low(i)
        stages += pair_gather_stages(up_of, pairs[3], "dp", n, i, 2.0, 71.9)
        stages += pair_gather_stages(low_of, pairs[4], "dp", n, i, 2.0, 71.9)

        def back():
            mine = pl.ds(pl.multiple_of(j * share, share), share)
            stream_own = stream_ref[mine, :]
            scale = rms_scale(stream_own)
            grad = total[...]
            out[j] = (hidden_ref[...] + norm_back(stream_own, scale, gain_ref[...], grad)).astype(BF)
            gain_grad[...] = jnp.sum(stream_own * scale * grad, axis=0, keepdims=True)

        stages.append((71.0, back))
        for half in range(2):
            cols = slice(half * (D // 2), (half + 1) * (D // 2))
            begin = 72.0 + 0.1 * half * (m - 1.5)
            stages += [
                (when if when < 90 else 199.0, run)
                for when, run in line_gather_stages(out, pairs[5 + 5 * half], "mp", m, j, begin, 0.1, cols)
            ]
        project_of, put_project = gather_setup([project_sum], project_out)
        output_of, put_output = gather_setup([output_sum], output_out)

        def put_sums():
            put_project(i)
            line_held[j] = output_sum[0].astype(BF)

        target = i // (n // m)

        def line_send():
            @pl.when(j != target)
            def _():
                remote(line_held.at[j], line_held.at[j], pairs[7], j, "mp", target).start()

        def line_done():
            @pl.when(j != target)
            def _():
                remote(line_held.at[j], line_held.at[j], pairs[7], j, "mp", target).wait_send()

            @pl.when(j == target)
            def _():
                for p in range(m):

                    @pl.when(j != p)
                    def _(p=p):
                        remote(line_held.at[p], line_held.at[p], pairs[7], p, "mp", target).wait_recv()

                summed = line_held[0].astype(F32)
                for p in range(1, m):
                    summed = summed + line_held[p].astype(F32)
                output_sum[0] = summed

            put_output(i)

        stages = [(60.0 if when == 80.0 else when, run) for when, run in stages]
        stages.append((72.01, put_sums))
        stages += [
            (when, run)
            for when, run in zip(
                (72.02, 72.25, 198.0),
                [run for _, run in pair_gather_stages(project_of, pairs[6], "dp", n, i, 0, 0)],
            )
        ]
        late_line = 72.0 + 0.1 * 2 * m
        stages += [(72.03, line_send), (late_line + 0.01, line_done)]
        stages += [
            (when, run)
            for when, run in zip(
                (late_line + 0.02, 81.5, 198.5),
                [run for _, run in pair_gather_stages(output_of, pairs[8], "dp", n, i, 0, 0)],
            )
        ]

        def pick(half):
            cols = slice(half * (D // 2), (half + 1) * (D // 2))
            rows = out[:, :, cols].reshape(words, D // 2)
            number = lax.broadcasted_iota(jnp.int32, (words, block), 0)
            for d in list(range(1, n)) + [0]:
                peer = lax.rem(i + d, n)
                picked[peer, :, cols] = tn((number == row_ref[peer]).astype(BF), rows).astype(BF)
                if d:
                    remote(
                        picked.at[peer, :, cols], came.at[i, :, cols], pairs[9 + 2 * half], d, "dp", peer
                    ).start()
            came[i, :, cols] = picked[i, :, cols]

        for half in range(2):
            begin = 72.0 + 0.1 * half * (m - 1.5)
            stages.append((begin + 0.1 * (m - 1) + 0.011, functools.partial(pick, half)))

        def place():
            for half in range(2):
                cols = slice(half * (D // 2), (half + 1) * (D // 2))
                for d in range(1, n):
                    remote(
                        picked.at[i, :, cols], came.at[i, :, cols], pairs[9 + 2 * half], d, "dp", i
                    ).wait()
            spread = spread_blocks(slot_ref[...], total_words, vectors.shape[0], width)
            vectors[...] = tn(spread, came[...].reshape(total_words, D)).astype(BF)

        stages.append((82.0, place))
        run_stages(stages)

    held_of = lambda a: pltpu.VMEM(a.shape[:1] + a.shape[2:], BF)
    results = call_remote(
        kernel,
        "stream_grads",
        6,
        [
            jax.ShapeDtypeStruct((m, share, D), BF),
            jax.ShapeDtypeStruct((1, D), F32),
            jax.ShapeDtypeStruct((slots * width, D), BF),
        ]
        + [shape for shape, _ in made],
        [
            pltpu.VMEM((2, m, share, D), BF),
            pltpu.VMEM((share, D), F32),
            pltpu.VMEM((1,) + parts[0].shape[2:], F32),
            pltpu.VMEM((1,) + parts[1].shape[2:], F32),
            pltpu.VMEM((m,) + parts[1].shape[2:], BF),
            pltpu.VMEM((n, block, D), BF),
            pltpu.VMEM((n, block, D), BF),
            held_of(parts[0]),
            held_of(parts[0]),
            held_of(parts[1]),
            held_of(parts[1]),
        ]
        + dma_sems(2 * max(n, m)) * 12,
        [
            part_one,
            stream,
            grad_hidden,
            gain.reshape(1, D),
            own_row,
            to_slot,
            sums[0][None],
            sums[1][None],
        ]
        + parts,
    )
    return list(results[:3]) + [shaper(a) for (_, shaper), a in zip(made, results[3:])]


def local(
    word_inputs,
    character_embeddings,
    cotangent,
    char_count,
    word_place,
    block_home,
    documents,
    char_gain,
    word_gains,
    char_mixer,
    char_mixer_left,
    char_mixer_right,
    char_mixer_left_root,
    char_mixer_right_root,
    char_lift,
    char_lift_left,
    char_lift_right,
    char_lift_left_root,
    char_lift_right_root,
    word_project,
    word_project_left,
    word_project_right,
    word_project_left_root,
    word_project_right_root,
    word_output,
    word_output_left,
    word_output_right,
    word_output_left_root,
    word_output_right_root,
    feed_upper,
    feed_upper_left,
    feed_upper_right,
    feed_upper_left_root,
    feed_upper_right_root,
    feed_lower,
    feed_lower_left,
    feed_lower_right,
    feed_lower_left_root,
    feed_lower_right_root,
):
    slot_count, share_rows = (character_embeddings.shape[0], character_embeddings.shape[1])
    peer_count = lax.axis_size("dp")
    part_count = lax.axis_size("mp")
    owner_index = lax.axis_index("dp")
    words_dev = word_inputs.shape[0] * word_inputs.shape[1]
    position = jnp.stack([owner_index, lax.axis_index("mp")]).astype(jnp.int32)

    char_whole, output_line, to_slot, live, live_place, own_row = gather_char(
        char_mixer, char_lift, word_output, block_home, word_place
    )
    word_vectors, kept, pooled, msum = char_forward(
        character_embeddings, block_home, char_count, char_gain, char_whole
    )
    live_vectors, project_mat, upper_mat, lower_mat, output_mat = send_vectors(
        word_vectors,
        to_slot,
        live,
        share_rows,
        word_project.reshape((3,) + word_project.shape[2:]),
        feed_upper,
        feed_lower,
        output_line,
    )
    stream, normed_one, qkv, probs, mixed = word_forward(
        live_vectors,
        live_place,
        word_inputs.reshape(words_dev, D),
        documents,
        word_gains[0],
        project_mat,
    )
    mixed_all, mixer_root, lift_root = exchange(
        "gather_mixed",
        3,
        [
            ("line_gather", "mp", [mixed]),
            ("gather", "dp", [char_mixer_right_root]),
            ("gather", "dp", [char_lift_right_root]),
        ],
    )
    flat_cotangent = cotangent.reshape(words_dev, D)
    hidden, feed_part, part_two, grad_upper, grad_lower = feed(
        mixed_all, output_mat, stream, flat_cotangent, word_gains[1], upper_mat, lower_mat
    )
    shares = (part_count, words_dev // part_count, D)
    grad_hidden, grad_mixed, grad_output_mat, gain_two, part_upper, part_lower, *word_roots = hidden_grads(
        part_two.reshape(shares),
        hidden,
        flat_cotangent,
        mixed_all,
        output_mat,
        word_gains[1],
        grad_upper,
        grad_lower,
        [
            word_project_right_root.reshape((3,) + word_project_right_root.shape[2:]),
            word_output_right_root,
            feed_upper_right_root,
            feed_lower_right_root,
        ],
    )
    project_root, output_root, upper_root, lower_root = word_roots
    part_one, grad_project = word_backward(
        probs, qkv, grad_mixed.reshape(words_dev, -1), normed_one, project_mat
    )
    grad_words, gain_one, grad_vectors, sum_upper, sum_lower, sum_project, sum_output = stream_grads(
        part_one.reshape(shares),
        stream,
        grad_hidden,
        word_gains[0],
        own_row,
        to_slot,
        (part_upper, part_lower),
        grad_project,
        grad_output_mat,
        slot_count,
    )
    word_inputs_gradient = grad_words.reshape(word_inputs.shape)
    grad_vectors, feed_part = lax.optimization_barrier((grad_vectors, feed_part))
    feed_total = lax.psum(feed_part, "mp")
    char_embeds_gradient, char_grads, grad_char_gain = char_backward(
        character_embeddings, block_home, char_count, char_gain, char_whole, kept, pooled, msum, grad_vectors
    )
    word_sums = (sum_project, sum_output, sum_upper, sum_lower)
    char_sums, small_sums = sum_char_grads(
        char_grads, (grad_char_gain, gain_one, gain_two), word_sums, word_output.shape[1] * peer_count
    )
    parameter_count = (
        sum(
            part_count * w.size * peer_count
            for w in (word_project, word_output, feed_upper, feed_lower)
        )
        + peer_count * (char_mixer.size + char_lift.size)
        + char_gain.size
        + word_gains.size
    )
    flat = lambda a: a.reshape((-1,) + a.shape[-2:])
    results = shampoo(
        0.5 * math.sqrt(parameter_count),
        position,
        char_sums,
        small_sums,
        char_gain,
        word_gains,
        word_sums,
        hidden,
        feed_total,
        [
            tuple(flat(a) for a in group[:4]) + (group[4],)
            for group in (
                (char_mixer, char_mixer_left, char_mixer_right, char_mixer_left_root, mixer_root),
                (char_lift, char_lift_left, char_lift_right, char_lift_left_root, lift_root),
                (word_project, word_project_left, word_project_right, word_project_left_root, project_root),
                (word_output, word_output_left, word_output_right, word_output_left_root, output_root),
                (feed_upper, feed_upper_left, feed_upper_right, feed_upper_left_root, upper_root),
                (feed_lower, feed_lower_left, feed_lower_right, feed_lower_left_root, lower_root),
            )
        ],
    )
    norm, gain_grad, gains_grad, gain_new, gains_new, block_out = results[:6]
    stepped = []
    for t, group in enumerate(
        (
            (char_mixer, char_mixer_left, char_mixer_right),
            (char_lift, char_lift_left, char_lift_right),
            (word_project, word_project_left, word_project_right),
            (word_output, word_output_left, word_output_right),
            (feed_upper, feed_upper_left, feed_upper_right),
            (feed_lower, feed_lower_left, feed_lower_right),
        )
    ):
        master, left, right = group
        stepped += [
            a.reshape(b.shape)
            for a, b in zip(results[6 + 5 * t : 11 + 5 * t], (master, left, right, master, master))
        ]
    return (
        block_out.reshape(word_inputs.shape),
        word_inputs_gradient,
        char_embeds_gradient,
        gain_grad[0],
        gains_grad,
        gain_new[0],
        gains_new,
        norm[0, 0],
        *stepped,
    )


def solution(mesh):
    placed = (
        P("dp", None, None),
        P("dp", "mp", None, None),
        P("dp", None, None),
        P("dp", "mp"),
        P("dp", None),
        P("dp"),
        P("dp", None),
        P(),
        P(),
        P(None, "dp", None),
        P(None, "dp", None),
        P(None, "dp", None),
        P(None, "dp", None),
        P(None, "dp", None),
        P(None, "dp", None),
        P(None, "dp", None),
        P(None, "dp", None),
        P(None, "dp", None),
        P(None, "dp", None),
        P(None, "mp", "dp", None),
        P(None, "mp", "dp", None),
        P(None, "mp", "dp", None),
        P(None, "mp", "dp", None),
        P(None, "mp", "dp", None),
        P("mp", "dp", None),
        P("mp", "dp", None),
        P("mp", "dp", None),
        P("mp", "dp", None),
        P("mp", "dp", None),
        P("mp", "dp", None),
        P("mp", "dp", None),
        P("mp", "dp", None),
        P("mp", "dp", None),
        P("mp", "dp", None),
        P("mp", "dp", None),
        P("mp", "dp", None),
        P("mp", "dp", None),
        P("mp", "dp", None),
        P("mp", "dp", None),
    )
    return jax.shard_map(
        local,
        mesh=mesh,
        in_specs=placed,
        out_specs=(
            P("dp", None, None),
            P("dp", None, None),
            P("dp", "mp", None, None),
            P(),
            P(),
            P(),
            P(),
            P(),
            P(None, "dp", None),
            P(None, "dp", None),
            P(None, "dp", None),
            P(None, "dp", None),
            P(None, "dp", None),
            P(None, "dp", None),
            P(None, "dp", None),
            P(None, "dp", None),
            P(None, "dp", None),
            P(None, "dp", None),
            P(None, "mp", "dp", None),
            P(None, "mp", "dp", None),
            P(None, "mp", "dp", None),
            P(None, "mp", "dp", None),
            P(None, "mp", "dp", None),
            P("mp", "dp", None),
            P("mp", "dp", None),
            P("mp", "dp", None),
            P("mp", "dp", None),
            P("mp", "dp", None),
            P("mp", "dp", None),
            P("mp", "dp", None),
            P("mp", "dp", None),
            P("mp", "dp", None),
            P("mp", "dp", None),
            P("mp", "dp", None),
            P("mp", "dp", None),
            P("mp", "dp", None),
            P("mp", "dp", None),
            P("mp", "dp", None),
        ),
        check_vma=False,
    )
```

```python
import functools
import math

import jax
import jax.numpy as jnp
from jax import lax
from jax.experimental import pallas as pl
from jax.experimental.pallas import tpu as pltpu
from jax.sharding import PartitionSpec as P

D = 512
HD = 64
FF = 2048
CHAR_BLOCK_WIDTH = 256
OWNER_BLOCKS = 10
decay_rate = 0.5
learn_rate = 1.0
gain_rate = 0.4
negative_big = -1e30

CW = 256
CHEADS = 4
CHD = 64
SPOTS = 16
KEPT = 3 * CW + CHEADS * 128 + CW
epsilon = 1e-05
BF = jnp.bfloat16
F32 = jnp.float32


def nn(a, b):
    return lax.dot_general(a, b, (((1,), (0,)), ((), ())), preferred_element_type=F32)


def nt(a, b):
    return lax.dot_general(a, b, (((1,), (1,)), ((), ())), preferred_element_type=F32)


def tn(a, b):
    return lax.dot_general(a, b, (((0,), (0,)), ((), ())), preferred_element_type=F32)


GROUPS = 4


def char_classes(share):
    listed = [(1, 4, 32), (2, 8, 16), (4, 16, 8)]
    return [(c, p, w, GROUPS // (share // w)) for c, p, w in listed if w <= share]


def order_matrix(places, words):
    row = lax.broadcasted_iota(jnp.int32, (128, SPOTS * words), 0)
    col = lax.broadcasted_iota(jnp.int32, (128, SPOTS * words), 1)
    return ((row % words) * SPOTS + row // words == col).astype(BF)


def back_matrix(places, words):
    row = lax.broadcasted_iota(jnp.int32, (SPOTS * words, 128), 0)
    col = lax.broadcasted_iota(jnp.int32, (SPOTS * words, 128), 1)
    return ((col % words) * SPOTS + col // words == row).astype(BF)


def head_stack(rows, scale):
    lane = lax.broadcasted_iota(jnp.int32, (1, CW), 1) // CHD
    return jnp.concatenate(
        [rows * jnp.where(lane == h, scale, 0.0).astype(BF) for h in range(CHEADS)], axis=0
    )


def char_forward_kernel(
    classes, home, first, x_in, counts_in, gain_ref, mats_ref, *refs
):
    orders, refs = refs[-len(classes) :], refs[: -len(classes)]
    vec_ref, kept_out, pooled_ref, msum_ref, kept, sumx, x_ref, vec, count_ref, kind, ids, batch_kind, target, taken, sems, x_sems = refs
    slots, share = count_ref.shape[:2]
    batches = plan_batches(classes, home, first, kind, ids, batch_kind)

    def load_x(slot):
        return pltpu.make_async_copy(x_in.at[slot], x_ref.at[slot], x_sems.at[slot])

    def begin(number, carry):
        for which, places, words, per in classes:

            @pl.when(batch_kind[number] == which)
            def _(per=per):
                for t in range(per):
                    slot = ids[number * GROUPS + t]

                    @pl.when(slot >= 0)
                    def _(slot=slot):
                        load_x(slot).start()

        return carry

    lax.fori_loop(0, batches, begin, 0)
    count_ref[...] = spread_counts(counts_in[...]).reshape(count_ref.shape)
    for (_, places, words, _), order_ref in zip(classes, orders):
        order_ref[...] = order_matrix(places, words)
    sumx[...] = jnp.zeros_like(sumx)
    msum_ref[...] = jnp.zeros_like(msum_ref)

    def save(slot, rows):
        return pltpu.make_async_copy(
            kept.at[slot, pl.ds(0, rows)], kept_out.at[slot, pl.ds(0, rows)], sems.at[slot]
        )

    def block(places, words, per, order_ref, number):
        picked = [ids[number * GROUPS + t] for t in range(per)]
        for slot in picked:

            @pl.when(slot >= 0)
            def _(slot=slot):
                load_x(slot).wait()

        chosen = [jnp.where(c < 0, picked[0], c) for c in picked]
        groups = [(c, g) for c in chosen for g in range(share // words)]
        cnts = [count_ref[c, pl.ds(g * words, words), :] for c, g in groups]
        xs = [
            nn(order_ref[...], x_ref[c, pl.ds(g * words * SPOTS, words * SPOTS), :]) for c, g in groups
        ]
        normed = jnp.concatenate(
            [
                (
                    x * lax.rsqrt(jnp.mean(x * x, axis=-1, keepdims=True) + epsilon) * gain_ref[...]
                ).astype(BF)
                for x in xs
            ],
            axis=0,
        )
        qkv = nn(normed, mats_ref[:, : 3 * CW]).astype(BF)
        place = lax.broadcasted_iota(jnp.int32, (places, words, CW), 0).astype(F32)
        lane = lax.broadcasted_iota(jnp.int32, (words, CHEADS * 128), 1) % 128
        word = lax.broadcasted_iota(jnp.int32, (words, CHEADS * 128), 0)
        mine = lane % words == word
        spot = (lane // words).astype(F32)
        head_row = lax.broadcasted_iota(jnp.int32, (CHEADS * 128, CW), 0) // 128
        head_col = lax.broadcasted_iota(jnp.int32, (CHEADS * 128, CW), 1) // CHD
        same_head = (head_row == head_col).astype(BF)
        far = lax.broadcasted_iota(jnp.int32, (places, words, CHEADS * 128), 0).astype(F32)
        scores = []
        for t in range(GROUPS):
            rows = qkv[t * 128 : (t + 1) * 128]
            scores.append(nt(rows[:, CW : 2 * CW], head_stack(rows[:, :CW], 1.0 / math.sqrt(CHD))))
        sums = []
        for t in range(GROUPS):
            shown = place < jnp.concatenate([cnts[t], cnts[t]], axis=1)[None]
            sums.append(jnp.sum(jnp.where(shown, xs[t].reshape(places, words, CW), 0.0), axis=0))
        probs = []
        for t in range(GROUPS):
            cnt4 = jnp.concatenate([cnts[t]] * CHEADS, axis=1)
            s = jnp.where(far < cnt4[None], scores[t].reshape(places, words, CHEADS * 128), -1e30)
            e = jnp.exp(s - jnp.max(s, axis=0)[None])
            r = jnp.where(mine & (spot < cnt4), 1.0 / jnp.sum(e, axis=0), 0.0)
            probs.append((e * r[None]).astype(BF).reshape(128, CHEADS * 128))
        columns = [nn(p, same_head) for p in probs]
        for t, (c, g) in enumerate(groups):
            rows = qkv[t * 128 : (t + 1) * 128]
            at = pl.ds(g * 128, 128)
            kept[c, at, : 3 * CW] = rows
            kept[c, at, 3 * CW : 3 * CW + CHEADS * 128] = probs[t]
            kept[c, at, 3 * CW + CHEADS * 128 :] = columns[t].astype(BF)
            own = pl.ds(pl.multiple_of(c * share + g * words, words), words)
            msum_ref[own, :] = jnp.sum(
                (columns[t] * rows[:, 2 * CW :].astype(F32)).reshape(places, words, CW), axis=0
            )
            sumx[own, :] = sums[t]
        for t in range(per):
            slot = ids[number * GROUPS + t]

            @pl.when(slot >= 0)
            def _(slot=slot):
                save(slot, share * places).start()

    def batch(number, carry):
        for (which, places, words, per), order_ref in zip(classes, orders):
            pl.when(batch_kind[number] == which)(
                functools.partial(block, places, words, per, order_ref, number)
            )
        return carry

    lax.fori_loop(0, batches, batch, 0)
    cnt2 = jnp.concatenate([count_ref[...].reshape(slots * share, 128)] * 2, axis=1)
    summed = sumx[...] + nn(msum_ref[...].astype(BF), mats_ref[:, 3 * CW : 4 * CW])
    pooled = (summed / cnt2).astype(BF)
    pooled_ref[...] = pooled
    vec[...] = nn(pooled, mats_ref[:, 4 * CW :]).astype(BF)
    plan_targets(home, target, taken, taken.shape[0])
    vec_ref[...] = jnp.zeros_like(vec_ref)

    def put(slot, carry):
        @pl.when(target[slot] >= 0)
        def _():
            vec_ref[target[slot]] = vec[pl.ds(pl.multiple_of(slot * share, share), share), :]

        return carry

    lax.fori_loop(0, slots, put, 0)

    def finish(slot, carry):
        for which, places, words, per in classes:

            @pl.when(kind[slot] == which)
            def _(places=places):
                save(slot, share * places).wait()

        return carry

    lax.fori_loop(0, slots, finish, 0)


def plan_batches(classes, home, count, kind, ids, batch_kind):
    slots = home.shape[0]
    coarse = classes[0][0] == 1

    def sort(slot, carry):
        places = count[slot, 0]
        which = jnp.where(places <= 8, 2, 4)
        if coarse:
            which = jnp.where(places <= 4, 1, which)
        kind[slot] = jnp.where(home[slot] >= 0, which, 0)
        for t in range(GROUPS):
            ids[slot * GROUPS + t] = -1
        return carry

    lax.fori_loop(0, slots, sort, 0)
    batch = jnp.int32(0)
    for which, _, _, per in classes:

        def take(slot, carry):
            batch, place = carry
            hit = kind[slot] == which

            @pl.when(hit)
            def _():
                ids[batch * GROUPS + place] = slot
                batch_kind[batch] = which

            place = jnp.where(hit, place + 1, place)
            full = place == per
            return jnp.where(full, batch + 1, batch), jnp.where(full, 0, place)

        batch, place = lax.fori_loop(0, slots, take, (batch, jnp.int32(0)))
        batch = jnp.where(place > 0, batch + 1, batch)
    return batch


def plan_targets(home, target, taken, owners):
    slots = home.shape[0]
    cap = -(-slots // owners)

    def clear(owner, carry):
        taken[owner] = 0
        return carry

    lax.fori_loop(0, owners, clear, 0)

    def take(slot, carry):
        owner = jnp.maximum(home[slot], 0)
        live = home[slot] >= 0
        target[slot] = jnp.where(live, owner * cap + taken[owner], -1)
        taken[owner] = taken[owner] + jnp.where(live, 1, 0)
        return carry

    lax.fori_loop(0, slots, take, 0)


def spread_counts(count):
    slots, share = count.shape
    row = lax.broadcasted_iota(jnp.int32, (slots * share, slots), 0) // share
    pick = (row == lax.broadcasted_iota(jnp.int32, (slots * share, slots), 1)).astype(BF)
    wide = nn(pick, count.astype(F32).astype(BF))
    mine = lax.broadcasted_iota(jnp.int32, (slots * share, share), 0) % share
    mine = mine == lax.broadcasted_iota(jnp.int32, (slots * share, share), 1)
    return nn(jnp.where(mine, wide, 0.0).astype(BF), jnp.ones((share, 128), BF))


def char_call(kernel, name, inputs, scalars, outs, scratch, in_hbm, out_hbm, flops, limit):
    vmem = pl.BlockSpec(memory_space=pltpu.VMEM)
    smem = pl.BlockSpec(memory_space=pltpu.SMEM)
    hbm = pl.BlockSpec(memory_space=pltpu.HBM)
    return pl.pallas_call(
        kernel,
        in_specs=[smem] * len(scalars) + [hbm if t in in_hbm else vmem for t in range(len(inputs))],
        out_specs=[hbm if t in out_hbm else vmem for t in range(len(outs))],
        out_shape=outs,
        scratch_shapes=scratch,
        cost_estimate=pl.CostEstimate(flops=flops, bytes_accessed=60 << 20, transcendentals=0),
        compiler_params=pltpu.CompilerParams(vmem_limit_bytes=limit << 20),
        name=name,
    )(*scalars, *inputs)


def plan_scratch(slots, share, owners):
    return [
        pltpu.VMEM((slots, share, 128), F32),
        pltpu.SMEM((slots,), jnp.int32),
        pltpu.SMEM((slots * GROUPS,), jnp.int32),
        pltpu.SMEM((slots,), jnp.int32),
        pltpu.SMEM((slots,), jnp.int32),
        pltpu.SMEM((owners,), jnp.int32),
    ]


def char_forward(x, home, counts, gain, mats, owners):
    slots, share = x.shape[:2]
    total = -(-slots // owners) * owners
    classes = char_classes(share)
    rows = share * SPOTS
    orders = [pltpu.VMEM((128, SPOTS * c[2]), BF) for c in classes]
    words_all = slots * share
    return char_call(
        functools.partial(char_forward_kernel, classes),
        "char_forward",
        [x.reshape(slots, rows, CW), counts, gain.reshape(1, CW), mats],
        (home, counts),
        [
            jax.ShapeDtypeStruct((total, share, D), BF),
            jax.ShapeDtypeStruct((slots, rows, KEPT), BF),
            jax.ShapeDtypeStruct((words_all, CW), BF),
            jax.ShapeDtypeStruct((words_all, CW), F32),
        ],
        [
            pltpu.VMEM((slots, rows, KEPT), BF),
            pltpu.VMEM((words_all, CW), F32),
            pltpu.VMEM((slots, rows, CW), BF),
            pltpu.VMEM((words_all, D), BF),
        ]
        + plan_scratch(slots, share, owners)
        + [pltpu.SemaphoreType.DMA((slots,))] * 2
        + orders,
        (0,),
        (1,),
        slots * rows * CW * CW * 16,
        60,
    )


def char_backward_kernel(
    classes, home, first, x_in, counts_in, kept_in, gv_ref, pooled_ref, msum_ref, gain_ref, mats_ref, stream_in, *refs
):
    backs, refs = refs[-len(classes) :], refs[: -len(classes)]
    orders, refs = refs[-len(classes) :], refs[: -len(classes)]
    dx_out, grads_ref, dgain_ref, stream_out, x_ref, kept, dx_ref, gp_all, gm_all, dqkv_sum, gv_all, count_ref = refs[:12]
    kind, ids, batch_kind, target, taken, x_sems, kept_sems, dx_sems, stream_sem = refs[12:]
    slots, share = count_ref.shape[:2]
    batches = plan_batches(classes, home, first, kind, ids, batch_kind)

    def load_x(slot):
        return pltpu.make_async_copy(x_in.at[slot], x_ref.at[slot], x_sems.at[slot])

    def load_kept(slot, rows):
        return pltpu.make_async_copy(
            kept_in.at[slot, pl.ds(0, rows)], kept.at[slot, pl.ds(0, rows)], kept_sems.at[slot]
        )

    def save(slot):
        return pltpu.make_async_copy(dx_ref.at[slot], dx_out.at[slot], dx_sems.at[slot])

    def begin(number, carry):
        for which, places, words, per in classes:

            @pl.when(batch_kind[number] == which)
            def _(places=places, per=per):
                for t in range(per):
                    slot = ids[number * GROUPS + t]

                    @pl.when(slot >= 0)
                    def _(slot=slot):
                        load_x(slot).start()
                        load_kept(slot, share * places).start()

        return carry

    lax.fori_loop(0, batches, begin, 0)
    stream_copy = pltpu.make_async_copy(stream_in, stream_out, stream_sem.at[0])
    stream_copy.start()

    count_ref[...] = spread_counts(counts_in[...]).reshape(count_ref.shape)
    for (_, places, words, _), order_ref, back_ref in zip(classes, orders, backs):
        order_ref[...] = order_matrix(places, words)
        back_ref[...] = back_matrix(places, words)
    plan_targets(home, target, taken, taken.shape[0])

    def take(slot, carry):
        here = pl.ds(pl.multiple_of(slot * share, share), share)

        @pl.when(target[slot] >= 0)
        def _():
            gv_all[here, :] = gv_ref[target[slot]]

        @pl.when(target[slot] < 0)
        def _():
            gv_all[here, :] = jnp.zeros((share, D), BF)

        return carry

    lax.fori_loop(0, slots, take, 0)
    gv = gv_all[...]
    cnt2 = jnp.concatenate([count_ref[...].reshape(slots * share, 128)] * 2, axis=1)
    gp = nt(gv, mats_ref[:, 4 * CW :]) / cnt2
    gp_all[...] = gp
    gpb = gp.astype(BF)
    gm_all[...] = nt(gpb, mats_ref[:, 3 * CW : 4 * CW]).astype(BF).astype(F32)
    grads_ref[:, 4 * CW :] = tn(pooled_ref[...], gv).astype(BF)
    grads_ref[:, 3 * CW : 4 * CW] = tn(msum_ref[...].astype(BF), gpb).astype(BF)
    dqkv_sum[...] = jnp.zeros_like(dqkv_sum)
    dgain_ref[...] = jnp.zeros_like(dgain_ref)

    def block(places, words, per, order_ref, back_ref, number):
        picked = [ids[number * GROUPS + t] for t in range(per)]
        chosen = [jnp.where(c < 0, picked[0], c) for c in picked]
        weights = [jnp.where(c < 0, 0.0, 1.0) for c in picked]
        targets = [jnp.where(c < 0, slots, c) for c in picked]
        for slot in picked:

            @pl.when(slot >= 0)
            def _(slot=slot):
                load_x(slot).wait()
                load_kept(slot, share * places).wait()

        groups = [
            (c, g, weight, target)
            for c, weight, target in zip(chosen, weights, targets)
            for g in range(share // words)
        ]
        gain = gain_ref[...]
        eighth = 1.0 / math.sqrt(CHD)
        place = lax.broadcasted_iota(jnp.int32, (places, words, CW), 0).astype(F32)
        word_grads = []
        row_grads = []
        out_grads = []
        for t, (c, g, weight, _) in enumerate(groups):
            mine = pl.ds(pl.multiple_of(c * share + g * words, words), words)
            cnt = count_ref[c, pl.ds(g * words, words), :]
            shown = place < jnp.concatenate([cnt, cnt], axis=1)[None]
            word_grads.append(gm_all[mine, :] * weight)
            out_grads.append(jnp.where(shown, (gp_all[mine, :] * weight)[None], 0.0).reshape(128, CW))
            row_grads.append(
                jnp.where(shown, word_grads[t][None], 0.0).reshape(128, CW).astype(BF)
            )
        at = [pl.ds(g * 128, 128) for _, g, _, _ in groups]
        queries = [kept[c, at[t], :CW] for t, (c, *_) in enumerate(groups)]
        keys = [kept[c, at[t], CW : 2 * CW] for t, (c, *_) in enumerate(groups)]
        products = [
            nt(kept[c, at[t], 2 * CW : 3 * CW], head_stack(row_grads[t], 1.0))
            for t, (c, *_) in enumerate(groups)
        ]
        scores = []
        for t, (c, *_) in enumerate(groups):
            p = kept[c, at[t], 3 * CW : 3 * CW + CHEADS * 128].astype(F32)
            p3 = p.reshape(places, words, CHEADS * 128)
            u = p3 * products[t].reshape(places, words, CHEADS * 128)
            scores.append((u - p3 * jnp.sum(u, axis=0)[None]).astype(BF).reshape(128, CHEADS * 128))
        xs = [
            nn(order_ref[...], x_ref[c, pl.ds(g * words * SPOTS, words * SPOTS), :])
            for c, g, _, _ in groups
        ]
        scales = [lax.rsqrt(jnp.mean(x * x, axis=-1, keepdims=True) + epsilon) for x in xs]
        normed = jnp.concatenate([(x * s * gain).astype(BF) for x, s in zip(xs, scales)], axis=0)
        grads = []
        for t, (c, *_) in enumerate(groups):
            dk = nn(scores[t], head_stack(queries[t], eighth))
            stacked = jnp.concatenate(
                [scores[t][:, h * 128 : (h + 1) * 128] for h in range(CHEADS)], axis=0
            )
            dq = tn(stacked, head_stack(keys[t], eighth))
            column = kept[c, at[t], 3 * CW + CHEADS * 128 :].astype(F32)
            dv = (column.reshape(places, words, CW) * word_grads[t][None]).reshape(128, CW)
            grads.append(jnp.concatenate([dq.astype(BF), dk.astype(BF), dv.astype(BF)], axis=1))
        grads = jnp.concatenate(grads, axis=0)
        dn_all = nt(grads, mats_ref[:, : 3 * CW])
        dqkv_sum[...] += tn(normed, grads)
        dgain = jnp.zeros((1, CW), F32)
        for t, (c, g, _, target) in enumerate(groups):
            x, scale = xs[t], scales[t]
            dn = dn_all[t * 128 : (t + 1) * 128]
            xr = x * scale
            dgain = dgain + jnp.sum(xr * dn, axis=0, keepdims=True)
            w = dn * gain
            inner = jnp.mean(xr * w, axis=-1, keepdims=True)
            dx = out_grads[t] + scale * (w - xr * inner)
            dx_ref[target, pl.ds(g * words * SPOTS, words * SPOTS), :] = nn(
                back_ref[...], dx.astype(BF)
            ).astype(BF)
        dgain_ref[...] += dgain
        for slot in picked:

            @pl.when(slot >= 0)
            def _(slot=slot):
                save(slot).start()

    def batch(number, carry):
        for (which, places, words, per), order_ref, back_ref in zip(classes, orders, backs):
            pl.when(batch_kind[number] == which)(
                functools.partial(block, places, words, per, order_ref, back_ref, number)
            )
        return carry

    lax.fori_loop(0, batches, batch, 0)
    grads_ref[:, : 3 * CW] = dqkv_sum[...].astype(BF)

    def empty(slot, carry):
        @pl.when(kind[slot] == 0)
        def _():
            dx_ref[slot] = jnp.zeros(dx_ref.shape[1:], BF)
            save(slot).start()

        return carry

    lax.fori_loop(0, slots, empty, 0)

    def finish(slot, carry):
        save(slot).wait()
        return carry

    lax.fori_loop(0, slots, finish, 0)
    stream_copy.wait()


def char_backward(x, home, counts, gain, mats, kept, pooled, msum, grad_vectors, grad_stream, owners):
    slots, share = x.shape[:2]
    classes = char_classes(share)
    rows = share * SPOTS
    orders = [pltpu.VMEM((128, SPOTS * c[2]), BF) for c in classes]
    words_all = slots * share
    dx, grads, dgain, stream = char_call(
        functools.partial(char_backward_kernel, classes),
        "char_backward",
        [
            x.reshape(slots, rows, CW), counts, kept, grad_vectors, pooled, msum, gain.reshape(1, CW), mats,
            grad_stream,
        ],
        (home, counts),
        [
            jax.ShapeDtypeStruct((slots, rows, CW), BF),
            jax.ShapeDtypeStruct(mats.shape, BF),
            jax.ShapeDtypeStruct((1, CW), F32),
            jax.ShapeDtypeStruct(grad_stream.shape, grad_stream.dtype),
        ],
        [
            pltpu.VMEM((slots, rows, CW), BF),
            pltpu.VMEM((slots, rows, KEPT), BF),
            pltpu.VMEM((slots + 1, rows, CW), BF),
            pltpu.VMEM((words_all, CW), F32),
            pltpu.VMEM((words_all, CW), F32),
            pltpu.VMEM((CW, 3 * CW), F32),
            pltpu.VMEM((words_all, D), BF),
        ]
        + plan_scratch(slots, share, owners)
        + [pltpu.SemaphoreType.DMA((slots,))] * 3
        + [pltpu.SemaphoreType.DMA((1,))]
        + orders
        + [pltpu.VMEM((SPOTS * c[2], 128), BF) for c in classes],
        (0, 2),
        (0, 3),
        slots * rows * CW * CW * 28,
        53,
    )
    return dx.reshape(x.shape), grads, dgain, stream


MESH_ID = pl.DeviceIdType.MESH


def greet(sizes, me):
    barrier = pltpu.get_barrier_semaphore()
    for axis, n in sizes.items():
        for d in range(1, n):
            pl.semaphore_signal(
                barrier, inc=1, device_id={axis: lax.rem(me[axis] + d, n)}, device_id_type=MESH_ID
            )
    pl.semaphore_wait(barrier, sum(n - 1 for n in sizes.values()))


def remote(source, target, sems, at, axis, peer):
    return pltpu.make_async_remote_copy(
        src_ref=source,
        dst_ref=target,
        send_sem=sems[0].at[at],
        recv_sem=sems[1].at[at],
        device_id={axis: peer},
        device_id_type=MESH_ID,
    )


def pair_gather_stages(own_of, sems, axis, n, mine, begin, late):
    chips = n // 2
    core = lax.rem(mine, 2)
    chip = mine // 2
    sibling = chip * 2 + 1 - core

    def start():
        for d in range(1, chips):
            there = lax.rem(chip + d, chips) * 2 + core
            remote(own_of(mine), own_of(mine), sems, d, axis, there).start()
        remote(own_of(mine), own_of(mine), sems, chips, axis, sibling).start()

    def hand_on():
        for d in range(1, chips):
            came = lax.rem(chip + chips - d, chips) * 2 + core
            remote(own_of(mine), own_of(came), sems, d, axis, sibling).wait_recv()
            remote(own_of(came), own_of(came), sems, chips + d, axis, sibling).start()

    def finish():
        for d in range(1, 2 * chips):
            remote(own_of(mine), own_of(mine), sems, d, axis, sibling).wait_send()
            if d >= chips:
                remote(own_of(mine), own_of(mine), sems, d, axis, sibling).wait_recv()

    return [(begin, start), (late, hand_on), (90.0, finish)]


def pair_part_stages(x, held, came, out, sems, axis, n, mine, begin, late):
    chips = n // 2
    core = lax.rem(mine, 2)
    chip = mine // 2
    sibling = chip * 2 + 1 - core

    def start():
        remote(x.at[:, 1 - core], came, sems, 0, axis, sibling).start()

    def onward():
        remote(x.at[:, 1 - core], came, sems, 0, axis, sibling).wait()
        for d in range(chips):
            there = lax.rem(chip + 1 + d, chips)
            came[there] = (came[there].astype(F32) + x[there, core].astype(F32)).astype(came.dtype)
            if d < chips - 1:
                remote(
                    came.at[there], held.at[chip], sems, 1 + d, axis, there * 2 + core
                ).start()

    def finish():
        held[chip] = came[chip]
        for d in range(chips - 1):
            remote(came.at[chip], held.at[chip], sems, 1 + d, axis, sibling).wait()
        total = held[0].astype(F32)
        for p in range(1, chips):
            total = total + held[p].astype(F32)
        out[...] = total.astype(out.dtype)

    return [(begin, start), (late, onward), (80.0, finish)]


def line_gather_stages(out, sems, axis, n, mine, begin, each, cut=()):
    def piece(block):
        return out.at[(block,) + cut]

    def step(k):
        for way in range(2):
            block = mine - k if way == 0 else mine + k
            here = (block >= 0) & (block < n)
            block = jnp.clip(block, 0, n - 1)
            onward = mine + 1 if way == 0 else mine - 1
            room = (onward >= 0) & (onward < n)
            peer = jnp.clip(onward, 0, n - 1)
            if k > 0:

                @pl.when(here)
                def _(way=way, block=block):
                    remote(piece(block), piece(block), sems, way * n + k - 1, axis, mine).wait_recv()

            if k < n - 1:

                @pl.when(here & room)
                def _(way=way, block=block, peer=peer):
                    remote(piece(block), piece(block), sems, way * n + k, axis, peer).start()

    def finish():
        for way in range(2):
            for k in range(n - 1):
                block = mine - k if way == 0 else mine + k
                sent = (mine < n - 1) & (block >= 0) if way == 0 else (mine > 0) & (block < n)

                @pl.when(sent)
                def _(way=way, k=k):
                    remote(piece(mine), piece(mine), sems, way * n + k, axis, mine).wait_send()

    stages = [(begin + each * k, functools.partial(step, k)) for k in range(n)]
    return stages + [(95.0, finish)]


def line_part_stages(x, held, out, sems, axis, n, mine, begin, each, end=70.0, cut=()):
    def step(t):
        for way in range(2):
            distance = mine if way == 0 else n - 1 - mine
            turn = t - distance
            here = (turn >= 0) & (turn < n - 1 - distance)
            turn = jnp.clip(turn, 0, n - 1)
            block = n - 1 - turn if way == 0 else turn
            peer = jnp.clip(mine + 1 if way == 0 else mine - 1, 0, n - 1)
            at = way * n + block

            @pl.when(here & (distance == 0))
            def _(way=way, block=block, peer=peer, at=at):
                remote(
                    x.at[(block,) + cut], held.at[(way, block) + cut], sems, at, axis, peer
                ).start()

            @pl.when(here & (distance > 0))
            def _(way=way, block=block, peer=peer, at=at):
                place = held.at[(way, block) + cut]
                remote(place, place, sems, at, axis, mine).wait_recv()
                held[(way, block) + cut] = (
                    held[(way, block) + cut].astype(F32) + x[(block,) + cut].astype(F32)
                ).astype(x.dtype)
                remote(place, place, sems, at, axis, peer).start()

    def finish():
        out[cut or ...] = x[(mine,) + cut].astype(F32)
        for way, there in ((0, mine > 0), (1, mine < n - 1)):

            @pl.when(there)
            def _(way=way):
                here = held.at[(way, mine) + cut]
                remote(here, here, sems, way * n + mine, axis, mine).wait_recv()
                out[cut or ...] += held[(way, mine) + cut].astype(F32)

        for way in range(2):
            for block in range(n):
                further = block > mine if way == 0 else block < mine

                @pl.when(further)
                def _(way=way, block=block):
                    here = held.at[(way, block) + cut]
                    remote(here, here, sems, way * n + block, axis, mine).wait_send()

    stages = [(begin + each * k, functools.partial(step, k)) for k in range(n - 1)]
    return stages + [(end, finish)]


def halves(rows):
    return [(slice(h * (rows // 2), (h + 1) * (rows // 2)), slice(None)) for h in range(2)]


def direct_stages(source_of, target, sems, axis, n, mine, begin, done, end, cols=None):
    def piece(block):
        return target.at[block] if cols is None else target.at[block, :, cols]

    def start():
        for d in range(1, n):
            peer = lax.rem(mine + d, n)
            remote(source_of(peer), piece(mine), sems, d, axis, peer).start()

    def finish():
        for d in range(1, n):
            remote(source_of(mine), piece(mine), sems, d, axis, mine).wait()
        done()

    return [(begin, start), (end, finish)]


def exchange(name, number, tasks):
    sizes = {axis: lax.axis_size(axis) for _, axis, _ in tasks}
    outs, scratch, counts, shapers = [], [], [], []
    for kind, axis, arrays in tasks:
        n = sizes[axis]
        array = arrays[0]
        shaper = lambda a: a
        if kind == "gather":
            rows = array.shape[1]
            cols = sum(a.shape[0] * a.shape[2] for a in arrays)
            made = jax.ShapeDtypeStruct((n * rows, cols) if rows % 16 == 0 else (n, rows, cols), BF)
            shaper = lambda a, rows=rows, cols=cols, n=n: a.reshape(n * rows, cols)
        elif kind == "gather_mid":
            lead, rows, cols = array.shape
            made = jax.ShapeDtypeStruct(
                (lead, n * rows, cols) if rows % 16 == 0 else (n, lead, rows, cols), array.dtype
            )
            if rows % 16:
                shaper = lambda a, lead=lead, rows=rows, cols=cols, n=n: a.transpose(1, 0, 2, 3).reshape(
                    lead, n * rows, cols
                )
        else:
            block = array.shape if kind in ("line_gather", "total") else array.shape[1:]
            if kind == "part":
                block = array.shape[2:]
            summed = kind in ("part", "line_part", "total")
            made = jax.ShapeDtypeStruct(block if summed else (n,) + block, F32 if summed else array.dtype)
        outs.append(made)
        shapers.append(shaper)
        counts.append(len(arrays))
        scratch += [pltpu.SemaphoreType.DMA((4 * n,)), pltpu.SemaphoreType.DMA((4 * n,))]
        if kind == "part":
            scratch += [pltpu.VMEM((n // 2,) + block, array.dtype)] * 2
        if kind == "total":
            scratch.append(pltpu.VMEM((n,) + block, array.dtype))
        if kind == "line_part":
            scratch.append(pltpu.VMEM((2, n) + block, array.dtype))
    total_ins = sum(counts)

    def kernel(*refs):
        ins, at = [], 0
        for count in counts:
            ins.append(refs[at : at + count])
            at += count
        results = refs[at : at + len(tasks)]
        rest = list(refs[at + len(tasks) :])
        me = {axis: lax.axis_index(axis) for axis in sizes}
        greet(sizes, me)
        stages = []
        for (kind, axis, _), xs, out in zip(tasks, ins, results):
            sems = (rest.pop(0), rest.pop(0))
            n, mine, x = sizes[axis], me[axis], xs[0]
            if kind == "line_gather":
                out[mine] = x[...]
                for h, cut in enumerate(halves(x.shape[0])):
                    sems_half = tuple(s.at[pl.ds(2 * n * h, 2 * n)] for s in sems)
                    stages += line_gather_stages(out, sems_half, axis, n, mine, 0.05 * h, 6.0, cut)
            elif kind == "line_part":
                stages += line_part_stages(x, rest.pop(0), out, sems, axis, n, mine, 0.0, 6.0)
            elif kind == "part":
                held, came = rest.pop(0), rest.pop(0)
                stages += pair_part_stages(x, held, came, out, sems, axis, n, mine, 0.1, 1.0)
            elif kind in ("gather", "gather_mid"):
                if kind == "gather":
                    rows = x.shape[1]
                    if rows % 16 == 0:
                        own_of = lambda i, out=out, rows=rows: out.at[
                            pl.ds(pl.multiple_of(i * rows, 16), rows), :
                        ]
                    else:
                        own_of = lambda i, out=out: out.at[i]
                    own, col = own_of(mine), 0
                    for piece in xs:
                        for t in range(piece.shape[0]):
                            own[:, col : col + piece.shape[2]] = piece[t].astype(BF)
                            col += piece.shape[2]
                else:
                    rows = x.shape[1]
                    if rows % 16 == 0:
                        own_of = lambda i, out=out, rows=rows: out.at[
                            :, pl.ds(pl.multiple_of(i * rows, 16), rows), :
                        ]
                    else:
                        own_of = lambda i, out=out: out.at[i]
                    own_of(mine)[...] = x[...]
                if axis == "dp":
                    stages += pair_gather_stages(own_of, sems, axis, n, mine, 0.2, 6.0 * lax.axis_size("mp") - 11.5)
                else:

                    def start(own_of=own_of, sems=sems, axis=axis, n=n, mine=mine):
                        for d in range(1, n):
                            peer = lax.rem(mine + d, n)
                            remote(own_of(mine), own_of(mine), sems, d, axis, peer).start()

                    def finish(own_of=own_of, sems=sems, axis=axis, n=n, mine=mine):
                        for d in range(1, n):
                            remote(own_of(mine), own_of(mine), sems, d, axis, mine).wait()

                    stages += [(0.15, start), (90.0, finish)]
            elif kind == "total":
                held = rest.pop(0)
                held[mine] = x[...]

                def done(held=held, out=out, n=n):
                    total = held[0].astype(F32)
                    for p in range(1, n):
                        total = total + held[p].astype(F32)
                    out[...] = total

                stages += direct_stages(
                    lambda p, held=held, mine=mine: held.at[mine], held, sems, axis, n, mine, 0.3, done, 60.0
                )
            else:
                out[mine] = x[mine]
                stages += direct_stages(
                    lambda p, x=x: x.at[p], out, sems, axis, n, mine, 0.0, lambda: None, 60.0
                )
        for _, run in sorted(stages, key=lambda stage: stage[0]):
            run()

    vmem = pl.BlockSpec(memory_space=pltpu.VMEM)
    results = pl.pallas_call(
        kernel,
        out_shape=outs,
        in_specs=[vmem] * total_ins,
        out_specs=[vmem] * len(tasks),
        scratch_shapes=scratch,
        compiler_params=pltpu.CompilerParams(
            collective_id=number, has_side_effects=True, vmem_limit_bytes=24 << 20
        ),
        name=name,
    )(*[array for _, _, arrays in tasks for array in arrays])
    return [shaper(a) for shaper, a in zip(shapers, results)]


def by_chip(array):
    return array.reshape(lax.axis_size("dp") // 2, 2, -1, array.shape[-1])


def sum_char_grads(grads, gains, word_sums, block_rows):
    n, m = lax.axis_size("dp"), lax.axis_size("mp")
    grads = by_chip(grads)
    rows, cols = grads.shape[2:]
    slim = cols // m
    small = jax.ShapeDtypeStruct((8, D), F32)

    def kernel(x, gain_char, gain_one, gain_two, *refs):
        words = refs[: len(word_sums)]
        (out, small_out, held, came, total_dp, cut, cut_held, merged, small_dp, small_mp, *sems) = refs[len(word_sums) :]
        pairs = [tuple(sems[2 * t : 2 * t + 2]) for t in range(6)]
        i, j = lax.axis_index("dp"), lax.axis_index("mp")
        greet({"dp": n, "mp": m}, {"dp": i, "mp": j})
        part = [
            run for _, run in pair_part_stages(x, held, came, total_dp, pairs[0], "dp", n, i, 0.0, 0.0)
        ]
        part[0]()
        squares = jnp.zeros((1, 1), F32)
        for t, word in enumerate(words):
            if t == 1:
                wide = word[pl.ds(pl.multiple_of(j * block_rows, 16), block_rows), :].astype(F32)
            else:
                wide = word[...].astype(F32)
            squares = squares + jnp.sum(jnp.sum(wide * wide, axis=0, keepdims=True), axis=1, keepdims=True)
        row = lax.broadcasted_iota(jnp.int32, (8, D), 0)
        small_dp[i] = jnp.where(row == 3, squares * (1.0 / n), 0.0)
        small_dp[i, 0:1, : gain_char.shape[1]] = gain_char[...]
        small_dp[i, 1:2, :] = gain_one[...]
        small_dp[i, 2:3, :] = gain_two[...]
        part[1]()

        def small_done():
            total = small_dp[0]
            for p in range(1, n):
                total = total + small_dp[p]
            small_mp[j] = total

        def small_end():
            total = small_mp[0]
            for p in range(1, m):
                total = total + small_mp[p]
            small_out[...] = total

        def cut_done():
            total = cut_held[0].astype(F32)
            for p in range(1, m):
                total = total + cut_held[p].astype(F32)
            merged[j] = total.astype(BF)

        one = direct_stages(lambda p: small_dp.at[i], small_dp, pairs[1], "dp", n, i, 0, small_done, 0)
        two = direct_stages(lambda p: small_mp.at[j], small_mp, pairs[2], "mp", m, j, 0, small_end, 0)
        three = direct_stages(lambda p: cut.at[p], cut_held, pairs[3], "mp", m, j, 0, cut_done, 0)
        four = direct_stages(lambda p: merged.at[j], merged, pairs[4], "mp", m, j, 0, lambda: None, 0)
        one[0][1]()
        part[2]()
        for p in range(m):
            cut[p] = total_dp[:, p * slim : (p + 1) * slim]
        cut_held[j] = cut[j]
        three[0][1]()
        one[1][1]()
        two[0][1]()
        three[1][1]()
        four[0][1]()
        two[1][1]()
        four[1][1]()
        if rows % 16 == 0:
            own_of = lambda d: out.at[pl.ds(pl.multiple_of(d * rows, 16), rows), :]
        else:
            own_of = lambda d: out.at[d]
        own = own_of(i)
        for p in range(m):
            own[:, p * slim : (p + 1) * slim] = merged[p]
        for _, run in pair_gather_stages(own_of, pairs[5], "dp", n, i, 0, 0):
            run()

    vmem = pl.BlockSpec(memory_space=pltpu.VMEM)
    sums, smalls = pl.pallas_call(
        kernel,
        out_shape=[
            jax.ShapeDtypeStruct((n * rows, cols) if rows % 16 == 0 else (n, rows, cols), BF),
            jax.ShapeDtypeStruct(small.shape, F32),
        ],
        in_specs=[vmem] * (4 + len(word_sums)),
        out_specs=[vmem] * 2,
        scratch_shapes=[
            pltpu.VMEM((n // 2, rows, cols), BF),
            pltpu.VMEM((n // 2, rows, cols), BF),
            pltpu.VMEM((rows, cols), BF),
            pltpu.VMEM((m, rows, slim), BF),
            pltpu.VMEM((m, rows, slim), BF),
            pltpu.VMEM((m, rows, slim), BF),
            pltpu.VMEM((n,) + small.shape, F32),
            pltpu.VMEM((m,) + small.shape, F32),
        ]
        + [pltpu.SemaphoreType.DMA((2 * max(n, m),))] * 12,
        compiler_params=pltpu.CompilerParams(
            collective_id=20, has_side_effects=True, vmem_limit_bytes=24 << 20
        ),
        name="sum_char_grads",
    )(grads, *gains, *word_sums)
    return sums.reshape(n * rows, cols), smalls


ROWS = 256


def rms_scale(values):
    return lax.rsqrt(jnp.mean(values * values, axis=-1, keepdims=True) + epsilon)


def norm_back(values, scale, gain_row, grad):
    weighted = grad * gain_row
    inner = jnp.mean(values * weighted, axis=-1, keepdims=True)
    return scale * weighted - values * (scale * scale * scale) * inner


def word_forward_kernel(
    width, vec_ref, place_ref, words_ref, doc_all_ref, doc_row_ref, gain_ref, project_ref,
    stream_ref, normed_ref, qkv_ref, probs_ref, mixed_ref, keys, values, doc_ref, placed
):
    step = pl.program_id(0)
    parts, kept_rows = vec_ref.shape[:2]
    words = kept_rows // OWNER_BLOCKS

    @pl.when(step == 0)
    def _():
        doc_ref[...] = tn(doc_all_ref[...].astype(F32).astype(BF), jnp.ones((1, 128), BF))
        numbers = lax.broadcasted_iota(jnp.int32, (placed.shape[0], parts * words), 0)
        hits = [(numbers == place_ref[b : b + 1, :]).astype(BF) for b in range(OWNER_BLOCKS)]
        vectors = [
            vec_ref[p, b * words : (b + 1) * words, :] for b in range(OWNER_BLOCKS) for p in range(parts)
        ]
        placed[...] = nn(jnp.concatenate(hits, axis=1), jnp.concatenate(vectors, axis=0))

    here = pl.ds(pl.multiple_of(step * ROWS, ROWS), ROWS)
    stream = words_ref[...].astype(F32) + placed[here, :]
    stream_ref[...] = stream
    normed = (stream * rms_scale(stream) * gain_ref[...]).astype(BF)
    normed_ref[...] = normed
    qkv = nn(normed, project_ref[...]).astype(BF)
    qkv_ref[...] = qkv
    first = pl.ds(pl.multiple_of(step * ROWS, ROWS), ROWS)
    keys[first, :] = qkv[:, width : 2 * width]
    values[first, :] = qkv[:, 2 * width :]
    queries = (qkv[:, :width].astype(F32) * (1.0 / math.sqrt(HD))).astype(BF)

    def attend(number):
        count = (number + 1) * ROWS
        same = jnp.concatenate([doc_ref[:count, :]] * (ROWS // 128), axis=1) == doc_row_ref[...].astype(F32)
        key_at = lax.broadcasted_iota(jnp.int32, (count, ROWS), 0)
        query_at = lax.broadcasted_iota(jnp.int32, (count, ROWS), 1) + number * ROWS
        allowed = same & (key_at <= query_at)
        parts = []
        for head in range(width // HD):
            at = slice(head * HD, (head + 1) * HD)
            scores = jnp.where(allowed, nt(keys[:count, at], queries[:, at]), negative_big)
            raised = jnp.exp(scores - jnp.max(scores, axis=0, keepdims=True))
            probs = (raised * (1.0 / jnp.sum(raised, axis=0, keepdims=True))).astype(BF)
            probs_ref[head, :count, :] = probs
            parts.append(tn(values[:count, at], probs).T)
        mixed_ref[...] = jnp.concatenate(parts, axis=1).astype(BF)

    for number in range(doc_all_ref.shape[1] // ROWS):
        pl.when(step == number)(functools.partial(attend, number))


def word_forward(vectors, places, words, documents, gain, project):
    length = words.shape[0]
    width = project.shape[1] // 3
    heads = width // HD
    rows = lambda cols: pl.BlockSpec((ROWS, cols), lambda i: (i, 0))
    full = lambda shape: pl.BlockSpec(shape, lambda i: (0,) * len(shape))
    return pl.pallas_call(
        functools.partial(word_forward_kernel, width),
        grid=(length // ROWS,),
        in_specs=[
            full(vectors.shape),
            full(places.shape),
            rows(D),
            full((1, length)),
            pl.BlockSpec((1, ROWS), lambda i: (0, i)),
            full((1, D)),
            full(project.shape),
        ],
        out_specs=[
            rows(D),
            rows(D),
            rows(3 * width),
            pl.BlockSpec((heads, length, ROWS), lambda i: (0, 0, i)),
            rows(width),
        ],
        out_shape=[
            jax.ShapeDtypeStruct((length, D), F32),
            jax.ShapeDtypeStruct((length, D), BF),
            jax.ShapeDtypeStruct((length, 3 * width), BF),
            jax.ShapeDtypeStruct((heads, length, length), BF),
            jax.ShapeDtypeStruct((length, width), BF),
        ],
        scratch_shapes=[
            pltpu.VMEM((length, width), BF),
            pltpu.VMEM((length, width), BF),
            pltpu.VMEM((length, 128), F32),
            pltpu.VMEM((length, D), F32),
        ],
        compiler_params=pltpu.CompilerParams(vmem_limit_bytes=32 << 20),
        name="word_forward",
    )(
        vectors,
        places,
        words,
        documents.reshape(1, length),
        documents.reshape(1, length),
        gain.reshape(1, D),
        project,
    )


FEED_ROWS = 512


def feed_kernel(
    mixed_ref, output_ref, stream_ref, cot_ref, gain_ref, upper_ref, lower_ref,
    hidden_ref, feed_ref, part_ref, grad_upper_ref, grad_lower_ref, upper_sum, lower_sum
):
    step = pl.program_id(0)

    @pl.when(step == 0)
    def _():
        upper_sum[...] = jnp.zeros_like(upper_sum)
        lower_sum[...] = jnp.zeros_like(lower_sum)

    parts, _, width = mixed_ref.shape
    hidden = stream_ref[...]
    for j in range(parts):
        hidden = hidden + nn(mixed_ref[j], output_ref[j * width : (j + 1) * width, :])
    hidden_ref[...] = hidden
    normed = (hidden * rms_scale(hidden) * gain_ref[...]).astype(BF)
    raised = nn(normed, upper_ref[...])
    constant = math.sqrt(2.0 / math.pi)
    square = raised * raised
    curve = jnp.tanh(constant * raised * (1.0 + 0.044715 * square))
    half = 0.5 * (1.0 + curve)
    active = (raised * half).astype(BF)
    slope = half + 0.5 * raised * (1.0 - curve * curve) * constant * (1.0 + 3.0 * 0.044715 * square)
    feed_ref[...] = nn(active, lower_ref[...]).astype(BF)
    grad_feed = cot_ref[...]
    grad_raised = (nt(grad_feed, lower_ref[...]) * slope).astype(BF)
    part_ref[...] = nt(grad_raised, upper_ref[...]).astype(BF)
    lower_sum[...] += tn(active, grad_feed)
    upper_sum[...] += tn(normed, grad_raised)

    @pl.when(step == pl.num_programs(0) - 1)
    def _():
        grad_upper_ref[...] = upper_sum[...].astype(BF)
        grad_lower_ref[...] = lower_sum[...].astype(BF)


def feed(mixed, output, stream, cotangent, gain, upper, lower):
    length = stream.shape[0]
    rows = pl.BlockSpec((FEED_ROWS, D), lambda i: (i, 0))
    full = lambda shape: pl.BlockSpec(shape, lambda i: (0,) * len(shape))
    return pl.pallas_call(
        feed_kernel,
        grid=(length // FEED_ROWS,),
        in_specs=[
            pl.BlockSpec((mixed.shape[0], FEED_ROWS, mixed.shape[2]), lambda i: (0, i, 0)),
            full(output.shape),
            rows,
            rows,
            full((1, D)),
            full(upper.shape),
            full(lower.shape),
        ],
        out_specs=[rows, rows, rows, full(upper.shape), full(lower.shape)],
        out_shape=[
            jax.ShapeDtypeStruct((length, D), F32),
            jax.ShapeDtypeStruct((length, D), BF),
            jax.ShapeDtypeStruct((length, D), BF),
            jax.ShapeDtypeStruct(upper.shape, BF),
            jax.ShapeDtypeStruct(lower.shape, BF),
        ],
        scratch_shapes=[pltpu.VMEM(upper.shape, F32), pltpu.VMEM(lower.shape, F32)],
        compiler_params=pltpu.CompilerParams(vmem_limit_bytes=32 << 20),
        name="feed",
    )(mixed, output, stream, cotangent, gain.reshape(1, D), upper, lower)


def hidden_back_kernel(
    own, grad_ref, hidden_ref, cot_ref, mixed_ref, output_ref, gain_ref,
    grad_hidden_ref, grad_mixed_ref, grad_output_ref, gain_grad_ref
):
    hidden = hidden_ref[...]
    scale = rms_scale(hidden)
    grad = grad_ref[...]
    grad_hidden = cot_ref[...].astype(F32) + norm_back(hidden, scale, gain_ref[...], grad)
    grad_hidden_ref[...] = grad_hidden
    gain_grad_ref[...] = jnp.sum(hidden * scale * grad, axis=0, keepdims=True)
    attend = grad_hidden.astype(BF)
    parts, _, width = mixed_ref.shape
    for j in range(parts):
        at = slice(j * width, (j + 1) * width)
        grad_mixed_ref[j] = nt(attend, output_ref[at, :]).astype(BF)
        grad_output_ref[at, :] = tn(mixed_ref[j], attend).astype(BF)


def hidden_back(own, grad, hidden, cotangent, mixed, output, gain):
    share = grad.shape[0]
    parts, _, width = mixed.shape
    mine = pl.BlockSpec((share, D), lambda i, own: (own[0], 0))
    full = lambda shape: pl.BlockSpec(shape, lambda i, own: (0,) * len(shape))
    return pl.pallas_call(
        hidden_back_kernel,
        grid_spec=pltpu.PrefetchScalarGridSpec(
            num_scalar_prefetch=1,
            grid=(1,),
            in_specs=[
                full((share, D)),
                mine,
                mine,
                pl.BlockSpec((parts, share, width), lambda i, own: (0, own[0], 0)),
                full(output.shape),
                full((1, D)),
            ],
            out_specs=[
                full((share, D)),
                full((parts, share, width)),
                full(output.shape),
                full((1, D)),
            ],
        ),
        out_shape=[
            jax.ShapeDtypeStruct((share, D), F32),
            jax.ShapeDtypeStruct((parts, share, width), BF),
            jax.ShapeDtypeStruct(output.shape, BF),
            jax.ShapeDtypeStruct((1, D), F32),
        ],
        compiler_params=pltpu.CompilerParams(vmem_limit_bytes=32 << 20),
        name="hidden_back",
    )(own, grad, hidden, cotangent, mixed, output, gain.reshape(1, D))


def word_backward_kernel(
    width, probs_ref, qkv_ref, all_ref, grad_ref, normed_ref, project_ref,
    part_ref, grad_project_ref, grads, key_sum, value_sum
):
    step = pl.program_id(0)
    steps = all_ref.shape[0] // ROWS
    first = pl.ds(pl.multiple_of(step * ROWS, ROWS), ROWS)
    eighth = 1.0 / math.sqrt(HD)
    queries = (qkv_ref[:, :width].astype(F32) * eighth).astype(BF)

    @pl.when(step == 0)
    def _():
        key_sum[...] = jnp.zeros_like(key_sum)
        value_sum[...] = jnp.zeros_like(value_sum)

    def attend(number):
        count = (number + 1) * ROWS
        parts = []
        for head in range(width // HD):
            at = slice(head * HD, (head + 1) * HD)
            keys = all_ref[:count, width + head * HD : width + (head + 1) * HD]
            values = all_ref[:count, 2 * width + head * HD : 2 * width + (head + 1) * HD]
            grad = grad_ref[:, at]
            probs = probs_ref[head, :count, :]
            wide = probs.astype(F32)
            product = wide * nt(values, grad)
            scores = (product - wide * jnp.sum(product, axis=0, keepdims=True)).astype(BF)
            key_sum[head, :count, :] += nn(scores, queries[:, at])
            value_sum[head, :count, :] += nn(probs, grad)
            parts.append(tn(keys, scores).T * eighth)
        grads[first, :width] = jnp.concatenate(parts, axis=1).astype(BF)

    for number in range(steps):
        pl.when(step == number)(functools.partial(attend, number))

    @pl.when(step == steps - 1)
    def _():
        for head in range(width // HD):
            grads[:, width + head * HD : width + (head + 1) * HD] = key_sum[head].astype(BF)
            grads[:, 2 * width + head * HD : 2 * width + (head + 1) * HD] = value_sum[head].astype(BF)
        grad_project_ref[...] = tn(normed_ref[...], grads[...]).astype(BF)
        part_ref[...] = nt(grads[...], project_ref[...]).astype(BF)


def word_backward(probs, qkv, grad_mixed, normed, project):
    length = qkv.shape[0]
    width = project.shape[1] // 3
    heads = width // HD
    rows = lambda cols: pl.BlockSpec((ROWS, cols), lambda i: (i, 0))
    full = lambda shape: pl.BlockSpec(shape, lambda i: (0,) * len(shape))
    return pl.pallas_call(
        functools.partial(word_backward_kernel, width),
        grid=(length // ROWS,),
        in_specs=[
            pl.BlockSpec((heads, length, ROWS), lambda i: (0, 0, i)),
            rows(3 * width),
            full(qkv.shape),
            rows(width),
            full(normed.shape),
            full(project.shape),
        ],
        out_specs=[full((length, D)), full(project.shape)],
        out_shape=[
            jax.ShapeDtypeStruct((length, D), BF),
            jax.ShapeDtypeStruct(project.shape, BF),
        ],
        scratch_shapes=[
            pltpu.VMEM(qkv.shape, BF),
            pltpu.VMEM((heads, length, HD), F32),
            pltpu.VMEM((heads, length, HD), F32),
        ],
        compiler_params=pltpu.CompilerParams(vmem_limit_bytes=32 << 20),
        name="word_backward",
    )(probs, qkv, qkv, grad_mixed, normed, project)


def stream_back_kernel(own, grad_ref, stream_ref, hidden_grad_ref, gain_ref, out_ref, gain_grad_ref):
    stream = stream_ref[...]
    scale = rms_scale(stream)
    grad = grad_ref[...]
    total = hidden_grad_ref[...] + norm_back(stream, scale, gain_ref[...], grad)
    out_ref[...] = total.astype(BF)
    gain_grad_ref[...] = jnp.sum(stream * scale * grad, axis=0, keepdims=True)


def stream_back(own, grad, stream, hidden_grad, gain):
    share = grad.shape[0]
    full = lambda shape: pl.BlockSpec(shape, lambda i, own: (0,) * len(shape))
    return pl.pallas_call(
        stream_back_kernel,
        grid_spec=pltpu.PrefetchScalarGridSpec(
            num_scalar_prefetch=1,
            grid=(1,),
            in_specs=[
                full((share, D)),
                pl.BlockSpec((share, D), lambda i, own: (own[0], 0)),
                full((share, D)),
                full((1, D)),
            ],
            out_specs=[full((share, D)), full((1, D))],
        ),
        out_shape=[
            jax.ShapeDtypeStruct((share, D), BF),
            jax.ShapeDtypeStruct((1, D), F32),
        ],
        name="stream_back",
    )(own, grad, stream, hidden_grad, gain.reshape(1, D))


def shampoo_kernel(
    threshold, position, char_ref, small_ref, gain_ref, gains_ref, project, output, upper, lower, hidden_in, feed_in, *refs
):
    given_in, refs = refs[:30], refs[30:]
    norm_ref, gain_grad_ref, gains_grad_ref, gain_new_ref, gains_new_ref, block_out = refs[:6]
    made_out, refs = refs[6:36], refs[36:]
    given, made = refs[:30], refs[30:60]
    hidden, feed_sum, total, in_sems, out_sems = refs[60:]
    loads = [pltpu.make_async_copy(a, b, in_sems.at[t]) for t, (a, b) in enumerate(zip(given_in, given))]
    loads += [
        pltpu.make_async_copy(hidden_in, hidden, in_sems.at[30]),
        pltpu.make_async_copy(feed_in, feed_sum, in_sems.at[31]),
    ]
    order = (4, 5, 2, 3, 0, 1)
    for number in order:
        for t in range(5):
            loads[5 * number + t].start()
    loads[30].start()
    loads[31].start()
    saves = [pltpu.make_async_copy(a, b, out_sems.at[t]) for t, (a, b) in enumerate(zip(made, made_out))]
    saves.append(pltpu.make_async_copy(total, block_out, out_sems.at[30]))
    me = position[0]
    char = char_ref[...].astype(F32)
    small = small_ref[...]
    lanes = lax.broadcasted_iota(jnp.int32, small.shape, 0)
    squares = (
        jnp.sum(jnp.sum(char * char, axis=0, keepdims=True), axis=1, keepdims=True)
        + jnp.sum(
            jnp.sum(jnp.where(lanes < 3, small * small, 0.0), axis=0, keepdims=True),
            axis=1,
            keepdims=True,
        )
        + small[3:4, :1]
    )
    norm = jnp.sqrt(squares)
    factor = jnp.minimum(1.0, threshold / norm)
    norm_ref[...] = norm
    gain_grad = small[0:1, :CW] * factor
    gain_grad_ref[...] = gain_grad
    gain_new_ref[...] = gain_ref[...] - gain_rate * gain_grad
    gains_grad = small[1:3, :] * factor
    gains_grad_ref[...] = gains_grad
    gains_new_ref[...] = gains_ref[...] - gain_rate * gains_grad
    width = project.shape[1] // 3
    own = pl.ds(pl.multiple_of(position[1] * width, 16), width)

    def whole_of(number, t):
        if number == 0:
            return char_ref[:, t * CW : (t + 1) * CW]
        if number == 1:
            return char_ref[:, 4 * CW :]
        if number == 2:
            return project[:, t * width : (t + 1) * width]
        return (output[own, :], upper[...], lower[...])[number - 3]

    def chosen(rows, cols):
        row = lax.broadcasted_iota(jnp.int32, (rows, cols), 0) + me * rows
        return (row == lax.broadcasted_iota(jnp.int32, (rows, cols), 1)).astype(BF)

    half = (1.0 - decay_rate) * factor * factor
    for number in order:
        for t in range(5):
            loads[5 * number + t].wait()
        master, left, right, left_root, right_root = given[5 * number : 5 * number + 5]
        grad_out, left_out, right_out, new_out, copy_out = made[5 * number : 5 * number + 5]
        for t in range(master.shape[0]):
            grad = whole_of(number, t)
            rows = nn(chosen(master.shape[1], grad.shape[0]), grad)
            grad_out[t] = rows * factor
            left_out[t] = decay_rate * left[t] + half * nt(rows.astype(BF), grad)
            cols = nt(grad, chosen(right.shape[1], grad.shape[1])).astype(BF)
            right_out[t] = decay_rate * right[t] + half * tn(cols, grad)
            turned = (nn(left_root[t].astype(BF), grad) * factor).astype(BF)
            root = right_root[:, t * grad.shape[1] : (t + 1) * grad.shape[1]]
            new = master[t] - learn_rate * nn(turned, root)
            new_out[t] = new
            copy_out[t] = new.astype(BF)
        for t in range(5):
            saves[5 * number + t].start()
    loads[30].wait()
    loads[31].wait()
    total[...] = (hidden[...] + feed_sum[...].astype(F32)).astype(BF)
    saves[30].start()
    for save in saves:
        save.wait()


def shampoo(threshold, position, char_sums, small, gain, gains, word_sums, hidden, feed_sum, given):
    flat = []
    shapes = []
    for master, left, right, left_root, right_root in given:
        flat += [master, left, right, left_root, right_root]
        shapes += [
            jax.ShapeDtypeStruct(a.shape, F32) for a in (master, left, right, master)
        ] + [jax.ShapeDtypeStruct(master.shape, BF)]
    first = [
        jax.ShapeDtypeStruct((1, 1), F32),
        jax.ShapeDtypeStruct((1, CW), F32),
        jax.ShapeDtypeStruct((2, D), F32),
        jax.ShapeDtypeStruct((1, CW), F32),
        jax.ShapeDtypeStruct((2, D), F32),
    ]
    vmem = pl.BlockSpec(memory_space=pltpu.VMEM)
    smem = pl.BlockSpec(memory_space=pltpu.SMEM)
    hbm = pl.BlockSpec(memory_space=pltpu.HBM)
    return pl.pallas_call(
        functools.partial(shampoo_kernel, threshold),
        in_specs=[smem] + [vmem] * 8 + [hbm] * 32,
        out_specs=[vmem] * 5 + [hbm] * 31,
        out_shape=first + [jax.ShapeDtypeStruct(feed_sum.shape, BF)] + shapes,
        scratch_shapes=[pltpu.VMEM(a.shape, a.dtype) for a in flat]
        + [pltpu.VMEM(a.shape, a.dtype) for a in shapes]
        + [
            pltpu.VMEM(hidden.shape, F32),
            pltpu.VMEM(feed_sum.shape, BF),
            pltpu.VMEM(feed_sum.shape, BF),
            pltpu.SemaphoreType.DMA((32,)),
            pltpu.SemaphoreType.DMA((31,)),
        ],
        compiler_params=pltpu.CompilerParams(vmem_limit_bytes=60 << 20),
        name="shampoo",
    )(position, char_sums, small, gain.reshape(1, CW), gains, *word_sums, hidden, feed_sum, *flat)


def run_stages(stages):
    for _, run in sorted(stages, key=lambda stage: stage[0]):
        run()


def gather_setup(xs, out):
    rows = xs[0].shape[1]

    def own_of(i):
        if rows % 16 == 0:
            return out.at[pl.ds(pl.multiple_of(i * rows, 16), rows), :]
        return out.at[i]

    def put(mine):
        own, col = own_of(mine), 0
        for piece in xs:
            for t in range(piece.shape[0]):
                own[:, col : col + piece.shape[2]] = piece[t].astype(BF)
                col += piece.shape[2]

    return own_of, put


def gather_shape(arrays, n):
    rows = arrays[0].shape[1]
    cols = sum(a.shape[0] * a.shape[2] for a in arrays)
    shape = (n * rows, cols) if rows % 16 == 0 else (n, rows, cols)
    return jax.ShapeDtypeStruct(shape, BF), lambda a: a.reshape(n * rows, cols)


def dma_sems(count):
    return [pltpu.SemaphoreType.DMA((count,))] * 2


def call_remote(kernel, name, number, outs, scratch, inputs):
    vmem = pl.BlockSpec(memory_space=pltpu.VMEM)
    return pl.pallas_call(
        kernel,
        out_shape=outs,
        in_specs=[vmem] * len(inputs),
        out_specs=[vmem] * len(outs),
        scratch_shapes=scratch,
        compiler_params=pltpu.CompilerParams(
            collective_id=number, has_side_effects=True, vmem_limit_bytes=28 << 20
        ),
        name=name,
    )(*inputs)


def gather_char(mixer, lift, output, home, places):
    n, m = lax.axis_size("dp"), lax.axis_size("mp")
    slots, block_words = places.shape
    cap = -(-slots // n)
    total = n * cap
    share = block_words // m
    shape, shaper = gather_shape([mixer, lift], n)
    rows = output.shape[1]

    def kernel(
        mixer_in, lift_in, output_in, home_row, place_ref,
        mats, line, live, live_place, own_row, mixer_ref, lift_ref, output_ref, sent, came, local, *sems
    ):
        pairs = [tuple(sems[2 * t : 2 * t + 2]) for t in range(3)]
        i, j = lax.axis_index("dp"), lax.axis_index("mp")
        loads = [
            pltpu.make_async_copy(a, b, local.at[t])
            for t, (a, b) in enumerate(
                ((mixer_in, mixer_ref), (lift_in, lift_ref), (output_in, output_ref))
            )
        ]
        for load in loads:
            load.start()
        own_of, put = gather_setup([mixer_ref, lift_ref], mats)
        greet({"dp": n, "mp": m}, {"dp": i, "mp": j})
        for load in loads:
            load.wait()
        put(i)
        line[j] = output_ref[0].astype(BF)
        stages = pair_gather_stages(own_of, pairs[0], "dp", n, i, 0.0, 2.0)

        def send_places():
            before = lax.broadcasted_iota(jnp.int32, (slots, slots), 0)
            before = before < lax.broadcasted_iota(jnp.int32, (slots, slots), 1)
            home_col = tn(home_row[...].astype(F32).astype(BF), jnp.ones((1, 128), BF))[:, :slots]
            same = (home_col == home_row[...].astype(F32)) & before
            rank = jnp.sum(same.astype(F32), axis=0, keepdims=True)
            target = jnp.where(
                home_row[...] >= 0, home_row[...].astype(F32) * cap + rank, float(total)
            )
            hit = lax.broadcasted_iota(jnp.int32, (total, slots), 0).astype(F32) == target
            chosen = hit.astype(F32)
            placed = jnp.zeros((total, block_words), F32) - 1.0
            for s in range(slots):
                placed = jnp.where(
                    chosen[:, s : s + 1] > 0.0, place_ref[s : s + 1, :].astype(F32), placed
                )
            for p in range(n):
                sent[p] = placed[p * cap : (p + 1) * cap, :].astype(jnp.int32)
            came[i] = sent[i]

        def use_places():
            placed = jnp.concatenate([came[p] for p in range(n)], axis=0).astype(F32)
            held = jnp.max(placed, axis=1, keepdims=True) >= 0.0
            filled = jnp.where(held, jnp.ones((total, 128), F32), 0.0)
            lower = lax.broadcasted_iota(jnp.int32, (total, total), 1)
            lower = (lower < lax.broadcasted_iota(jnp.int32, (total, total), 0)).astype(BF)
            rank = nn(lower, filled.astype(BF))
            lane = lax.broadcasted_iota(jnp.int32, (total, 128), 1).astype(F32)
            chosen = jnp.where((rank == lane) & (filled > 0.0), 1.0, 0.0).astype(BF)
            live[...] = chosen
            high = jnp.floor((placed + 1.0) * (1.0 / 32.0))
            low = placed + 1.0 - high * 32.0
            high, low = high.astype(BF), low.astype(BF)
            found = tn(chosen, high) * 32.0 + tn(chosen, low) - 1.0
            live_place[...] = found[: live_place.shape[0], :].astype(jnp.int32)
            block = cap * share
            for p in range(n):
                col = lax.broadcasted_iota(jnp.int32, (block_words, block), 1) % share + j * share
                pick = (col == lax.broadcasted_iota(jnp.int32, (block_words, block), 0)).astype(BF)
                row = lax.broadcasted_iota(jnp.int32, (total, block), 0) - p * cap
                mine = row == lax.broadcasted_iota(jnp.int32, (total, block), 1) // share
                value = nn(high, pick) * 32.0 + nn(low, pick) - 1.0
                own_row[p] = jnp.sum(jnp.where(mine, value, 0.0), axis=0, keepdims=True).astype(jnp.int32)

        stages.append((0.1, send_places))
        stages += direct_stages(lambda p: sent.at[p], came, pairs[1], "dp", n, i, 0.2, lambda: None, 1.0)
        stages += direct_stages(lambda p: line.at[j], line, pairs[2], "mp", m, j, 0.3, lambda: None, 50.0)
        stages.append((1.5, use_places))
        run_stages(stages)

    vmem = pl.BlockSpec(memory_space=pltpu.VMEM)
    hbm = pl.BlockSpec(memory_space=pltpu.HBM)
    lines = max(16, -(-OWNER_BLOCKS // 8) * 8)
    results = pl.pallas_call(
        kernel,
        out_shape=[
            shape,
            jax.ShapeDtypeStruct((m, rows, D), BF),
            jax.ShapeDtypeStruct((total, 128), BF),
            jax.ShapeDtypeStruct((lines, block_words), jnp.int32),
            jax.ShapeDtypeStruct((n, 1, cap * share), jnp.int32),
        ],
        in_specs=[hbm] * 3 + [vmem] * 2,
        out_specs=[vmem] * 5,
        scratch_shapes=[
            pltpu.VMEM(mixer.shape, F32),
            pltpu.VMEM(lift.shape, F32),
            pltpu.VMEM(output.shape, F32),
            pltpu.VMEM((n, cap, block_words), jnp.int32),
            pltpu.VMEM((n, cap, block_words), jnp.int32),
            pltpu.SemaphoreType.DMA((3,)),
        ]
        + dma_sems(2 * max(n, m)) * 3,
        compiler_params=pltpu.CompilerParams(
            collective_id=0, has_side_effects=True, vmem_limit_bytes=60 << 20
        ),
        name="gather_char",
    )(mixer, lift, output, home.reshape(1, slots), places)
    return [shaper(results[0])] + list(results[1:])


def send_vectors(sent, to_live, share, project, upper, lower, output_line):
    n, m = lax.axis_size("dp"), lax.axis_size("mp")
    block = sent.shape[1]
    total = n * block
    kept = OWNER_BLOCKS * share
    made = [gather_shape([a], n) for a in (project, upper, lower)]
    made[0] = gather_shape([project], n)
    lead, line_rows, line_cols = output_line.shape
    aligned = line_rows % 16 == 0
    output_shape = (lead, n * line_rows, line_cols) if aligned else (n, lead, line_rows, line_cols)

    def kernel(sent, live, *refs):
        weights, line = refs[:3], refs[3]
        out, wides, output = refs[4], refs[5:8], refs[8]
        came, spread, *sems = refs[9:]
        pairs = [tuple(sems[2 * t : 2 * t + 2]) for t in range(8)]
        i, j = lax.axis_index("dp"), lax.axis_index("mp")
        greet({"dp": n, "mp": m}, {"dp": i, "mp": j})
        came[i] = sent[i]
        stages = []

        def make_spread():
            up = lax.broadcasted_iota(jnp.int32, (kept, 128), 0) // share
            up = (up == lax.broadcasted_iota(jnp.int32, (kept, 128), 1)).astype(BF)
            blocks = nt(up, live[...]).astype(BF)
            down = lax.broadcasted_iota(jnp.int32, (blocks.shape[1], total), 1) // share
            down = (down == lax.broadcasted_iota(jnp.int32, (blocks.shape[1], total), 0)).astype(BF)
            row = lax.broadcasted_iota(jnp.int32, (kept, total), 0) % share
            col = lax.broadcasted_iota(jnp.int32, (kept, total), 1) % share
            spread[...] = jnp.where(row == col, nn(blocks, down), 0.0).astype(BF)

        stages.append((0.4, make_spread))

        def compact(cols):
            out[j, :, cols] = nn(spread[...], came[:, :, cols].reshape(total, D // 2)).astype(BF)

        for half in range(2):
            cols = slice(half * (D // 2), (half + 1) * (D // 2))
            stages += direct_stages(
                lambda p, cols=cols: sent.at[p, :, cols], came, pairs[6 * half], "dp", n, i, 0.1 * half,
                functools.partial(compact, cols), 1.0 + half, cols,
            )
            stages += line_gather_stages(
                out, pairs[1 + 6 * half], "mp", m, j, 1.5 + 0.6 * half, 1.0, (slice(None), cols)
            )
        for t, (x, wide) in enumerate(zip(weights, wides)):
            own_of, put = gather_setup([x], wide)
            put(i)
            stages += pair_gather_stages(own_of, pairs[2 + t], "dp", n, i, 0.3, 2.0 * m + 0.5)
        if aligned:
            output_of = lambda d: output.at[:, pl.ds(pl.multiple_of(d * line_rows, 16), line_rows), :]
        else:
            output_of = lambda d: output.at[d]
        output_of(i)[...] = line[...]
        stages += pair_gather_stages(output_of, pairs[5], "dp", n, i, 0.3, 2.0 * m + 0.5)
        run_stages(stages)

    results = call_remote(
        kernel,
        "send_vectors",
        1,
        [jax.ShapeDtypeStruct((m, kept, D), BF)]
        + [shape for shape, _ in made]
        + [jax.ShapeDtypeStruct(output_shape, BF)],
        [pltpu.VMEM((n, block, D), BF), pltpu.VMEM((kept, total), BF)] + dma_sems(2 * max(n, m)) * 8,
        [sent, to_live, project, upper, lower, output_line],
    )
    output = results[4]
    if not aligned:
        output = output.transpose(1, 0, 2, 3)
    return (
        [results[0]]
        + [shaper(a) for (_, shaper), a in zip(made, results[1:4])]
        + [output.reshape(-1, line_cols)]
    )


def hidden_grads(part_two, hidden, cotangent, mixed, output, gain, grad_upper, grad_lower, roots):
    n, m = lax.axis_size("dp"), lax.axis_size("mp")
    share = part_two.shape[1]
    width = mixed.shape[2]
    made = [gather_shape([a], n) for a in roots]
    parts = [by_chip(grad_upper), by_chip(grad_lower)]

    def kernel(part, hidden_ref, cot, mix, out_mat, gain_ref, up, low, *refs):
        roots_in, refs = refs[: len(roots)], refs[len(roots) :]
        grad_hidden, grad_mixed, grad_output, gain_grad, up_sum, low_sum = refs[:6]
        roots_out, refs = refs[6 : 6 + len(roots)], refs[6 + len(roots) :]
        held, total, swapped, up_held, up_came, low_held, low_came, *sems = refs
        pairs = [tuple(sems[2 * t : 2 * t + 2]) for t in range(5 + len(roots))]
        i, j = lax.axis_index("dp"), lax.axis_index("mp")
        greet({"dp": n, "mp": m}, {"dp": i, "mp": j})
        stages = []
        for h, cut in enumerate(halves(share)):
            stages += line_part_stages(
                part, held, total, pairs[(0, 4 + len(roots))[h]], "mp", m, j, 0.05 * h, 6.0, 70.0 + 0.1 * h, cut
            )
        stages += pair_part_stages(up, up_held, up_came, up_sum, pairs[1], "dp", n, i, 0.1, 1.0)
        stages += pair_part_stages(low, low_held, low_came, low_sum, pairs[2], "dp", n, i, 0.1, 1.0)
        for t, (x, out) in enumerate(zip(roots_in, roots_out)):
            own_of, put = gather_setup([x], out)
            put(i)
            stages += pair_gather_stages(own_of, pairs[4 + t], "dp", n, i, 2.0, 72.5)

        def back():
            mine = pl.ds(pl.multiple_of(j * share, share), share)
            hidden_own = hidden_ref[mine, :]
            scale = rms_scale(hidden_own)
            grad = total[...]
            whole_grad = cot[mine, :].astype(F32) + norm_back(hidden_own, scale, gain_ref[...], grad)
            grad_hidden[...] = whole_grad
            gain_grad[...] = jnp.sum(hidden_own * scale * grad, axis=0, keepdims=True)
            attend = whole_grad.astype(BF)
            for p in range(m):
                swapped[p] = nt(attend, out_mat[p * width : (p + 1) * width, :]).astype(BF)
            grad_mixed[j] = swapped[j]

        def output_grad():
            mine = pl.ds(pl.multiple_of(j * share, share), share)
            attend = grad_hidden[...].astype(BF)
            for p in range(m):
                grad_output[p * width : (p + 1) * width, :] = tn(mix[p, mine, :], attend).astype(BF)

        stages += [(71.0, back), (73.0, output_grad)]
        stages += direct_stages(
            lambda p: swapped.at[p], grad_mixed, pairs[3], "mp", m, j, 72.0, lambda: None, 75.0
        )
        run_stages(stages)

    block = lambda a: pltpu.VMEM(a.shape[:1] + a.shape[2:], BF)
    results = call_remote(
        kernel,
        "hidden_grads",
        4,
        [
            jax.ShapeDtypeStruct((share, D), F32),
            jax.ShapeDtypeStruct((m, share, width), BF),
            jax.ShapeDtypeStruct(output.shape, BF),
            jax.ShapeDtypeStruct((1, D), F32),
            jax.ShapeDtypeStruct(parts[0].shape[2:], F32),
            jax.ShapeDtypeStruct(parts[1].shape[2:], F32),
        ]
        + [shape for shape, _ in made],
        [
            pltpu.VMEM((2, m, share, D), BF),
            pltpu.VMEM((share, D), F32),
            pltpu.VMEM((m, share, width), BF),
            block(parts[0]),
            block(parts[0]),
            block(parts[1]),
            block(parts[1]),
        ]
        + dma_sems(2 * max(n, m)) * (5 + len(roots)),
        [part_two, hidden, cotangent, mixed, output, gain.reshape(1, D)] + parts + roots,
    )
    return list(results[:6]) + [shaper(a) for (_, shaper), a in zip(made, results[6:])]


def stream_grads(part_one, stream, grad_hidden, gain, own_row, sums, grad_project, grad_output):
    n, m = lax.axis_size("dp"), lax.axis_size("mp")
    share = part_one.shape[1]
    block = own_row.shape[2]
    total_words = n * block
    words = share * m
    parts = [by_chip(grad_project), by_chip(grad_output)]
    chunk = lambda a: jax.ShapeDtypeStruct((1,) + a.shape[-2:], F32)
    made = [gather_shape([chunk(a)], n) for a in (sums[0], sums[1], parts[0], parts[1])]

    def kernel(part, stream_ref, hidden_ref, gain_ref, row_ref, up, low, project, output, *refs):
        out, gain_grad, came, up_out, low_out, project_out, output_out = refs[:7]
        (held, total, project_sum, output_sum, line_held, picked, hits,
         p_held, p_came, o_held, o_came, *sems) = refs[7:]
        pairs = [tuple(sems[2 * t : 2 * t + 2]) for t in range(13)]
        i, j = lax.axis_index("dp"), lax.axis_index("mp")
        greet({"dp": n, "mp": m}, {"dp": i, "mp": j})
        stages = []
        for h, cut in enumerate(halves(share)):
            stages += line_part_stages(
                part, held, total, pairs[(0, 12)[h]], "mp", m, j, 0.05 * h, 6.0, 70.0 + 0.1 * h, cut
            )
        stages += pair_part_stages(project, p_held, p_came, project_sum.at[0], pairs[1], "dp", n, i, 0.1, 1.0)
        stages += pair_part_stages(output, o_held, o_came, output_sum.at[0], pairs[2], "dp", n, i, 0.1, 1.0)
        up_of, put_up = gather_setup([up], up_out)
        low_of, put_low = gather_setup([low], low_out)
        put_up(i)
        put_low(i)
        stages += pair_gather_stages(up_of, pairs[3], "dp", n, i, 2.0, 71.9)
        stages += pair_gather_stages(low_of, pairs[4], "dp", n, i, 2.0, 71.9)

        def back():
            mine = pl.ds(pl.multiple_of(j * share, share), share)
            stream_own = stream_ref[mine, :]
            scale = rms_scale(stream_own)
            grad = total[...]
            out[j] = (hidden_ref[...] + norm_back(stream_own, scale, gain_ref[...], grad)).astype(BF)
            gain_grad[...] = jnp.sum(stream_own * scale * grad, axis=0, keepdims=True)

        stages.append((71.0, back))
        for half in range(2):
            cols = slice(half * (D // 2), (half + 1) * (D // 2))
            stages += [
                (when if when < 90 else 199.0, run)
                for when, run in line_gather_stages(
                    out, pairs[5 + 5 * half], "mp", m, j, 72.0 + 0.05 * half, 0.1, (slice(None), cols)
                )
            ]
        project_of, put_project = gather_setup([project_sum], project_out)
        output_of, put_output = gather_setup([output_sum], output_out)

        def put_sums():
            put_project(i)
            line_held[j] = output_sum[0].astype(BF)

        target = i // (n // m)

        def line_send():
            @pl.when(j != target)
            def _():
                remote(line_held.at[j], line_held.at[j], pairs[7], j, "mp", target).start()

        def line_done():
            @pl.when(j != target)
            def _():
                remote(line_held.at[j], line_held.at[j], pairs[7], j, "mp", target).wait_send()

            @pl.when(j == target)
            def _():
                for p in range(m):

                    @pl.when(j != p)
                    def _(p=p):
                        remote(line_held.at[p], line_held.at[p], pairs[7], p, "mp", target).wait_recv()

                summed = line_held[0].astype(F32)
                for p in range(1, m):
                    summed = summed + line_held[p].astype(F32)
                output_sum[0] = summed

            put_output(i)

        stages = [(60.0 if when == 80.0 else when, run) for when, run in stages]
        stages.append((72.01, put_sums))
        stages += [
            (when, run)
            for when, run in zip(
                (72.02, 72.25, 198.0),
                [run for _, run in pair_gather_stages(project_of, pairs[6], "dp", n, i, 0, 0)],
            )
        ]
        late_line = 72.0 + 0.1 * 2 * m
        stages += [(72.03, line_send), (late_line + 0.01, line_done)]
        stages += [
            (when, run)
            for when, run in zip(
                (late_line + 0.02, 81.5, 198.5),
                [run for _, run in pair_gather_stages(output_of, pairs[8], "dp", n, i, 0, 0)],
            )
        ]

        def make_hits():
            lane = lax.broadcasted_iota(jnp.int32, (block, 128), 1).astype(F32)
            ones = jnp.ones((1, 128), BF)
            for p in range(n):
                place = row_ref[p].astype(F32) + 1.0
                high = jnp.floor(place * (1.0 / 32.0))
                low = place - high * 32.0
                col = tn(high.astype(BF), ones) * 32.0 + tn(low.astype(BF), ones) - 1.0
                for t in range(words // 128):
                    hits[p * block : (p + 1) * block, t * 128 : (t + 1) * 128] = (
                        col == lane + 128.0 * t
                    ).astype(BF)

        stages.append((2.5, make_hits))

        def pick(half):
            cols = slice(half * (D // 2), (half + 1) * (D // 2))
            rows = nn(hits[...], out[:, :, cols].reshape(words, D // 2)).astype(BF)
            picked[:, :, cols] = rows.reshape(n, block, D // 2)
            for d in range(1, n):
                peer = lax.rem(i + d, n)
                remote(
                    picked.at[peer, :, cols], came.at[i, :, cols], pairs[9 + 2 * half], d, "dp", peer
                ).start()
            came[i, :, cols] = picked[i, :, cols]

        for half in range(2):
            stages.append((72.011 + 0.1 * (m - 1) + 0.05 * half, functools.partial(pick, half)))

        def place():
            for half in range(2):
                cols = slice(half * (D // 2), (half + 1) * (D // 2))
                for d in range(1, n):
                    remote(
                        picked.at[i, :, cols], came.at[i, :, cols], pairs[9 + 2 * half], d, "dp", i
                    ).wait()

        stages.append((82.0, place))
        run_stages(stages)

    held_of = lambda a: pltpu.VMEM(a.shape[:1] + a.shape[2:], BF)
    results = call_remote(
        kernel,
        "stream_grads",
        6,
        [
            jax.ShapeDtypeStruct((m, share, D), BF),
            jax.ShapeDtypeStruct((1, D), F32),
            jax.ShapeDtypeStruct((n, block, D), BF),
        ]
        + [shape for shape, _ in made],
        [
            pltpu.VMEM((2, m, share, D), BF),
            pltpu.VMEM((share, D), F32),
            pltpu.VMEM((1,) + parts[0].shape[2:], F32),
            pltpu.VMEM((1,) + parts[1].shape[2:], F32),
            pltpu.VMEM((m,) + parts[1].shape[2:], BF),
            pltpu.VMEM((n, block, D), BF),
            pltpu.VMEM((total_words, words), BF),
            held_of(parts[0]),
            held_of(parts[0]),
            held_of(parts[1]),
            held_of(parts[1]),
        ]
        + dma_sems(2 * max(n, m)) * 13,
        [
            part_one,
            stream,
            grad_hidden,
            gain.reshape(1, D),
            own_row,
            sums[0][None],
            sums[1][None],
        ]
        + parts,
    )
    return list(results[:3]) + [shaper(a) for (_, shaper), a in zip(made, results[3:])]


def local(
    word_inputs,
    character_embeddings,
    cotangent,
    char_count,
    word_place,
    block_home,
    documents,
    char_gain,
    word_gains,
    char_mixer,
    char_mixer_left,
    char_mixer_right,
    char_mixer_left_root,
    char_mixer_right_root,
    char_lift,
    char_lift_left,
    char_lift_right,
    char_lift_left_root,
    char_lift_right_root,
    word_project,
    word_project_left,
    word_project_right,
    word_project_left_root,
    word_project_right_root,
    word_output,
    word_output_left,
    word_output_right,
    word_output_left_root,
    word_output_right_root,
    feed_upper,
    feed_upper_left,
    feed_upper_right,
    feed_upper_left_root,
    feed_upper_right_root,
    feed_lower,
    feed_lower_left,
    feed_lower_right,
    feed_lower_left_root,
    feed_lower_right_root,
):
    slot_count, share_rows = (character_embeddings.shape[0], character_embeddings.shape[1])
    peer_count = lax.axis_size("dp")
    part_count = lax.axis_size("mp")
    owner_index = lax.axis_index("dp")
    words_dev = word_inputs.shape[0] * word_inputs.shape[1]
    position = jnp.stack([owner_index, lax.axis_index("mp")]).astype(jnp.int32)

    char_whole, output_line, live, live_place, own_row = gather_char(
        char_mixer, char_lift, word_output, block_home, word_place
    )
    word_vectors, kept, pooled, msum = char_forward(
        character_embeddings, block_home, char_count, char_gain, char_whole, peer_count
    )
    live_vectors, project_mat, upper_mat, lower_mat, output_mat = send_vectors(
        word_vectors.reshape(peer_count, -1, D),
        live,
        share_rows,
        word_project.reshape((3,) + word_project.shape[2:]),
        feed_upper,
        feed_lower,
        output_line,
    )
    stream, normed_one, qkv, probs, mixed = word_forward(
        live_vectors,
        live_place,
        word_inputs.reshape(words_dev, D),
        documents,
        word_gains[0],
        project_mat,
    )
    mixed_all, mixer_root, lift_root = exchange(
        "gather_mixed",
        3,
        [
            ("line_gather", "mp", [mixed]),
            ("gather", "dp", [char_mixer_right_root]),
            ("gather", "dp", [char_lift_right_root]),
        ],
    )
    flat_cotangent = cotangent.reshape(words_dev, D)
    hidden, feed_part, part_two, grad_upper, grad_lower = feed(
        mixed_all, output_mat, stream, flat_cotangent, word_gains[1], upper_mat, lower_mat
    )
    shares = (part_count, words_dev // part_count, D)
    grad_hidden, grad_mixed, grad_output_mat, gain_two, part_upper, part_lower, *word_roots = hidden_grads(
        part_two.reshape(shares),
        hidden,
        flat_cotangent,
        mixed_all,
        output_mat,
        word_gains[1],
        grad_upper,
        grad_lower,
        [
            word_project_right_root.reshape((3,) + word_project_right_root.shape[2:]),
            word_output_right_root,
            feed_upper_right_root,
            feed_lower_right_root,
        ],
    )
    project_root, output_root, upper_root, lower_root = word_roots
    part_one, grad_project = word_backward(
        probs, qkv, grad_mixed.reshape(words_dev, -1), normed_one, project_mat
    )
    grad_words, gain_one, grad_vectors, sum_upper, sum_lower, sum_project, sum_output = stream_grads(
        part_one.reshape(shares),
        stream,
        grad_hidden,
        word_gains[0],
        own_row,
        (part_upper, part_lower),
        grad_project,
        grad_output_mat,
    )
    grad_vectors, feed_part = lax.optimization_barrier((grad_vectors, feed_part))
    feed_total = lax.psum(feed_part, "mp")
    char_embeds_gradient, char_grads, grad_char_gain, grad_stream = char_backward(
        character_embeddings, block_home, char_count, char_gain, char_whole, kept, pooled, msum,
        grad_vectors.reshape(-1, share_rows, D),
        grad_words,
        peer_count,
    )
    word_sums = (sum_project, sum_output, sum_upper, sum_lower)
    char_sums, small_sums = sum_char_grads(
        char_grads, (grad_char_gain, gain_one, gain_two), word_sums, word_output.shape[1] * peer_count
    )
    parameter_count = (
        sum(
            part_count * w.size * peer_count
            for w in (word_project, word_output, feed_upper, feed_lower)
        )
        + peer_count * (char_mixer.size + char_lift.size)
        + char_gain.size
        + word_gains.size
    )
    flat = lambda a: a.reshape((-1,) + a.shape[-2:])
    results = shampoo(
        0.5 * math.sqrt(parameter_count),
        position,
        char_sums,
        small_sums,
        char_gain,
        word_gains,
        word_sums,
        hidden,
        feed_total,
        [
            tuple(flat(a) for a in group[:4]) + (group[4],)
            for group in (
                (char_mixer, char_mixer_left, char_mixer_right, char_mixer_left_root, mixer_root),
                (char_lift, char_lift_left, char_lift_right, char_lift_left_root, lift_root),
                (word_project, word_project_left, word_project_right, word_project_left_root, project_root),
                (word_output, word_output_left, word_output_right, word_output_left_root, output_root),
                (feed_upper, feed_upper_left, feed_upper_right, feed_upper_left_root, upper_root),
                (feed_lower, feed_lower_left, feed_lower_right, feed_lower_left_root, lower_root),
            )
        ],
    )
    norm, gain_grad, gains_grad, gain_new, gains_new, block_out = results[:6]
    stepped = []
    for t, group in enumerate(
        (
            (char_mixer, char_mixer_left, char_mixer_right),
            (char_lift, char_lift_left, char_lift_right),
            (word_project, word_project_left, word_project_right),
            (word_output, word_output_left, word_output_right),
            (feed_upper, feed_upper_left, feed_upper_right),
            (feed_lower, feed_lower_left, feed_lower_right),
        )
    ):
        master, left, right = group
        stepped += [
            a.reshape(b.shape)
            for a, b in zip(results[6 + 5 * t : 11 + 5 * t], (master, left, right, master, master))
        ]
    return (
        block_out.reshape(word_inputs.shape),
        grad_stream.reshape(word_inputs.shape),
        char_embeds_gradient,
        gain_grad[0],
        gains_grad,
        gain_new[0],
        gains_new,
        norm[0, 0],
        *stepped,
    )


def solution(mesh):
    placed = (
        P("dp", None, None),
        P("dp", "mp", None, None),
        P("dp", None, None),
        P("dp", "mp"),
        P("dp", None),
        P("dp"),
        P("dp", None),
        P(),
        P(),
        P(None, "dp", None),
        P(None, "dp", None),
        P(None, "dp", None),
        P(None, "dp", None),
        P(None, "dp", None),
        P(None, "dp", None),
        P(None, "dp", None),
        P(None, "dp", None),
        P(None, "dp", None),
        P(None, "dp", None),
        P(None, "mp", "dp", None),
        P(None, "mp", "dp", None),
        P(None, "mp", "dp", None),
        P(None, "mp", "dp", None),
        P(None, "mp", "dp", None),
        P("mp", "dp", None),
        P("mp", "dp", None),
        P("mp", "dp", None),
        P("mp", "dp", None),
        P("mp", "dp", None),
        P("mp", "dp", None),
        P("mp", "dp", None),
        P("mp", "dp", None),
        P("mp", "dp", None),
        P("mp", "dp", None),
        P("mp", "dp", None),
        P("mp", "dp", None),
        P("mp", "dp", None),
        P("mp", "dp", None),
        P("mp", "dp", None),
    )
    return jax.shard_map(
        local,
        mesh=mesh,
        in_specs=placed,
        out_specs=(
            P("dp", None, None),
            P("dp", None, None),
            P("dp", "mp", None, None),
            P(),
            P(),
            P(),
            P(),
            P(),
            P(None, "dp", None),
            P(None, "dp", None),
            P(None, "dp", None),
            P(None, "dp", None),
            P(None, "dp", None),
            P(None, "dp", None),
            P(None, "dp", None),
            P(None, "dp", None),
            P(None, "dp", None),
            P(None, "dp", None),
            P(None, "mp", "dp", None),
            P(None, "mp", "dp", None),
            P(None, "mp", "dp", None),
            P(None, "mp", "dp", None),
            P(None, "mp", "dp", None),
            P("mp", "dp", None),
            P("mp", "dp", None),
            P("mp", "dp", None),
            P("mp", "dp", None),
            P("mp", "dp", None),
            P("mp", "dp", None),
            P("mp", "dp", None),
            P("mp", "dp", None),
            P("mp", "dp", None),
            P("mp", "dp", None),
            P("mp", "dp", None),
            P("mp", "dp", None),
            P("mp", "dp", None),
            P("mp", "dp", None),
            P("mp", "dp", None),
        ),
        check_vma=False,
    )
```

```python
import functools
import math

import jax
import jax.numpy as jnp
from jax import lax
from jax.experimental import pallas as pl
from jax.experimental.pallas import tpu as pltpu
from jax.sharding import PartitionSpec as P

D = 512
HD = 64
FF = 2048
CHAR_BLOCK_WIDTH = 256
OWNER_BLOCKS = 10
decay_rate = 0.5
learn_rate = 1.0
gain_rate = 0.4
negative_big = -1e30

CW = 256
CHEADS = 4
CHD = 64
SPOTS = 16
KEPT = 3 * CW + CHEADS * 128 + CW
epsilon = 1e-05
BF = jnp.bfloat16
F32 = jnp.float32


def nn(a, b):
    return lax.dot_general(a, b, (((1,), (0,)), ((), ())), preferred_element_type=F32)


def nt(a, b):
    return lax.dot_general(a, b, (((1,), (1,)), ((), ())), preferred_element_type=F32)


def tn(a, b):
    return lax.dot_general(a, b, (((0,), (0,)), ((), ())), preferred_element_type=F32)


GROUPS = 4


def char_classes(share):
    listed = [(1, 4, 32), (2, 8, 16), (4, 16, 8)]
    return [(c, p, w, GROUPS // (share // w)) for c, p, w in listed if w <= share]


def order_matrix(places, words):
    row = lax.broadcasted_iota(jnp.int32, (128, SPOTS * words), 0)
    col = lax.broadcasted_iota(jnp.int32, (128, SPOTS * words), 1)
    return ((row % words) * SPOTS + row // words == col).astype(BF)


def back_matrix(places, words):
    row = lax.broadcasted_iota(jnp.int32, (SPOTS * words, 128), 0)
    col = lax.broadcasted_iota(jnp.int32, (SPOTS * words, 128), 1)
    return ((col % words) * SPOTS + col // words == row).astype(BF)


def head_stack(rows, scale):
    lane = lax.broadcasted_iota(jnp.int32, (1, CW), 1) // CHD
    return jnp.concatenate(
        [rows * jnp.where(lane == h, scale, 0.0).astype(BF) for h in range(CHEADS)], axis=0
    )


def char_forward_kernel(
    classes, home, first, x_in, counts_in, gain_ref, mats_ref, *refs
):
    orders, refs = refs[-len(classes) :], refs[: -len(classes)]
    vec_ref, kept_out, pooled_ref, msum_ref, kept, sumx, x_ref, vec, count_ref, kind, ids, batch_kind, target, taken, sems, x_sems = refs
    slots, share = count_ref.shape[:2]
    batches = plan_batches(classes, home, first, kind, ids, batch_kind)

    def load_x(slot):
        return pltpu.make_async_copy(x_in.at[slot], x_ref.at[slot], x_sems.at[slot])

    def begin(number, carry):
        for which, places, words, per in classes:

            @pl.when(batch_kind[number] == which)
            def _(per=per):
                for t in range(per):
                    slot = ids[number * GROUPS + t]

                    @pl.when(slot >= 0)
                    def _(slot=slot):
                        load_x(slot).start()

        return carry

    lax.fori_loop(0, batches, begin, 0)
    count_ref[...] = spread_counts(counts_in[...]).reshape(count_ref.shape)
    for (_, places, words, _), order_ref in zip(classes, orders):
        order_ref[...] = order_matrix(places, words)
    sumx[...] = jnp.zeros_like(sumx)
    msum_ref[...] = jnp.zeros_like(msum_ref)

    def save(slot, rows):
        return pltpu.make_async_copy(
            kept.at[slot, pl.ds(0, rows)], kept_out.at[slot, pl.ds(0, rows)], sems.at[slot]
        )

    def block(places, words, per, order_ref, number):
        picked = [ids[number * GROUPS + t] for t in range(per)]
        for slot in picked:

            @pl.when(slot >= 0)
            def _(slot=slot):
                load_x(slot).wait()

        chosen = [jnp.where(c < 0, picked[0], c) for c in picked]
        groups = [(c, g) for c in chosen for g in range(share // words)]
        cnts = [count_ref[c, pl.ds(g * words, words), :] for c, g in groups]
        xs = [
            nn(order_ref[...], x_ref[c, pl.ds(g * words * SPOTS, words * SPOTS), :]) for c, g in groups
        ]
        normed = jnp.concatenate(
            [
                (
                    x * lax.rsqrt(jnp.mean(x * x, axis=-1, keepdims=True) + epsilon) * gain_ref[...]
                ).astype(BF)
                for x in xs
            ],
            axis=0,
        )
        qkv = nn(normed, mats_ref[:, : 3 * CW]).astype(BF)
        place = lax.broadcasted_iota(jnp.int32, (places, words, CW), 0).astype(F32)
        lane = lax.broadcasted_iota(jnp.int32, (words, CHEADS * 128), 1) % 128
        word = lax.broadcasted_iota(jnp.int32, (words, CHEADS * 128), 0)
        mine = lane % words == word
        spot = (lane // words).astype(F32)
        head_row = lax.broadcasted_iota(jnp.int32, (CHEADS * 128, CW), 0) // 128
        head_col = lax.broadcasted_iota(jnp.int32, (CHEADS * 128, CW), 1) // CHD
        same_head = (head_row == head_col).astype(BF)
        far = lax.broadcasted_iota(jnp.int32, (places, words, CHEADS * 128), 0).astype(F32)
        scores = []
        for t in range(GROUPS):
            rows = qkv[t * 128 : (t + 1) * 128]
            scores.append(nt(rows[:, CW : 2 * CW], head_stack(rows[:, :CW], 1.0 / math.sqrt(CHD))))
        sums = []
        for t in range(GROUPS):
            shown = place < jnp.concatenate([cnts[t], cnts[t]], axis=1)[None]
            sums.append(jnp.sum(jnp.where(shown, xs[t].reshape(places, words, CW), 0.0), axis=0))
        probs = []
        for t in range(GROUPS):
            cnt4 = jnp.concatenate([cnts[t]] * CHEADS, axis=1)
            s = jnp.where(far < cnt4[None], scores[t].reshape(places, words, CHEADS * 128), -1e30)
            e = jnp.exp(s - jnp.max(s, axis=0)[None])
            r = jnp.where(mine & (spot < cnt4), 1.0 / jnp.sum(e, axis=0), 0.0)
            probs.append((e * r[None]).astype(BF).reshape(128, CHEADS * 128))
        columns = [nn(p, same_head) for p in probs]
        for t, (c, g) in enumerate(groups):
            rows = qkv[t * 128 : (t + 1) * 128]
            at = pl.ds(g * 128, 128)
            kept[c, at, : 3 * CW] = rows
            kept[c, at, 3 * CW : 3 * CW + CHEADS * 128] = probs[t]
            kept[c, at, 3 * CW + CHEADS * 128 :] = columns[t].astype(BF)
            own = pl.ds(pl.multiple_of(c * share + g * words, words), words)
            msum_ref[own, :] = jnp.sum(
                (columns[t] * rows[:, 2 * CW :].astype(F32)).reshape(places, words, CW), axis=0
            )
            sumx[own, :] = sums[t]
        for t in range(per):
            slot = ids[number * GROUPS + t]

            @pl.when(slot >= 0)
            def _(slot=slot):
                save(slot, share * places).start()

    def batch(number, carry):
        for (which, places, words, per), order_ref in zip(classes, orders):
            pl.when(batch_kind[number] == which)(
                functools.partial(block, places, words, per, order_ref, number)
            )
        return carry

    lax.fori_loop(0, batches, batch, 0)
    cnt2 = jnp.concatenate([count_ref[...].reshape(slots * share, 128)] * 2, axis=1)
    summed = sumx[...] + nn(msum_ref[...].astype(BF), mats_ref[:, 3 * CW : 4 * CW])
    pooled = (summed / cnt2).astype(BF)
    pooled_ref[...] = pooled
    vec[...] = nn(pooled, mats_ref[:, 4 * CW :]).astype(BF)
    plan_targets(home, target, taken, taken.shape[0])
    vec_ref[...] = jnp.zeros_like(vec_ref)

    def put(slot, carry):
        @pl.when(target[slot] >= 0)
        def _():
            vec_ref[target[slot]] = vec[pl.ds(pl.multiple_of(slot * share, share), share), :]

        return carry

    lax.fori_loop(0, slots, put, 0)

    def finish(slot, carry):
        for which, places, words, per in classes:

            @pl.when(kind[slot] == which)
            def _(places=places):
                save(slot, share * places).wait()

        return carry

    lax.fori_loop(0, slots, finish, 0)


def plan_batches(classes, home, count, kind, ids, batch_kind):
    slots = home.shape[0]
    coarse = classes[0][0] == 1

    def sort(slot, carry):
        places = count[slot, 0]
        which = jnp.where(places <= 8, 2, 4)
        if coarse:
            which = jnp.where(places <= 4, 1, which)
        kind[slot] = jnp.where(home[slot] >= 0, which, 0)
        for t in range(GROUPS):
            ids[slot * GROUPS + t] = -1
        return carry

    lax.fori_loop(0, slots, sort, 0)
    batch = jnp.int32(0)
    for which, _, _, per in classes:

        def take(slot, carry):
            batch, place = carry
            hit = kind[slot] == which

            @pl.when(hit)
            def _():
                ids[batch * GROUPS + place] = slot
                batch_kind[batch] = which

            place = jnp.where(hit, place + 1, place)
            full = place == per
            return jnp.where(full, batch + 1, batch), jnp.where(full, 0, place)

        batch, place = lax.fori_loop(0, slots, take, (batch, jnp.int32(0)))
        batch = jnp.where(place > 0, batch + 1, batch)
    return batch


def plan_targets(home, target, taken, owners):
    slots = home.shape[0]
    cap = -(-slots // owners)

    def clear(owner, carry):
        taken[owner] = 0
        return carry

    lax.fori_loop(0, owners, clear, 0)

    def take(slot, carry):
        owner = jnp.maximum(home[slot], 0)
        live = home[slot] >= 0
        target[slot] = jnp.where(live, owner * cap + taken[owner], -1)
        taken[owner] = taken[owner] + jnp.where(live, 1, 0)
        return carry

    lax.fori_loop(0, slots, take, 0)


def spread_counts(count):
    slots, share = count.shape
    row = lax.broadcasted_iota(jnp.int32, (slots * share, slots), 0) // share
    pick = (row == lax.broadcasted_iota(jnp.int32, (slots * share, slots), 1)).astype(BF)
    wide = nn(pick, count.astype(F32).astype(BF))
    mine = lax.broadcasted_iota(jnp.int32, (slots * share, share), 0) % share
    mine = mine == lax.broadcasted_iota(jnp.int32, (slots * share, share), 1)
    return nn(jnp.where(mine, wide, 0.0).astype(BF), jnp.ones((share, 128), BF))


def char_call(kernel, name, inputs, scalars, outs, scratch, in_hbm, out_hbm, flops, limit):
    vmem = pl.BlockSpec(memory_space=pltpu.VMEM)
    smem = pl.BlockSpec(memory_space=pltpu.SMEM)
    hbm = pl.BlockSpec(memory_space=pltpu.HBM)
    return pl.pallas_call(
        kernel,
        in_specs=[smem] * len(scalars) + [hbm if t in in_hbm else vmem for t in range(len(inputs))],
        out_specs=[hbm if t in out_hbm else vmem for t in range(len(outs))],
        out_shape=outs,
        scratch_shapes=scratch,
        cost_estimate=pl.CostEstimate(flops=flops, bytes_accessed=60 << 20, transcendentals=0),
        compiler_params=pltpu.CompilerParams(vmem_limit_bytes=limit << 20),
        name=name,
    )(*scalars, *inputs)


def plan_scratch(slots, share, owners):
    return [
        pltpu.VMEM((slots, share, 128), F32),
        pltpu.SMEM((slots,), jnp.int32),
        pltpu.SMEM((slots * GROUPS,), jnp.int32),
        pltpu.SMEM((slots,), jnp.int32),
        pltpu.SMEM((slots,), jnp.int32),
        pltpu.SMEM((owners,), jnp.int32),
    ]


def char_forward(x, home, counts, gain, mats, owners):
    slots, share = x.shape[:2]
    total = -(-slots // owners) * owners
    classes = char_classes(share)
    rows = share * SPOTS
    orders = [pltpu.VMEM((128, SPOTS * c[2]), BF) for c in classes]
    words_all = slots * share
    return char_call(
        functools.partial(char_forward_kernel, classes),
        "char_forward",
        [x.reshape(slots, rows, CW), counts, gain.reshape(1, CW), mats],
        (home, counts),
        [
            jax.ShapeDtypeStruct((total, share, D), BF),
            jax.ShapeDtypeStruct((slots, rows, KEPT), BF),
            jax.ShapeDtypeStruct((words_all, CW), BF),
            jax.ShapeDtypeStruct((words_all, CW), F32),
        ],
        [
            pltpu.VMEM((slots, rows, KEPT), BF),
            pltpu.VMEM((words_all, CW), F32),
            pltpu.VMEM((slots, rows, CW), BF),
            pltpu.VMEM((words_all, D), BF),
        ]
        + plan_scratch(slots, share, owners)
        + [pltpu.SemaphoreType.DMA((slots,))] * 2
        + orders,
        (0,),
        (1,),
        slots * rows * CW * CW * 16,
        60,
    )


def char_backward_kernel(
    classes, home, first, x_in, counts_in, kept_in, gv_ref, pooled_ref, msum_ref, gain_ref, mats_ref, stream_in, *refs
):
    backs, refs = refs[-len(classes) :], refs[: -len(classes)]
    orders, refs = refs[-len(classes) :], refs[: -len(classes)]
    dx_out, grads_ref, dgain_ref, stream_out, x_ref, kept, dx_ref, gp_all, gm_all, dqkv_sum, gv_all, count_ref = refs[:12]
    kind, ids, batch_kind, target, taken, x_sems, kept_sems, dx_sems, stream_sem = refs[12:]
    slots, share = count_ref.shape[:2]
    batches = plan_batches(classes, home, first, kind, ids, batch_kind)

    def load_x(slot):
        return pltpu.make_async_copy(x_in.at[slot], x_ref.at[slot], x_sems.at[slot])

    def load_kept(slot, rows):
        return pltpu.make_async_copy(
            kept_in.at[slot, pl.ds(0, rows)], kept.at[slot, pl.ds(0, rows)], kept_sems.at[slot]
        )

    def save(slot):
        return pltpu.make_async_copy(dx_ref.at[slot], dx_out.at[slot], dx_sems.at[slot])

    def begin(number, carry):
        for which, places, words, per in classes:

            @pl.when(batch_kind[number] == which)
            def _(places=places, per=per):
                for t in range(per):
                    slot = ids[number * GROUPS + t]

                    @pl.when(slot >= 0)
                    def _(slot=slot):
                        load_x(slot).start()
                        load_kept(slot, share * places).start()

        return carry

    lax.fori_loop(0, batches, begin, 0)
    stream_copy = pltpu.make_async_copy(stream_in, stream_out, stream_sem.at[0])
    stream_copy.start()

    count_ref[...] = spread_counts(counts_in[...]).reshape(count_ref.shape)
    for (_, places, words, _), order_ref, back_ref in zip(classes, orders, backs):
        order_ref[...] = order_matrix(places, words)
        back_ref[...] = back_matrix(places, words)
    plan_targets(home, target, taken, taken.shape[0])

    def take(slot, carry):
        here = pl.ds(pl.multiple_of(slot * share, share), share)

        @pl.when(target[slot] >= 0)
        def _():
            gv_all[here, :] = gv_ref[target[slot]]

        @pl.when(target[slot] < 0)
        def _():
            gv_all[here, :] = jnp.zeros((share, D), BF)

        return carry

    lax.fori_loop(0, slots, take, 0)
    gv = gv_all[...]
    cnt2 = jnp.concatenate([count_ref[...].reshape(slots * share, 128)] * 2, axis=1)
    gp = nt(gv, mats_ref[:, 4 * CW :]) / cnt2
    gp_all[...] = gp
    gpb = gp.astype(BF)
    gm_all[...] = nt(gpb, mats_ref[:, 3 * CW : 4 * CW]).astype(BF).astype(F32)
    grads_ref[:, 4 * CW :] = tn(pooled_ref[...], gv).astype(BF)
    grads_ref[:, 3 * CW : 4 * CW] = tn(msum_ref[...].astype(BF), gpb).astype(BF)
    dqkv_sum[...] = jnp.zeros_like(dqkv_sum)
    dgain_ref[...] = jnp.zeros_like(dgain_ref)

    def block(places, words, per, order_ref, back_ref, number):
        picked = [ids[number * GROUPS + t] for t in range(per)]
        chosen = [jnp.where(c < 0, picked[0], c) for c in picked]
        weights = [jnp.where(c < 0, 0.0, 1.0) for c in picked]
        targets = [jnp.where(c < 0, slots, c) for c in picked]
        for slot in picked:

            @pl.when(slot >= 0)
            def _(slot=slot):
                load_x(slot).wait()
                load_kept(slot, share * places).wait()

        groups = [
            (c, g, weight, target)
            for c, weight, target in zip(chosen, weights, targets)
            for g in range(share // words)
        ]
        gain = gain_ref[...]
        eighth = 1.0 / math.sqrt(CHD)
        place = lax.broadcasted_iota(jnp.int32, (places, words, CW), 0).astype(F32)
        word_grads = []
        row_grads = []
        out_grads = []
        for t, (c, g, weight, _) in enumerate(groups):
            mine = pl.ds(pl.multiple_of(c * share + g * words, words), words)
            cnt = count_ref[c, pl.ds(g * words, words), :]
            shown = place < jnp.concatenate([cnt, cnt], axis=1)[None]
            word_grads.append(gm_all[mine, :] * weight)
            out_grads.append(jnp.where(shown, (gp_all[mine, :] * weight)[None], 0.0).reshape(128, CW))
            row_grads.append(
                jnp.where(shown, word_grads[t][None], 0.0).reshape(128, CW).astype(BF)
            )
        at = [pl.ds(g * 128, 128) for _, g, _, _ in groups]
        queries = [kept[c, at[t], :CW] for t, (c, *_) in enumerate(groups)]
        keys = [kept[c, at[t], CW : 2 * CW] for t, (c, *_) in enumerate(groups)]
        products = [
            nt(kept[c, at[t], 2 * CW : 3 * CW], head_stack(row_grads[t], 1.0))
            for t, (c, *_) in enumerate(groups)
        ]
        scores = []
        for t, (c, *_) in enumerate(groups):
            p = kept[c, at[t], 3 * CW : 3 * CW + CHEADS * 128].astype(F32)
            p3 = p.reshape(places, words, CHEADS * 128)
            u = p3 * products[t].reshape(places, words, CHEADS * 128)
            scores.append((u - p3 * jnp.sum(u, axis=0)[None]).astype(BF).reshape(128, CHEADS * 128))
        xs = [
            nn(order_ref[...], x_ref[c, pl.ds(g * words * SPOTS, words * SPOTS), :])
            for c, g, _, _ in groups
        ]
        scales = [lax.rsqrt(jnp.mean(x * x, axis=-1, keepdims=True) + epsilon) for x in xs]
        normed = jnp.concatenate([(x * s * gain).astype(BF) for x, s in zip(xs, scales)], axis=0)
        grads = []
        for t, (c, *_) in enumerate(groups):
            dk = nn(scores[t], head_stack(queries[t], eighth))
            stacked = jnp.concatenate(
                [scores[t][:, h * 128 : (h + 1) * 128] for h in range(CHEADS)], axis=0
            )
            dq = tn(stacked, head_stack(keys[t], eighth))
            column = kept[c, at[t], 3 * CW + CHEADS * 128 :].astype(F32)
            dv = (column.reshape(places, words, CW) * word_grads[t][None]).reshape(128, CW)
            grads.append(jnp.concatenate([dq.astype(BF), dk.astype(BF), dv.astype(BF)], axis=1))
        grads = jnp.concatenate(grads, axis=0)
        dn_all = nt(grads, mats_ref[:, : 3 * CW])
        dqkv_sum[...] += tn(normed, grads)
        dgain = jnp.zeros((1, CW), F32)
        for t, (c, g, _, target) in enumerate(groups):
            x, scale = xs[t], scales[t]
            dn = dn_all[t * 128 : (t + 1) * 128]
            xr = x * scale
            dgain = dgain + jnp.sum(xr * dn, axis=0, keepdims=True)
            w = dn * gain
            inner = jnp.mean(xr * w, axis=-1, keepdims=True)
            dx = out_grads[t] + scale * (w - xr * inner)
            dx_ref[target, pl.ds(g * words * SPOTS, words * SPOTS), :] = nn(
                back_ref[...], dx.astype(BF)
            ).astype(BF)
        dgain_ref[...] += dgain
        for slot in picked:

            @pl.when(slot >= 0)
            def _(slot=slot):
                save(slot).start()

    def batch(number, carry):
        for (which, places, words, per), order_ref, back_ref in zip(classes, orders, backs):
            pl.when(batch_kind[number] == which)(
                functools.partial(block, places, words, per, order_ref, back_ref, number)
            )
        return carry

    lax.fori_loop(0, batches, batch, 0)
    grads_ref[:, : 3 * CW] = dqkv_sum[...].astype(BF)

    def empty(slot, carry):
        @pl.when(kind[slot] == 0)
        def _():
            dx_ref[slot] = jnp.zeros(dx_ref.shape[1:], BF)
            save(slot).start()

        return carry

    lax.fori_loop(0, slots, empty, 0)

    def finish(slot, carry):
        save(slot).wait()
        return carry

    lax.fori_loop(0, slots, finish, 0)
    stream_copy.wait()


def char_backward(x, home, counts, gain, mats, kept, pooled, msum, grad_vectors, grad_stream, owners):
    slots, share = x.shape[:2]
    classes = char_classes(share)
    rows = share * SPOTS
    orders = [pltpu.VMEM((128, SPOTS * c[2]), BF) for c in classes]
    words_all = slots * share
    dx, grads, dgain, stream = char_call(
        functools.partial(char_backward_kernel, classes),
        "char_backward",
        [
            x.reshape(slots, rows, CW), counts, kept, grad_vectors, pooled, msum, gain.reshape(1, CW), mats,
            grad_stream,
        ],
        (home, counts),
        [
            jax.ShapeDtypeStruct((slots, rows, CW), BF),
            jax.ShapeDtypeStruct(mats.shape, BF),
            jax.ShapeDtypeStruct((1, CW), F32),
            jax.ShapeDtypeStruct(grad_stream.shape, grad_stream.dtype),
        ],
        [
            pltpu.VMEM((slots, rows, CW), BF),
            pltpu.VMEM((slots, rows, KEPT), BF),
            pltpu.VMEM((slots + 1, rows, CW), BF),
            pltpu.VMEM((words_all, CW), F32),
            pltpu.VMEM((words_all, CW), F32),
            pltpu.VMEM((CW, 3 * CW), F32),
            pltpu.VMEM((words_all, D), BF),
        ]
        + plan_scratch(slots, share, owners)
        + [pltpu.SemaphoreType.DMA((slots,))] * 3
        + [pltpu.SemaphoreType.DMA((1,))]
        + orders
        + [pltpu.VMEM((SPOTS * c[2], 128), BF) for c in classes],
        (0, 2),
        (0, 3),
        slots * rows * CW * CW * 28,
        53,
    )
    return dx.reshape(x.shape), grads, dgain, stream


MESH_ID = pl.DeviceIdType.MESH


def greet_start(sizes, me):
    barrier = pltpu.get_barrier_semaphore()
    for axis, n in sizes.items():
        for d in range(1, n):
            pl.semaphore_signal(
                barrier, inc=1, device_id={axis: lax.rem(me[axis] + d, n)}, device_id_type=MESH_ID
            )


def greet_wait(sizes):
    pl.semaphore_wait(pltpu.get_barrier_semaphore(), sum(n - 1 for n in sizes.values()))


def greet(sizes, me):
    greet_start(sizes, me)
    greet_wait(sizes)


def remote(source, target, sems, at, axis, peer):
    return pltpu.make_async_remote_copy(
        src_ref=source,
        dst_ref=target,
        send_sem=sems[0].at[at],
        recv_sem=sems[1].at[at],
        device_id={axis: peer},
        device_id_type=MESH_ID,
    )


def pair_gather_stages(own_of, sems, axis, n, mine, begin, late):
    chips = n // 2
    core = lax.rem(mine, 2)
    chip = mine // 2
    sibling = chip * 2 + 1 - core

    def start():
        for d in range(1, chips):
            there = lax.rem(chip + d, chips) * 2 + core
            remote(own_of(mine), own_of(mine), sems, d, axis, there).start()
        remote(own_of(mine), own_of(mine), sems, chips, axis, sibling).start()

    def hand_on():
        for d in range(1, chips):
            came = lax.rem(chip + chips - d, chips) * 2 + core
            remote(own_of(mine), own_of(came), sems, d, axis, sibling).wait_recv()
            remote(own_of(came), own_of(came), sems, chips + d, axis, sibling).start()

    def finish():
        for d in range(1, 2 * chips):
            remote(own_of(mine), own_of(mine), sems, d, axis, sibling).wait_send()
            if d >= chips:
                remote(own_of(mine), own_of(mine), sems, d, axis, sibling).wait_recv()

    return [(begin, start), (late, hand_on), (90.0, finish)]


def pair_part_stages(x, held, came, out, sems, axis, n, mine, begin, late):
    chips = n // 2
    core = lax.rem(mine, 2)
    chip = mine // 2
    sibling = chip * 2 + 1 - core

    def start():
        remote(x.at[:, 1 - core], came, sems, 0, axis, sibling).start()

    def onward():
        remote(x.at[:, 1 - core], came, sems, 0, axis, sibling).wait()
        for d in range(chips):
            there = lax.rem(chip + 1 + d, chips)
            came[there] = (came[there].astype(F32) + x[there, core].astype(F32)).astype(came.dtype)
            if d < chips - 1:
                remote(
                    came.at[there], held.at[chip], sems, 1 + d, axis, there * 2 + core
                ).start()

    def finish():
        held[chip] = came[chip]
        for d in range(chips - 1):
            remote(came.at[chip], held.at[chip], sems, 1 + d, axis, sibling).wait()
        total = held[0].astype(F32)
        for p in range(1, chips):
            total = total + held[p].astype(F32)
        out[...] = total.astype(out.dtype)

    return [(begin, start), (late, onward), (80.0, finish)]


def line_gather_stages(out, sems, axis, n, mine, begin, each, cut=()):
    def piece(block):
        return out.at[(block,) + cut]

    def step(k):
        for way in range(2):
            block = mine - k if way == 0 else mine + k
            here = (block >= 0) & (block < n)
            block = jnp.clip(block, 0, n - 1)
            onward = mine + 1 if way == 0 else mine - 1
            room = (onward >= 0) & (onward < n)
            peer = jnp.clip(onward, 0, n - 1)
            if k > 0:

                @pl.when(here)
                def _(way=way, block=block):
                    remote(piece(block), piece(block), sems, way * n + k - 1, axis, mine).wait_recv()

            if k < n - 1:

                @pl.when(here & room)
                def _(way=way, block=block, peer=peer):
                    remote(piece(block), piece(block), sems, way * n + k, axis, peer).start()

    def finish():
        for way in range(2):
            for k in range(n - 1):
                block = mine - k if way == 0 else mine + k
                sent = (mine < n - 1) & (block >= 0) if way == 0 else (mine > 0) & (block < n)

                @pl.when(sent)
                def _(way=way, k=k):
                    remote(piece(mine), piece(mine), sems, way * n + k, axis, mine).wait_send()

    stages = [(begin + each * k, functools.partial(step, k)) for k in range(n)]
    return stages + [(95.0, finish)]


def line_part_stages(x, held, out, sems, axis, n, mine, begin, each, end=70.0, cut=()):
    def step(t):
        for way in range(2):
            distance = mine if way == 0 else n - 1 - mine
            turn = t - distance
            here = (turn >= 0) & (turn < n - 1 - distance)
            turn = jnp.clip(turn, 0, n - 1)
            block = n - 1 - turn if way == 0 else turn
            peer = jnp.clip(mine + 1 if way == 0 else mine - 1, 0, n - 1)
            at = way * n + block

            @pl.when(here & (distance == 0))
            def _(way=way, block=block, peer=peer, at=at):
                remote(
                    x.at[(block,) + cut], held.at[(way, block) + cut], sems, at, axis, peer
                ).start()

            @pl.when(here & (distance > 0))
            def _(way=way, block=block, peer=peer, at=at):
                place = held.at[(way, block) + cut]
                remote(place, place, sems, at, axis, mine).wait_recv()
                held[(way, block) + cut] = (
                    held[(way, block) + cut].astype(F32) + x[(block,) + cut].astype(F32)
                ).astype(x.dtype)
                remote(place, place, sems, at, axis, peer).start()

    def finish():
        out[cut or ...] = x[(mine,) + cut].astype(F32)
        for way, there in ((0, mine > 0), (1, mine < n - 1)):

            @pl.when(there)
            def _(way=way):
                here = held.at[(way, mine) + cut]
                remote(here, here, sems, way * n + mine, axis, mine).wait_recv()
                out[cut or ...] += held[(way, mine) + cut].astype(F32)

        for way in range(2):
            for block in range(n):
                further = block > mine if way == 0 else block < mine

                @pl.when(further)
                def _(way=way, block=block):
                    here = held.at[(way, block) + cut]
                    remote(here, here, sems, way * n + block, axis, mine).wait_send()

    stages = [(begin + each * k, functools.partial(step, k)) for k in range(n - 1)]
    return stages + [(end, finish)]


def halves(rows):
    return [(slice(h * (rows // 2), (h + 1) * (rows // 2)), slice(None)) for h in range(2)]


def direct_stages(source_of, target, sems, axis, n, mine, begin, done, end, cols=None):
    def piece(block):
        return target.at[block] if cols is None else target.at[block, :, cols]

    def start():
        for d in range(1, n):
            peer = lax.rem(mine + d, n)
            remote(source_of(peer), piece(mine), sems, d, axis, peer).start()

    def finish():
        for d in range(1, n):
            remote(source_of(mine), piece(mine), sems, d, axis, mine).wait()
        done()

    return [(begin, start), (end, finish)]


def exchange(name, number, tasks):
    sizes = {axis: lax.axis_size(axis) for _, axis, _ in tasks}
    outs, scratch, counts, shapers = [], [], [], []
    for kind, axis, arrays in tasks:
        n = sizes[axis]
        array = arrays[0]
        shaper = lambda a: a
        if kind == "gather":
            rows = array.shape[1]
            cols = sum(a.shape[0] * a.shape[2] for a in arrays)
            made = jax.ShapeDtypeStruct((n * rows, cols) if rows % 16 == 0 else (n, rows, cols), BF)
            shaper = lambda a, rows=rows, cols=cols, n=n: a.reshape(n * rows, cols)
        elif kind == "gather_mid":
            lead, rows, cols = array.shape
            made = jax.ShapeDtypeStruct(
                (lead, n * rows, cols) if rows % 16 == 0 else (n, lead, rows, cols), array.dtype
            )
            if rows % 16:
                shaper = lambda a, lead=lead, rows=rows, cols=cols, n=n: a.transpose(1, 0, 2, 3).reshape(
                    lead, n * rows, cols
                )
        else:
            block = array.shape if kind in ("line_gather", "total") else array.shape[1:]
            if kind == "part":
                block = array.shape[2:]
            summed = kind in ("part", "line_part", "total")
            made = jax.ShapeDtypeStruct(block if summed else (n,) + block, F32 if summed else array.dtype)
        outs.append(made)
        shapers.append(shaper)
        counts.append(len(arrays))
        scratch += [pltpu.SemaphoreType.DMA((4 * n,)), pltpu.SemaphoreType.DMA((4 * n,))]
        if kind == "part":
            scratch += [pltpu.VMEM((n // 2,) + block, array.dtype)] * 2
        if kind == "total":
            scratch.append(pltpu.VMEM((n,) + block, array.dtype))
        if kind == "line_part":
            scratch.append(pltpu.VMEM((2, n) + block, array.dtype))
    total_ins = sum(counts)

    def kernel(*refs):
        ins, at = [], 0
        for count in counts:
            ins.append(refs[at : at + count])
            at += count
        results = refs[at : at + len(tasks)]
        rest = list(refs[at + len(tasks) :])
        me = {axis: lax.axis_index(axis) for axis in sizes}
        greet(sizes, me)
        stages = []
        for (kind, axis, _), xs, out in zip(tasks, ins, results):
            sems = (rest.pop(0), rest.pop(0))
            n, mine, x = sizes[axis], me[axis], xs[0]
            if kind == "line_gather":
                out[mine] = x[...]
                for h, cut in enumerate(halves(x.shape[0])):
                    sems_half = tuple(s.at[pl.ds(2 * n * h, 2 * n)] for s in sems)
                    stages += line_gather_stages(out, sems_half, axis, n, mine, 0.05 * h, 6.0, cut)
            elif kind == "line_part":
                stages += line_part_stages(x, rest.pop(0), out, sems, axis, n, mine, 0.0, 6.0)
            elif kind == "part":
                held, came = rest.pop(0), rest.pop(0)
                stages += pair_part_stages(x, held, came, out, sems, axis, n, mine, 0.1, 1.0)
            elif kind in ("gather", "gather_mid"):
                if kind == "gather":
                    rows = x.shape[1]
                    if rows % 16 == 0:
                        own_of = lambda i, out=out, rows=rows: out.at[
                            pl.ds(pl.multiple_of(i * rows, 16), rows), :
                        ]
                    else:
                        own_of = lambda i, out=out: out.at[i]
                    own, col = own_of(mine), 0
                    for piece in xs:
                        for t in range(piece.shape[0]):
                            own[:, col : col + piece.shape[2]] = piece[t].astype(BF)
                            col += piece.shape[2]
                else:
                    rows = x.shape[1]
                    if rows % 16 == 0:
                        own_of = lambda i, out=out, rows=rows: out.at[
                            :, pl.ds(pl.multiple_of(i * rows, 16), rows), :
                        ]
                    else:
                        own_of = lambda i, out=out: out.at[i]
                    own_of(mine)[...] = x[...]
                if axis == "dp":
                    stages += pair_gather_stages(own_of, sems, axis, n, mine, 0.2, 6.0 * lax.axis_size("mp") - 11.5)
                else:

                    def start(own_of=own_of, sems=sems, axis=axis, n=n, mine=mine):
                        for d in range(1, n):
                            peer = lax.rem(mine + d, n)
                            remote(own_of(mine), own_of(mine), sems, d, axis, peer).start()

                    def finish(own_of=own_of, sems=sems, axis=axis, n=n, mine=mine):
                        for d in range(1, n):
                            remote(own_of(mine), own_of(mine), sems, d, axis, mine).wait()

                    stages += [(0.15, start), (90.0, finish)]
            elif kind == "total":
                held = rest.pop(0)
                held[mine] = x[...]

                def done(held=held, out=out, n=n):
                    total = held[0].astype(F32)
                    for p in range(1, n):
                        total = total + held[p].astype(F32)
                    out[...] = total

                stages += direct_stages(
                    lambda p, held=held, mine=mine: held.at[mine], held, sems, axis, n, mine, 0.3, done, 60.0
                )
            else:
                out[mine] = x[mine]
                stages += direct_stages(
                    lambda p, x=x: x.at[p], out, sems, axis, n, mine, 0.0, lambda: None, 60.0
                )
        for _, run in sorted(stages, key=lambda stage: stage[0]):
            run()

    vmem = pl.BlockSpec(memory_space=pltpu.VMEM)
    results = pl.pallas_call(
        kernel,
        out_shape=outs,
        in_specs=[vmem] * total_ins,
        out_specs=[vmem] * len(tasks),
        scratch_shapes=scratch,
        compiler_params=pltpu.CompilerParams(
            collective_id=number, has_side_effects=True, vmem_limit_bytes=24 << 20
        ),
        name=name,
    )(*[array for _, _, arrays in tasks for array in arrays])
    return [shaper(a) for shaper, a in zip(shapers, results)]


def by_chip(array):
    return array.reshape(lax.axis_size("dp") // 2, 2, -1, array.shape[-1])


def sum_char_grads(grads, gains, word_sums, block_rows):
    n, m = lax.axis_size("dp"), lax.axis_size("mp")
    grads = by_chip(grads)
    rows, cols = grads.shape[2:]
    slim = cols // m
    small = jax.ShapeDtypeStruct((8, D), F32)

    def kernel(x, gain_char, gain_one, gain_two, *refs):
        words = refs[: len(word_sums)]
        (out, small_out, held, came, total_dp, cut, cut_held, merged, small_dp, small_mp, *sems) = refs[len(word_sums) :]
        pairs = [tuple(sems[2 * t : 2 * t + 2]) for t in range(6)]
        i, j = lax.axis_index("dp"), lax.axis_index("mp")
        greet({"dp": n, "mp": m}, {"dp": i, "mp": j})
        part = [
            run for _, run in pair_part_stages(x, held, came, total_dp, pairs[0], "dp", n, i, 0.0, 0.0)
        ]
        part[0]()
        squares = jnp.zeros((1, 1), F32)
        for t, word in enumerate(words):
            if t == 1:
                wide = word[pl.ds(pl.multiple_of(j * block_rows, 16), block_rows), :].astype(F32)
            else:
                wide = word[...].astype(F32)
            squares = squares + jnp.sum(jnp.sum(wide * wide, axis=0, keepdims=True), axis=1, keepdims=True)
        row = lax.broadcasted_iota(jnp.int32, (8, D), 0)
        small_dp[i] = jnp.where(row == 3, squares * (1.0 / n), 0.0)
        small_dp[i, 0:1, : gain_char.shape[1]] = gain_char[...]
        small_dp[i, 1:2, :] = gain_one[...]
        small_dp[i, 2:3, :] = gain_two[...]
        part[1]()

        def small_done():
            total = small_dp[0]
            for p in range(1, n):
                total = total + small_dp[p]
            small_mp[j] = total

        def small_end():
            total = small_mp[0]
            for p in range(1, m):
                total = total + small_mp[p]
            small_out[...] = total

        def cut_done():
            total = cut_held[0].astype(F32)
            for p in range(1, m):
                total = total + cut_held[p].astype(F32)
            merged[j] = total.astype(BF)

        one = direct_stages(lambda p: small_dp.at[i], small_dp, pairs[1], "dp", n, i, 0, small_done, 0)
        two = direct_stages(lambda p: small_mp.at[j], small_mp, pairs[2], "mp", m, j, 0, small_end, 0)
        three = direct_stages(lambda p: cut.at[p], cut_held, pairs[3], "mp", m, j, 0, cut_done, 0)
        four = direct_stages(lambda p: merged.at[j], merged, pairs[4], "mp", m, j, 0, lambda: None, 0)
        one[0][1]()
        part[2]()
        for p in range(m):
            cut[p] = total_dp[:, p * slim : (p + 1) * slim]
        cut_held[j] = cut[j]
        three[0][1]()
        one[1][1]()
        two[0][1]()
        three[1][1]()
        four[0][1]()
        two[1][1]()
        four[1][1]()
        if rows % 16 == 0:
            own_of = lambda d: out.at[pl.ds(pl.multiple_of(d * rows, 16), rows), :]
        else:
            own_of = lambda d: out.at[d]
        own = own_of(i)
        for p in range(m):
            own[:, p * slim : (p + 1) * slim] = merged[p]
        for _, run in pair_gather_stages(own_of, pairs[5], "dp", n, i, 0, 0):
            run()

    vmem = pl.BlockSpec(memory_space=pltpu.VMEM)
    sums, smalls = pl.pallas_call(
        kernel,
        out_shape=[
            jax.ShapeDtypeStruct((n * rows, cols) if rows % 16 == 0 else (n, rows, cols), BF),
            jax.ShapeDtypeStruct(small.shape, F32),
        ],
        in_specs=[vmem] * (4 + len(word_sums)),
        out_specs=[vmem] * 2,
        scratch_shapes=[
            pltpu.VMEM((n // 2, rows, cols), BF),
            pltpu.VMEM((n // 2, rows, cols), BF),
            pltpu.VMEM((rows, cols), BF),
            pltpu.VMEM((m, rows, slim), BF),
            pltpu.VMEM((m, rows, slim), BF),
            pltpu.VMEM((m, rows, slim), BF),
            pltpu.VMEM((n,) + small.shape, F32),
            pltpu.VMEM((m,) + small.shape, F32),
        ]
        + [pltpu.SemaphoreType.DMA((2 * max(n, m),))] * 12,
        compiler_params=pltpu.CompilerParams(
            collective_id=20, has_side_effects=True, vmem_limit_bytes=24 << 20
        ),
        name="sum_char_grads",
    )(grads, *gains, *word_sums)
    return sums.reshape(n * rows, cols), smalls


ROWS = 256


def rms_scale(values):
    return lax.rsqrt(jnp.mean(values * values, axis=-1, keepdims=True) + epsilon)


def norm_back(values, scale, gain_row, grad):
    weighted = grad * gain_row
    inner = jnp.mean(values * weighted, axis=-1, keepdims=True)
    return scale * weighted - values * (scale * scale * scale) * inner


def word_forward_kernel(
    width, vec_ref, place_ref, words_ref, doc_all_ref, doc_row_ref, gain_ref, project_ref,
    stream_ref, normed_ref, qkv_ref, probs_ref, mixed_ref, keys, values, doc_ref, placed
):
    step = pl.program_id(0)
    parts, kept_rows = vec_ref.shape[:2]
    words = kept_rows // OWNER_BLOCKS

    @pl.when(step == 0)
    def _():
        doc_ref[...] = tn(doc_all_ref[...].astype(F32).astype(BF), jnp.ones((1, 128), BF))
        numbers = lax.broadcasted_iota(jnp.int32, (placed.shape[0], parts * words), 0)
        hits = [(numbers == place_ref[b : b + 1, :]).astype(BF) for b in range(OWNER_BLOCKS)]
        vectors = [
            vec_ref[p, b * words : (b + 1) * words, :] for b in range(OWNER_BLOCKS) for p in range(parts)
        ]
        placed[...] = nn(jnp.concatenate(hits, axis=1), jnp.concatenate(vectors, axis=0))

    here = pl.ds(pl.multiple_of(step * ROWS, ROWS), ROWS)
    stream = words_ref[...].astype(F32) + placed[here, :]
    stream_ref[...] = stream
    normed = (stream * rms_scale(stream) * gain_ref[...]).astype(BF)
    normed_ref[...] = normed
    qkv = nn(normed, project_ref[...]).astype(BF)
    qkv_ref[...] = qkv
    first = pl.ds(pl.multiple_of(step * ROWS, ROWS), ROWS)
    keys[first, :] = qkv[:, width : 2 * width]
    values[first, :] = qkv[:, 2 * width :]
    queries = (qkv[:, :width].astype(F32) * (1.0 / math.sqrt(HD))).astype(BF)

    def attend(number):
        count = (number + 1) * ROWS
        same = jnp.concatenate([doc_ref[:count, :]] * (ROWS // 128), axis=1) == doc_row_ref[...].astype(F32)
        key_at = lax.broadcasted_iota(jnp.int32, (count, ROWS), 0)
        query_at = lax.broadcasted_iota(jnp.int32, (count, ROWS), 1) + number * ROWS
        allowed = same & (key_at <= query_at)
        parts = []
        for head in range(width // HD):
            at = slice(head * HD, (head + 1) * HD)
            scores = jnp.where(allowed, nt(keys[:count, at], queries[:, at]), negative_big)
            raised = jnp.exp(scores - jnp.max(scores, axis=0, keepdims=True))
            probs = (raised * (1.0 / jnp.sum(raised, axis=0, keepdims=True))).astype(BF)
            probs_ref[head, :count, :] = probs
            parts.append(tn(values[:count, at], probs).T)
        mixed_ref[...] = jnp.concatenate(parts, axis=1).astype(BF)

    for number in range(doc_all_ref.shape[1] // ROWS):
        pl.when(step == number)(functools.partial(attend, number))


def word_forward(vectors, places, words, documents, gain, project):
    length = words.shape[0]
    width = project.shape[1] // 3
    heads = width // HD
    rows = lambda cols: pl.BlockSpec((ROWS, cols), lambda i: (i, 0))
    full = lambda shape: pl.BlockSpec(shape, lambda i: (0,) * len(shape))
    return pl.pallas_call(
        functools.partial(word_forward_kernel, width),
        grid=(length // ROWS,),
        in_specs=[
            full(vectors.shape),
            full(places.shape),
            rows(D),
            full((1, length)),
            pl.BlockSpec((1, ROWS), lambda i: (0, i)),
            full((1, D)),
            full(project.shape),
        ],
        out_specs=[
            rows(D),
            rows(D),
            rows(3 * width),
            pl.BlockSpec((heads, length, ROWS), lambda i: (0, 0, i)),
            rows(width),
        ],
        out_shape=[
            jax.ShapeDtypeStruct((length, D), F32),
            jax.ShapeDtypeStruct((length, D), BF),
            jax.ShapeDtypeStruct((length, 3 * width), BF),
            jax.ShapeDtypeStruct((heads, length, length), BF),
            jax.ShapeDtypeStruct((length, width), BF),
        ],
        scratch_shapes=[
            pltpu.VMEM((length, width), BF),
            pltpu.VMEM((length, width), BF),
            pltpu.VMEM((length, 128), F32),
            pltpu.VMEM((length, D), F32),
        ],
        compiler_params=pltpu.CompilerParams(vmem_limit_bytes=32 << 20),
        name="word_forward",
    )(
        vectors,
        places,
        words,
        documents.reshape(1, length),
        documents.reshape(1, length),
        gain.reshape(1, D),
        project,
    )


FEED_ROWS = 512


def feed_rows(mixed, output_ref, stream, grad_feed, gain, upper, lower):
    hidden = stream
    for j, part in enumerate(mixed):
        width = part.shape[1]
        hidden = hidden + nn(part, output_ref[j * width : (j + 1) * width, :])
    normed = (hidden * rms_scale(hidden) * gain).astype(BF)
    raised = nn(normed, upper)
    constant = math.sqrt(2.0 / math.pi)
    square = raised * raised
    curve = jnp.tanh(constant * raised * (1.0 + 0.044715 * square))
    half = 0.5 * (1.0 + curve)
    active = (raised * half).astype(BF)
    slope = half + 0.5 * raised * (1.0 - curve * curve) * constant * (1.0 + 3.0 * 0.044715 * square)
    grad_raised = (nt(grad_feed, lower) * slope).astype(BF)
    return (
        hidden,
        nn(active, lower).astype(BF),
        nt(grad_raised, upper).astype(BF),
        tn(normed, grad_raised),
        tn(active, grad_feed),
    )


def attention_back(width, probs_ref, qkv_ref, grad_ref, grads, key_sum, value_sum):
    eighth = 1.0 / math.sqrt(HD)
    key_sum[...] = jnp.zeros_like(key_sum)
    value_sum[...] = jnp.zeros_like(value_sum)
    for number in range(qkv_ref.shape[0] // ROWS):
        rows = slice(number * ROWS, (number + 1) * ROWS)
        count = (number + 1) * ROWS
        queries = (qkv_ref[rows, :width].astype(F32) * eighth).astype(BF)
        parts = []
        for head in range(width // HD):
            at = slice(head * HD, (head + 1) * HD)
            keys = qkv_ref[:count, width + head * HD : width + (head + 1) * HD]
            values = qkv_ref[:count, 2 * width + head * HD : 2 * width + (head + 1) * HD]
            grad = grad_ref[rows, at]
            probs = probs_ref[head, :count, rows]
            wide = probs.astype(F32)
            product = wide * nt(values, grad)
            scores = (product - wide * jnp.sum(product, axis=0, keepdims=True)).astype(BF)
            key_sum[head, :count, :] += nn(scores, queries[:, at])
            value_sum[head, :count, :] += nn(probs, grad)
            parts.append(tn(keys, scores).T * eighth)
        grads[rows, :width] = jnp.concatenate(parts, axis=1).astype(BF)
    for head in range(width // HD):
        grads[:, width + head * HD : width + (head + 1) * HD] = key_sum[head].astype(BF)
        grads[:, 2 * width + head * HD : 2 * width + (head + 1) * HD] = value_sum[head].astype(BF)


def shampoo_kernel(
    threshold, position, char_ref, small_ref, gain_ref, gains_ref, project, output, upper, lower, hidden_in, feed_in, *refs
):
    given_in, refs = refs[:30], refs[30:]
    norm_ref, gain_grad_ref, gains_grad_ref, gain_new_ref, gains_new_ref, block_out = refs[:6]
    made_out, refs = refs[6:36], refs[36:]
    given, made = refs[:30], refs[30:60]
    hidden, feed_sum, total, in_sems, out_sems = refs[60:]
    loads = [pltpu.make_async_copy(a, b, in_sems.at[t]) for t, (a, b) in enumerate(zip(given_in, given))]
    loads += [
        pltpu.make_async_copy(hidden_in, hidden, in_sems.at[30]),
        pltpu.make_async_copy(feed_in, feed_sum, in_sems.at[31]),
    ]
    order = (4, 5, 2, 3, 0, 1)
    for number in order:
        for t in range(5):
            loads[5 * number + t].start()
    loads[30].start()
    loads[31].start()
    saves = [pltpu.make_async_copy(a, b, out_sems.at[t]) for t, (a, b) in enumerate(zip(made, made_out))]
    saves.append(pltpu.make_async_copy(total, block_out, out_sems.at[30]))
    me = position[0]
    char = char_ref[...].astype(F32)
    small = small_ref[...]
    lanes = lax.broadcasted_iota(jnp.int32, small.shape, 0)
    squares = (
        jnp.sum(jnp.sum(char * char, axis=0, keepdims=True), axis=1, keepdims=True)
        + jnp.sum(
            jnp.sum(jnp.where(lanes < 3, small * small, 0.0), axis=0, keepdims=True),
            axis=1,
            keepdims=True,
        )
        + small[3:4, :1]
    )
    norm = jnp.sqrt(squares)
    factor = jnp.minimum(1.0, threshold / norm)
    norm_ref[...] = norm
    gain_grad = small[0:1, :CW] * factor
    gain_grad_ref[...] = gain_grad
    gain_new_ref[...] = gain_ref[...] - gain_rate * gain_grad
    gains_grad = small[1:3, :] * factor
    gains_grad_ref[...] = gains_grad
    gains_new_ref[...] = gains_ref[...] - gain_rate * gains_grad
    width = project.shape[1] // 3
    own = pl.ds(pl.multiple_of(position[1] * width, 16), width)

    def whole_of(number, t):
        if number == 0:
            return char_ref[:, t * CW : (t + 1) * CW]
        if number == 1:
            return char_ref[:, 4 * CW :]
        if number == 2:
            return project[:, t * width : (t + 1) * width]
        return (output[own, :], upper[...], lower[...])[number - 3]

    def chosen(rows, cols):
        row = lax.broadcasted_iota(jnp.int32, (rows, cols), 0) + me * rows
        return (row == lax.broadcasted_iota(jnp.int32, (rows, cols), 1)).astype(BF)

    half = (1.0 - decay_rate) * factor * factor
    for number in order:
        for t in range(5):
            loads[5 * number + t].wait()
        master, left, right, left_root, right_root = given[5 * number : 5 * number + 5]
        grad_out, left_out, right_out, new_out, copy_out = made[5 * number : 5 * number + 5]
        for t in range(master.shape[0]):
            grad = whole_of(number, t)
            rows = nn(chosen(master.shape[1], grad.shape[0]), grad)
            grad_out[t] = rows * factor
            left_out[t] = decay_rate * left[t] + half * nt(rows.astype(BF), grad)
            cols = nt(grad, chosen(right.shape[1], grad.shape[1])).astype(BF)
            right_out[t] = decay_rate * right[t] + half * tn(cols, grad)
            turned = (nn(left_root[t].astype(BF), grad) * factor).astype(BF)
            root = right_root[:, t * grad.shape[1] : (t + 1) * grad.shape[1]]
            new = master[t] - learn_rate * nn(turned, root)
            new_out[t] = new
            copy_out[t] = new.astype(BF)
        for t in range(5):
            saves[5 * number + t].start()
    loads[30].wait()
    loads[31].wait()
    total[...] = (hidden[...] + feed_sum[...].astype(F32)).astype(BF)
    saves[30].start()
    for save in saves:
        save.wait()


def shampoo(threshold, position, char_sums, small, gain, gains, word_sums, hidden, feed_sum, given):
    flat = []
    shapes = []
    for master, left, right, left_root, right_root in given:
        flat += [master, left, right, left_root, right_root]
        shapes += [
            jax.ShapeDtypeStruct(a.shape, F32) for a in (master, left, right, master)
        ] + [jax.ShapeDtypeStruct(master.shape, BF)]
    first = [
        jax.ShapeDtypeStruct((1, 1), F32),
        jax.ShapeDtypeStruct((1, CW), F32),
        jax.ShapeDtypeStruct((2, D), F32),
        jax.ShapeDtypeStruct((1, CW), F32),
        jax.ShapeDtypeStruct((2, D), F32),
    ]
    vmem = pl.BlockSpec(memory_space=pltpu.VMEM)
    smem = pl.BlockSpec(memory_space=pltpu.SMEM)
    hbm = pl.BlockSpec(memory_space=pltpu.HBM)
    return pl.pallas_call(
        functools.partial(shampoo_kernel, threshold),
        in_specs=[smem] + [vmem] * 8 + [hbm] * 32,
        out_specs=[vmem] * 5 + [hbm] * 31,
        out_shape=first + [jax.ShapeDtypeStruct(feed_sum.shape, BF)] + shapes,
        scratch_shapes=[pltpu.VMEM(a.shape, a.dtype) for a in flat]
        + [pltpu.VMEM(a.shape, a.dtype) for a in shapes]
        + [
            pltpu.VMEM(hidden.shape, F32),
            pltpu.VMEM(feed_sum.shape, BF),
            pltpu.VMEM(feed_sum.shape, BF),
            pltpu.SemaphoreType.DMA((32,)),
            pltpu.SemaphoreType.DMA((31,)),
        ],
        compiler_params=pltpu.CompilerParams(vmem_limit_bytes=60 << 20),
        name="shampoo",
    )(position, char_sums, small, gain.reshape(1, CW), gains, *word_sums, hidden, feed_sum, *flat)


def run_stages(stages):
    for _, run in sorted(stages, key=lambda stage: stage[0]):
        run()


def gather_setup(xs, out):
    rows = xs[0].shape[1]

    def own_of(i):
        if rows % 16 == 0:
            return out.at[pl.ds(pl.multiple_of(i * rows, 16), rows), :]
        return out.at[i]

    def put(mine):
        own, col = own_of(mine), 0
        for piece in xs:
            for t in range(piece.shape[0]):
                own[:, col : col + piece.shape[2]] = piece[t].astype(BF)
                col += piece.shape[2]

    return own_of, put


def gather_shape(arrays, n):
    rows = arrays[0].shape[1]
    cols = sum(a.shape[0] * a.shape[2] for a in arrays)
    shape = (n * rows, cols) if rows % 16 == 0 else (n, rows, cols)
    return jax.ShapeDtypeStruct(shape, BF), lambda a: a.reshape(n * rows, cols)


def dma_sems(count):
    return [pltpu.SemaphoreType.DMA((count,))] * 2


def call_remote(kernel, name, number, outs, scratch, inputs):
    vmem = pl.BlockSpec(memory_space=pltpu.VMEM)
    return pl.pallas_call(
        kernel,
        out_shape=outs,
        in_specs=[vmem] * len(inputs),
        out_specs=[vmem] * len(outs),
        scratch_shapes=scratch,
        compiler_params=pltpu.CompilerParams(
            collective_id=number, has_side_effects=True, vmem_limit_bytes=36 << 20
        ),
        name=name,
    )(*inputs)


def gather_char(mixer, lift, output, home, places):
    n, m = lax.axis_size("dp"), lax.axis_size("mp")
    slots, block_words = places.shape
    cap = -(-slots // n)
    total = n * cap
    share = block_words // m
    shape, shaper = gather_shape([mixer, lift], n)
    rows = output.shape[1]

    def kernel(
        mixer_in, lift_in, output_in, home_row, place_ref,
        mats, line, live, live_place, own_row, mixer_ref, lift_ref, output_ref, sent, came, local, *sems
    ):
        pairs = [tuple(sems[2 * t : 2 * t + 2]) for t in range(3)]
        i, j = lax.axis_index("dp"), lax.axis_index("mp")
        loads = [
            pltpu.make_async_copy(a, b, local.at[t])
            for t, (a, b) in enumerate(
                ((mixer_in, mixer_ref), (lift_in, lift_ref), (output_in, output_ref))
            )
        ]
        for load in loads:
            load.start()
        own_of, put = gather_setup([mixer_ref, lift_ref], mats)
        greet({"dp": n, "mp": m}, {"dp": i, "mp": j})
        for load in loads:
            load.wait()
        put(i)
        line[j] = output_ref[0].astype(BF)
        stages = pair_gather_stages(own_of, pairs[0], "dp", n, i, 0.0, 2.0)

        def send_places():
            before = lax.broadcasted_iota(jnp.int32, (slots, slots), 0)
            before = before < lax.broadcasted_iota(jnp.int32, (slots, slots), 1)
            home_col = tn(home_row[...].astype(F32).astype(BF), jnp.ones((1, 128), BF))[:, :slots]
            same = (home_col == home_row[...].astype(F32)) & before
            rank = jnp.sum(same.astype(F32), axis=0, keepdims=True)
            target = jnp.where(
                home_row[...] >= 0, home_row[...].astype(F32) * cap + rank, float(total)
            )
            hit = lax.broadcasted_iota(jnp.int32, (total, slots), 0).astype(F32) == target
            chosen = hit.astype(F32)
            placed = jnp.zeros((total, block_words), F32) - 1.0
            for s in range(slots):
                placed = jnp.where(
                    chosen[:, s : s + 1] > 0.0, place_ref[s : s + 1, :].astype(F32), placed
                )
            for p in range(n):
                sent[p] = placed[p * cap : (p + 1) * cap, :].astype(jnp.int32)
            came[i] = sent[i]

        def use_places():
            placed = jnp.concatenate([came[p] for p in range(n)], axis=0).astype(F32)
            held = jnp.max(placed, axis=1, keepdims=True) >= 0.0
            filled = jnp.where(held, jnp.ones((total, 128), F32), 0.0)
            lower = lax.broadcasted_iota(jnp.int32, (total, total), 1)
            lower = (lower < lax.broadcasted_iota(jnp.int32, (total, total), 0)).astype(BF)
            rank = nn(lower, filled.astype(BF))
            lane = lax.broadcasted_iota(jnp.int32, (total, 128), 1).astype(F32)
            chosen = jnp.where((rank == lane) & (filled > 0.0), 1.0, 0.0).astype(BF)
            live[...] = chosen
            high = jnp.floor((placed + 1.0) * (1.0 / 32.0))
            low = placed + 1.0 - high * 32.0
            high, low = high.astype(BF), low.astype(BF)
            found = tn(chosen, high) * 32.0 + tn(chosen, low) - 1.0
            live_place[...] = found[: live_place.shape[0], :].astype(jnp.int32)
            block = cap * share
            for p in range(n):
                col = lax.broadcasted_iota(jnp.int32, (block_words, block), 1) % share + j * share
                pick = (col == lax.broadcasted_iota(jnp.int32, (block_words, block), 0)).astype(BF)
                row = lax.broadcasted_iota(jnp.int32, (total, block), 0) - p * cap
                mine = row == lax.broadcasted_iota(jnp.int32, (total, block), 1) // share
                value = nn(high, pick) * 32.0 + nn(low, pick) - 1.0
                own_row[p] = jnp.sum(jnp.where(mine, value, 0.0), axis=0, keepdims=True).astype(jnp.int32)

        stages.append((0.1, send_places))
        stages += direct_stages(lambda p: sent.at[p], came, pairs[1], "dp", n, i, 0.2, lambda: None, 1.0)
        stages += direct_stages(lambda p: line.at[j], line, pairs[2], "mp", m, j, 0.3, lambda: None, 50.0)
        stages.append((1.5, use_places))
        run_stages(stages)

    vmem = pl.BlockSpec(memory_space=pltpu.VMEM)
    hbm = pl.BlockSpec(memory_space=pltpu.HBM)
    lines = max(16, -(-OWNER_BLOCKS // 8) * 8)
    results = pl.pallas_call(
        kernel,
        out_shape=[
            shape,
            jax.ShapeDtypeStruct((m, rows, D), BF),
            jax.ShapeDtypeStruct((total, 128), BF),
            jax.ShapeDtypeStruct((lines, block_words), jnp.int32),
            jax.ShapeDtypeStruct((n, 1, cap * share), jnp.int32),
        ],
        in_specs=[hbm] * 3 + [vmem] * 2,
        out_specs=[vmem] * 5,
        scratch_shapes=[
            pltpu.VMEM(mixer.shape, F32),
            pltpu.VMEM(lift.shape, F32),
            pltpu.VMEM(output.shape, F32),
            pltpu.VMEM((n, cap, block_words), jnp.int32),
            pltpu.VMEM((n, cap, block_words), jnp.int32),
            pltpu.SemaphoreType.DMA((3,)),
        ]
        + dma_sems(2 * max(n, m)) * 3,
        compiler_params=pltpu.CompilerParams(
            collective_id=0, has_side_effects=True, vmem_limit_bytes=60 << 20
        ),
        name="gather_char",
    )(mixer, lift, output, home.reshape(1, slots), places)
    return [shaper(results[0])] + list(results[1:])


def send_vectors(sent, to_live, share, project, upper, lower, output_line):
    n, m = lax.axis_size("dp"), lax.axis_size("mp")
    block = sent.shape[1]
    total = n * block
    kept = OWNER_BLOCKS * share
    made = [gather_shape([a], n) for a in (project, upper, lower)]
    made[0] = gather_shape([project], n)
    lead, line_rows, line_cols = output_line.shape
    aligned = line_rows % 16 == 0
    output_shape = (lead, n * line_rows, line_cols) if aligned else (n, lead, line_rows, line_cols)

    def kernel(sent, live, *refs):
        weights, line = refs[:3], refs[3]
        out, wides, output = refs[4], refs[5:8], refs[8]
        came, spread, *sems = refs[9:]
        pairs = [tuple(sems[2 * t : 2 * t + 2]) for t in range(8)]
        i, j = lax.axis_index("dp"), lax.axis_index("mp")
        greet({"dp": n, "mp": m}, {"dp": i, "mp": j})
        came[i] = sent[i]
        stages = []

        def make_spread():
            up = lax.broadcasted_iota(jnp.int32, (kept, 128), 0) // share
            up = (up == lax.broadcasted_iota(jnp.int32, (kept, 128), 1)).astype(BF)
            blocks = nt(up, live[...]).astype(BF)
            down = lax.broadcasted_iota(jnp.int32, (blocks.shape[1], total), 1) // share
            down = (down == lax.broadcasted_iota(jnp.int32, (blocks.shape[1], total), 0)).astype(BF)
            row = lax.broadcasted_iota(jnp.int32, (kept, total), 0) % share
            col = lax.broadcasted_iota(jnp.int32, (kept, total), 1) % share
            spread[...] = jnp.where(row == col, nn(blocks, down), 0.0).astype(BF)

        stages.append((0.4, make_spread))

        def compact(cols):
            out[j, :, cols] = nn(spread[...], came[:, :, cols].reshape(total, D // 2)).astype(BF)

        for half in range(2):
            cols = slice(half * (D // 2), (half + 1) * (D // 2))
            stages += direct_stages(
                lambda p, cols=cols: sent.at[p, :, cols], came, pairs[6 * half], "dp", n, i, 0.1 * half,
                functools.partial(compact, cols), 1.0 + half, cols,
            )
            stages += line_gather_stages(
                out, pairs[1 + 6 * half], "mp", m, j, 1.5 + 0.6 * half, 1.0, (slice(None), cols)
            )
        for t, (x, wide) in enumerate(zip(weights, wides)):
            own_of, put = gather_setup([x], wide)
            put(i)
            stages += pair_gather_stages(own_of, pairs[2 + t], "dp", n, i, 0.3, 2.0 * m + 0.5)
        if aligned:
            output_of = lambda d: output.at[:, pl.ds(pl.multiple_of(d * line_rows, 16), line_rows), :]
        else:
            output_of = lambda d: output.at[d]
        output_of(i)[...] = line[...]
        stages += pair_gather_stages(output_of, pairs[5], "dp", n, i, 0.3, 2.0 * m + 0.5)
        run_stages(stages)

    results = call_remote(
        kernel,
        "send_vectors",
        1,
        [jax.ShapeDtypeStruct((m, kept, D), BF)]
        + [shape for shape, _ in made]
        + [jax.ShapeDtypeStruct(output_shape, BF)],
        [pltpu.VMEM((n, block, D), BF), pltpu.VMEM((kept, total), BF)] + dma_sems(2 * max(n, m)) * 8,
        [sent, to_live, project, upper, lower, output_line],
    )
    output = results[4]
    if not aligned:
        output = output.transpose(1, 0, 2, 3)
    return (
        [results[0]]
        + [shaper(a) for (_, shaper), a in zip(made, results[1:4])]
        + [output.reshape(-1, line_cols)]
    )


def feed_step(mixed, stream, cotangent, output, gain, upper, lower, roots):
    n, m = lax.axis_size("dp"), lax.axis_size("mp")
    length, width = mixed.shape
    share = length // m
    made = [gather_shape([a], n) for a in roots]
    chip_shape = lambda a: (n // 2, 2, a.shape[0] // n, a.shape[1])

    def kernel(mixed_ref, stream_ref, cot, out_mat, gain_ref, upper_ref, lower_ref, *refs):
        roots_in, refs = refs[: len(roots)], refs[len(roots) :]
        hidden_ref, feed_ref, grad_hidden, grad_mixed, grad_output, gain_grad, up_sum, low_sum = refs[:8]
        roots_out, refs = refs[8 : 8 + len(roots)], refs[8 + len(roots) :]
        mix, part, up, low, held, total, swapped, up_held, up_came, low_held, low_came, *sems = refs
        pairs = [tuple(sems[2 * t : 2 * t + 2]) for t in range(7 + len(roots))]
        i, j = lax.axis_index("dp"), lax.axis_index("mp")
        greet({"dp": n, "mp": m}, {"dp": i, "mp": j})
        stages = []
        mix[j] = mixed_ref[...]
        for h, cut in enumerate(halves(length)):
            stages += line_gather_stages(
                mix, pairs[5 + len(roots) + h], "mp", m, j, -50.0 + 0.05 * h, 6.0, cut
            )

        def run_feed():
            grad_upper = jnp.zeros(upper_ref.shape, F32)
            grad_lower = jnp.zeros(lower_ref.shape, F32)
            for first in range(0, length, FEED_ROWS):
                rows = slice(first, first + FEED_ROWS)
                hidden, fed, part_rows, more_upper, more_lower = feed_rows(
                    [mix[p, rows, :] for p in range(m)], out_mat, stream_ref[rows, :], cot[rows, :],
                    gain_ref[...], upper_ref[...], lower_ref[...],
                )
                hidden_ref[rows, :] = hidden
                feed_ref[rows, :] = fed
                for p in range(FEED_ROWS // share):
                    part[first // share + p] = part_rows[p * share : (p + 1) * share]
                grad_upper = grad_upper + more_upper
                grad_lower = grad_lower + more_lower
            up[...] = grad_upper.astype(BF).reshape(up.shape)
            low[...] = grad_lower.astype(BF).reshape(low.shape)

        stages.append((-0.5, run_feed))
        for h, cut in enumerate(halves(share)):
            stages += line_part_stages(
                part, held, total, pairs[(0, 4 + len(roots))[h]], "mp", m, j, 0.05 * h, 6.0, 70.0 + 0.1 * h, cut
            )
        stages += pair_part_stages(up, up_held, up_came, up_sum, pairs[1], "dp", n, i, 0.1, 1.0)
        stages += pair_part_stages(low, low_held, low_came, low_sum, pairs[2], "dp", n, i, 0.1, 1.0)
        for t, (x, out) in enumerate(zip(roots_in, roots_out)):
            own_of, put = gather_setup([x], out)
            put(i)
            stages += pair_gather_stages(own_of, pairs[4 + t], "dp", n, i, -49.8, 72.5)

        def back():
            mine = pl.ds(pl.multiple_of(j * share, share), share)
            hidden_own = hidden_ref[mine, :]
            scale = rms_scale(hidden_own)
            grad = total[...]
            whole_grad = cot[mine, :].astype(F32) + norm_back(hidden_own, scale, gain_ref[...], grad)
            grad_hidden[...] = whole_grad
            gain_grad[...] = jnp.sum(hidden_own * scale * grad, axis=0, keepdims=True)
            attend = whole_grad.astype(BF)
            for p in range(m):
                swapped[p] = nt(attend, out_mat[p * width : (p + 1) * width, :]).astype(BF)
            grad_mixed[j] = swapped[j]

        def output_grad():
            mine = pl.ds(pl.multiple_of(j * share, share), share)
            attend = grad_hidden[...].astype(BF)
            for p in range(m):
                grad_output[p * width : (p + 1) * width, :] = tn(mix[p, mine, :], attend).astype(BF)

        stages += [(71.0, back), (73.0, output_grad)]
        stages += direct_stages(
            lambda p: swapped.at[p], grad_mixed, pairs[3], "mp", m, j, 72.0, lambda: None, 75.0
        )
        run_stages(stages)

    chips = lambda a: pltpu.VMEM(chip_shape(a), BF)
    block = lambda a: pltpu.VMEM(chip_shape(a)[:1] + chip_shape(a)[2:], BF)
    results = call_remote(
        kernel,
        "feed_step",
        4,
        [
            jax.ShapeDtypeStruct((length, D), F32),
            jax.ShapeDtypeStruct((length, D), BF),
            jax.ShapeDtypeStruct((share, D), F32),
            jax.ShapeDtypeStruct((m, share, width), BF),
            jax.ShapeDtypeStruct(output.shape, BF),
            jax.ShapeDtypeStruct((1, D), F32),
            jax.ShapeDtypeStruct(chip_shape(upper)[2:], F32),
            jax.ShapeDtypeStruct(chip_shape(lower)[2:], F32),
        ]
        + [shape for shape, _ in made],
        [
            pltpu.VMEM((m, length, width), BF),
            pltpu.VMEM((m, share, D), BF),
            chips(upper),
            chips(lower),
            pltpu.VMEM((2, m, share, D), BF),
            pltpu.VMEM((share, D), F32),
            pltpu.VMEM((m, share, width), BF),
            block(upper),
            block(upper),
            block(lower),
            block(lower),
        ]
        + dma_sems(2 * max(n, m)) * (7 + len(roots)),
        [mixed, stream, cotangent, output, gain.reshape(1, D), upper, lower] + roots,
    )
    return list(results[:8]) + [shaper(a) for (_, shaper), a in zip(made, results[8:])]


def stream_grads(probs, qkv, grad_mixed, normed, project_mat, stream, grad_hidden, gain, own_row, sums, grad_output):
    n, m = lax.axis_size("dp"), lax.axis_size("mp")
    share = stream.shape[0] // m
    width = project_mat.shape[1] // 3
    heads = width // HD
    block = own_row.shape[2]
    total_words = n * block
    words = share * m
    project_chips = (n // 2, 2, project_mat.shape[0] // n, project_mat.shape[1])
    parts = [jax.ShapeDtypeStruct(project_chips, BF), by_chip(grad_output)]
    chunk = lambda a: jax.ShapeDtypeStruct((1,) + a.shape[-2:], F32)
    made = [gather_shape([chunk(a)], n) for a in (sums[0], sums[1], parts[0], parts[1])]

    def kernel(
        probs_ref, qkv_ref, mixed_grad, normed_ref, mat_ref, stream_ref, hidden_ref, gain_ref, row_ref, up, low, output, *refs
    ):
        out, gain_grad, came, up_out, low_out, project_out, output_out = refs[:7]
        (part, project, head_grads, key_sum, value_sum, held, total, project_sum, output_sum, line_held, picked, hits,
         p_held, p_came, o_held, o_came, *sems) = refs[7:]
        pairs = [tuple(sems[2 * t : 2 * t + 2]) for t in range(13)]
        i, j = lax.axis_index("dp"), lax.axis_index("mp")
        greet_start({"dp": n, "mp": m}, {"dp": i, "mp": j})
        attention_back(width, probs_ref, qkv_ref, mixed_grad, head_grads, key_sum, value_sum)
        grads = head_grads[...]
        part[...] = nt(grads, mat_ref[...]).astype(BF).reshape(part.shape)
        project[...] = tn(normed_ref[...], grads).astype(BF).reshape(project.shape)
        greet_wait({"dp": n, "mp": m})
        stages = []
        for h, cut in enumerate(halves(share)):
            stages += line_part_stages(
                part, held, total, pairs[(0, 12)[h]], "mp", m, j, 0.05 * h, 6.0, 70.0 + 0.1 * h, cut
            )
        stages += pair_part_stages(project, p_held, p_came, project_sum.at[0], pairs[1], "dp", n, i, 0.1, 1.0)
        stages += pair_part_stages(output, o_held, o_came, output_sum.at[0], pairs[2], "dp", n, i, 0.1, 1.0)
        up_of, put_up = gather_setup([up], up_out)
        low_of, put_low = gather_setup([low], low_out)
        put_up(i)
        put_low(i)
        stages += pair_gather_stages(up_of, pairs[3], "dp", n, i, 2.0, 71.9)
        stages += pair_gather_stages(low_of, pairs[4], "dp", n, i, 2.0, 71.9)

        def back():
            mine = pl.ds(pl.multiple_of(j * share, share), share)
            stream_own = stream_ref[mine, :]
            scale = rms_scale(stream_own)
            grad = total[...]
            out[j] = (hidden_ref[...] + norm_back(stream_own, scale, gain_ref[...], grad)).astype(BF)
            gain_grad[...] = jnp.sum(stream_own * scale * grad, axis=0, keepdims=True)

        stages.append((71.0, back))
        for half in range(2):
            cols = slice(half * (D // 2), (half + 1) * (D // 2))
            stages += [
                (when if when < 90 else 199.0, run)
                for when, run in line_gather_stages(
                    out, pairs[5 + 5 * half], "mp", m, j, 72.0 + 0.05 * half, 0.1, (slice(None), cols)
                )
            ]
        project_of, put_project = gather_setup([project_sum], project_out)
        output_of, put_output = gather_setup([output_sum], output_out)

        def put_sums():
            put_project(i)
            line_held[j] = output_sum[0].astype(BF)

        target = i // (n // m)

        def line_send():
            @pl.when(j != target)
            def _():
                remote(line_held.at[j], line_held.at[j], pairs[7], j, "mp", target).start()

        def line_done():
            @pl.when(j != target)
            def _():
                remote(line_held.at[j], line_held.at[j], pairs[7], j, "mp", target).wait_send()

            @pl.when(j == target)
            def _():
                for p in range(m):

                    @pl.when(j != p)
                    def _(p=p):
                        remote(line_held.at[p], line_held.at[p], pairs[7], p, "mp", target).wait_recv()

                summed = line_held[0].astype(F32)
                for p in range(1, m):
                    summed = summed + line_held[p].astype(F32)
                output_sum[0] = summed

            put_output(i)

        stages = [(60.0 if when == 80.0 else when, run) for when, run in stages]
        stages.append((72.01, put_sums))
        stages += [
            (when, run)
            for when, run in zip(
                (72.02, 72.25, 198.0),
                [run for _, run in pair_gather_stages(project_of, pairs[6], "dp", n, i, 0, 0)],
            )
        ]
        late_line = 72.0 + 0.1 * 2 * m
        stages += [(72.03, line_send), (late_line + 0.01, line_done)]
        stages += [
            (when, run)
            for when, run in zip(
                (late_line + 0.02, 81.5, 198.5),
                [run for _, run in pair_gather_stages(output_of, pairs[8], "dp", n, i, 0, 0)],
            )
        ]

        def make_hits():
            lane = lax.broadcasted_iota(jnp.int32, (block, 128), 1).astype(F32)
            ones = jnp.ones((1, 128), BF)
            for p in range(n):
                place = row_ref[p].astype(F32) + 1.0
                high = jnp.floor(place * (1.0 / 32.0))
                low = place - high * 32.0
                col = tn(high.astype(BF), ones) * 32.0 + tn(low.astype(BF), ones) - 1.0
                for t in range(words // 128):
                    hits[p * block : (p + 1) * block, t * 128 : (t + 1) * 128] = (
                        col == lane + 128.0 * t
                    ).astype(BF)

        stages.append((2.5, make_hits))

        def pick(half):
            cols = slice(half * (D // 2), (half + 1) * (D // 2))
            rows = nn(hits[...], out[:, :, cols].reshape(words, D // 2)).astype(BF)
            picked[:, :, cols] = rows.reshape(n, block, D // 2)
            for d in range(1, n):
                peer = lax.rem(i + d, n)
                remote(
                    picked.at[peer, :, cols], came.at[i, :, cols], pairs[9 + 2 * half], d, "dp", peer
                ).start()
            came[i, :, cols] = picked[i, :, cols]

        for half in range(2):
            stages.append((72.011 + 0.1 * (m - 1) + 0.05 * half, functools.partial(pick, half)))

        def place():
            for half in range(2):
                cols = slice(half * (D // 2), (half + 1) * (D // 2))
                for d in range(1, n):
                    remote(
                        picked.at[i, :, cols], came.at[i, :, cols], pairs[9 + 2 * half], d, "dp", i
                    ).wait()

        stages.append((82.0, place))
        run_stages(stages)

    held_of = lambda a: pltpu.VMEM(a.shape[:1] + a.shape[2:], BF)
    results = call_remote(
        kernel,
        "stream_grads",
        6,
        [
            jax.ShapeDtypeStruct((m, share, D), BF),
            jax.ShapeDtypeStruct((1, D), F32),
            jax.ShapeDtypeStruct((n, block, D), BF),
        ]
        + [shape for shape, _ in made],
        [
            pltpu.VMEM((m, share, D), BF),
            pltpu.VMEM(project_chips, BF),
            pltpu.VMEM(qkv.shape, BF),
            pltpu.VMEM((heads, words, HD), F32),
            pltpu.VMEM((heads, words, HD), F32),
            pltpu.VMEM((2, m, share, D), BF),
            pltpu.VMEM((share, D), F32),
            pltpu.VMEM((1,) + parts[0].shape[2:], F32),
            pltpu.VMEM((1,) + parts[1].shape[2:], F32),
            pltpu.VMEM((m,) + parts[1].shape[2:], BF),
            pltpu.VMEM((n, block, D), BF),
            pltpu.VMEM((total_words, words), BF),
            held_of(parts[0]),
            held_of(parts[0]),
            held_of(parts[1]),
            held_of(parts[1]),
        ]
        + dma_sems(2 * max(n, m)) * 13,
        [
            probs,
            qkv,
            grad_mixed,
            normed,
            project_mat,
            stream,
            grad_hidden,
            gain.reshape(1, D),
            own_row,
            sums[0][None],
            sums[1][None],
            parts[1],
        ],
    )
    return list(results[:3]) + [shaper(a) for (_, shaper), a in zip(made, results[3:])]


def local(
    word_inputs,
    character_embeddings,
    cotangent,
    char_count,
    word_place,
    block_home,
    documents,
    char_gain,
    word_gains,
    char_mixer,
    char_mixer_left,
    char_mixer_right,
    char_mixer_left_root,
    char_mixer_right_root,
    char_lift,
    char_lift_left,
    char_lift_right,
    char_lift_left_root,
    char_lift_right_root,
    word_project,
    word_project_left,
    word_project_right,
    word_project_left_root,
    word_project_right_root,
    word_output,
    word_output_left,
    word_output_right,
    word_output_left_root,
    word_output_right_root,
    feed_upper,
    feed_upper_left,
    feed_upper_right,
    feed_upper_left_root,
    feed_upper_right_root,
    feed_lower,
    feed_lower_left,
    feed_lower_right,
    feed_lower_left_root,
    feed_lower_right_root,
):
    slot_count, share_rows = (character_embeddings.shape[0], character_embeddings.shape[1])
    peer_count = lax.axis_size("dp")
    part_count = lax.axis_size("mp")
    owner_index = lax.axis_index("dp")
    words_dev = word_inputs.shape[0] * word_inputs.shape[1]
    position = jnp.stack([owner_index, lax.axis_index("mp")]).astype(jnp.int32)

    char_whole, output_line, live, live_place, own_row = gather_char(
        char_mixer, char_lift, word_output, block_home, word_place
    )
    word_vectors, kept, pooled, msum = char_forward(
        character_embeddings, block_home, char_count, char_gain, char_whole, peer_count
    )
    live_vectors, project_mat, upper_mat, lower_mat, output_mat = send_vectors(
        word_vectors.reshape(peer_count, -1, D),
        live,
        share_rows,
        word_project.reshape((3,) + word_project.shape[2:]),
        feed_upper,
        feed_lower,
        output_line,
    )
    stream, normed_one, qkv, probs, mixed = word_forward(
        live_vectors,
        live_place,
        word_inputs.reshape(words_dev, D),
        documents,
        word_gains[0],
        project_mat,
    )
    hidden, feed_part, grad_hidden, grad_mixed, grad_output_mat, gain_two, part_upper, part_lower, *every_root = feed_step(
        mixed,
        stream,
        cotangent.reshape(words_dev, D),
        output_mat,
        word_gains[1],
        upper_mat,
        lower_mat,
        [
            char_mixer_right_root,
            char_lift_right_root,
            word_project_right_root.reshape((3,) + word_project_right_root.shape[2:]),
            word_output_right_root,
            feed_upper_right_root,
            feed_lower_right_root,
        ],
    )
    mixer_root, lift_root, project_root, output_root, upper_root, lower_root = every_root
    grad_words, gain_one, grad_vectors, sum_upper, sum_lower, sum_project, sum_output = stream_grads(
        probs,
        qkv,
        grad_mixed.reshape(words_dev, -1),
        normed_one,
        project_mat,
        stream,
        grad_hidden,
        word_gains[0],
        own_row,
        (part_upper, part_lower),
        grad_output_mat,
    )
    grad_vectors, feed_part = lax.optimization_barrier((grad_vectors, feed_part))
    feed_total = lax.psum(feed_part, "mp")
    char_embeds_gradient, char_grads, grad_char_gain, grad_stream = char_backward(
        character_embeddings, block_home, char_count, char_gain, char_whole, kept, pooled, msum,
        grad_vectors.reshape(-1, share_rows, D),
        grad_words,
        peer_count,
    )
    word_sums = (sum_project, sum_output, sum_upper, sum_lower)
    char_sums, small_sums = sum_char_grads(
        char_grads, (grad_char_gain, gain_one, gain_two), word_sums, word_output.shape[1] * peer_count
    )
    parameter_count = (
        sum(
            part_count * w.size * peer_count
            for w in (word_project, word_output, feed_upper, feed_lower)
        )
        + peer_count * (char_mixer.size + char_lift.size)
        + char_gain.size
        + word_gains.size
    )
    flat = lambda a: a.reshape((-1,) + a.shape[-2:])
    results = shampoo(
        0.5 * math.sqrt(parameter_count),
        position,
        char_sums,
        small_sums,
        char_gain,
        word_gains,
        word_sums,
        hidden,
        feed_total,
        [
            tuple(flat(a) for a in group[:4]) + (group[4],)
            for group in (
                (char_mixer, char_mixer_left, char_mixer_right, char_mixer_left_root, mixer_root),
                (char_lift, char_lift_left, char_lift_right, char_lift_left_root, lift_root),
                (word_project, word_project_left, word_project_right, word_project_left_root, project_root),
                (word_output, word_output_left, word_output_right, word_output_left_root, output_root),
                (feed_upper, feed_upper_left, feed_upper_right, feed_upper_left_root, upper_root),
                (feed_lower, feed_lower_left, feed_lower_right, feed_lower_left_root, lower_root),
            )
        ],
    )
    norm, gain_grad, gains_grad, gain_new, gains_new, block_out = results[:6]
    stepped = []
    for t, group in enumerate(
        (
            (char_mixer, char_mixer_left, char_mixer_right),
            (char_lift, char_lift_left, char_lift_right),
            (word_project, word_project_left, word_project_right),
            (word_output, word_output_left, word_output_right),
            (feed_upper, feed_upper_left, feed_upper_right),
            (feed_lower, feed_lower_left, feed_lower_right),
        )
    ):
        master, left, right = group
        stepped += [
            a.reshape(b.shape)
            for a, b in zip(results[6 + 5 * t : 11 + 5 * t], (master, left, right, master, master))
        ]
    return (
        block_out.reshape(word_inputs.shape),
        grad_stream.reshape(word_inputs.shape),
        char_embeds_gradient,
        gain_grad[0],
        gains_grad,
        gain_new[0],
        gains_new,
        norm[0, 0],
        *stepped,
    )


def solution(mesh):
    placed = (
        P("dp", None, None),
        P("dp", "mp", None, None),
        P("dp", None, None),
        P("dp", "mp"),
        P("dp", None),
        P("dp"),
        P("dp", None),
        P(),
        P(),
        P(None, "dp", None),
        P(None, "dp", None),
        P(None, "dp", None),
        P(None, "dp", None),
        P(None, "dp", None),
        P(None, "dp", None),
        P(None, "dp", None),
        P(None, "dp", None),
        P(None, "dp", None),
        P(None, "dp", None),
        P(None, "mp", "dp", None),
        P(None, "mp", "dp", None),
        P(None, "mp", "dp", None),
        P(None, "mp", "dp", None),
        P(None, "mp", "dp", None),
        P("mp", "dp", None),
        P("mp", "dp", None),
        P("mp", "dp", None),
        P("mp", "dp", None),
        P("mp", "dp", None),
        P("mp", "dp", None),
        P("mp", "dp", None),
        P("mp", "dp", None),
        P("mp", "dp", None),
        P("mp", "dp", None),
        P("mp", "dp", None),
        P("mp", "dp", None),
        P("mp", "dp", None),
        P("mp", "dp", None),
        P("mp", "dp", None),
    )
    return jax.shard_map(
        local,
        mesh=mesh,
        in_specs=placed,
        out_specs=(
            P("dp", None, None),
            P("dp", None, None),
            P("dp", "mp", None, None),
            P(),
            P(),
            P(),
            P(),
            P(),
            P(None, "dp", None),
            P(None, "dp", None),
            P(None, "dp", None),
            P(None, "dp", None),
            P(None, "dp", None),
            P(None, "dp", None),
            P(None, "dp", None),
            P(None, "dp", None),
            P(None, "dp", None),
            P(None, "dp", None),
            P(None, "mp", "dp", None),
            P(None, "mp", "dp", None),
            P(None, "mp", "dp", None),
            P(None, "mp", "dp", None),
            P(None, "mp", "dp", None),
            P("mp", "dp", None),
            P("mp", "dp", None),
            P("mp", "dp", None),
            P("mp", "dp", None),
            P("mp", "dp", None),
            P("mp", "dp", None),
            P("mp", "dp", None),
            P("mp", "dp", None),
            P("mp", "dp", None),
            P("mp", "dp", None),
            P("mp", "dp", None),
            P("mp", "dp", None),
            P("mp", "dp", None),
            P("mp", "dp", None),
            P("mp", "dp", None),
        ),
        check_vma=False,
    )
```

```python
import functools
import math

import jax
import jax.numpy as jnp
from jax import lax
from jax.experimental import pallas as pl
from jax.experimental.pallas import tpu as pltpu
from jax.sharding import PartitionSpec as P

D = 512
HD = 64
FF = 2048
CHAR_BLOCK_WIDTH = 256
OWNER_BLOCKS = 10
decay_rate = 0.5
learn_rate = 1.0
gain_rate = 0.4
negative_big = -1e30

CW = 256
CHEADS = 4
CHD = 64
SPOTS = 16
KEPT = 3 * CW + CHEADS * 128 + CW
epsilon = 1e-05
BF = jnp.bfloat16
F32 = jnp.float32


def nn(a, b):
    return lax.dot_general(a, b, (((1,), (0,)), ((), ())), preferred_element_type=F32)


def nt(a, b):
    return lax.dot_general(a, b, (((1,), (1,)), ((), ())), preferred_element_type=F32)


def tn(a, b):
    return lax.dot_general(a, b, (((0,), (0,)), ((), ())), preferred_element_type=F32)


GROUPS = 4


def char_classes(share):
    listed = [(1, 4, 32), (2, 8, 16), (4, 16, 8)]
    return [(c, p, w, GROUPS // (share // w)) for c, p, w in listed if w <= share]


def order_matrix(places, words):
    row = lax.broadcasted_iota(jnp.int32, (128, SPOTS * words), 0)
    col = lax.broadcasted_iota(jnp.int32, (128, SPOTS * words), 1)
    return ((row % words) * SPOTS + row // words == col).astype(BF)


def back_matrix(places, words):
    row = lax.broadcasted_iota(jnp.int32, (SPOTS * words, 128), 0)
    col = lax.broadcasted_iota(jnp.int32, (SPOTS * words, 128), 1)
    return ((col % words) * SPOTS + col // words == row).astype(BF)


def head_stack(rows, scale):
    lane = lax.broadcasted_iota(jnp.int32, (1, CW), 1) // CHD
    return jnp.concatenate(
        [rows * jnp.where(lane == h, scale, 0.0).astype(BF) for h in range(CHEADS)], axis=0
    )


def char_forward_kernel(
    classes, home, first, x_in, counts_in, gain_ref, mats_ref, *refs
):
    orders, refs = refs[-len(classes) :], refs[: -len(classes)]
    vec_ref, kept_out, pooled_ref, msum_ref, kept, sumx, x_ref, vec, count_ref, kind, ids, batch_kind, target, taken, sems, x_sems = refs
    slots, share = count_ref.shape[:2]
    batches = plan_batches(classes, home, first, kind, ids, batch_kind)

    def load_x(slot):
        return pltpu.make_async_copy(x_in.at[slot], x_ref.at[slot], x_sems.at[slot])

    def begin(number, carry):
        for which, places, words, per in classes:

            @pl.when(batch_kind[number] == which)
            def _(per=per):
                for t in range(per):
                    slot = ids[number * GROUPS + t]

                    @pl.when(slot >= 0)
                    def _(slot=slot):
                        load_x(slot).start()

        return carry

    lax.fori_loop(0, batches, begin, 0)
    count_ref[...] = spread_counts(counts_in[...]).reshape(count_ref.shape)
    for (_, places, words, _), order_ref in zip(classes, orders):
        order_ref[...] = order_matrix(places, words)
    sumx[...] = jnp.zeros_like(sumx)
    msum_ref[...] = jnp.zeros_like(msum_ref)

    def save(slot, rows):
        return pltpu.make_async_copy(
            kept.at[slot, pl.ds(0, rows)], kept_out.at[slot, pl.ds(0, rows)], sems.at[slot]
        )

    def block(places, words, per, order_ref, number):
        picked = [ids[number * GROUPS + t] for t in range(per)]
        for slot in picked:

            @pl.when(slot >= 0)
            def _(slot=slot):
                load_x(slot).wait()

        chosen = [jnp.where(c < 0, picked[0], c) for c in picked]
        groups = [(c, g) for c in chosen for g in range(share // words)]
        cnts = [count_ref[c, pl.ds(g * words, words), :] for c, g in groups]
        xs = [
            nn(order_ref[...], x_ref[c, pl.ds(g * words * SPOTS, words * SPOTS), :]) for c, g in groups
        ]
        normed = jnp.concatenate(
            [
                (
                    x * lax.rsqrt(jnp.mean(x * x, axis=-1, keepdims=True) + epsilon) * gain_ref[...]
                ).astype(BF)
                for x in xs
            ],
            axis=0,
        )
        qkv = nn(normed, mats_ref[:, : 3 * CW]).astype(BF)
        place = lax.broadcasted_iota(jnp.int32, (places, words, CW), 0).astype(F32)
        lane = lax.broadcasted_iota(jnp.int32, (words, CHEADS * 128), 1) % 128
        word = lax.broadcasted_iota(jnp.int32, (words, CHEADS * 128), 0)
        mine = lane % words == word
        spot = (lane // words).astype(F32)
        head_row = lax.broadcasted_iota(jnp.int32, (CHEADS * 128, CW), 0) // 128
        head_col = lax.broadcasted_iota(jnp.int32, (CHEADS * 128, CW), 1) // CHD
        same_head = (head_row == head_col).astype(BF)
        far = lax.broadcasted_iota(jnp.int32, (places, words, CHEADS * 128), 0).astype(F32)
        scores = []
        for t in range(GROUPS):
            rows = qkv[t * 128 : (t + 1) * 128]
            scores.append(nt(rows[:, CW : 2 * CW], head_stack(rows[:, :CW], 1.0 / math.sqrt(CHD))))
        sums = []
        for t in range(GROUPS):
            shown = place < jnp.concatenate([cnts[t], cnts[t]], axis=1)[None]
            sums.append(jnp.sum(jnp.where(shown, xs[t].reshape(places, words, CW), 0.0), axis=0))
        probs = []
        for t in range(GROUPS):
            cnt4 = jnp.concatenate([cnts[t]] * CHEADS, axis=1)
            s = jnp.where(far < cnt4[None], scores[t].reshape(places, words, CHEADS * 128), -1e30)
            e = jnp.exp(s - jnp.max(s, axis=0)[None])
            r = jnp.where(mine & (spot < cnt4), 1.0 / jnp.sum(e, axis=0), 0.0)
            probs.append((e * r[None]).astype(BF).reshape(128, CHEADS * 128))
        columns = [nn(p, same_head) for p in probs]
        for t, (c, g) in enumerate(groups):
            rows = qkv[t * 128 : (t + 1) * 128]
            at = pl.ds(g * 128, 128)
            kept[c, at, : 3 * CW] = rows
            kept[c, at, 3 * CW : 3 * CW + CHEADS * 128] = probs[t]
            kept[c, at, 3 * CW + CHEADS * 128 :] = columns[t].astype(BF)
            own = pl.ds(pl.multiple_of(c * share + g * words, words), words)
            msum_ref[own, :] = jnp.sum(
                (columns[t] * rows[:, 2 * CW :].astype(F32)).reshape(places, words, CW), axis=0
            )
            sumx[own, :] = sums[t]
        for t in range(per):
            slot = ids[number * GROUPS + t]

            @pl.when(slot >= 0)
            def _(slot=slot):
                save(slot, share * places).start()

    def batch(number, carry):
        for (which, places, words, per), order_ref in zip(classes, orders):
            pl.when(batch_kind[number] == which)(
                functools.partial(block, places, words, per, order_ref, number)
            )
        return carry

    lax.fori_loop(0, batches, batch, 0)
    cnt2 = jnp.concatenate([count_ref[...].reshape(slots * share, 128)] * 2, axis=1)
    summed = sumx[...] + nn(msum_ref[...].astype(BF), mats_ref[:, 3 * CW : 4 * CW])
    pooled = (summed / cnt2).astype(BF)
    pooled_ref[...] = pooled
    vec[...] = nn(pooled, mats_ref[:, 4 * CW :]).astype(BF)
    plan_targets(home, target, taken, taken.shape[0])
    vec_ref[...] = jnp.zeros_like(vec_ref)

    def put(slot, carry):
        @pl.when(target[slot] >= 0)
        def _():
            vec_ref[target[slot]] = vec[pl.ds(pl.multiple_of(slot * share, share), share), :]

        return carry

    lax.fori_loop(0, slots, put, 0)

    def finish(slot, carry):
        for which, places, words, per in classes:

            @pl.when(kind[slot] == which)
            def _(places=places):
                save(slot, share * places).wait()

        return carry

    lax.fori_loop(0, slots, finish, 0)


def plan_batches(classes, home, count, kind, ids, batch_kind):
    slots = home.shape[0]
    coarse = classes[0][0] == 1

    def sort(slot, carry):
        places = count[slot, 0]
        which = jnp.where(places <= 8, 2, 4)
        if coarse:
            which = jnp.where(places <= 4, 1, which)
        kind[slot] = jnp.where(home[slot] >= 0, which, 0)
        for t in range(GROUPS):
            ids[slot * GROUPS + t] = -1
        return carry

    lax.fori_loop(0, slots, sort, 0)
    batch = jnp.int32(0)
    for which, _, _, per in classes:

        def take(slot, carry):
            batch, place = carry
            hit = kind[slot] == which

            @pl.when(hit)
            def _():
                ids[batch * GROUPS + place] = slot
                batch_kind[batch] = which

            place = jnp.where(hit, place + 1, place)
            full = place == per
            return jnp.where(full, batch + 1, batch), jnp.where(full, 0, place)

        batch, place = lax.fori_loop(0, slots, take, (batch, jnp.int32(0)))
        batch = jnp.where(place > 0, batch + 1, batch)
    return batch


def plan_targets(home, target, taken, owners):
    slots = home.shape[0]
    cap = -(-slots // owners)

    def clear(owner, carry):
        taken[owner] = 0
        return carry

    lax.fori_loop(0, owners, clear, 0)

    def take(slot, carry):
        owner = jnp.maximum(home[slot], 0)
        live = home[slot] >= 0
        target[slot] = jnp.where(live, owner * cap + taken[owner], -1)
        taken[owner] = taken[owner] + jnp.where(live, 1, 0)
        return carry

    lax.fori_loop(0, slots, take, 0)


def spread_counts(count):
    slots, share = count.shape
    row = lax.broadcasted_iota(jnp.int32, (slots * share, slots), 0) // share
    pick = (row == lax.broadcasted_iota(jnp.int32, (slots * share, slots), 1)).astype(BF)
    wide = nn(pick, count.astype(F32).astype(BF))
    mine = lax.broadcasted_iota(jnp.int32, (slots * share, share), 0) % share
    mine = mine == lax.broadcasted_iota(jnp.int32, (slots * share, share), 1)
    return nn(jnp.where(mine, wide, 0.0).astype(BF), jnp.ones((share, 128), BF))


def char_call(kernel, name, inputs, scalars, outs, scratch, in_hbm, out_hbm, flops, limit):
    vmem = pl.BlockSpec(memory_space=pltpu.VMEM)
    smem = pl.BlockSpec(memory_space=pltpu.SMEM)
    hbm = pl.BlockSpec(memory_space=pltpu.HBM)
    return pl.pallas_call(
        kernel,
        in_specs=[smem] * len(scalars) + [hbm if t in in_hbm else vmem for t in range(len(inputs))],
        out_specs=[hbm if t in out_hbm else vmem for t in range(len(outs))],
        out_shape=outs,
        scratch_shapes=scratch,
        cost_estimate=pl.CostEstimate(flops=flops, bytes_accessed=60 << 20, transcendentals=0),
        compiler_params=pltpu.CompilerParams(vmem_limit_bytes=limit << 20),
        name=name,
    )(*scalars, *inputs)


def plan_scratch(slots, share, owners):
    return [
        pltpu.VMEM((slots, share, 128), F32),
        pltpu.SMEM((slots,), jnp.int32),
        pltpu.SMEM((slots * GROUPS,), jnp.int32),
        pltpu.SMEM((slots,), jnp.int32),
        pltpu.SMEM((slots,), jnp.int32),
        pltpu.SMEM((owners,), jnp.int32),
    ]


def char_forward(x, home, counts, gain, mats, owners):
    slots, share = x.shape[:2]
    total = -(-slots // owners) * owners
    classes = char_classes(share)
    rows = share * SPOTS
    orders = [pltpu.VMEM((128, SPOTS * c[2]), BF) for c in classes]
    words_all = slots * share
    return char_call(
        functools.partial(char_forward_kernel, classes),
        "char_forward",
        [x.reshape(slots, rows, CW), counts, gain.reshape(1, CW), mats],
        (home, counts),
        [
            jax.ShapeDtypeStruct((total, share, D), BF),
            jax.ShapeDtypeStruct((slots, rows, KEPT), BF),
            jax.ShapeDtypeStruct((words_all, CW), BF),
            jax.ShapeDtypeStruct((words_all, CW), F32),
        ],
        [
            pltpu.VMEM((slots, rows, KEPT), BF),
            pltpu.VMEM((words_all, CW), F32),
            pltpu.VMEM((slots, rows, CW), BF),
            pltpu.VMEM((words_all, D), BF),
        ]
        + plan_scratch(slots, share, owners)
        + [pltpu.SemaphoreType.DMA((slots,))] * 2
        + orders,
        (0,),
        (1,),
        slots * rows * CW * CW * 16,
        60,
    )


def char_backward_kernel(
    classes, home, first, x_in, counts_in, kept_in, gv_ref, pooled_ref, msum_ref, gain_ref, mats_ref, stream_in, *refs
):
    backs, refs = refs[-len(classes) :], refs[: -len(classes)]
    orders, refs = refs[-len(classes) :], refs[: -len(classes)]
    dx_out, grads_ref, dgain_ref, stream_out, x_ref, kept, dx_ref, gp_all, gm_all, dqkv_sum, gv_all, count_ref = refs[:12]
    kind, ids, batch_kind, target, taken, x_sems, kept_sems, dx_sems, stream_sem = refs[12:]
    slots, share = count_ref.shape[:2]
    batches = plan_batches(classes, home, first, kind, ids, batch_kind)

    def load_x(slot):
        return pltpu.make_async_copy(x_in.at[slot], x_ref.at[slot], x_sems.at[slot])

    def load_kept(slot, rows):
        return pltpu.make_async_copy(
            kept_in.at[slot, pl.ds(0, rows)], kept.at[slot, pl.ds(0, rows)], kept_sems.at[slot]
        )

    def save(slot):
        return pltpu.make_async_copy(dx_ref.at[slot], dx_out.at[slot], dx_sems.at[slot])

    def begin(number, carry):
        for which, places, words, per in classes:

            @pl.when(batch_kind[number] == which)
            def _(places=places, per=per):
                for t in range(per):
                    slot = ids[number * GROUPS + t]

                    @pl.when(slot >= 0)
                    def _(slot=slot):
                        load_x(slot).start()
                        load_kept(slot, share * places).start()

        return carry

    lax.fori_loop(0, batches, begin, 0)
    stream_copy = pltpu.make_async_copy(stream_in, stream_out, stream_sem.at[0])
    stream_copy.start()

    count_ref[...] = spread_counts(counts_in[...]).reshape(count_ref.shape)
    for (_, places, words, _), order_ref, back_ref in zip(classes, orders, backs):
        order_ref[...] = order_matrix(places, words)
        back_ref[...] = back_matrix(places, words)
    plan_targets(home, target, taken, taken.shape[0])

    def take(slot, carry):
        here = pl.ds(pl.multiple_of(slot * share, share), share)

        @pl.when(target[slot] >= 0)
        def _():
            gv_all[here, :] = gv_ref[target[slot]]

        @pl.when(target[slot] < 0)
        def _():
            gv_all[here, :] = jnp.zeros((share, D), BF)

        return carry

    lax.fori_loop(0, slots, take, 0)
    gv = gv_all[...]
    cnt2 = jnp.concatenate([count_ref[...].reshape(slots * share, 128)] * 2, axis=1)
    gp = nt(gv, mats_ref[:, 4 * CW :]) / cnt2
    gp_all[...] = gp
    gpb = gp.astype(BF)
    gm_all[...] = nt(gpb, mats_ref[:, 3 * CW : 4 * CW]).astype(BF).astype(F32)
    grads_ref[:, 4 * CW :] = tn(pooled_ref[...], gv).astype(BF)
    grads_ref[:, 3 * CW : 4 * CW] = tn(msum_ref[...].astype(BF), gpb).astype(BF)
    dqkv_sum[...] = jnp.zeros_like(dqkv_sum)
    dgain_ref[...] = jnp.zeros_like(dgain_ref)

    def block(places, words, per, order_ref, back_ref, number):
        picked = [ids[number * GROUPS + t] for t in range(per)]
        chosen = [jnp.where(c < 0, picked[0], c) for c in picked]
        weights = [jnp.where(c < 0, 0.0, 1.0) for c in picked]
        targets = [jnp.where(c < 0, slots, c) for c in picked]
        for slot in picked:

            @pl.when(slot >= 0)
            def _(slot=slot):
                load_x(slot).wait()
                load_kept(slot, share * places).wait()

        groups = [
            (c, g, weight, target)
            for c, weight, target in zip(chosen, weights, targets)
            for g in range(share // words)
        ]
        gain = gain_ref[...]
        eighth = 1.0 / math.sqrt(CHD)
        place = lax.broadcasted_iota(jnp.int32, (places, words, CW), 0).astype(F32)
        word_grads = []
        row_grads = []
        out_grads = []
        for t, (c, g, weight, _) in enumerate(groups):
            mine = pl.ds(pl.multiple_of(c * share + g * words, words), words)
            cnt = count_ref[c, pl.ds(g * words, words), :]
            shown = place < jnp.concatenate([cnt, cnt], axis=1)[None]
            word_grads.append(gm_all[mine, :] * weight)
            out_grads.append(jnp.where(shown, (gp_all[mine, :] * weight)[None], 0.0).reshape(128, CW))
            row_grads.append(
                jnp.where(shown, word_grads[t][None], 0.0).reshape(128, CW).astype(BF)
            )
        at = [pl.ds(g * 128, 128) for _, g, _, _ in groups]
        queries = [kept[c, at[t], :CW] for t, (c, *_) in enumerate(groups)]
        keys = [kept[c, at[t], CW : 2 * CW] for t, (c, *_) in enumerate(groups)]
        products = [
            nt(kept[c, at[t], 2 * CW : 3 * CW], head_stack(row_grads[t], 1.0))
            for t, (c, *_) in enumerate(groups)
        ]
        scores = []
        for t, (c, *_) in enumerate(groups):
            p = kept[c, at[t], 3 * CW : 3 * CW + CHEADS * 128].astype(F32)
            p3 = p.reshape(places, words, CHEADS * 128)
            u = p3 * products[t].reshape(places, words, CHEADS * 128)
            scores.append((u - p3 * jnp.sum(u, axis=0)[None]).astype(BF).reshape(128, CHEADS * 128))
        xs = [
            nn(order_ref[...], x_ref[c, pl.ds(g * words * SPOTS, words * SPOTS), :])
            for c, g, _, _ in groups
        ]
        scales = [lax.rsqrt(jnp.mean(x * x, axis=-1, keepdims=True) + epsilon) for x in xs]
        normed = jnp.concatenate([(x * s * gain).astype(BF) for x, s in zip(xs, scales)], axis=0)
        grads = []
        for t, (c, *_) in enumerate(groups):
            dk = nn(scores[t], head_stack(queries[t], eighth))
            stacked = jnp.concatenate(
                [scores[t][:, h * 128 : (h + 1) * 128] for h in range(CHEADS)], axis=0
            )
            dq = tn(stacked, head_stack(keys[t], eighth))
            column = kept[c, at[t], 3 * CW + CHEADS * 128 :].astype(F32)
            dv = (column.reshape(places, words, CW) * word_grads[t][None]).reshape(128, CW)
            grads.append(jnp.concatenate([dq.astype(BF), dk.astype(BF), dv.astype(BF)], axis=1))
        grads = jnp.concatenate(grads, axis=0)
        dn_all = nt(grads, mats_ref[:, : 3 * CW])
        dqkv_sum[...] += tn(normed, grads)
        dgain = jnp.zeros((1, CW), F32)
        for t, (c, g, _, target) in enumerate(groups):
            x, scale = xs[t], scales[t]
            dn = dn_all[t * 128 : (t + 1) * 128]
            xr = x * scale
            dgain = dgain + jnp.sum(xr * dn, axis=0, keepdims=True)
            w = dn * gain
            inner = jnp.mean(xr * w, axis=-1, keepdims=True)
            dx = out_grads[t] + scale * (w - xr * inner)
            dx_ref[target, pl.ds(g * words * SPOTS, words * SPOTS), :] = nn(
                back_ref[...], dx.astype(BF)
            ).astype(BF)
        dgain_ref[...] += dgain
        for slot in picked:

            @pl.when(slot >= 0)
            def _(slot=slot):
                save(slot).start()

    def batch(number, carry):
        for (which, places, words, per), order_ref, back_ref in zip(classes, orders, backs):
            pl.when(batch_kind[number] == which)(
                functools.partial(block, places, words, per, order_ref, back_ref, number)
            )
        return carry

    lax.fori_loop(0, batches, batch, 0)
    grads_ref[:, : 3 * CW] = dqkv_sum[...].astype(BF)

    def empty(slot, carry):
        @pl.when(kind[slot] == 0)
        def _():
            dx_ref[slot] = jnp.zeros(dx_ref.shape[1:], BF)
            save(slot).start()

        return carry

    lax.fori_loop(0, slots, empty, 0)

    def finish(slot, carry):
        save(slot).wait()
        return carry

    lax.fori_loop(0, slots, finish, 0)
    stream_copy.wait()


def char_backward(x, home, counts, gain, mats, kept, pooled, msum, grad_vectors, grad_stream, owners):
    slots, share = x.shape[:2]
    classes = char_classes(share)
    rows = share * SPOTS
    orders = [pltpu.VMEM((128, SPOTS * c[2]), BF) for c in classes]
    words_all = slots * share
    dx, grads, dgain, stream = char_call(
        functools.partial(char_backward_kernel, classes),
        "char_backward",
        [
            x.reshape(slots, rows, CW), counts, kept, grad_vectors, pooled, msum, gain.reshape(1, CW), mats,
            grad_stream,
        ],
        (home, counts),
        [
            jax.ShapeDtypeStruct((slots, rows, CW), BF),
            jax.ShapeDtypeStruct(mats.shape, BF),
            jax.ShapeDtypeStruct((1, CW), F32),
            jax.ShapeDtypeStruct(grad_stream.shape, grad_stream.dtype),
        ],
        [
            pltpu.VMEM((slots, rows, CW), BF),
            pltpu.VMEM((slots, rows, KEPT), BF),
            pltpu.VMEM((slots + 1, rows, CW), BF),
            pltpu.VMEM((words_all, CW), F32),
            pltpu.VMEM((words_all, CW), F32),
            pltpu.VMEM((CW, 3 * CW), F32),
            pltpu.VMEM((words_all, D), BF),
        ]
        + plan_scratch(slots, share, owners)
        + [pltpu.SemaphoreType.DMA((slots,))] * 3
        + [pltpu.SemaphoreType.DMA((1,))]
        + orders
        + [pltpu.VMEM((SPOTS * c[2], 128), BF) for c in classes],
        (0, 2),
        (0, 3),
        slots * rows * CW * CW * 28,
        53,
    )
    return dx.reshape(x.shape), grads, dgain, stream


MESH_ID = pl.DeviceIdType.MESH


def greet_start(sizes, me):
    barrier = pltpu.get_barrier_semaphore()
    for axis, n in sizes.items():
        for d in range(1, n):
            pl.semaphore_signal(
                barrier, inc=1, device_id={axis: lax.rem(me[axis] + d, n)}, device_id_type=MESH_ID
            )


def greet_wait(sizes):
    pl.semaphore_wait(pltpu.get_barrier_semaphore(), sum(n - 1 for n in sizes.values()))


def greet(sizes, me):
    greet_start(sizes, me)
    greet_wait(sizes)


def remote(source, target, sems, at, axis, peer):
    return pltpu.make_async_remote_copy(
        src_ref=source,
        dst_ref=target,
        send_sem=sems[0].at[at],
        recv_sem=sems[1].at[at],
        device_id={axis: peer},
        device_id_type=MESH_ID,
    )


def pair_gather_stages(own_of, sems, axis, n, mine, begin, late):
    chips = n // 2
    core = lax.rem(mine, 2)
    chip = mine // 2
    sibling = chip * 2 + 1 - core

    def start():
        for d in range(1, chips):
            there = lax.rem(chip + d, chips) * 2 + core
            remote(own_of(mine), own_of(mine), sems, d, axis, there).start()
        remote(own_of(mine), own_of(mine), sems, chips, axis, sibling).start()

    def hand_on():
        for d in range(1, chips):
            came = lax.rem(chip + chips - d, chips) * 2 + core
            remote(own_of(mine), own_of(came), sems, d, axis, sibling).wait_recv()
            remote(own_of(came), own_of(came), sems, chips + d, axis, sibling).start()

    def finish():
        for d in range(1, 2 * chips):
            remote(own_of(mine), own_of(mine), sems, d, axis, sibling).wait_send()
            if d >= chips:
                remote(own_of(mine), own_of(mine), sems, d, axis, sibling).wait_recv()

    return [(begin, start), (late, hand_on), (90.0, finish)]


def pair_part_stages(x, held, came, out, sems, axis, n, mine, begin, late):
    chips = n // 2
    core = lax.rem(mine, 2)
    chip = mine // 2
    sibling = chip * 2 + 1 - core

    def start():
        remote(x.at[:, 1 - core], came, sems, 0, axis, sibling).start()

    def onward():
        remote(x.at[:, 1 - core], came, sems, 0, axis, sibling).wait()
        for d in range(chips):
            there = lax.rem(chip + 1 + d, chips)
            came[there] = (came[there].astype(F32) + x[there, core].astype(F32)).astype(came.dtype)
            if d < chips - 1:
                remote(
                    came.at[there], held.at[chip], sems, 1 + d, axis, there * 2 + core
                ).start()

    def finish():
        held[chip] = came[chip]
        for d in range(chips - 1):
            remote(came.at[chip], held.at[chip], sems, 1 + d, axis, sibling).wait()
        total = held[0].astype(F32)
        for p in range(1, chips):
            total = total + held[p].astype(F32)
        out[...] = total.astype(out.dtype)

    return [(begin, start), (late, onward), (80.0, finish)]


def line_gather_stages(out, sems, axis, n, mine, begin, each, cut=()):
    def piece(block):
        return out.at[(block,) + cut]

    def step(k):
        for way in range(2):
            block = mine - k if way == 0 else mine + k
            here = (block >= 0) & (block < n)
            block = jnp.clip(block, 0, n - 1)
            onward = mine + 1 if way == 0 else mine - 1
            room = (onward >= 0) & (onward < n)
            peer = jnp.clip(onward, 0, n - 1)
            if k > 0:

                @pl.when(here)
                def _(way=way, block=block):
                    remote(piece(block), piece(block), sems, way * n + k - 1, axis, mine).wait_recv()

            if k < n - 1:

                @pl.when(here & room)
                def _(way=way, block=block, peer=peer):
                    remote(piece(block), piece(block), sems, way * n + k, axis, peer).start()

    def finish():
        for way in range(2):
            for k in range(n - 1):
                block = mine - k if way == 0 else mine + k
                sent = (mine < n - 1) & (block >= 0) if way == 0 else (mine > 0) & (block < n)

                @pl.when(sent)
                def _(way=way, k=k):
                    remote(piece(mine), piece(mine), sems, way * n + k, axis, mine).wait_send()

    stages = [(begin + each * k, functools.partial(step, k)) for k in range(n)]
    return stages + [(95.0, finish)]


def line_part_stages(x, held, out, sems, axis, n, mine, begin, each, end=70.0, cut=()):
    def step(t):
        for way in range(2):
            distance = mine if way == 0 else n - 1 - mine
            turn = t - distance
            here = (turn >= 0) & (turn < n - 1 - distance)
            turn = jnp.clip(turn, 0, n - 1)
            block = n - 1 - turn if way == 0 else turn
            peer = jnp.clip(mine + 1 if way == 0 else mine - 1, 0, n - 1)
            at = way * n + block

            @pl.when(here & (distance == 0))
            def _(way=way, block=block, peer=peer, at=at):
                remote(
                    x.at[(block,) + cut], held.at[(way, block) + cut], sems, at, axis, peer
                ).start()

            @pl.when(here & (distance > 0))
            def _(way=way, block=block, peer=peer, at=at):
                place = held.at[(way, block) + cut]
                remote(place, place, sems, at, axis, mine).wait_recv()
                held[(way, block) + cut] = (
                    held[(way, block) + cut].astype(F32) + x[(block,) + cut].astype(F32)
                ).astype(x.dtype)
                remote(place, place, sems, at, axis, peer).start()

    def finish():
        out[cut or ...] = x[(mine,) + cut].astype(F32)
        for way, there in ((0, mine > 0), (1, mine < n - 1)):

            @pl.when(there)
            def _(way=way):
                here = held.at[(way, mine) + cut]
                remote(here, here, sems, way * n + mine, axis, mine).wait_recv()
                out[cut or ...] += held[(way, mine) + cut].astype(F32)

        for way in range(2):
            for block in range(n):
                further = block > mine if way == 0 else block < mine

                @pl.when(further)
                def _(way=way, block=block):
                    here = held.at[(way, block) + cut]
                    remote(here, here, sems, way * n + block, axis, mine).wait_send()

    stages = [(begin + each * k, functools.partial(step, k)) for k in range(n - 1)]
    return stages + [(end, finish)]


def halves(rows):
    return [(slice(h * (rows // 2), (h + 1) * (rows // 2)), slice(None)) for h in range(2)]


def direct_stages(source_of, target, sems, axis, n, mine, begin, done, end, cols=None):
    def piece(block):
        return target.at[block] if cols is None else target.at[block, :, cols]

    def start():
        for d in range(1, n):
            peer = lax.rem(mine + d, n)
            remote(source_of(peer), piece(mine), sems, d, axis, peer).start()

    def finish():
        for d in range(1, n):
            remote(source_of(mine), piece(mine), sems, d, axis, mine).wait()
        done()

    return [(begin, start), (end, finish)]


def exchange(name, number, tasks):
    sizes = {axis: lax.axis_size(axis) for _, axis, _ in tasks}
    outs, scratch, counts, shapers = [], [], [], []
    for kind, axis, arrays in tasks:
        n = sizes[axis]
        array = arrays[0]
        shaper = lambda a: a
        if kind == "gather":
            rows = array.shape[1]
            cols = sum(a.shape[0] * a.shape[2] for a in arrays)
            made = jax.ShapeDtypeStruct((n * rows, cols) if rows % 16 == 0 else (n, rows, cols), BF)
            shaper = lambda a, rows=rows, cols=cols, n=n: a.reshape(n * rows, cols)
        elif kind == "gather_mid":
            lead, rows, cols = array.shape
            made = jax.ShapeDtypeStruct(
                (lead, n * rows, cols) if rows % 16 == 0 else (n, lead, rows, cols), array.dtype
            )
            if rows % 16:
                shaper = lambda a, lead=lead, rows=rows, cols=cols, n=n: a.transpose(1, 0, 2, 3).reshape(
                    lead, n * rows, cols
                )
        else:
            block = array.shape if kind in ("line_gather", "total") else array.shape[1:]
            if kind == "part":
                block = array.shape[2:]
            summed = kind in ("part", "line_part", "total")
            made = jax.ShapeDtypeStruct(block if summed else (n,) + block, F32 if summed else array.dtype)
        outs.append(made)
        shapers.append(shaper)
        counts.append(len(arrays))
        scratch += [pltpu.SemaphoreType.DMA((4 * n,)), pltpu.SemaphoreType.DMA((4 * n,))]
        if kind == "part":
            scratch += [pltpu.VMEM((n // 2,) + block, array.dtype)] * 2
        if kind == "total":
            scratch.append(pltpu.VMEM((n,) + block, array.dtype))
        if kind == "line_part":
            scratch.append(pltpu.VMEM((2, n) + block, array.dtype))
    total_ins = sum(counts)

    def kernel(*refs):
        ins, at = [], 0
        for count in counts:
            ins.append(refs[at : at + count])
            at += count
        results = refs[at : at + len(tasks)]
        rest = list(refs[at + len(tasks) :])
        me = {axis: lax.axis_index(axis) for axis in sizes}
        greet(sizes, me)
        stages = []
        for (kind, axis, _), xs, out in zip(tasks, ins, results):
            sems = (rest.pop(0), rest.pop(0))
            n, mine, x = sizes[axis], me[axis], xs[0]
            if kind == "line_gather":
                out[mine] = x[...]
                for h, cut in enumerate(halves(x.shape[0])):
                    sems_half = tuple(s.at[pl.ds(2 * n * h, 2 * n)] for s in sems)
                    stages += line_gather_stages(out, sems_half, axis, n, mine, 0.05 * h, 6.0, cut)
            elif kind == "line_part":
                stages += line_part_stages(x, rest.pop(0), out, sems, axis, n, mine, 0.0, 6.0)
            elif kind == "part":
                held, came = rest.pop(0), rest.pop(0)
                stages += pair_part_stages(x, held, came, out, sems, axis, n, mine, 0.1, 1.0)
            elif kind in ("gather", "gather_mid"):
                if kind == "gather":
                    rows = x.shape[1]
                    if rows % 16 == 0:
                        own_of = lambda i, out=out, rows=rows: out.at[
                            pl.ds(pl.multiple_of(i * rows, 16), rows), :
                        ]
                    else:
                        own_of = lambda i, out=out: out.at[i]
                    own, col = own_of(mine), 0
                    for piece in xs:
                        for t in range(piece.shape[0]):
                            own[:, col : col + piece.shape[2]] = piece[t].astype(BF)
                            col += piece.shape[2]
                else:
                    rows = x.shape[1]
                    if rows % 16 == 0:
                        own_of = lambda i, out=out, rows=rows: out.at[
                            :, pl.ds(pl.multiple_of(i * rows, 16), rows), :
                        ]
                    else:
                        own_of = lambda i, out=out: out.at[i]
                    own_of(mine)[...] = x[...]
                if axis == "dp":
                    stages += pair_gather_stages(own_of, sems, axis, n, mine, 0.2, 6.0 * lax.axis_size("mp") - 11.5)
                else:

                    def start(own_of=own_of, sems=sems, axis=axis, n=n, mine=mine):
                        for d in range(1, n):
                            peer = lax.rem(mine + d, n)
                            remote(own_of(mine), own_of(mine), sems, d, axis, peer).start()

                    def finish(own_of=own_of, sems=sems, axis=axis, n=n, mine=mine):
                        for d in range(1, n):
                            remote(own_of(mine), own_of(mine), sems, d, axis, mine).wait()

                    stages += [(0.15, start), (90.0, finish)]
            elif kind == "total":
                held = rest.pop(0)
                held[mine] = x[...]

                def done(held=held, out=out, n=n):
                    total = held[0].astype(F32)
                    for p in range(1, n):
                        total = total + held[p].astype(F32)
                    out[...] = total

                stages += direct_stages(
                    lambda p, held=held, mine=mine: held.at[mine], held, sems, axis, n, mine, 0.3, done, 60.0
                )
            else:
                out[mine] = x[mine]
                stages += direct_stages(
                    lambda p, x=x: x.at[p], out, sems, axis, n, mine, 0.0, lambda: None, 60.0
                )
        for _, run in sorted(stages, key=lambda stage: stage[0]):
            run()

    vmem = pl.BlockSpec(memory_space=pltpu.VMEM)
    results = pl.pallas_call(
        kernel,
        out_shape=outs,
        in_specs=[vmem] * total_ins,
        out_specs=[vmem] * len(tasks),
        scratch_shapes=scratch,
        compiler_params=pltpu.CompilerParams(
            collective_id=number, has_side_effects=True, vmem_limit_bytes=24 << 20
        ),
        name=name,
    )(*[array for _, _, arrays in tasks for array in arrays])
    return [shaper(a) for shaper, a in zip(shapers, results)]


def by_chip(array):
    return array.reshape(lax.axis_size("dp") // 2, 2, -1, array.shape[-1])


def sum_char_grads(grads, gains, word_sums, block_rows, block_own):
    n, m = lax.axis_size("dp"), lax.axis_size("mp")
    grads = by_chip(grads)
    rows, cols = grads.shape[2:]
    slim = cols // m
    small = jax.ShapeDtypeStruct((8, D), F32)

    share = block_own.shape[0]

    def kernel(x, gain_char, gain_one, gain_two, own_ref, *refs):
        words = refs[: len(word_sums)]
        (out, small_out, block_out, held, came, total_dp, cut, cut_held, merged, small_dp, small_mp, *sems) = refs[len(word_sums) :]
        pairs = [tuple(sems[2 * t : 2 * t + 2]) for t in range(8)]
        i, j = lax.axis_index("dp"), lax.axis_index("mp")
        greet_start({"dp": n, "mp": m}, {"dp": i, "mp": j})
        block_out[j] = own_ref[...]
        greet_wait({"dp": n, "mp": m})
        line = []
        for h, span in enumerate(halves(share)):
            line += line_gather_stages(block_out, pairs[6 + h], "mp", m, j, 0.05 * h, 1.0, span)
        line = [run for _, run in sorted(line, key=lambda stage: stage[0])]
        part = [
            run for _, run in pair_part_stages(x, held, came, total_dp, pairs[0], "dp", n, i, 0.0, 0.0)
        ]
        part[0]()
        line.pop(0)()
        line.pop(0)()
        squares = jnp.zeros((1, 1), F32)
        for t, word in enumerate(words):
            if t == 1:
                wide = word[pl.ds(pl.multiple_of(j * block_rows, 16), block_rows), :].astype(F32)
            else:
                wide = word[...].astype(F32)
            squares = squares + jnp.sum(jnp.sum(wide * wide, axis=0, keepdims=True), axis=1, keepdims=True)
        row = lax.broadcasted_iota(jnp.int32, (8, D), 0)
        small_dp[i] = jnp.where(row == 3, squares * (1.0 / n), 0.0)
        small_dp[i, 0:1, : gain_char.shape[1]] = gain_char[...]
        small_dp[i, 1:2, :] = gain_one[...]
        small_dp[i, 2:3, :] = gain_two[...]
        part[1]()

        def small_done():
            total = small_dp[0]
            for p in range(1, n):
                total = total + small_dp[p]
            small_mp[j] = total

        def small_end():
            total = small_mp[0]
            for p in range(1, m):
                total = total + small_mp[p]
            small_out[...] = total

        def cut_done():
            total = cut_held[0].astype(F32)
            for p in range(1, m):
                total = total + cut_held[p].astype(F32)
            merged[j] = total.astype(BF)

        one = direct_stages(lambda p: small_dp.at[i], small_dp, pairs[1], "dp", n, i, 0, small_done, 0)
        two = direct_stages(lambda p: small_mp.at[j], small_mp, pairs[2], "mp", m, j, 0, small_end, 0)
        three = direct_stages(lambda p: cut.at[p], cut_held, pairs[3], "mp", m, j, 0, cut_done, 0)
        four = direct_stages(lambda p: merged.at[j], merged, pairs[4], "mp", m, j, 0, lambda: None, 0)
        one[0][1]()
        part[2]()
        line.pop(0)()
        line.pop(0)()
        for p in range(m):
            cut[p] = total_dp[:, p * slim : (p + 1) * slim]
        cut_held[j] = cut[j]
        three[0][1]()
        one[1][1]()
        two[0][1]()
        three[1][1]()
        four[0][1]()
        two[1][1]()
        four[1][1]()
        line.pop(0)()
        line.pop(0)()
        if rows % 16 == 0:
            own_of = lambda d: out.at[pl.ds(pl.multiple_of(d * rows, 16), rows), :]
        else:
            own_of = lambda d: out.at[d]
        own = own_of(i)
        for p in range(m):
            own[:, p * slim : (p + 1) * slim] = merged[p]
        for _, run in pair_gather_stages(own_of, pairs[5], "dp", n, i, 0, 0):
            run()
        for run in line:
            run()

    vmem = pl.BlockSpec(memory_space=pltpu.VMEM)
    sums, smalls, block = pl.pallas_call(
        kernel,
        out_shape=[
            jax.ShapeDtypeStruct((n * rows, cols) if rows % 16 == 0 else (n, rows, cols), BF),
            jax.ShapeDtypeStruct(small.shape, F32),
            jax.ShapeDtypeStruct((m,) + block_own.shape, BF),
        ],
        in_specs=[vmem] * (5 + len(word_sums)),
        out_specs=[vmem] * 3,
        scratch_shapes=[
            pltpu.VMEM((n // 2, rows, cols), BF),
            pltpu.VMEM((n // 2, rows, cols), BF),
            pltpu.VMEM((rows, cols), BF),
            pltpu.VMEM((m, rows, slim), BF),
            pltpu.VMEM((m, rows, slim), BF),
            pltpu.VMEM((m, rows, slim), BF),
            pltpu.VMEM((n,) + small.shape, F32),
            pltpu.VMEM((m,) + small.shape, F32),
        ]
        + [pltpu.SemaphoreType.DMA((2 * max(n, m),))] * 16,
        compiler_params=pltpu.CompilerParams(
            collective_id=20, has_side_effects=True, vmem_limit_bytes=24 << 20
        ),
        name="sum_char_grads",
    )(grads, *gains, block_own, *word_sums)
    return sums.reshape(n * rows, cols), smalls, block


ROWS = 256


def rms_scale(values):
    return lax.rsqrt(jnp.mean(values * values, axis=-1, keepdims=True) + epsilon)


def norm_back(values, scale, gain_row, grad):
    weighted = grad * gain_row
    inner = jnp.mean(values * weighted, axis=-1, keepdims=True)
    return scale * weighted - values * (scale * scale * scale) * inner


def word_forward_kernel(
    width, vec_ref, place_ref, words_ref, doc_all_ref, doc_row_ref, gain_ref, project_ref,
    stream_ref, normed_ref, qkv_ref, probs_ref, mixed_ref, keys, values, doc_ref, placed
):
    step = pl.program_id(0)
    parts, kept_rows = vec_ref.shape[:2]
    words = kept_rows // OWNER_BLOCKS

    @pl.when(step == 0)
    def _():
        doc_ref[...] = tn(doc_all_ref[...].astype(F32).astype(BF), jnp.ones((1, 128), BF))
        numbers = lax.broadcasted_iota(jnp.int32, (placed.shape[0], parts * words), 0)
        hits = [(numbers == place_ref[b : b + 1, :]).astype(BF) for b in range(OWNER_BLOCKS)]
        vectors = [
            vec_ref[p, b * words : (b + 1) * words, :] for b in range(OWNER_BLOCKS) for p in range(parts)
        ]
        placed[...] = nn(jnp.concatenate(hits, axis=1), jnp.concatenate(vectors, axis=0))

    here = pl.ds(pl.multiple_of(step * ROWS, ROWS), ROWS)
    stream = words_ref[...].astype(F32) + placed[here, :]
    stream_ref[...] = stream
    normed = (stream * rms_scale(stream) * gain_ref[...]).astype(BF)
    normed_ref[...] = normed
    qkv = nn(normed, project_ref[...]).astype(BF)
    qkv_ref[...] = qkv
    first = pl.ds(pl.multiple_of(step * ROWS, ROWS), ROWS)
    keys[first, :] = qkv[:, width : 2 * width]
    values[first, :] = qkv[:, 2 * width :]
    queries = (qkv[:, :width].astype(F32) * (1.0 / math.sqrt(HD))).astype(BF)

    def attend(number):
        count = (number + 1) * ROWS
        same = jnp.concatenate([doc_ref[:count, :]] * (ROWS // 128), axis=1) == doc_row_ref[...].astype(F32)
        key_at = lax.broadcasted_iota(jnp.int32, (count, ROWS), 0)
        query_at = lax.broadcasted_iota(jnp.int32, (count, ROWS), 1) + number * ROWS
        allowed = same & (key_at <= query_at)
        parts = []
        for head in range(width // HD):
            at = slice(head * HD, (head + 1) * HD)
            scores = jnp.where(allowed, nt(keys[:count, at], queries[:, at]), negative_big)
            raised = jnp.exp(scores - jnp.max(scores, axis=0, keepdims=True))
            probs = (raised * (1.0 / jnp.sum(raised, axis=0, keepdims=True))).astype(BF)
            probs_ref[head, :count, :] = probs
            parts.append(tn(values[:count, at], probs).T)
        mixed_ref[...] = jnp.concatenate(parts, axis=1).astype(BF)

    for number in range(doc_all_ref.shape[1] // ROWS):
        pl.when(step == number)(functools.partial(attend, number))


def word_forward(vectors, places, words, documents, gain, project):
    length = words.shape[0]
    width = project.shape[1] // 3
    heads = width // HD
    rows = lambda cols: pl.BlockSpec((ROWS, cols), lambda i: (i, 0))
    full = lambda shape: pl.BlockSpec(shape, lambda i: (0,) * len(shape))
    return pl.pallas_call(
        functools.partial(word_forward_kernel, width),
        grid=(length // ROWS,),
        in_specs=[
            full(vectors.shape),
            full(places.shape),
            rows(D),
            full((1, length)),
            pl.BlockSpec((1, ROWS), lambda i: (0, i)),
            full((1, D)),
            full(project.shape),
        ],
        out_specs=[
            rows(D),
            rows(D),
            rows(3 * width),
            pl.BlockSpec((heads, length, ROWS), lambda i: (0, 0, i)),
            rows(width),
        ],
        out_shape=[
            jax.ShapeDtypeStruct((length, D), F32),
            jax.ShapeDtypeStruct((length, D), BF),
            jax.ShapeDtypeStruct((length, 3 * width), BF),
            jax.ShapeDtypeStruct((heads, length, length), BF),
            jax.ShapeDtypeStruct((length, width), BF),
        ],
        scratch_shapes=[
            pltpu.VMEM((length, width), BF),
            pltpu.VMEM((length, width), BF),
            pltpu.VMEM((length, 128), F32),
            pltpu.VMEM((length, D), F32),
        ],
        compiler_params=pltpu.CompilerParams(vmem_limit_bytes=32 << 20),
        name="word_forward",
    )(
        vectors,
        places,
        words,
        documents.reshape(1, length),
        documents.reshape(1, length),
        gain.reshape(1, D),
        project,
    )


FEED_ROWS = 512


def feed_rows(mixed, output_ref, stream, grad_feed, gain, upper, lower):
    hidden = stream
    for j, part in enumerate(mixed):
        width = part.shape[1]
        hidden = hidden + nn(part, output_ref[j * width : (j + 1) * width, :])
    normed = (hidden * rms_scale(hidden) * gain).astype(BF)
    raised = nn(normed, upper)
    constant = math.sqrt(2.0 / math.pi)
    square = raised * raised
    curve = jnp.tanh(constant * raised * (1.0 + 0.044715 * square))
    half = 0.5 * (1.0 + curve)
    active = (raised * half).astype(BF)
    slope = half + 0.5 * raised * (1.0 - curve * curve) * constant * (1.0 + 3.0 * 0.044715 * square)
    grad_raised = (nt(grad_feed, lower) * slope).astype(BF)
    return (
        hidden,
        nn(active, lower).astype(BF),
        nt(grad_raised, upper).astype(BF),
        tn(normed, grad_raised),
        tn(active, grad_feed),
    )


def attention_back(width, probs_ref, qkv_ref, grad_ref, grads, key_sum, value_sum):
    eighth = 1.0 / math.sqrt(HD)
    key_sum[...] = jnp.zeros_like(key_sum)
    value_sum[...] = jnp.zeros_like(value_sum)
    for number in range(qkv_ref.shape[0] // ROWS):
        rows = slice(number * ROWS, (number + 1) * ROWS)
        count = (number + 1) * ROWS
        queries = (qkv_ref[rows, :width].astype(F32) * eighth).astype(BF)
        parts = []
        for head in range(width // HD):
            at = slice(head * HD, (head + 1) * HD)
            keys = qkv_ref[:count, width + head * HD : width + (head + 1) * HD]
            values = qkv_ref[:count, 2 * width + head * HD : 2 * width + (head + 1) * HD]
            grad = grad_ref[rows, at]
            probs = probs_ref[head, :count, rows]
            wide = probs.astype(F32)
            product = wide * nt(values, grad)
            scores = (product - wide * jnp.sum(product, axis=0, keepdims=True)).astype(BF)
            key_sum[head, :count, :] += nn(scores, queries[:, at])
            value_sum[head, :count, :] += nn(probs, grad)
            parts.append(tn(keys, scores).T * eighth)
        grads[rows, :width] = jnp.concatenate(parts, axis=1).astype(BF)
    for head in range(width // HD):
        grads[:, width + head * HD : width + (head + 1) * HD] = key_sum[head].astype(BF)
        grads[:, 2 * width + head * HD : 2 * width + (head + 1) * HD] = value_sum[head].astype(BF)


def shampoo_kernel(
    threshold, position, char_ref, small_ref, gain_ref, gains_ref, project, output, upper, lower, block_in, *refs
):
    given_in, refs = refs[:30], refs[30:]
    norm_ref, gain_grad_ref, gains_grad_ref, gain_new_ref, gains_new_ref, block_out = refs[:6]
    made_out, refs = refs[6:36], refs[36:]
    given, made = refs[:30], refs[30:60]
    in_sems, out_sems = refs[60:]
    loads = [pltpu.make_async_copy(a, b, in_sems.at[t]) for t, (a, b) in enumerate(zip(given_in, given))]
    order = (4, 5, 2, 3, 0, 1)
    for number in order:
        for t in range(5):
            loads[5 * number + t].start()
    saves = [pltpu.make_async_copy(a, b, out_sems.at[t]) for t, (a, b) in enumerate(zip(made, made_out))]
    saves.append(pltpu.make_async_copy(block_in, block_out, out_sems.at[30]))
    saves[30].start()
    me = position[0]
    char = char_ref[...].astype(F32)
    small = small_ref[...]
    lanes = lax.broadcasted_iota(jnp.int32, small.shape, 0)
    squares = (
        jnp.sum(jnp.sum(char * char, axis=0, keepdims=True), axis=1, keepdims=True)
        + jnp.sum(
            jnp.sum(jnp.where(lanes < 3, small * small, 0.0), axis=0, keepdims=True),
            axis=1,
            keepdims=True,
        )
        + small[3:4, :1]
    )
    norm = jnp.sqrt(squares)
    factor = jnp.minimum(1.0, threshold / norm)
    norm_ref[...] = norm
    gain_grad = small[0:1, :CW] * factor
    gain_grad_ref[...] = gain_grad
    gain_new_ref[...] = gain_ref[...] - gain_rate * gain_grad
    gains_grad = small[1:3, :] * factor
    gains_grad_ref[...] = gains_grad
    gains_new_ref[...] = gains_ref[...] - gain_rate * gains_grad
    width = project.shape[1] // 3
    own = pl.ds(pl.multiple_of(position[1] * width, 16), width)

    def whole_of(number, t):
        if number == 0:
            return char_ref[:, t * CW : (t + 1) * CW]
        if number == 1:
            return char_ref[:, 4 * CW :]
        if number == 2:
            return project[:, t * width : (t + 1) * width]
        return (output[own, :], upper[...], lower[...])[number - 3]

    def chosen(rows, cols):
        row = lax.broadcasted_iota(jnp.int32, (rows, cols), 0) + me * rows
        return (row == lax.broadcasted_iota(jnp.int32, (rows, cols), 1)).astype(BF)

    half = (1.0 - decay_rate) * factor * factor
    for number in order:
        for t in range(5):
            loads[5 * number + t].wait()
        master, left, right, left_root, right_root = given[5 * number : 5 * number + 5]
        grad_out, left_out, right_out, new_out, copy_out = made[5 * number : 5 * number + 5]
        for t in range(master.shape[0]):
            grad = whole_of(number, t)
            rows = nn(chosen(master.shape[1], grad.shape[0]), grad)
            grad_out[t] = rows * factor
            left_out[t] = decay_rate * left[t] + half * nt(rows.astype(BF), grad)
            cols = nt(grad, chosen(right.shape[1], grad.shape[1])).astype(BF)
            right_out[t] = decay_rate * right[t] + half * tn(cols, grad)
            turned = (nn(left_root[t].astype(BF), grad) * factor).astype(BF)
            root = right_root[:, t * grad.shape[1] : (t + 1) * grad.shape[1]]
            new = master[t] - learn_rate * nn(turned, root)
            new_out[t] = new
            copy_out[t] = new.astype(BF)
        for t in range(5):
            saves[5 * number + t].start()
    for save in saves:
        save.wait()


def shampoo(threshold, position, char_sums, small, gain, gains, word_sums, block_out, given):
    flat = []
    shapes = []
    for master, left, right, left_root, right_root in given:
        flat += [master, left, right, left_root, right_root]
        shapes += [
            jax.ShapeDtypeStruct(a.shape, F32) for a in (master, left, right, master)
        ] + [jax.ShapeDtypeStruct(master.shape, BF)]
    first = [
        jax.ShapeDtypeStruct((1, 1), F32),
        jax.ShapeDtypeStruct((1, CW), F32),
        jax.ShapeDtypeStruct((2, D), F32),
        jax.ShapeDtypeStruct((1, CW), F32),
        jax.ShapeDtypeStruct((2, D), F32),
    ]
    vmem = pl.BlockSpec(memory_space=pltpu.VMEM)
    smem = pl.BlockSpec(memory_space=pltpu.SMEM)
    hbm = pl.BlockSpec(memory_space=pltpu.HBM)
    return pl.pallas_call(
        functools.partial(shampoo_kernel, threshold),
        in_specs=[smem] + [vmem] * 9 + [hbm] * 30,
        out_specs=[vmem] * 5 + [hbm] * 31,
        out_shape=first + [jax.ShapeDtypeStruct(block_out.shape, BF)] + shapes,
        scratch_shapes=[pltpu.VMEM(a.shape, a.dtype) for a in flat]
        + [pltpu.VMEM(a.shape, a.dtype) for a in shapes]
        + [
            pltpu.SemaphoreType.DMA((30,)),
            pltpu.SemaphoreType.DMA((31,)),
        ],
        compiler_params=pltpu.CompilerParams(vmem_limit_bytes=60 << 20),
        name="shampoo",
    )(position, char_sums, small, gain.reshape(1, CW), gains, *word_sums, block_out, *flat)


def run_stages(stages):
    for _, run in sorted(stages, key=lambda stage: stage[0]):
        run()


def gather_setup(xs, out):
    rows = xs[0].shape[1]

    def own_of(i):
        if rows % 16 == 0:
            return out.at[pl.ds(pl.multiple_of(i * rows, 16), rows), :]
        return out.at[i]

    def put(mine):
        own, col = own_of(mine), 0
        for piece in xs:
            for t in range(piece.shape[0]):
                own[:, col : col + piece.shape[2]] = piece[t].astype(BF)
                col += piece.shape[2]

    return own_of, put


def gather_shape(arrays, n):
    rows = arrays[0].shape[1]
    cols = sum(a.shape[0] * a.shape[2] for a in arrays)
    shape = (n * rows, cols) if rows % 16 == 0 else (n, rows, cols)
    return jax.ShapeDtypeStruct(shape, BF), lambda a: a.reshape(n * rows, cols)


def dma_sems(count):
    return [pltpu.SemaphoreType.DMA((count,))] * 2


def call_remote(kernel, name, number, outs, scratch, inputs):
    vmem = pl.BlockSpec(memory_space=pltpu.VMEM)
    return pl.pallas_call(
        kernel,
        out_shape=outs,
        in_specs=[vmem] * len(inputs),
        out_specs=[vmem] * len(outs),
        scratch_shapes=scratch,
        compiler_params=pltpu.CompilerParams(
            collective_id=number, has_side_effects=True, vmem_limit_bytes=36 << 20
        ),
        name=name,
    )(*inputs)


def gather_char(mixer, lift, output, home, places):
    n, m = lax.axis_size("dp"), lax.axis_size("mp")
    slots, block_words = places.shape
    cap = -(-slots // n)
    total = n * cap
    share = block_words // m
    shape, shaper = gather_shape([mixer, lift], n)
    rows = output.shape[1]

    def kernel(
        mixer_in, lift_in, output_in, home_row, place_ref,
        mats, line, live, live_place, own_row, mixer_ref, lift_ref, output_ref, sent, came, local, *sems
    ):
        pairs = [tuple(sems[2 * t : 2 * t + 2]) for t in range(3)]
        i, j = lax.axis_index("dp"), lax.axis_index("mp")
        loads = [
            pltpu.make_async_copy(a, b, local.at[t])
            for t, (a, b) in enumerate(
                ((mixer_in, mixer_ref), (lift_in, lift_ref), (output_in, output_ref))
            )
        ]
        for load in loads:
            load.start()
        own_of, put = gather_setup([mixer_ref, lift_ref], mats)
        greet({"dp": n, "mp": m}, {"dp": i, "mp": j})
        for load in loads:
            load.wait()
        put(i)
        line[j] = output_ref[0].astype(BF)
        stages = pair_gather_stages(own_of, pairs[0], "dp", n, i, 0.0, 2.0)

        def send_places():
            before = lax.broadcasted_iota(jnp.int32, (slots, slots), 0)
            before = before < lax.broadcasted_iota(jnp.int32, (slots, slots), 1)
            home_col = tn(home_row[...].astype(F32).astype(BF), jnp.ones((1, 128), BF))[:, :slots]
            same = (home_col == home_row[...].astype(F32)) & before
            rank = jnp.sum(same.astype(F32), axis=0, keepdims=True)
            target = jnp.where(
                home_row[...] >= 0, home_row[...].astype(F32) * cap + rank, float(total)
            )
            hit = lax.broadcasted_iota(jnp.int32, (total, slots), 0).astype(F32) == target
            chosen = hit.astype(F32)
            placed = jnp.zeros((total, block_words), F32) - 1.0
            for s in range(slots):
                placed = jnp.where(
                    chosen[:, s : s + 1] > 0.0, place_ref[s : s + 1, :].astype(F32), placed
                )
            for p in range(n):
                sent[p] = placed[p * cap : (p + 1) * cap, :].astype(jnp.int32)
            came[i] = sent[i]

        def use_places():
            placed = jnp.concatenate([came[p] for p in range(n)], axis=0).astype(F32)
            held = jnp.max(placed, axis=1, keepdims=True) >= 0.0
            filled = jnp.where(held, jnp.ones((total, 128), F32), 0.0)
            lower = lax.broadcasted_iota(jnp.int32, (total, total), 1)
            lower = (lower < lax.broadcasted_iota(jnp.int32, (total, total), 0)).astype(BF)
            rank = nn(lower, filled.astype(BF))
            lane = lax.broadcasted_iota(jnp.int32, (total, 128), 1).astype(F32)
            chosen = jnp.where((rank == lane) & (filled > 0.0), 1.0, 0.0).astype(BF)
            live[...] = chosen
            high = jnp.floor((placed + 1.0) * (1.0 / 32.0))
            low = placed + 1.0 - high * 32.0
            high, low = high.astype(BF), low.astype(BF)
            found = tn(chosen, high) * 32.0 + tn(chosen, low) - 1.0
            live_place[...] = found[: live_place.shape[0], :].astype(jnp.int32)
            block = cap * share
            for p in range(n):
                col = lax.broadcasted_iota(jnp.int32, (block_words, block), 1) % share + j * share
                pick = (col == lax.broadcasted_iota(jnp.int32, (block_words, block), 0)).astype(BF)
                row = lax.broadcasted_iota(jnp.int32, (total, block), 0) - p * cap
                mine = row == lax.broadcasted_iota(jnp.int32, (total, block), 1) // share
                value = nn(high, pick) * 32.0 + nn(low, pick) - 1.0
                own_row[p] = jnp.sum(jnp.where(mine, value, 0.0), axis=0, keepdims=True).astype(jnp.int32)

        stages.append((0.1, send_places))
        stages += direct_stages(lambda p: sent.at[p], came, pairs[1], "dp", n, i, 0.2, lambda: None, 1.0)
        stages += direct_stages(lambda p: line.at[j], line, pairs[2], "mp", m, j, 0.3, lambda: None, 50.0)
        stages.append((1.5, use_places))
        run_stages(stages)

    vmem = pl.BlockSpec(memory_space=pltpu.VMEM)
    hbm = pl.BlockSpec(memory_space=pltpu.HBM)
    lines = max(16, -(-OWNER_BLOCKS // 8) * 8)
    results = pl.pallas_call(
        kernel,
        out_shape=[
            shape,
            jax.ShapeDtypeStruct((m, rows, D), BF),
            jax.ShapeDtypeStruct((total, 128), BF),
            jax.ShapeDtypeStruct((lines, block_words), jnp.int32),
            jax.ShapeDtypeStruct((n, 1, cap * share), jnp.int32),
        ],
        in_specs=[hbm] * 3 + [vmem] * 2,
        out_specs=[vmem] * 5,
        scratch_shapes=[
            pltpu.VMEM(mixer.shape, F32),
            pltpu.VMEM(lift.shape, F32),
            pltpu.VMEM(output.shape, F32),
            pltpu.VMEM((n, cap, block_words), jnp.int32),
            pltpu.VMEM((n, cap, block_words), jnp.int32),
            pltpu.SemaphoreType.DMA((3,)),
        ]
        + dma_sems(2 * max(n, m)) * 3,
        compiler_params=pltpu.CompilerParams(
            collective_id=0, has_side_effects=True, vmem_limit_bytes=60 << 20
        ),
        name="gather_char",
    )(mixer, lift, output, home.reshape(1, slots), places)
    return [shaper(results[0])] + list(results[1:])


def send_vectors(sent, to_live, share, project, upper, lower, output_line):
    n, m = lax.axis_size("dp"), lax.axis_size("mp")
    block = sent.shape[1]
    total = n * block
    kept = OWNER_BLOCKS * share
    made = [gather_shape([a], n) for a in (project, upper, lower)]
    made[0] = gather_shape([project], n)
    lead, line_rows, line_cols = output_line.shape
    aligned = line_rows % 16 == 0
    output_shape = (lead, n * line_rows, line_cols) if aligned else (n, lead, line_rows, line_cols)

    def kernel(sent, live, *refs):
        weights, line = refs[:3], refs[3]
        out, wides, output = refs[4], refs[5:8], refs[8]
        came, spread, *sems = refs[9:]
        pairs = [tuple(sems[2 * t : 2 * t + 2]) for t in range(8)]
        i, j = lax.axis_index("dp"), lax.axis_index("mp")
        greet({"dp": n, "mp": m}, {"dp": i, "mp": j})
        came[i] = sent[i]
        stages = []

        def make_spread():
            up = lax.broadcasted_iota(jnp.int32, (kept, 128), 0) // share
            up = (up == lax.broadcasted_iota(jnp.int32, (kept, 128), 1)).astype(BF)
            blocks = nt(up, live[...]).astype(BF)
            down = lax.broadcasted_iota(jnp.int32, (blocks.shape[1], total), 1) // share
            down = (down == lax.broadcasted_iota(jnp.int32, (blocks.shape[1], total), 0)).astype(BF)
            row = lax.broadcasted_iota(jnp.int32, (kept, total), 0) % share
            col = lax.broadcasted_iota(jnp.int32, (kept, total), 1) % share
            spread[...] = jnp.where(row == col, nn(blocks, down), 0.0).astype(BF)

        stages.append((0.4, make_spread))

        def compact(cols):
            out[j, :, cols] = nn(spread[...], came[:, :, cols].reshape(total, D // 2)).astype(BF)

        for half in range(2):
            cols = slice(half * (D // 2), (half + 1) * (D // 2))
            stages += direct_stages(
                lambda p, cols=cols: sent.at[p, :, cols], came, pairs[6 * half], "dp", n, i, 0.1 * half,
                functools.partial(compact, cols), 1.0 + half, cols,
            )
            stages += line_gather_stages(
                out, pairs[1 + 6 * half], "mp", m, j, 1.5 + 0.6 * half, 1.0, (slice(None), cols)
            )
        for t, (x, wide) in enumerate(zip(weights, wides)):
            own_of, put = gather_setup([x], wide)
            put(i)
            stages += pair_gather_stages(own_of, pairs[2 + t], "dp", n, i, 0.3, 2.0 * m + 0.5)
        if aligned:
            output_of = lambda d: output.at[:, pl.ds(pl.multiple_of(d * line_rows, 16), line_rows), :]
        else:
            output_of = lambda d: output.at[d]
        output_of(i)[...] = line[...]
        stages += pair_gather_stages(output_of, pairs[5], "dp", n, i, 0.3, 2.0 * m + 0.5)
        run_stages(stages)

    results = call_remote(
        kernel,
        "send_vectors",
        1,
        [jax.ShapeDtypeStruct((m, kept, D), BF)]
        + [shape for shape, _ in made]
        + [jax.ShapeDtypeStruct(output_shape, BF)],
        [pltpu.VMEM((n, block, D), BF), pltpu.VMEM((kept, total), BF)] + dma_sems(2 * max(n, m)) * 8,
        [sent, to_live, project, upper, lower, output_line],
    )
    output = results[4]
    if not aligned:
        output = output.transpose(1, 0, 2, 3)
    return (
        [results[0]]
        + [shaper(a) for (_, shaper), a in zip(made, results[1:4])]
        + [output.reshape(-1, line_cols)]
    )


def feed_step(mixed, stream, cotangent, output, gain, upper, lower, roots):
    n, m = lax.axis_size("dp"), lax.axis_size("mp")
    length, width = mixed.shape
    share = length // m
    made = [gather_shape([a], n) for a in roots]
    chip_shape = lambda a: (n // 2, 2, a.shape[0] // n, a.shape[1])

    def kernel(mixed_ref, stream_ref, cot, out_mat, gain_ref, upper_ref, lower_ref, *refs):
        roots_in, refs = refs[: len(roots)], refs[len(roots) :]
        hidden_ref, feed_ref, grad_hidden, grad_mixed, grad_output, gain_grad, up_sum, low_sum = refs[:8]
        roots_out, refs = refs[8 : 8 + len(roots)], refs[8 + len(roots) :]
        mix, part, up, low, held, total, swapped, up_held, up_came, low_held, low_came, *sems = refs
        pairs = [tuple(sems[2 * t : 2 * t + 2]) for t in range(7 + len(roots))]
        i, j = lax.axis_index("dp"), lax.axis_index("mp")
        greet({"dp": n, "mp": m}, {"dp": i, "mp": j})
        stages = []
        mix[j] = mixed_ref[...]
        for h, cut in enumerate(halves(length)):
            stages += line_gather_stages(
                mix, pairs[5 + len(roots) + h], "mp", m, j, -50.0 + 0.05 * h, 6.0, cut
            )

        def run_feed():
            grad_upper = jnp.zeros(upper_ref.shape, F32)
            grad_lower = jnp.zeros(lower_ref.shape, F32)
            for first in range(0, length, FEED_ROWS):
                rows = slice(first, first + FEED_ROWS)
                hidden, fed, part_rows, more_upper, more_lower = feed_rows(
                    [mix[p, rows, :] for p in range(m)], out_mat, stream_ref[rows, :], cot[rows, :],
                    gain_ref[...], upper_ref[...], lower_ref[...],
                )
                hidden_ref[rows, :] = hidden
                feed_ref[rows, :] = fed
                for p in range(FEED_ROWS // share):
                    part[first // share + p] = part_rows[p * share : (p + 1) * share]
                grad_upper = grad_upper + more_upper
                grad_lower = grad_lower + more_lower
            up[...] = grad_upper.astype(BF).reshape(up.shape)
            low[...] = grad_lower.astype(BF).reshape(low.shape)

        stages.append((-0.5, run_feed))
        for h, cut in enumerate(halves(share)):
            stages += line_part_stages(
                part, held, total, pairs[(0, 4 + len(roots))[h]], "mp", m, j, 0.05 * h, 6.0, 70.0 + 0.1 * h, cut
            )
        stages += pair_part_stages(up, up_held, up_came, up_sum, pairs[1], "dp", n, i, 0.1, 1.0)
        stages += pair_part_stages(low, low_held, low_came, low_sum, pairs[2], "dp", n, i, 0.1, 1.0)
        for t, (x, out) in enumerate(zip(roots_in, roots_out)):
            own_of, put = gather_setup([x], out)
            put(i)
            stages += pair_gather_stages(own_of, pairs[4 + t], "dp", n, i, -49.8, 72.5)

        def back():
            mine = pl.ds(pl.multiple_of(j * share, share), share)
            hidden_own = hidden_ref[mine, :]
            scale = rms_scale(hidden_own)
            grad = total[...]
            whole_grad = cot[mine, :].astype(F32) + norm_back(hidden_own, scale, gain_ref[...], grad)
            grad_hidden[...] = whole_grad
            gain_grad[...] = jnp.sum(hidden_own * scale * grad, axis=0, keepdims=True)
            attend = whole_grad.astype(BF)
            for p in range(m):
                swapped[p] = nt(attend, out_mat[p * width : (p + 1) * width, :]).astype(BF)
            grad_mixed[j] = swapped[j]

        def output_grad():
            mine = pl.ds(pl.multiple_of(j * share, share), share)
            attend = grad_hidden[...].astype(BF)
            for p in range(m):
                grad_output[p * width : (p + 1) * width, :] = tn(mix[p, mine, :], attend).astype(BF)

        stages += [(71.0, back), (73.0, output_grad)]
        stages += direct_stages(
            lambda p: swapped.at[p], grad_mixed, pairs[3], "mp", m, j, 72.0, lambda: None, 75.0
        )
        run_stages(stages)

    chips = lambda a: pltpu.VMEM(chip_shape(a), BF)
    block = lambda a: pltpu.VMEM(chip_shape(a)[:1] + chip_shape(a)[2:], BF)
    results = call_remote(
        kernel,
        "feed_step",
        4,
        [
            jax.ShapeDtypeStruct((length, D), F32),
            jax.ShapeDtypeStruct((length, D), BF),
            jax.ShapeDtypeStruct((share, D), F32),
            jax.ShapeDtypeStruct((m, share, width), BF),
            jax.ShapeDtypeStruct(output.shape, BF),
            jax.ShapeDtypeStruct((1, D), F32),
            jax.ShapeDtypeStruct(chip_shape(upper)[2:], F32),
            jax.ShapeDtypeStruct(chip_shape(lower)[2:], F32),
        ]
        + [shape for shape, _ in made],
        [
            pltpu.VMEM((m, length, width), BF),
            pltpu.VMEM((m, share, D), BF),
            chips(upper),
            chips(lower),
            pltpu.VMEM((2, m, share, D), BF),
            pltpu.VMEM((share, D), F32),
            pltpu.VMEM((m, share, width), BF),
            block(upper),
            block(upper),
            block(lower),
            block(lower),
        ]
        + dma_sems(2 * max(n, m)) * (7 + len(roots)),
        [mixed, stream, cotangent, output, gain.reshape(1, D), upper, lower] + roots,
    )
    return list(results[:8]) + [shaper(a) for (_, shaper), a in zip(made, results[8:])]


def stream_grads(probs, qkv, grad_mixed, normed, project_mat, stream, grad_hidden, gain, own_row, sums, grad_output, fed, hidden):
    n, m = lax.axis_size("dp"), lax.axis_size("mp")
    share = stream.shape[0] // m
    width = project_mat.shape[1] // 3
    heads = width // HD
    block = own_row.shape[2]
    total_words = n * block
    words = share * m
    project_chips = (n // 2, 2, project_mat.shape[0] // n, project_mat.shape[1])
    parts = [jax.ShapeDtypeStruct(project_chips, BF), by_chip(grad_output)]
    chunk = lambda a: jax.ShapeDtypeStruct((1,) + a.shape[-2:], F32)
    made = [gather_shape([chunk(a)], n) for a in (sums[0], sums[1], parts[0], parts[1])]

    def kernel(
        probs_ref, qkv_ref, mixed_grad, normed_ref, mat_ref, stream_ref, hidden_ref, gain_ref, row_ref, up, low, output, fed_ref, hidden_in, *refs
    ):
        out, gain_grad, came, block_own, up_out, low_out, project_out, output_out = refs[:8]
        (part, project, head_grads, key_sum, value_sum, held, total, project_sum, output_sum, line_held, picked, hits,
         p_held, p_came, o_held, o_came, fed_held, fed_sum, *sems) = refs[8:]
        pairs = [tuple(sems[2 * t : 2 * t + 2]) for t in range(15)]
        i, j = lax.axis_index("dp"), lax.axis_index("mp")
        greet_start({"dp": n, "mp": m}, {"dp": i, "mp": j})
        attention_back(width, probs_ref, qkv_ref, mixed_grad, head_grads, key_sum, value_sum)
        grads = head_grads[...]
        part[...] = nt(grads, mat_ref[...]).astype(BF).reshape(part.shape)
        project[...] = tn(normed_ref[...], grads).astype(BF).reshape(project.shape)
        greet_wait({"dp": n, "mp": m})
        stages = []
        for h, cut in enumerate(halves(share)):
            stages += line_part_stages(
                part, held, total, pairs[(0, 12)[h]], "mp", m, j, 0.05 * h, 6.0, 70.0 + 0.1 * h, cut
            )
        stages += pair_part_stages(project, p_held, p_came, project_sum.at[0], pairs[1], "dp", n, i, 0.1, 1.0)
        stages += pair_part_stages(output, o_held, o_came, output_sum.at[0], pairs[2], "dp", n, i, 0.1, 1.0)
        up_of, put_up = gather_setup([up], up_out)
        low_of, put_low = gather_setup([low], low_out)
        put_up(i)
        put_low(i)
        stages += pair_gather_stages(up_of, pairs[3], "dp", n, i, 2.0, 71.9)
        stages += pair_gather_stages(low_of, pairs[4], "dp", n, i, 2.0, 71.9)

        def back():
            mine = pl.ds(pl.multiple_of(j * share, share), share)
            stream_own = stream_ref[mine, :]
            scale = rms_scale(stream_own)
            grad = total[...]
            out[j] = (hidden_ref[...] + norm_back(stream_own, scale, gain_ref[...], grad)).astype(BF)
            gain_grad[...] = jnp.sum(stream_own * scale * grad, axis=0, keepdims=True)

        stages.append((71.0, back))
        for half in range(2):
            cols = slice(half * (D // 2), (half + 1) * (D // 2))
            stages += [
                (when if when < 90 else 199.0, run)
                for when, run in line_gather_stages(
                    out, pairs[5 + 5 * half], "mp", m, j, 72.0 + 0.05 * half, 0.1, (slice(None), cols)
                )
            ]
        project_of, put_project = gather_setup([project_sum], project_out)
        output_of, put_output = gather_setup([output_sum], output_out)

        def put_sums():
            put_project(i)
            line_held[j] = output_sum[0].astype(BF)

        target = i // (n // m)

        def line_send():
            @pl.when(j != target)
            def _():
                remote(line_held.at[j], line_held.at[j], pairs[7], j, "mp", target).start()

        def line_done():
            @pl.when(j != target)
            def _():
                remote(line_held.at[j], line_held.at[j], pairs[7], j, "mp", target).wait_send()

            @pl.when(j == target)
            def _():
                for p in range(m):

                    @pl.when(j != p)
                    def _(p=p):
                        remote(line_held.at[p], line_held.at[p], pairs[7], p, "mp", target).wait_recv()

                summed = line_held[0].astype(F32)
                for p in range(1, m):
                    summed = summed + line_held[p].astype(F32)
                output_sum[0] = summed

            put_output(i)

        stages = [(60.0 if when == 80.0 else when, run) for when, run in stages]
        stages.append((72.01, put_sums))
        stages += [
            (when, run)
            for when, run in zip(
                (72.02, 72.25, 198.0),
                [run for _, run in pair_gather_stages(project_of, pairs[6], "dp", n, i, 0, 0)],
            )
        ]
        late_line = 72.0 + 0.1 * 2 * m
        stages += [(72.03, line_send), (late_line + 0.01, line_done)]
        stages += [
            (when, run)
            for when, run in zip(
                (late_line + 0.02, 81.5, 198.5),
                [run for _, run in pair_gather_stages(output_of, pairs[8], "dp", n, i, 0, 0)],
            )
        ]

        def make_hits():
            lane = lax.broadcasted_iota(jnp.int32, (block, 128), 1).astype(F32)
            ones = jnp.ones((1, 128), BF)
            for p in range(n):
                place = row_ref[p].astype(F32) + 1.0
                high = jnp.floor(place * (1.0 / 32.0))
                low = place - high * 32.0
                col = tn(high.astype(BF), ones) * 32.0 + tn(low.astype(BF), ones) - 1.0
                for t in range(words // 128):
                    hits[p * block : (p + 1) * block, t * 128 : (t + 1) * 128] = (
                        col == lane + 128.0 * t
                    ).astype(BF)

        stages.append((2.5, make_hits))

        def pick(half):
            cols = slice(half * (D // 2), (half + 1) * (D // 2))
            rows = nn(hits[...], out[:, :, cols].reshape(words, D // 2)).astype(BF)
            picked[:, :, cols] = rows.reshape(n, block, D // 2)
            for d in range(1, n):
                peer = lax.rem(i + d, n)
                remote(
                    picked.at[peer, :, cols], came.at[i, :, cols], pairs[9 + 2 * half], d, "dp", peer
                ).start()
            came[i, :, cols] = picked[i, :, cols]

        for half in range(2):
            stages.append((72.011 + 0.1 * (m - 1) + 0.05 * half, functools.partial(pick, half)))

        def place():
            for half in range(2):
                cols = slice(half * (D // 2), (half + 1) * (D // 2))
                for d in range(1, n):
                    remote(
                        picked.at[i, :, cols], came.at[i, :, cols], pairs[9 + 2 * half], d, "dp", i
                    ).wait()

        stages.append((82.0, place))
        for h, cut in enumerate(halves(share)):
            stages += line_part_stages(
                fed_ref, fed_held, fed_sum, pairs[13 + h], "mp", m, j, 73.5 + 0.005 * h, 0.1, 90.0 + h, cut
            )

        def add_hidden():
            mine = pl.ds(pl.multiple_of(j * share, share), share)
            block_own[...] = (hidden_in[mine, :] + fed_sum[...]).astype(BF)

        stages.append((92.0, add_hidden))
        run_stages(stages)

    held_of = lambda a: pltpu.VMEM(a.shape[:1] + a.shape[2:], BF)
    results = call_remote(
        kernel,
        "stream_grads",
        6,
        [
            jax.ShapeDtypeStruct((m, share, D), BF),
            jax.ShapeDtypeStruct((1, D), F32),
            jax.ShapeDtypeStruct((n, block, D), BF),
            jax.ShapeDtypeStruct((share, D), BF),
        ]
        + [shape for shape, _ in made],
        [
            pltpu.VMEM((m, share, D), BF),
            pltpu.VMEM(project_chips, BF),
            pltpu.VMEM(qkv.shape, BF),
            pltpu.VMEM((heads, words, HD), F32),
            pltpu.VMEM((heads, words, HD), F32),
            pltpu.VMEM((2, m, share, D), BF),
            pltpu.VMEM((share, D), F32),
            pltpu.VMEM((1,) + parts[0].shape[2:], F32),
            pltpu.VMEM((1,) + parts[1].shape[2:], F32),
            pltpu.VMEM((m,) + parts[1].shape[2:], BF),
            pltpu.VMEM((n, block, D), BF),
            pltpu.VMEM((total_words, words), BF),
            held_of(parts[0]),
            held_of(parts[0]),
            held_of(parts[1]),
            held_of(parts[1]),
        ]
        + [pltpu.VMEM((2, m, share, D), BF), pltpu.VMEM((share, D), F32)]
        + dma_sems(2 * max(n, m)) * 15,
        [
            probs,
            qkv,
            grad_mixed,
            normed,
            project_mat,
            stream,
            grad_hidden,
            gain.reshape(1, D),
            own_row,
            sums[0][None],
            sums[1][None],
            parts[1],
            fed,
            hidden,
        ],
    )
    return list(results[:4]) + [shaper(a) for (_, shaper), a in zip(made, results[4:])]


def local(
    word_inputs,
    character_embeddings,
    cotangent,
    char_count,
    word_place,
    block_home,
    documents,
    char_gain,
    word_gains,
    char_mixer,
    char_mixer_left,
    char_mixer_right,
    char_mixer_left_root,
    char_mixer_right_root,
    char_lift,
    char_lift_left,
    char_lift_right,
    char_lift_left_root,
    char_lift_right_root,
    word_project,
    word_project_left,
    word_project_right,
    word_project_left_root,
    word_project_right_root,
    word_output,
    word_output_left,
    word_output_right,
    word_output_left_root,
    word_output_right_root,
    feed_upper,
    feed_upper_left,
    feed_upper_right,
    feed_upper_left_root,
    feed_upper_right_root,
    feed_lower,
    feed_lower_left,
    feed_lower_right,
    feed_lower_left_root,
    feed_lower_right_root,
):
    slot_count, share_rows = (character_embeddings.shape[0], character_embeddings.shape[1])
    peer_count = lax.axis_size("dp")
    part_count = lax.axis_size("mp")
    owner_index = lax.axis_index("dp")
    words_dev = word_inputs.shape[0] * word_inputs.shape[1]
    position = jnp.stack([owner_index, lax.axis_index("mp")]).astype(jnp.int32)

    char_whole, output_line, live, live_place, own_row = gather_char(
        char_mixer, char_lift, word_output, block_home, word_place
    )
    word_vectors, kept, pooled, msum = char_forward(
        character_embeddings, block_home, char_count, char_gain, char_whole, peer_count
    )
    live_vectors, project_mat, upper_mat, lower_mat, output_mat = send_vectors(
        word_vectors.reshape(peer_count, -1, D),
        live,
        share_rows,
        word_project.reshape((3,) + word_project.shape[2:]),
        feed_upper,
        feed_lower,
        output_line,
    )
    stream, normed_one, qkv, probs, mixed = word_forward(
        live_vectors,
        live_place,
        word_inputs.reshape(words_dev, D),
        documents,
        word_gains[0],
        project_mat,
    )
    hidden, feed_part, grad_hidden, grad_mixed, grad_output_mat, gain_two, part_upper, part_lower, *every_root = feed_step(
        mixed,
        stream,
        cotangent.reshape(words_dev, D),
        output_mat,
        word_gains[1],
        upper_mat,
        lower_mat,
        [
            char_mixer_right_root,
            char_lift_right_root,
            word_project_right_root.reshape((3,) + word_project_right_root.shape[2:]),
            word_output_right_root,
            feed_upper_right_root,
            feed_lower_right_root,
        ],
    )
    mixer_root, lift_root, project_root, output_root, upper_root, lower_root = every_root
    grad_words, gain_one, grad_vectors, block_own, sum_upper, sum_lower, sum_project, sum_output = stream_grads(
        probs,
        qkv,
        grad_mixed.reshape(words_dev, -1),
        normed_one,
        project_mat,
        stream,
        grad_hidden,
        word_gains[0],
        own_row,
        (part_upper, part_lower),
        grad_output_mat,
        feed_part.reshape(part_count, words_dev // part_count, D),
        hidden,
    )
    char_embeds_gradient, char_grads, grad_char_gain, grad_stream = char_backward(
        character_embeddings, block_home, char_count, char_gain, char_whole, kept, pooled, msum,
        grad_vectors.reshape(-1, share_rows, D),
        grad_words,
        peer_count,
    )
    word_sums = (sum_project, sum_output, sum_upper, sum_lower)
    char_sums, small_sums, block_out = sum_char_grads(
        char_grads, (grad_char_gain, gain_one, gain_two), word_sums, word_output.shape[1] * peer_count,
        block_own,
    )
    parameter_count = (
        sum(
            part_count * w.size * peer_count
            for w in (word_project, word_output, feed_upper, feed_lower)
        )
        + peer_count * (char_mixer.size + char_lift.size)
        + char_gain.size
        + word_gains.size
    )
    flat = lambda a: a.reshape((-1,) + a.shape[-2:])
    results = shampoo(
        0.5 * math.sqrt(parameter_count),
        position,
        char_sums,
        small_sums,
        char_gain,
        word_gains,
        word_sums,
        block_out,
        [
            tuple(flat(a) for a in group[:4]) + (group[4],)
            for group in (
                (char_mixer, char_mixer_left, char_mixer_right, char_mixer_left_root, mixer_root),
                (char_lift, char_lift_left, char_lift_right, char_lift_left_root, lift_root),
                (word_project, word_project_left, word_project_right, word_project_left_root, project_root),
                (word_output, word_output_left, word_output_right, word_output_left_root, output_root),
                (feed_upper, feed_upper_left, feed_upper_right, feed_upper_left_root, upper_root),
                (feed_lower, feed_lower_left, feed_lower_right, feed_lower_left_root, lower_root),
            )
        ],
    )
    norm, gain_grad, gains_grad, gain_new, gains_new, block_out = results[:6]
    stepped = []
    for t, group in enumerate(
        (
            (char_mixer, char_mixer_left, char_mixer_right),
            (char_lift, char_lift_left, char_lift_right),
            (word_project, word_project_left, word_project_right),
            (word_output, word_output_left, word_output_right),
            (feed_upper, feed_upper_left, feed_upper_right),
            (feed_lower, feed_lower_left, feed_lower_right),
        )
    ):
        master, left, right = group
        stepped += [
            a.reshape(b.shape)
            for a, b in zip(results[6 + 5 * t : 11 + 5 * t], (master, left, right, master, master))
        ]
    return (
        block_out.reshape(word_inputs.shape),
        grad_stream.reshape(word_inputs.shape),
        char_embeds_gradient,
        gain_grad[0],
        gains_grad,
        gain_new[0],
        gains_new,
        norm[0, 0],
        *stepped,
    )


def solution(mesh):
    placed = (
        P("dp", None, None),
        P("dp", "mp", None, None),
        P("dp", None, None),
        P("dp", "mp"),
        P("dp", None),
        P("dp"),
        P("dp", None),
        P(),
        P(),
        P(None, "dp", None),
        P(None, "dp", None),
        P(None, "dp", None),
        P(None, "dp", None),
        P(None, "dp", None),
        P(None, "dp", None),
        P(None, "dp", None),
        P(None, "dp", None),
        P(None, "dp", None),
        P(None, "dp", None),
        P(None, "mp", "dp", None),
        P(None, "mp", "dp", None),
        P(None, "mp", "dp", None),
        P(None, "mp", "dp", None),
        P(None, "mp", "dp", None),
        P("mp", "dp", None),
        P("mp", "dp", None),
        P("mp", "dp", None),
        P("mp", "dp", None),
        P("mp", "dp", None),
        P("mp", "dp", None),
        P("mp", "dp", None),
        P("mp", "dp", None),
        P("mp", "dp", None),
        P("mp", "dp", None),
        P("mp", "dp", None),
        P("mp", "dp", None),
        P("mp", "dp", None),
        P("mp", "dp", None),
        P("mp", "dp", None),
    )
    return jax.shard_map(
        local,
        mesh=mesh,
        in_specs=placed,
        out_specs=(
            P("dp", None, None),
            P("dp", None, None),
            P("dp", "mp", None, None),
            P(),
            P(),
            P(),
            P(),
            P(),
            P(None, "dp", None),
            P(None, "dp", None),
            P(None, "dp", None),
            P(None, "dp", None),
            P(None, "dp", None),
            P(None, "dp", None),
            P(None, "dp", None),
            P(None, "dp", None),
            P(None, "dp", None),
            P(None, "dp", None),
            P(None, "mp", "dp", None),
            P(None, "mp", "dp", None),
            P(None, "mp", "dp", None),
            P(None, "mp", "dp", None),
            P(None, "mp", "dp", None),
            P("mp", "dp", None),
            P("mp", "dp", None),
            P("mp", "dp", None),
            P("mp", "dp", None),
            P("mp", "dp", None),
            P("mp", "dp", None),
            P("mp", "dp", None),
            P("mp", "dp", None),
            P("mp", "dp", None),
            P("mp", "dp", None),
            P("mp", "dp", None),
            P("mp", "dp", None),
            P("mp", "dp", None),
            P("mp", "dp", None),
            P("mp", "dp", None),
        ),
        check_vma=False,
    )
```
